32 devices in a mesh: groups: 2 (over y), shard: 4 (over z), feat: 2 (over x), rep: 2 (over core).
Axes of the slice: x: 2, y: 2, z: 4, core: 2. Of those that a mesh axis runs over, the one named last changes fastest.
Arguments:
- train: bfloat16 [8192, 4096], P(('groups', 'shard'), 'feat'), parts along dimension 0, may hold values from -6 to 6
- cluster_ids: int32 [8192], P('groups'), parts along dimension 0, may hold values from 0 to 3, as said below
- precond: bfloat16 [8, 4096, 4096], P(('groups', 'shard'), None, ('feat', 'rep')), parts along dimension 0, may hold values from -0.09375 to 0.09375
- query_store: bfloat16 [16, 128, 4096], P('shard', None, ('feat', 'rep')), may hold values from -0.09375 to 0.09375
- block_slot: int32 [16], replicated, may hold values from 0 to 15, as said below
- pattern: int32 [4, 4], replicated, may hold values from 0 to 15, as said below
Outputs:
- scores: float32 [8, 512, 1024], P(('groups', 'shard'), ('feat', 'rep')), parts along dimension 0
The draws below stay inside these ranges and needn't reach their ends.
There are 2 independent parts, one for each index of `groups`. The reference program is written for one: setup_inputs(seed, part) draws one part's arguments, and reference() takes and returns one part's arrays. A program takes and returns all parts, laid end to end along the dimension named above; an argument that names none is the same for every part. Nothing has to cross between parts.
Inputs may be any that keep to these rules, and one draw needn't show every extreme that they name: `cluster_ids`: every cluster is named by exactly 1024 rows. Among the 1024 rows of one index of shard, each cluster is named between 128 and 384 times, and on every index some cluster exactly 384 times. `block_slot`: a permutation; block b is the block of index block_slot[b] // 4 of shard. `pattern`: each cluster lists 4 blocks stored on 4 different indices of shard.
All inputs are finite; a program needn't handle non-finite values.
Results may differ from the reference program's by a relative error of at most 0.0029.
Values may be sent and summed in bfloat16 or wider, within the bound.
No kernel may reach another device: no remote copies, remote signals or barrier semaphores. Data moves between devices by JAX's collectives and lax.ppermute only.
A program may use at most 128 MiB of HBM per device.

```python
import jax
import jax.numpy as jnp
from jax import lax

D = 4096
ROWS_DEV = 1024
QB = 128
LIST = 4
QBLK_DEV = 4
CLUSTERS = 4
ROWS = 4096
NQB = 16
BASE = 256
SURPLUS = 128


def slot_table(key):
    return jax.random.permutation(key, NQB).astype(jnp.int32)


def draw_block_slot(key, part):
    storage = slot_table(key)
    return storage


def draw_pattern(key, part):
    storage = slot_table(key)
    key = jax.random.fold_in(key, 7)
    inverse = jnp.argsort(storage).astype(jnp.int32)
    owner_keys = jax.random.split(jax.random.fold_in(key, 1), CLUSTERS)
    owners = jax.vmap(lambda subkey: jax.random.permutation(subkey, CLUSTERS)[:LIST])(owner_keys).astype(jnp.int32)
    within = jax.random.randint(jax.random.fold_in(key, 2), (CLUSTERS, LIST), 0, QBLK_DEV).astype(jnp.int32)
    stored = owners * QBLK_DEV + within
    return inverse[stored].astype(jnp.int32)


def draw_cluster_ids(key, part):
    key = jax.random.fold_in(key, 5)
    shifted = jax.random.permutation(jax.random.fold_in(key, 1), CLUSTERS).astype(jnp.int32)
    labels = jnp.arange(CLUSTERS, dtype=jnp.int32)
    heavy_one = (labels[None, :] == shifted[:, None]).astype(jnp.int32)
    light_one = (labels[None, :] == jnp.roll(shifted, -1)[:, None]).astype(jnp.int32)
    counts = BASE + SURPLUS * heavy_one - SURPLUS * light_one
    upper_ends = jnp.cumsum(counts, axis=1)
    position = jnp.arange(ROWS_DEV, dtype=jnp.int32)
    ordered = jnp.sum((position[None, :, None] >= upper_ends[:, None, :]).astype(jnp.int32), axis=2)
    shuffle_keys = jax.random.split(jax.random.fold_in(key, 2), CLUSTERS)
    shuffled = jax.vmap(lambda subkey, line: jax.random.permutation(subkey, line))(shuffle_keys, ordered)
    return shuffled.reshape(-1).astype(jnp.int32)


def levels(key, extent, cuts, smallest, largest):
    def one(dim, shards_of):
        draws = jax.random.uniform(jax.random.fold_in(jax.random.fold_in(key, 6), dim), (shards_of,), jnp.float32, smallest / len(cuts), largest / len(cuts))
        return jnp.repeat(jnp.exp(draws), extent[dim] // shards_of).reshape((-1,) + (1,) * (len(extent) - dim - 1))

    level = one(*cuts[0])
    for cut in cuts[1:]:
        level = level * one(*cut)
    return level


def normal_values(rng, dims, spread, limit, pieces=(), held_as=jnp.bfloat16):
    array = jax.random.normal(rng, dims, jnp.float32) * spread
    if len(pieces) > 0:
        array = levels(rng, dims, pieces, -0.22, 0.18) * array
    return jnp.clip(array, min=-limit, max=limit).astype(held_as)


def setup_inputs(seed: int = 0, part: int = 0) -> dict:
    keys = jax.random.split(jax.random.key(seed), 7)
    part_splits = jax.random.split(jax.random.fold_in(keys[6], part), 7)
    train = normal_values(part_splits[0], (ROWS, D), 1.0, 6.0, ((0, 4), (1, 2)))
    cluster_ids = draw_cluster_ids(jax.random.fold_in(jax.random.fold_in(keys[6], part), 71), part)
    precond = normal_values(part_splits[2], (CLUSTERS, D, D), D ** -0.5, 0.09375, ((0, 4), (2, 4)))
    query_store = normal_values(keys[3], (NQB, QB, D), D ** -0.5, 0.09375, ((0, 4), (2, 4)))
    block_slot = draw_block_slot(jax.random.fold_in(keys[6], 71), part)
    pattern = draw_pattern(jax.random.fold_in(keys[6], 71), part)
    return dict(train=train, cluster_ids=cluster_ids, precond=precond, query_store=query_store, block_slot=block_slot, pattern=pattern)


def reference(train, cluster_ids, precond, query_store, block_slot, pattern):
    ordering = jnp.argsort(cluster_ids, stable=True).astype(jnp.int32)
    grouped = train[ordering].reshape(CLUSTERS, ROWS_DEV, D)

    def score_cluster(operands):
        row_block, matrix, listed = operands
        precon = jnp.dot(row_block, matrix, preferred_element_type=jnp.float32).astype(jnp.bfloat16)
        chosen = query_store[block_slot[listed]].reshape(LIST * QB, D)
        return lax.dot_general(chosen, precon, (((1,), (1,)), ((), ())), preferred_element_type=jnp.float32)

    return lax.map(score_cluster, (grouped, precond, pattern))
```

```python
import jax
import jax.numpy as jnp
from jax import lax
from jax.sharding import PartitionSpec as P


def shift(x, axis, size, by):
    return lax.ppermute(x, axis, [(i, (i + by) % size) for i in range(size)])


def contract(a, b):
    return lax.dot_general(a, b, (((1,), (1,)), ((), ())), preferred_element_type=jnp.float32)


def body(train, cluster_ids, precond, query_store, block_slot, pattern):
    n_group, n_shard = lax.axis_size("groups"), lax.axis_size("shard")
    n_feat, n_rep = lax.axis_size("feat"), lax.axis_size("rep")
    group, me = lax.axis_index("groups"), lax.axis_index("shard")
    feat, rep = lax.axis_index("feat"), lax.axis_index("rep")
    rows = train.shape[0]
    base = rows // n_shard
    capacity = base + base // 2
    columns = train.shape[1] // n_rep
    bf16 = jnp.bfloat16

    local_blocks, block_rows, width = query_store.shape
    n_list = pattern.shape[1]
    part = block_rows // n_group
    slots = block_slot[pattern]
    owners, places = slots // local_blocks, slots % local_blocks
    wanted = jnp.sum(jnp.where(owners == me, places, 0), axis=1)
    share = lax.dynamic_slice_in_dim(query_store, group * part, part, 1)

    def block_for(target):
        index = lax.dynamic_index_in_dim(wanted, target, 0, keepdims=False)
        return lax.dynamic_index_in_dim(share, index, 0, keepdims=False)

    parts_in = [block_for(me)]
    for d in range(1, n_shard):
        parts_in.append(shift(block_for((me + d) % n_shard), "shard", n_shard, d))
    arrived = jnp.stack(parts_in)
    my_owners = lax.dynamic_index_in_dim(owners, me, 0, keepdims=False)
    own_part = arrived[(me - my_owners) % n_shard]
    chosen = jnp.zeros((n_list, n_group, part, width), bf16)
    chosen = lax.dynamic_update_slice_in_dim(chosen, own_part[:, None], group, 1)
    for d in range(1, n_group):
        other = shift(own_part, "groups", n_group, d)
        chosen = lax.dynamic_update_slice_in_dim(chosen, other[:, None], (group - d) % n_group, 1)
    chosen = chosen.reshape(n_list * block_rows, width)

    labels = jnp.arange(n_shard, dtype=jnp.int32)
    own_ids = lax.dynamic_slice_in_dim(cluster_ids, me * rows, rows)
    onehot = (own_ids[:, None] == labels[None, :]).astype(jnp.int32)
    rank = jnp.sum((jnp.cumsum(onehot, axis=0) - onehot) * onehot, axis=1)
    half = lax.dynamic_slice_in_dim(train, rep * columns, columns, 1)

    def pack(target):
        goal = jnp.where(own_ids == target, rank, -1)
        pick = (jnp.arange(capacity, dtype=jnp.int32)[:, None] == goal[None, :]).astype(bf16)
        return jnp.dot(pick, half, preferred_element_type=jnp.float32).astype(bf16)

    received = [pack(me)]
    for d in range(1, n_shard):
        received.append(shift(pack((me + d) % n_shard), "shard", n_shard, d))

    id_grid = cluster_ids.reshape(n_shard, rows)
    counts = jnp.sum((id_grid == me).astype(jnp.int32), axis=1)
    starts = jnp.cumsum(counts) - counts

    matrix = precond[0]

    def weights(f, r):
        block = lax.dynamic_slice_in_dim(matrix, (f * n_rep + r) * columns, columns, 0)
        return contract(chosen, block)

    def summed_over_rep(f):
        away = [shift(weights(f, (rep + d) % n_rep), "rep", n_rep, d) for d in range(1, n_rep)]
        return sum(away, weights(f, rep))

    sent = [
        shift(summed_over_rep((feat + d) % n_feat).astype(bf16), "feat", n_feat, d)
        for d in range(1, n_feat)
    ]
    weight = summed_over_rep(feat)
    for piece in sent:
        weight = weight + piece.astype(jnp.float32)
    high = lax.reduce_precision(weight, 8, 7)
    low = (weight - high).astype(bf16)
    high = high.astype(bf16)

    grouped = jnp.zeros((rows, columns), jnp.float32)
    position = jnp.arange(rows, dtype=jnp.int32)
    for d in range(n_shard):
        source = (me - d) % n_shard
        count, start = counts[source], starts[source]
        offset = position - start
        offset = jnp.where((offset >= 0) & (offset < count), offset, -1)
        pick = (offset[:, None] == jnp.arange(capacity, dtype=jnp.int32)[None, :]).astype(bf16)
        grouped = grouped + jnp.dot(pick, received[d], preferred_element_type=jnp.float32)
    grouped = grouped.astype(bf16)
    scores = contract(high, grouped) + contract(low, grouped)
    share_rows = scores.shape[0] // (n_feat * n_rep)
    scores = scores.reshape(n_feat, n_rep, share_rows, rows)
    total = lax.dynamic_index_in_dim(scores, rep, 1, keepdims=False)
    for d in range(1, n_rep):
        away = lax.dynamic_index_in_dim(scores, (rep + d) % n_rep, 1, keepdims=False)
        total = total + shift(away, "rep", n_rep, d)
    result = lax.dynamic_index_in_dim(total, feat, 0, keepdims=False)
    for d in range(1, n_feat):
        away = lax.dynamic_index_in_dim(total, (feat + d) % n_feat, 0, keepdims=False)
        result = result + shift(away, "feat", n_feat, d)
    return result[None]


def solution(mesh):
    return jax.shard_map(
        body,
        mesh=mesh,
        in_specs=(
            P(("groups", "shard"), "feat"),
            P("groups"),
            P(("groups", "shard"), None, ("feat", "rep")),
            P("shard", None, ("feat", "rep")),
            P(),
            P(),
        ),
        out_specs=P(("groups", "shard"), ("feat", "rep"), None),
        check_vma=False,
    )
```

```python
import functools

import jax
import jax.numpy as jnp
from jax import lax
from jax.experimental import pallas as pl
from jax.experimental.pallas import tpu as pltpu
from jax.sharding import PartitionSpec as P

F32, BF16, I32 = jnp.float32, jnp.bfloat16, jnp.int32
VMEM = pl.BlockSpec(memory_space=pltpu.VMEM)
SMEM = pl.BlockSpec(memory_space=pltpu.SMEM)
PARAMS = pltpu.CompilerParams(vmem_limit_bytes=50 * 2**20)
LANES = 128


def shift(x, axis, size, by):
    return lax.ppermute(x, axis, [(i, (i + by) % size) for i in range(size)])


def swap(x, axis, size, bit):
    return lax.ppermute(x, axis, [(i, i ^ bit) for i in range(size)])


def dot(a, b):
    return jnp.dot(a, b, preferred_element_type=F32)


def cost(flops, nbytes):
    return pl.CostEstimate(flops=int(flops), bytes_accessed=int(nbytes), transcendentals=0)


def pick_queries(query_store, block_slot, pattern, n_group):
    local_blocks, block_rows, width = query_store.shape
    n_cluster, n_list = pattern.shape
    part = block_rows // n_group

    def place(t, pattern_ref, slot_ref):
        me = lax.axis_index("shard")
        found = jnp.int32(0)
        for k in range(n_list):
            slot = slot_ref[pattern_ref[t * n_list + k]]
            hit = (lax.div(slot, jnp.int32(local_blocks)) == me).astype(I32)
            found = found + hit * lax.rem(slot, jnp.int32(local_blocks))
        return found, lax.axis_index("groups"), 0

    def kernel(pattern_ref, slot_ref, in_ref, out_ref):
        out_ref[...] = in_ref[...]

    return pl.pallas_call(
        kernel,
        grid_spec=pltpu.PrefetchScalarGridSpec(
            num_scalar_prefetch=2,
            grid=(n_cluster,),
            in_specs=[pl.BlockSpec((1, part, width), place)],
            out_specs=pl.BlockSpec((1, part, width), lambda t, p, s: (t, 0, 0)),
        ),
        out_shape=jax.ShapeDtypeStruct((n_cluster, part, width), BF16),
        cost_estimate=cost(0, 4 * n_cluster * part * width),
        compiler_params=PARAMS,
        name="pick_queries",
    )(pattern.reshape(-1), block_slot, query_store)


def join_queries(parts, block_slot, pattern, local_blocks, n_feat, n_rep):
    n_group = len(parts)
    n_cluster, part, width = parts[0].shape
    n_list = pattern.shape[1]
    total = n_list * n_group * part
    share = total // (n_feat * n_rep)
    unit = min(share, part)

    def kernel(pattern_ref, slot_ref, *refs):
        out_ref = refs[-1]
        me, group = lax.axis_index("shard"), lax.axis_index("groups")
        for k in range(n_list):
            owner = lax.div(slot_ref[pattern_ref[me * n_list + k]], jnp.int32(local_blocks))
            for d in range(n_group):
                origin = lax.rem(group + (n_group - d), jnp.int32(n_group))
                for u in range(part // unit):
                    first = (k * n_group + origin) * part + u * unit
                    chunk = lax.div(first, jnp.int32(share))
                    goal = lax.rem(chunk, jnp.int32(n_rep)) * n_feat + lax.div(chunk, jnp.int32(n_rep))
                    goal = goal * share + lax.rem(first, jnp.int32(share))
                    out_ref[pl.ds(pl.multiple_of(goal, unit), unit), :] = refs[d][owner, u * unit:(u + 1) * unit, :]

    return pl.pallas_call(
        kernel,
        in_specs=[SMEM, SMEM] + [VMEM] * n_group,
        out_specs=VMEM,
        out_shape=jax.ShapeDtypeStruct((total, width), BF16),
        cost_estimate=cost(0, 4 * total * width),
        compiler_params=PARAMS,
        name="join_queries",
    )(pattern.reshape(-1), block_slot, *parts)


def pack_rows(train, ids, columns, bulk, extra):
    rows = train.shape[0]
    lines = rows // LANES
    n_shard = ids.shape[0] // lines
    tile = 128 if extra else bulk

    def kernel(ids_ref, train_ref, bulk_ref, *rest):
        extra_refs, goal_ref = rest[:-1], rest[-1]
        own = ids_ref[...]
        masks = [(own == c).astype(F32) for c in range(n_shard)]
        stacked = jnp.concatenate(masks, axis=0).astype(BF16)
        lane_from = lax.broadcasted_iota(I32, (LANES, LANES), 0)
        lane_to = lax.broadcasted_iota(I32, (LANES, LANES), 1)
        in_line = dot(stacked, (lane_from < lane_to).astype(F32).astype(BF16))
        line_sum = dot(stacked, jnp.ones((LANES, LANES), BF16)).astype(BF16)
        size = n_shard * lines
        to = lax.broadcasted_iota(I32, (size, size), 0)
        since = lax.broadcasted_iota(I32, (size, size), 1)
        same = (to // lines) == (since // lines)
        ahead = dot((same & (since < to)).astype(F32).astype(BF16), line_sum)
        whole = dot(same.astype(F32).astype(BF16), line_sum)
        rank = in_line + ahead
        goal = jnp.zeros((lines, LANES), F32)
        past = jnp.zeros((lines, LANES), F32)
        for c in range(n_shard):
            part = slice(c * lines, (c + 1) * lines)
            place = rank[part] + c * bulk
            if extra:
                surplus = n_shard * bulk + past + rank[part] - bulk
                place = jnp.where(rank[part] < bulk, place, surplus)
                past = past + jnp.floor((jnp.maximum(whole[part] - bulk, 0.0) + 7.0) * 0.125) * 8.0
            goal = goal + masks[c] * place
        goal_ref[...] = goal.astype(I32)

        def one_tile(base):
            index = lax.broadcasted_iota(I32, (tile, LANES), 0) + base
            pick = [(index == goal_ref[a:a + 1, :]).astype(F32).astype(BF16) for a in range(lines)]
            return dot(jnp.concatenate(pick, axis=1), train_ref[...]).astype(BF16)

        per = bulk // tile
        for c in range(n_shard):
            for j in range(per):
                bulk_ref[c, j * tile:(j + 1) * tile, :] = one_tile(c * bulk + j * tile)
        for j, ref in enumerate(extra_refs):
            ref[...] = one_tile(n_shard * bulk + j * extra)

    shapes = [jax.ShapeDtypeStruct((n_shard, bulk, columns), BF16)]
    shapes += [jax.ShapeDtypeStruct((extra, columns), BF16)] * (2 if extra else 0)
    packed = n_shard * bulk + 2 * extra
    return pl.pallas_call(
        kernel,
        grid=(1,),
        in_specs=[
            pl.BlockSpec((lines, LANES), lambda i: (lax.axis_index("shard"), 0)),
            pl.BlockSpec((rows, columns), lambda i: (0, lax.axis_index("rep"))),
        ],
        out_specs=[VMEM] * len(shapes),
        out_shape=shapes,
        scratch_shapes=[pltpu.VMEM((lines, LANES), I32)],
        cost_estimate=cost(2 * packed * rows * columns, 2 * (rows + packed) * columns),
        compiler_params=PARAMS,
        name="pack_rows",
    )(ids, train)


def row_table(ids, lines, bulk, extra):
    n_shard = ids.shape[0] // lines

    def kernel(ids_ref, table_ref, flag_ref):
        me = lax.axis_index("shard")
        start = jnp.int32(0)
        most = jnp.int32(0)
        for s in range(n_shard):
            line = ids_ref[s * lines:(s + 1) * lines, :]

            def count(c):
                return jnp.sum((line == c).astype(I32))

            mine = count(me)
            before = jnp.int32(0)
            if extra:
                surplus = jnp.int32(0)
                for c in range(n_shard):
                    over = lax.div(jnp.maximum(count(c) - bulk, 0) + 7, jnp.int32(8)) * 8
                    before = before + jnp.where(c < me, over, 0)
                    surplus = surplus + over
                most = jnp.maximum(most, surplus)
            table_ref[s, 0] = start
            table_ref[s, 1] = jnp.minimum(mine, bulk)
            table_ref[s, 2] = lax.div(before, jnp.int32(8))
            start = start + mine
        flag_ref[...] = jnp.full((8, LANES), (most > extra).astype(I32))

    return pl.pallas_call(
        kernel,
        in_specs=[VMEM],
        out_specs=[SMEM, VMEM],
        out_shape=[jax.ShapeDtypeStruct((n_shard, 3), I32), jax.ShapeDtypeStruct((8, LANES), I32)],
        cost_estimate=cost(0, 4 * ids.size),
        compiler_params=PARAMS,
        name="row_table",
    )(ids)


def split_weights(own, others, extras):
    depth, width = own.shape
    n_extra = sum(e.shape[0] for e in extras)
    n_other = len(others)

    def kernel(*refs):
        own_ref, other_refs, extra_refs = refs[0], refs[1:1 + n_other], refs[1 + n_other:-3]
        high_ref, low_ref, out_ref = refs[-3:]
        weight = own_ref[...]
        for ref in other_refs:
            weight = weight + ref[...].astype(F32)
        high = weight.astype(BF16)
        high_ref[...] = high
        low_ref[...] = (weight - high.astype(F32)).astype(BF16)
        base = 0
        for ref in extra_refs:
            x = ref[...]
            y = dot(x, high_ref[...]) + dot(x, low_ref[...])
            out_ref[base // 8:(base + x.shape[0]) // 8] = y.reshape(x.shape[0] // 8, 8, width)
            base += x.shape[0]
        out_ref[base // 8:] = jnp.zeros((LANES // 8, 8, width), F32)

    return pl.pallas_call(
        kernel,
        in_specs=[VMEM] * (1 + n_other + len(extras)),
        out_specs=[VMEM] * 3,
        out_shape=[jax.ShapeDtypeStruct((depth, width), BF16)] * 2
        + [jax.ShapeDtypeStruct(((n_extra + LANES) // 8, 8, width), F32)],
        cost_estimate=cost(4 * n_extra * depth * width, 10 * depth * width + n_extra * (2 * depth + 4 * width)),
        compiler_params=PARAMS,
        name="split_weights",
    )(own, *others, *extras)


def row_scores(table, bulk_rows, high, low, extra_scores, rows, n_rep, extra):
    n_shard, bulk, depth = bulk_rows.shape
    width = high.shape[1]
    half = width // n_rep

    def kernel(table_ref, rows_ref, high_ref, low_ref, extra_ref, *rest):
        outs, acc = rest[:-1], rest[-1]
        me, rep = lax.axis_index("shard"), lax.axis_index("rep")

        def put(x, start):
            tiles = x.shape[0]
            first, within = lax.div(start, jnp.int32(8)), lax.rem(start, jnp.int32(8))
            turned = pltpu.roll(x, within, 1)
            keep = lax.broadcasted_iota(I32, (1, 8, width), 1) < within
            acc[pl.ds(first, 1)] = jnp.where(keep, acc[pl.ds(first, 1)], turned[:1])
            acc[pl.ds(first + 1, tiles - 1)] = jnp.where(keep, turned[:-1], turned[1:])
            acc[pl.ds(first + tiles, 1)] = turned[-1:]

        for s in range(n_shard):
            x = rows_ref[s]
            start = table_ref[s, 0]
            y = dot(x, high_ref[...]) + dot(x, low_ref[...])
            put(y.reshape(bulk // 8, 8, width), start)
            if extra:
                apart = jnp.bitwise_xor(me, s)
                index = jnp.bitwise_and(apart, 1) * 2 + lax.div(apart, jnp.int32(2))
                first = index * (2 * extra // 8) + table_ref[s, 2]
                put(extra_ref[pl.ds(first, extra // 8)], start + table_ref[s, 1])
        for r in range(n_rep):
            @pl.when(rep == r)
            def _():
                for d, out in enumerate(outs):
                    at = ((r + d) % n_rep) * half
                    out[...] = acc[:rows // 8, :, at:at + half].reshape(rows, half)

    return pl.pallas_call(
        kernel,
        in_specs=[SMEM] + [VMEM] * 4,
        out_specs=[VMEM] * n_rep,
        out_shape=[jax.ShapeDtypeStruct((rows, half), F32)] * n_rep,
        scratch_shapes=[pltpu.VMEM(((rows + bulk + extra) // 8 + 1, 8, width), F32)],
        cost_estimate=cost(4 * n_shard * bulk * depth * width, 2 * n_shard * bulk * depth + 8 * rows * width),
        compiler_params=PARAMS,
        name="row_scores",
    )(table, bulk_rows, high, low, extra_scores)


def body(train, cluster_ids, precond, query_store, block_slot, pattern):
    n_group, n_shard = lax.axis_size("groups"), lax.axis_size("shard")
    n_feat, n_rep = lax.axis_size("feat"), lax.axis_size("rep")
    feat, rep = lax.axis_index("feat"), lax.axis_index("rep")
    rows = train.shape[0]
    lines = rows // LANES
    base = rows // n_shard
    columns = train.shape[1] // n_rep
    extra = base // 2 if n_shard == 4 else 0
    bulk = base if extra else base + base // 2
    ids = cluster_ids.reshape(-1, LANES)

    picked = pick_queries(query_store, block_slot, pattern, n_group)
    arrived = lax.all_to_all(picked, "shard", split_axis=0, concat_axis=0, tiled=True)

    packed = pack_rows(train, ids, columns, bulk, extra)
    bulk_rows = lax.all_to_all(packed[0], "shard", split_axis=0, concat_axis=0, tiled=True)
    table, flag = row_table(ids, lines, bulk, extra)

    def spread(x):
        far = swap(x, "shard", n_shard, 2)
        both = jnp.concatenate([x, far])
        near = swap(both, "shard", n_shard, 1)
        return jnp.concatenate([both, near])

    extras = []
    if extra:
        for d in range(1, n_group):
            flag = jnp.maximum(flag, shift(flag, "groups", n_group, d))
        first = spread(packed[1])
        second = lax.cond(
            flag[0, 0] > 0, spread, lambda x: jnp.zeros((n_shard * extra, columns), BF16), packed[2]
        )
        for j in range(n_shard):
            at = slice(j * extra, (j + 1) * extra)
            extras += [first[at], second[at]]

    parts = [arrived] + [shift(arrived, "groups", n_group, d) for d in range(1, n_group)]
    chosen = join_queries(parts, block_slot, pattern, query_store.shape[0], n_feat, n_rep)

    matrix = precond[0]

    def weights(f, r):
        block = lax.dynamic_slice_in_dim(matrix, (f * n_rep + r) * columns, columns, 0)
        return lax.dot_general(block, chosen, (((1,), (1,)), ((), ())), preferred_element_type=F32)

    def summed_over_rep(f):
        away = [shift(weights(f, (rep + d) % n_rep), "rep", n_rep, d) for d in range(1, n_rep)]
        return sum(away, weights(f, rep))

    others = [
        shift(summed_over_rep((feat + d) % n_feat).astype(BF16), "feat", n_feat, d)
        for d in range(1, n_feat)
    ]
    own = summed_over_rep(feat)
    high, low, extra_scores = split_weights(own, others, extras)

    shares = row_scores(table, bulk_rows, high, low, extra_scores, rows, n_rep, extra)
    total = shares[0]
    for d in range(1, n_rep):
        total = total + shift(shares[d], "rep", n_rep, d)
    share = total.shape[1] // n_feat

    def for_feat(f):
        return lax.dynamic_slice_in_dim(total, f * share, share, 1)

    result = for_feat(feat)
    for d in range(1, n_feat):
        result = result + shift(for_feat((feat + d) % n_feat).astype(BF16), "feat", n_feat, d).astype(F32)
    return result.T[None]


def solution(mesh):
    return jax.shard_map(
        body,
        mesh=mesh,
        in_specs=(
            P(("groups", "shard"), "feat"),
            P("groups"),
            P(("groups", "shard"), None, ("feat", "rep")),
            P("shard", None, ("feat", "rep")),
            P(),
            P(),
        ),
        out_specs=P(("groups", "shard"), ("feat", "rep"), None),
        check_vma=False,
    )
```

```python
import functools

import jax
import jax.numpy as jnp
from jax import lax
from jax.experimental import pallas as pl
from jax.experimental.pallas import tpu as pltpu
from jax.sharding import PartitionSpec as P

F32, BF16, I32 = jnp.float32, jnp.bfloat16, jnp.int32
VMEM = pl.BlockSpec(memory_space=pltpu.VMEM)
ANY = pl.BlockSpec(memory_space=pl.ANY)
SMEM = pl.BlockSpec(memory_space=pltpu.SMEM)
PARAMS = pltpu.CompilerParams(vmem_limit_bytes=50 * 2**20)
LANES = 128


def shift(x, axis, size, by):
    return lax.ppermute(x, axis, [(i, (i + by) % size) for i in range(size)])


def swap(x, axis, size, bit):
    return lax.ppermute(x, axis, [(i, i ^ bit) for i in range(size)])


def dot(a, b):
    return jnp.dot(a, b, preferred_element_type=F32)


def cost(flops, nbytes):
    return pl.CostEstimate(flops=1, bytes_accessed=1, transcendentals=0)


def after(x, *others):
    def kernel(*refs):
        pass

    return pl.pallas_call(
        kernel,
        in_specs=[ANY] * (1 + len(others)),
        out_specs=ANY,
        out_shape=jax.ShapeDtypeStruct(x.shape, x.dtype),
        input_output_aliases={0: 0},
        cost_estimate=cost(0, 0),
        compiler_params=PARAMS,
        name="after",
    )(x, *others)


def pick_queries(query_store, block_slot, pattern, n_group):
    local_blocks, block_rows, width = query_store.shape
    n_cluster, n_list = pattern.shape
    part = block_rows // n_group

    def place(t, pattern_ref, slot_ref):
        me = lax.axis_index("shard")
        found = jnp.int32(0)
        for k in range(n_list):
            slot = slot_ref[pattern_ref[lax.rem(me + t, jnp.int32(n_cluster)), k]]
            hit = (lax.div(slot, jnp.int32(local_blocks)) == me).astype(I32)
            found = found + hit * lax.rem(slot, jnp.int32(local_blocks))
        return found, lax.axis_index("groups"), 0

    def kernel(pattern_ref, slot_ref, in_ref, out_ref):
        out_ref[...] = in_ref[...]

    return pl.pallas_call(
        kernel,
        grid_spec=pltpu.PrefetchScalarGridSpec(
            num_scalar_prefetch=2,
            grid=(n_cluster,),
            in_specs=[pl.BlockSpec((1, part, width), place)],
            out_specs=pl.BlockSpec((1, part, width), lambda t, p, s: (t, 0, 0)),
        ),
        out_shape=jax.ShapeDtypeStruct((n_cluster, part, width), BF16),
        cost_estimate=cost(0, 4 * n_cluster * part * width),
        compiler_params=PARAMS,
        name="pick_queries",
    )(pattern, block_slot, query_store)


def join_queries(parts, block_slot, pattern, local_blocks, n_feat, n_rep, *others):
    n_group = len(parts)
    n_cluster, part, width = parts[0].shape
    n_list = pattern.shape[1]
    total = n_list * n_group * part
    share = total // (n_feat * n_rep)
    unit = min(share, part)

    def kernel(pattern_ref, slot_ref, *refs):
        out_ref = refs[-1]
        me, group = lax.axis_index("shard"), lax.axis_index("groups")
        for k in range(n_list):
            owner = lax.div(slot_ref[pattern_ref[me, k]], jnp.int32(local_blocks))
            hops = lax.rem(me + (n_cluster - owner), jnp.int32(n_cluster))
            for d in range(n_group):
                origin = lax.rem(group + (n_group - d), jnp.int32(n_group))
                for u in range(part // unit):
                    first = (k * n_group + origin) * part + u * unit
                    chunk = lax.div(first, jnp.int32(share))
                    goal = lax.rem(chunk, jnp.int32(n_rep)) * n_feat + lax.div(chunk, jnp.int32(n_rep))
                    goal = goal * share + lax.rem(first, jnp.int32(share))
                    out_ref[pl.ds(pl.multiple_of(goal, unit), unit), :] = refs[d][hops, u * unit:(u + 1) * unit, :]

    return pl.pallas_call(
        kernel,
        in_specs=[SMEM, SMEM] + [VMEM] * n_group + [ANY] * len(others),
        out_specs=VMEM,
        out_shape=jax.ShapeDtypeStruct((total, width), BF16),
        cost_estimate=cost(0, 4 * total * width),
        compiler_params=PARAMS,
        name="join_queries",
    )(pattern, block_slot, *parts, *others)


def pack_rows(train, ids, columns, bulk, extra, cuts):
    rows = train.shape[0]
    lines = rows // LANES
    n_shard = ids.shape[0] // lines

    def kernel(ids_ref, train_ref, *rest):
        outs, goal_ref = rest[:-1], rest[-1]
        me = lax.axis_index("shard")
        own = ids_ref[...]
        masks = [(own == c).astype(F32) for c in range(n_shard)]
        stacked = jnp.concatenate(masks, axis=0).astype(BF16)
        lane_from = lax.broadcasted_iota(I32, (LANES, LANES), 0)
        lane_to = lax.broadcasted_iota(I32, (LANES, LANES), 1)
        in_line = dot(stacked, (lane_from < lane_to).astype(F32).astype(BF16))
        line_sum = dot(stacked, jnp.ones((LANES, LANES), BF16)).astype(BF16)
        size = n_shard * lines
        to = lax.broadcasted_iota(I32, (size, size), 0)
        since = lax.broadcasted_iota(I32, (size, size), 1)
        same = (to // lines) == (since // lines)
        ahead = dot((same & (since < to)).astype(F32).astype(BF16), line_sum)
        whole = dot(same.astype(F32).astype(BF16), line_sum)
        rank = in_line + ahead
        goal = jnp.zeros((lines, LANES), F32)
        past = jnp.zeros((lines, LANES), F32)
        for c in range(n_shard):
            part = slice(c * lines, (c + 1) * lines)
            place = rank[part] + c * bulk
            if extra:
                surplus = n_shard * bulk + past + rank[part] - bulk
                place = jnp.where(rank[part] < bulk, place, surplus)
                past = past + jnp.floor((jnp.maximum(whole[part] - bulk, 0.0) + 7.0) * 0.125) * 8.0
            goal = goal + masks[c] * place
        goal_ref[...] = goal.astype(I32)

        def fill(out, base):
            size = out.shape[0]
            tile = 128 if size % 128 == 0 else size
            for at in range(0, size, tile):
                index = lax.broadcasted_iota(I32, (tile, LANES), 0) + (base + at)
                pick = [(index == goal_ref[a:a + 1, :]).astype(F32).astype(BF16) for a in range(lines)]
                out[at:at + tile, :] = dot(jnp.concatenate(pick, axis=1), train_ref[...]).astype(BF16)

        for out, (hops, first, _) in zip(outs, cuts):
            fill(out, lax.rem(me + hops, jnp.int32(n_shard)) * bulk + first)
        for j, out in enumerate(outs[len(cuts):]):
            fill(out, n_shard * bulk + j * extra)

    shapes = [jax.ShapeDtypeStruct((n, columns), BF16) for _, _, n in cuts]
    shapes += [jax.ShapeDtypeStruct((extra, columns), BF16)] * (2 if extra else 0)
    packed = n_shard * bulk + 2 * extra
    return pl.pallas_call(
        kernel,
        grid=(1,),
        in_specs=[
            pl.BlockSpec((lines, LANES), lambda i: (lax.axis_index("shard"), 0)),
            pl.BlockSpec((rows, columns), lambda i: (0, lax.axis_index("rep"))),
        ],
        out_specs=[VMEM] * len(shapes),
        out_shape=shapes,
        scratch_shapes=[pltpu.VMEM((lines, LANES), I32)],
        cost_estimate=cost(2 * packed * rows * columns, 2 * (rows + packed) * columns),
        compiler_params=PARAMS,
        name="pack_rows",
    )(ids, train)


def partial_weights(matrix, chosen, block, depth, *others):
    width = matrix.shape[1]
    tile = 256 if depth % 256 == 0 else depth
    steps = depth // tile

    def kernel(block_ref, matrix_ref, chosen_ref, *rest):
        rest[-1][...] = lax.dot_general(
            matrix_ref[...], chosen_ref[...], (((1,), (1,)), ((), ())), preferred_element_type=F32
        )

    total = chosen.shape[0]
    return pl.pallas_call(
        kernel,
        grid_spec=pltpu.PrefetchScalarGridSpec(
            num_scalar_prefetch=1,
            grid=(steps,),
            in_specs=[
                pl.BlockSpec((tile, width), lambda i, b: (b[0] * steps + i, 0)),
                pl.BlockSpec((total, width), lambda i, b: (0, 0)),
            ]
            + [ANY] * len(others),
            out_specs=pl.BlockSpec((tile, total), lambda i, b: (i, 0)),
        ),
        out_shape=jax.ShapeDtypeStruct((depth, total), F32),
        cost_estimate=cost(2 * depth * width * total, 2 * depth * width + 4 * depth * total),
        compiler_params=PARAMS,
        name="partial_weights",
    )(jnp.reshape(block, (1,)).astype(I32), matrix, chosen, *others)


def row_table(ids, lines, bulk, extra):
    n_shard = ids.shape[0] // lines

    def kernel(ids_ref, table_ref, flag_ref):
        me = lax.axis_index("shard")
        start = jnp.int32(0)
        most = jnp.int32(0)
        for s in range(n_shard):
            line = ids_ref[s * lines:(s + 1) * lines, :]

            def count(c):
                return jnp.sum((line == c).astype(I32))

            mine = count(me)
            before = jnp.int32(0)
            if extra:
                surplus = jnp.int32(0)
                for c in range(n_shard):
                    over = lax.div(jnp.maximum(count(c) - bulk, 0) + 7, jnp.int32(8)) * 8
                    before = before + jnp.where(c < me, over, 0)
                    surplus = surplus + over
                most = jnp.maximum(most, surplus)
            table_ref[s, 0] = start
            table_ref[s, 1] = jnp.minimum(mine, bulk)
            table_ref[s, 2] = lax.div(before, jnp.int32(8))
            start = start + mine
        flag_ref[...] = jnp.full((8, LANES), (most > extra).astype(I32))

    return pl.pallas_call(
        kernel,
        in_specs=[VMEM],
        out_specs=[SMEM, VMEM],
        out_shape=[jax.ShapeDtypeStruct((n_shard, 3), I32), jax.ShapeDtypeStruct((8, LANES), I32)],
        cost_estimate=cost(0, 4 * ids.size),
        compiler_params=PARAMS,
        name="row_table",
    )(ids)


def early_scores(own, others, pieces):
    depth, width = own.shape
    count = sum(p.shape[0] for p in pieces)
    n_other = len(others)

    def kernel(*refs):
        own_ref, other_refs, piece_refs = refs[0], refs[1:1 + n_other], refs[1 + n_other:-3]
        high_ref, low_ref, out_ref = refs[-3:]
        weight = own_ref[...]
        for ref in other_refs:
            weight = weight + ref[...].astype(F32)
        high = weight.astype(BF16)
        high_ref[...] = high
        low_ref[...] = (weight - high.astype(F32)).astype(BF16)
        base = 0
        for ref in piece_refs:
            x = ref[...]
            y = dot(x, high_ref[...]) + dot(x, low_ref[...])
            out_ref[base // 8:(base + x.shape[0]) // 8] = y.reshape(x.shape[0] // 8, 8, width)
            base += x.shape[0]
        out_ref[base // 8:] = jnp.zeros((LANES // 8, 8, width), F32)

    return pl.pallas_call(
        kernel,
        in_specs=[VMEM] * (1 + n_other + len(pieces)),
        out_specs=[VMEM] * 3,
        out_shape=[jax.ShapeDtypeStruct((depth, width), BF16)] * 2
        + [jax.ShapeDtypeStruct(((count + LANES) // 8, 8, width), F32)],
        cost_estimate=cost(4 * count * depth * width, 10 * depth * width + count * (2 * depth + 4 * width)),
        compiler_params=PARAMS,
        name="early_scores",
    )(own, *others, *pieces)


def row_scores(table, last, high, low, early, rows, n_rep, bulk, extra, cuts):
    n_shard = table.shape[0]
    width = high.shape[1]
    half = width // n_rep
    late_rows = last.shape[0]
    surplus_at = (n_shard * bulk - late_rows) // 8

    def kernel(table_ref, last_ref, high_ref, low_ref, early_ref, *rest):
        outs, late, acc = rest[:-2], rest[-2], rest[-1]
        me, rep = lax.axis_index("shard"), lax.axis_index("rep")
        x = last_ref[...]
        y = dot(x, high_ref[...]) + dot(x, low_ref[...])
        late[...] = y.reshape(late_rows // 8, 8, width)

        def put(x, start):
            tiles = x.shape[0]
            first, within = lax.div(start, jnp.int32(8)), lax.rem(start, jnp.int32(8))
            turned = pltpu.roll(x, within, 1)
            keep = lax.broadcasted_iota(I32, (1, 8, width), 1) < within
            acc[pl.ds(first, 1)] = jnp.where(keep, acc[pl.ds(first, 1)], turned[:1])
            acc[pl.ds(first + 1, tiles - 1)] = jnp.where(keep, turned[:-1], turned[1:])
            acc[pl.ds(first + tiles, 1)] = turned[-1:]

        for s in range(n_shard):
            start = table_ref[s, 0]
            for hops in range(n_shard):
                @pl.when(lax.rem(me + (n_shard - hops), jnp.int32(n_shard)) == s)
                def _():
                    base = 0
                    for h, first, n in cuts:
                        if h == hops:
                            if base + n <= n_shard * bulk - late_rows:
                                put(early_ref[base // 8:(base + n) // 8], start + first)
                            else:
                                put(late[...], start + first)
                        base += n
            if extra:
                apart = jnp.bitwise_xor(me, s)
                index = jnp.bitwise_and(apart, 1) * 2 + lax.div(apart, jnp.int32(2))
                first = surplus_at + index * (2 * extra // 8) + table_ref[s, 2]
                put(early_ref[pl.ds(first, extra // 8)], start + table_ref[s, 1])
        for r in range(n_rep):
            @pl.when(rep == r)
            def _():
                for d, out in enumerate(outs):
                    at = ((r + d) % n_rep) * half
                    out[...] = acc[:rows // 8, :, at:at + half].reshape(rows, half)

    return pl.pallas_call(
        kernel,
        in_specs=[SMEM] + [VMEM] * 4,
        out_specs=[VMEM] * n_rep,
        out_shape=[jax.ShapeDtypeStruct((rows, half), F32)] * n_rep,
        scratch_shapes=[
            pltpu.VMEM((late_rows // 8, 8, width), F32),
            pltpu.VMEM(((rows + bulk + extra) // 8 + 1, 8, width), F32),
        ],
        cost_estimate=cost(4 * late_rows * high.shape[0] * width, 8 * rows * width),
        compiler_params=PARAMS,
        name="row_scores",
    )(table, last, high, low, early)


def body(train, cluster_ids, precond, query_store, block_slot, pattern):
    n_group, n_shard = lax.axis_size("groups"), lax.axis_size("shard")
    n_feat, n_rep = lax.axis_size("feat"), lax.axis_size("rep")
    feat, rep = lax.axis_index("feat"), lax.axis_index("rep")
    rows = train.shape[0]
    lines = rows // LANES
    base = rows // n_shard
    columns = train.shape[1] // n_rep
    extra = base // 2 if n_shard == 4 else 0
    bulk = base if extra else base + base // 2
    ids = cluster_ids.reshape(-1, LANES)

    me = lax.axis_index("shard")
    picked = pick_queries(query_store, block_slot, pattern, n_group)
    pieces = [picked[:1]]
    for d in range(1, n_shard):
        pieces.append(shift(picked[d:d + 1], "shard", n_shard, d))

    order = [0] + sorted(range(1, n_shard), key=lambda d: (min(d, n_shard - d), d))
    cuts = [(d, 0, bulk) for d in order[:-1]]
    cuts += [(order[-1], 0, bulk // 2), (order[-1], bulk // 2, bulk // 2)]
    packed = pack_rows(train, ids, columns, bulk, extra, cuts)
    table, flag = row_table(ids, lines, bulk, extra)

    def swap_far(x):
        return jnp.concatenate([x, swap(x, "shard", n_shard, 2)])

    def swap_near(x):
        return jnp.concatenate([x, swap(x, "shard", n_shard, 1)])

    arrived = after(jnp.concatenate(pieces), packed[1])
    here = [packed[0]]
    marks = [arrived, arrived]
    for j, (hops, _, _) in enumerate(cuts[1:-1]):
        sent = packed[j + 1] if j == 0 else after(packed[j + 1], marks[-2])
        here.append(shift(sent, "shard", n_shard, hops))
        marks.append(here[-1])
        if extra and j == len(cuts) - 4:
            far = swap_far(after(packed[-2], marks[-2]))
            marks.append(far)
    last = shift(after(packed[len(cuts) - 1], marks[-2]), "shard", n_shard, cuts[-1][0])

    parts = [arrived] + [shift(arrived, "groups", n_group, d) for d in range(1, n_group)]
    chosen = join_queries(parts, block_slot, pattern, query_store.shape[0], n_feat, n_rep, here[1])

    matrix = precond[0]

    def weights(f, r, *others):
        return partial_weights(matrix, chosen, f * n_rep + r, columns, *others)

    def summed_over_rep(f, *others):
        away = [shift(weights(f, (rep + d) % n_rep, *others), "rep", n_rep, d) for d in range(1, n_rep)]
        return sum(away, weights(f, rep, *others))

    sends = [summed_over_rep((feat + d) % n_feat).astype(BF16) for d in range(1, n_feat)]
    others = [shift(x, "feat", n_feat, d + 1) for d, x in enumerate(sends)]
    own = summed_over_rep(feat, *sends)

    extras = []
    if extra:
        for d in range(1, n_group):
            flag = jnp.maximum(flag, shift(flag, "groups", n_group, d))
        first = swap_near(after(far, *sends))
        second = lax.cond(
            flag[0, 0] > 0,
            lambda x: swap_near(swap_far(x)),
            lambda x: jnp.zeros((n_shard * extra, columns), BF16),
            after(packed[-1], *sends),
        )
        for j in range(n_shard):
            at = slice(j * extra, (j + 1) * extra)
            extras += [first[at], second[at]]

    high, low, early = early_scores(own, others, here + extras)
    shares = row_scores(table, last, high, low, early, rows, n_rep, bulk, extra, cuts)
    total = shares[0]
    for d in range(1, n_rep):
        total = total + shift(shares[d], "rep", n_rep, d)
    share = total.shape[1] // n_feat

    def for_feat(f):
        return lax.dynamic_slice_in_dim(total, f * share, share, 1)

    result = for_feat(feat)
    for d in range(1, n_feat):
        result = result + shift(for_feat((feat + d) % n_feat).astype(BF16), "feat", n_feat, d).astype(F32)
    return result.T[None]


def solution(mesh):
    return jax.shard_map(
        body,
        mesh=mesh,
        in_specs=(
            P(("groups", "shard"), "feat"),
            P("groups"),
            P(("groups", "shard"), None, ("feat", "rep")),
            P("shard", None, ("feat", "rep")),
            P(),
            P(),
        ),
        out_specs=P(("groups", "shard"), ("feat", "rep"), None),
        check_vma=False,
    )
```

```python
import functools

import jax
import jax.numpy as jnp
from jax import lax
from jax.experimental import pallas as pl
from jax.experimental.pallas import tpu as pltpu
from jax.sharding import PartitionSpec as P

F32, BF16, I32 = jnp.float32, jnp.bfloat16, jnp.int32
VMEM = pl.BlockSpec(memory_space=pltpu.VMEM)
ANY = pl.BlockSpec(memory_space=pl.ANY)
SMEM = pl.BlockSpec(memory_space=pltpu.SMEM)
PARAMS = pltpu.CompilerParams(vmem_limit_bytes=50 * 2**20)
LANES = 128


def shift(x, axis, size, by):
    return lax.ppermute(x, axis, [(i, (i + by) % size) for i in range(size)])


def swap(x, axis, size, bit):
    return lax.ppermute(x, axis, [(i, i ^ bit) for i in range(size)])


def dot(a, b):
    return jnp.dot(a, b, preferred_element_type=F32)


def cost(flops, nbytes):
    return pl.CostEstimate(flops=1, bytes_accessed=1, transcendentals=0)


def after(x, *others):
    def kernel(*refs):
        pass

    return pl.pallas_call(
        kernel,
        in_specs=[ANY] * (1 + len(others)),
        out_specs=ANY,
        out_shape=jax.ShapeDtypeStruct(x.shape, x.dtype),
        input_output_aliases={0: 0},
        cost_estimate=cost(0, 0),
        compiler_params=PARAMS,
        name="after",
    )(x, *others)


def pick_queries(query_store, block_slot, pattern, n_group):
    local_blocks, block_rows, width = query_store.shape
    n_cluster, n_list = pattern.shape
    part = block_rows // n_group

    def place(t, pattern_ref, slot_ref):
        me = lax.axis_index("shard")
        found = jnp.int32(0)
        for k in range(n_list):
            slot = slot_ref[pattern_ref[lax.rem(me + t, jnp.int32(n_cluster)), k]]
            hit = (lax.div(slot, jnp.int32(local_blocks)) == me).astype(I32)
            found = found + hit * lax.rem(slot, jnp.int32(local_blocks))
        return found, lax.axis_index("groups"), 0

    def kernel(pattern_ref, slot_ref, in_ref, out_ref):
        out_ref[...] = in_ref[...]

    return pl.pallas_call(
        kernel,
        grid_spec=pltpu.PrefetchScalarGridSpec(
            num_scalar_prefetch=2,
            grid=(n_cluster,),
            in_specs=[pl.BlockSpec((1, part, width), place)],
            out_specs=pl.BlockSpec((1, part, width), lambda t, p, s: (t, 0, 0)),
        ),
        out_shape=jax.ShapeDtypeStruct((n_cluster, part, width), BF16),
        cost_estimate=cost(0, 4 * n_cluster * part * width),
        compiler_params=PARAMS,
        name="pick_queries",
    )(pattern, block_slot, query_store)


def join_queries(parts, block_slot, pattern, local_blocks, n_feat, n_rep, *others):
    n_group = len(parts)
    n_cluster, part, width = parts[0].shape
    n_list = pattern.shape[1]
    total = n_list * n_group * part
    share = total // (n_feat * n_rep)
    unit = min(share, part)

    def kernel(pattern_ref, slot_ref, *refs):
        out_ref, rows_ref = refs[-2:]
        me, group = lax.axis_index("shard"), lax.axis_index("groups")
        for k in range(n_list):
            owner = lax.div(slot_ref[pattern_ref[me, k]], jnp.int32(local_blocks))
            hops = lax.rem(me + (n_cluster - owner), jnp.int32(n_cluster))
            for d in range(n_group):
                origin = lax.rem(group + (n_group - d), jnp.int32(n_group))
                for u in range(part // unit):
                    first = (k * n_group + origin) * part + u * unit
                    chunk = lax.div(first, jnp.int32(share))
                    goal = lax.rem(chunk, jnp.int32(n_rep)) * n_feat + lax.div(chunk, jnp.int32(n_rep))
                    goal = goal * share + lax.rem(first, jnp.int32(share))
                    rows_ref[pl.ds(pl.multiple_of(goal, unit), unit), :] = refs[d][hops, u * unit:(u + 1) * unit, :]
        out_ref[...] = rows_ref[...].T

    return pl.pallas_call(
        kernel,
        in_specs=[SMEM, SMEM] + [VMEM] * n_group + [ANY] * len(others),
        out_specs=VMEM,
        out_shape=jax.ShapeDtypeStruct((width, total), BF16),
        scratch_shapes=[pltpu.VMEM((total, width), BF16)],
        cost_estimate=cost(0, 4 * total * width),
        compiler_params=PARAMS,
        name="join_queries",
    )(pattern, block_slot, *parts, *others)


def pack_rows(train, ids, columns, bulk, extra, cuts):
    rows = train.shape[0]
    lines = rows // LANES
    n_shard = ids.shape[0] // lines

    def kernel(ids_ref, train_ref, *rest):
        outs, goal_ref = rest[:-1], rest[-1]
        me = lax.axis_index("shard")
        own = ids_ref[...]
        masks = [(own == c).astype(F32) for c in range(n_shard)]
        stacked = jnp.concatenate(masks, axis=0).astype(BF16)
        lane_from = lax.broadcasted_iota(I32, (LANES, LANES), 0)
        lane_to = lax.broadcasted_iota(I32, (LANES, LANES), 1)
        in_line = dot(stacked, (lane_from < lane_to).astype(F32).astype(BF16))
        line_sum = dot(stacked, jnp.ones((LANES, LANES), BF16)).astype(BF16)
        size = n_shard * lines
        to = lax.broadcasted_iota(I32, (size, size), 0)
        since = lax.broadcasted_iota(I32, (size, size), 1)
        same = (to // lines) == (since // lines)
        ahead = dot((same & (since < to)).astype(F32).astype(BF16), line_sum)
        whole = dot(same.astype(F32).astype(BF16), line_sum)
        rank = in_line + ahead
        goal = jnp.zeros((lines, LANES), F32)
        past = jnp.zeros((lines, LANES), F32)
        for c in range(n_shard):
            part = slice(c * lines, (c + 1) * lines)
            place = rank[part] + c * bulk
            if extra:
                surplus = n_shard * bulk + past + rank[part] - bulk
                place = jnp.where(rank[part] < bulk, place, surplus)
                past = past + jnp.floor((jnp.maximum(whole[part] - bulk, 0.0) + 7.0) * 0.125) * 8.0
            goal = goal + masks[c] * place
        goal_ref[...] = goal.astype(I32)

        def fill(out, base):
            size = out.shape[0]
            tile = 128 if size % 128 == 0 else size
            for at in range(0, size, tile):
                index = lax.broadcasted_iota(I32, (tile, LANES), 0) + (base + at)
                pick = [(index == goal_ref[a:a + 1, :]).astype(F32).astype(BF16) for a in range(lines)]
                out[at:at + tile, :] = dot(jnp.concatenate(pick, axis=1), train_ref[...]).astype(BF16)

        for out, (hops, first, _) in zip(outs, cuts):
            fill(out, lax.rem(me + hops, jnp.int32(n_shard)) * bulk + first)
        for j, out in enumerate(outs[len(cuts):]):
            fill(out, n_shard * bulk + j * extra)

    shapes = [jax.ShapeDtypeStruct((n, columns), BF16) for _, _, n in cuts]
    shapes += [jax.ShapeDtypeStruct((extra, columns), BF16)] * (2 if extra else 0)
    packed = n_shard * bulk + 2 * extra
    return pl.pallas_call(
        kernel,
        grid=(1,),
        in_specs=[
            pl.BlockSpec((lines, LANES), lambda i: (lax.axis_index("shard"), 0)),
            pl.BlockSpec((rows, columns), lambda i: (0, lax.axis_index("rep"))),
        ],
        out_specs=[VMEM] * len(shapes),
        out_shape=shapes,
        scratch_shapes=[pltpu.VMEM((lines, LANES), I32)],
        cost_estimate=cost(2 * packed * rows * columns, 2 * (rows + packed) * columns),
        compiler_params=PARAMS,
        name="pack_rows",
    )(ids, train)


def partial_weights(matrix, chosen, block, depth):
    width, total = chosen.shape
    tile = 512 if depth % 512 == 0 else depth
    steps = depth // tile

    def kernel(block_ref, matrix_ref, chosen_ref, out_ref):
        out_ref[...] = dot(matrix_ref[...], chosen_ref[...])

    return pl.pallas_call(
        kernel,
        grid_spec=pltpu.PrefetchScalarGridSpec(
            num_scalar_prefetch=1,
            grid=(steps,),
            in_specs=[
                pl.BlockSpec((tile, width), lambda i, b: (b[0] * steps + i, 0)),
                pl.BlockSpec((width, total), lambda i, b: (0, 0)),
            ],
            out_specs=pl.BlockSpec((tile, total), lambda i, b: (i, 0)),
        ),
        out_shape=jax.ShapeDtypeStruct((depth, total), F32),
        cost_estimate=cost(2 * depth * width * total, 2 * depth * width + 4 * depth * total),
        compiler_params=PARAMS,
        name="partial_weights",
    )(jnp.reshape(block, (1,)).astype(I32), matrix, chosen)


def row_table(ids, lines, bulk, extra):
    n_shard = ids.shape[0] // lines

    def kernel(ids_ref, table_ref, flag_ref):
        me = lax.axis_index("shard")
        start = jnp.int32(0)
        most = jnp.int32(0)
        for s in range(n_shard):
            line = ids_ref[s * lines:(s + 1) * lines, :]

            def count(c):
                return jnp.sum((line == c).astype(I32))

            mine = count(me)
            before = jnp.int32(0)
            if extra:
                surplus = jnp.int32(0)
                for c in range(n_shard):
                    over = lax.div(jnp.maximum(count(c) - bulk, 0) + 7, jnp.int32(8)) * 8
                    before = before + jnp.where(c < me, over, 0)
                    surplus = surplus + over
                most = jnp.maximum(most, surplus)
            table_ref[s, 0] = start
            table_ref[s, 1] = jnp.minimum(mine, bulk)
            table_ref[s, 2] = lax.div(before, jnp.int32(8))
            start = start + mine
        flag_ref[...] = jnp.full((8, LANES), (most > extra).astype(I32))

    return pl.pallas_call(
        kernel,
        in_specs=[VMEM],
        out_specs=[SMEM, VMEM],
        out_shape=[jax.ShapeDtypeStruct((n_shard, 3), I32), jax.ShapeDtypeStruct((8, LANES), I32)],
        cost_estimate=cost(0, 4 * ids.size),
        compiler_params=PARAMS,
        name="row_table",
    )(ids)


def early_scores(own, others, pieces, flag, sure):
    depth, width = own.shape
    count = sum(p.shape[0] for p in pieces)
    n_other = len(others)

    def kernel(*refs):
        flag_ref, refs = refs[0], refs[1:]
        own_ref, other_refs, piece_refs = refs[0], refs[1:1 + n_other], refs[1 + n_other:-3]
        flagged = jnp.max(flag_ref[...]) > 0
        high_ref, low_ref, out_ref = refs[-3:]
        weight = own_ref[...]
        for ref in other_refs:
            weight = weight + ref[...].astype(F32)
        high = weight.astype(BF16)
        high_ref[...] = high
        low_ref[...] = (weight - high.astype(F32)).astype(BF16)
        base = 0

        def score(ref, at):
            x = ref[...]
            y = dot(x, high_ref[...]) + dot(x, low_ref[...])
            out_ref[at // 8:(at + x.shape[0]) // 8] = y.reshape(x.shape[0] // 8, 8, width)

        for ref, always in zip(piece_refs, sure):
            if always:
                score(ref, base)
            else:
                pl.when(flagged)(functools.partial(score, ref, base))
            base += ref.shape[0]

    return pl.pallas_call(
        kernel,
        in_specs=[VMEM] * (2 + n_other + len(pieces)),
        out_specs=[VMEM] * 3,
        out_shape=[jax.ShapeDtypeStruct((depth, width), BF16)] * 2
        + [jax.ShapeDtypeStruct(((count + LANES) // 8, 8, width), F32)],
        cost_estimate=cost(4 * count * depth * width, 10 * depth * width + count * (2 * depth + 4 * width)),
        compiler_params=PARAMS,
        name="early_scores",
    )(flag, own, *others, *pieces)


def row_scores(table, last, high, low, early, rows, n_rep, bulk, extra, cuts):
    n_shard = table.shape[0]
    width = high.shape[1]
    half = width // n_rep
    late_rows = last.shape[0]
    surplus_at = (n_shard * bulk - late_rows) // 8

    def kernel(table_ref, last_ref, high_ref, low_ref, early_ref, *rest):
        outs, late, acc = rest[:-2], rest[-2], rest[-1]
        me, rep = lax.axis_index("shard"), lax.axis_index("rep")
        x = last_ref[...]
        y = dot(x, high_ref[...]) + dot(x, low_ref[...])
        late[...] = y.reshape(late_rows // 8, 8, width)

        def put(x, start):
            tiles = x.shape[0]
            first, within = lax.div(start, jnp.int32(8)), lax.rem(start, jnp.int32(8))
            turned = pltpu.roll(x, within, 1)
            keep = lax.broadcasted_iota(I32, (1, 8, width), 1) < within
            acc[pl.ds(first, 1)] = jnp.where(keep, acc[pl.ds(first, 1)], turned[:1])
            acc[pl.ds(first + 1, tiles - 1)] = jnp.where(keep, turned[:-1], turned[1:])
            acc[pl.ds(first + tiles, 1)] = turned[-1:]

        for s in range(n_shard):
            start = table_ref[s, 0]
            for hops in range(n_shard):
                @pl.when(lax.rem(me + (n_shard - hops), jnp.int32(n_shard)) == s)
                def _():
                    base = 0
                    for h, first, n in cuts:
                        if h == hops:
                            if base + n <= n_shard * bulk - late_rows:
                                put(early_ref[base // 8:(base + n) // 8], start + first)
                            else:
                                put(late[...], start + first)
                        base += n
            if extra:
                apart = jnp.bitwise_xor(me, s)
                index = jnp.bitwise_and(apart, 1) * 2 + lax.div(apart, jnp.int32(2))
                first = surplus_at + index * (2 * extra // 8) + table_ref[s, 2]
                put(early_ref[pl.ds(first, extra // 8)], start + table_ref[s, 1])
        for r in range(n_rep):
            @pl.when(rep == r)
            def _():
                for d, out in enumerate(outs):
                    at = ((r + d) % n_rep) * half
                    out[...] = acc[:rows // 8, :, at:at + half].reshape(rows, half)

    return pl.pallas_call(
        kernel,
        in_specs=[SMEM] + [VMEM] * 4,
        out_specs=[VMEM] * n_rep,
        out_shape=[jax.ShapeDtypeStruct((rows, half), F32)] * n_rep,
        scratch_shapes=[
            pltpu.VMEM((late_rows // 8, 8, width), F32),
            pltpu.VMEM(((rows + bulk + extra) // 8 + 1, 8, width), F32),
        ],
        cost_estimate=cost(4 * late_rows * high.shape[0] * width, 8 * rows * width),
        compiler_params=PARAMS,
        name="row_scores",
    )(table, last, high, low, early)


def body(train, cluster_ids, precond, query_store, block_slot, pattern):
    n_group, n_shard = lax.axis_size("groups"), lax.axis_size("shard")
    n_feat, n_rep = lax.axis_size("feat"), lax.axis_size("rep")
    feat, rep = lax.axis_index("feat"), lax.axis_index("rep")
    rows = train.shape[0]
    lines = rows // LANES
    base = rows // n_shard
    columns = train.shape[1] // n_rep
    extra = base // 2 if n_shard == 4 else 0
    bulk = base if extra else base + base // 2
    ids = cluster_ids.reshape(-1, LANES)

    me = lax.axis_index("shard")
    picked = pick_queries(query_store, block_slot, pattern, n_group)
    pieces = [picked[:1]]
    for d in range(1, n_shard):
        pieces.append(shift(picked[d:d + 1], "shard", n_shard, d))

    cuts = [(d, 0, bulk) for d in range(n_shard)]
    packed = pack_rows(train, ids, columns, bulk, extra, cuts)
    here = [packed[0], shift(packed[1], "shard", n_shard, 1)]
    table, flag = row_table(ids, lines, bulk, extra)

    def swap_far(x):
        return jnp.concatenate([x, swap(x, "shard", n_shard, 2)])

    def swap_near(x):
        return jnp.concatenate([x, swap(x, "shard", n_shard, 1)])

    before_join, before_feat = [here[1]], []
    if extra:
        for d in range(1, n_group):
            flag = jnp.maximum(flag, shift(flag, "groups", n_group, d))
        second = lax.cond(
            flag[0, 0] > 0,
            lambda x: swap_near(swap_far(x)),
            lambda x: jnp.zeros((n_shard * extra, columns), BF16),
            packed[-1],
        )
        far = swap(after(packed[-2], here[1]), "shard", n_shard, 2)
        before_join.append(second)
        before_feat.append(far)

    arrived = after(jnp.concatenate(pieces), packed[1])
    parts = [arrived] + [shift(arrived, "groups", n_group, d) for d in range(1, n_group)]
    chosen = join_queries(parts, block_slot, pattern, query_store.shape[0], n_feat, n_rep, *before_join)

    matrix = precond[0]

    def weights(f, r):
        return partial_weights(matrix, chosen, f * n_rep + r, columns)

    targets = [(feat + d) % n_feat for d in range(1, n_feat)] + [feat]
    away = [[shift(weights(f, (rep + d) % n_rep), "rep", n_rep, d) for d in range(1, n_rep)] for f in targets]
    sums = [sum(x, weights(f, rep)) for f, x in zip(targets, away)]
    own = sums[-1]
    sends = [after(x.astype(BF16), own, *before_feat) for x in sums[:-1]]
    others = [shift(x, "feat", n_feat, d + 1) for d, x in enumerate(sends)]

    extras = []
    if extra:
        first = swap_near(jnp.concatenate([packed[-2], far]))
        for j in range(n_shard):
            at = slice(j * extra, (j + 1) * extra)
            extras += [first[at], second[at]]
    for d in range(2, n_shard - 1):
        here.append(shift(after(packed[d], *sends), "shard", n_shard, d))
    last = shift(after(packed[n_shard - 1], here[-1]), "shard", n_shard, n_shard - 1)

    sure = [True] * len(here) + [True, False] * (len(extras) // 2)
    high, low, early = early_scores(own, others, here + extras, flag, sure)
    shares = row_scores(table, last, high, low, early, rows, n_rep, bulk, extra, cuts)
    total = shares[0]
    for d in range(1, n_rep):
        total = total + shift(shares[d], "rep", n_rep, d)
    share = total.shape[1] // n_feat

    def for_feat(f):
        return lax.dynamic_slice_in_dim(total, f * share, share, 1)

    result = for_feat(feat)
    for d in range(1, n_feat):
        result = result + shift(for_feat((feat + d) % n_feat).astype(BF16), "feat", n_feat, d).astype(F32)
    return result.T[None]


def solution(mesh):
    return jax.shard_map(
        body,
        mesh=mesh,
        in_specs=(
            P(("groups", "shard"), "feat"),
            P("groups"),
            P(("groups", "shard"), None, ("feat", "rep")),
            P("shard", None, ("feat", "rep")),
            P(),
            P(),
        ),
        out_specs=P(("groups", "shard"), ("feat", "rep"), None),
        check_vma=False,
    )
```

```python
import functools

import jax
import jax.numpy as jnp
from jax import lax
from jax.experimental import pallas as pl
from jax.experimental.pallas import tpu as pltpu
from jax.sharding import PartitionSpec as P

F32, BF16, I32 = jnp.float32, jnp.bfloat16, jnp.int32
VMEM = pl.BlockSpec(memory_space=pltpu.VMEM)
ANY = pl.BlockSpec(memory_space=pl.ANY)
SMEM = pl.BlockSpec(memory_space=pltpu.SMEM)
PARAMS = pltpu.CompilerParams(vmem_limit_bytes=50 * 2**20)
FIRST = pltpu.CompilerParams(vmem_limit_bytes=60 * 2**20)
LANES = 128


def shift(x, axis, size, by):
    return lax.ppermute(x, axis, [(i, (i + by) % size) for i in range(size)])


def swap(x, axis, size, bit):
    return lax.ppermute(x, axis, [(i, i ^ bit) for i in range(size)])


def dot(a, b):
    return jnp.dot(a, b, preferred_element_type=F32)


def cost(flops, nbytes):
    return pl.CostEstimate(flops=1, bytes_accessed=1, transcendentals=0)


def after(x, *others):
    def kernel(*refs):
        pass

    return pl.pallas_call(
        kernel,
        in_specs=[ANY] * (1 + len(others)),
        out_specs=ANY,
        out_shape=jax.ShapeDtypeStruct(x.shape, x.dtype),
        input_output_aliases={0: 0},
        cost_estimate=cost(0, 0),
        compiler_params=PARAMS,
        name="after",
    )(x, *others)


def pick_queries(query_store, block_slot, pattern, n_group):
    local_blocks, block_rows, width = query_store.shape
    n_cluster, n_list = pattern.shape
    part = block_rows // n_group

    def place(t, pattern_ref, slot_ref):
        me = lax.axis_index("shard")
        found = jnp.int32(0)
        for k in range(n_list):
            slot = slot_ref[pattern_ref[lax.rem(me + t, jnp.int32(n_cluster)), k]]
            hit = (lax.div(slot, jnp.int32(local_blocks)) == me).astype(I32)
            found = found + hit * lax.rem(slot, jnp.int32(local_blocks))
        return found, lax.axis_index("groups"), 0

    def kernel(pattern_ref, slot_ref, in_ref, out_ref):
        out_ref[...] = in_ref[...]

    return pl.pallas_call(
        kernel,
        grid_spec=pltpu.PrefetchScalarGridSpec(
            num_scalar_prefetch=2,
            grid=(n_cluster,),
            in_specs=[pl.BlockSpec((1, part, width), place)],
            out_specs=pl.BlockSpec((1, part, width), lambda t, p, s: (t, 0, 0)),
        ),
        out_shape=jax.ShapeDtypeStruct((n_cluster, part, width), BF16),
        cost_estimate=cost(0, 4 * n_cluster * part * width),
        compiler_params=FIRST,
        name="pick_queries",
    )(pattern, block_slot, query_store)


def join_queries(parts, block_slot, pattern, local_blocks, n_feat, n_rep, *others):
    n_group = len(parts)
    n_cluster, part, width = parts[0].shape
    n_list = pattern.shape[1]
    total = n_list * n_group * part
    share = total // (n_feat * n_rep)
    unit = min(share, part)

    def kernel(pattern_ref, slot_ref, *refs):
        out_ref, rows_ref = refs[-2:]
        me, group = lax.axis_index("shard"), lax.axis_index("groups")
        for k in range(n_list):
            owner = lax.div(slot_ref[pattern_ref[me, k]], jnp.int32(local_blocks))
            hops = lax.rem(me + (n_cluster - owner), jnp.int32(n_cluster))
            for d in range(n_group):
                origin = lax.rem(group + (n_group - d), jnp.int32(n_group))
                for u in range(part // unit):
                    first = (k * n_group + origin) * part + u * unit
                    chunk = lax.div(first, jnp.int32(share))
                    goal = lax.rem(chunk, jnp.int32(n_rep)) * n_feat + lax.div(chunk, jnp.int32(n_rep))
                    goal = goal * share + lax.rem(first, jnp.int32(share))
                    rows_ref[pl.ds(pl.multiple_of(goal, unit), unit), :] = refs[d][hops, u * unit:(u + 1) * unit, :]
        out_ref[...] = rows_ref[...].T

    return pl.pallas_call(
        kernel,
        in_specs=[SMEM, SMEM] + [VMEM] * n_group + [ANY] * len(others),
        out_specs=VMEM,
        out_shape=jax.ShapeDtypeStruct((width, total), BF16),
        scratch_shapes=[pltpu.VMEM((total, width), BF16)],
        cost_estimate=cost(0, 4 * total * width),
        compiler_params=PARAMS,
        name="join_queries",
    )(pattern, block_slot, *parts, *others)


def pack_rows(train, ids, columns, bulk, extra, cuts):
    rows = train.shape[0]
    lines = rows // LANES
    n_shard = ids.shape[0] // lines

    def kernel(ids_ref, train_ref, *rest):
        outs, goal_ref = rest[:-1], rest[-1]
        me = lax.axis_index("shard")
        own = ids_ref[...]
        masks = [(own == c).astype(F32) for c in range(n_shard)]
        stacked = jnp.concatenate(masks, axis=0).astype(BF16)
        lane_from = lax.broadcasted_iota(I32, (LANES, LANES), 0)
        lane_to = lax.broadcasted_iota(I32, (LANES, LANES), 1)
        in_line = dot(stacked, (lane_from < lane_to).astype(F32).astype(BF16))
        line_sum = dot(stacked, jnp.ones((LANES, LANES), BF16)).astype(BF16)
        size = n_shard * lines
        to = lax.broadcasted_iota(I32, (size, size), 0)
        since = lax.broadcasted_iota(I32, (size, size), 1)
        same = (to // lines) == (since // lines)
        ahead = dot((same & (since < to)).astype(F32).astype(BF16), line_sum)
        whole = dot(same.astype(F32).astype(BF16), line_sum)
        rank = in_line + ahead
        goal = jnp.zeros((lines, LANES), F32)
        past = jnp.zeros((lines, LANES), F32)
        for c in range(n_shard):
            part = slice(c * lines, (c + 1) * lines)
            place = rank[part] + c * bulk
            if extra:
                surplus = n_shard * bulk + past + rank[part] - bulk
                place = jnp.where(rank[part] < bulk, place, surplus)
                past = past + jnp.floor((jnp.maximum(whole[part] - bulk, 0.0) + 15.0) * 0.0625) * 16.0
            goal = goal + masks[c] * place
        goal_ref[...] = goal.astype(I32)

        def fill(out, base):
            size = out.shape[0]
            tile = 128 if size % 128 == 0 else size
            for at in range(0, size, tile):
                index = lax.broadcasted_iota(I32, (tile, LANES), 0) + (base + at)
                pick = [(index == goal_ref[a:a + 1, :]).astype(F32).astype(BF16) for a in range(lines)]
                out[at:at + tile, :] = dot(jnp.concatenate(pick, axis=1), train_ref[...]).astype(BF16)

        for out, (hops, first, _) in zip(outs, cuts):
            fill(out, lax.rem(me + hops, jnp.int32(n_shard)) * bulk + first)
        for j, out in enumerate(outs[len(cuts):]):
            fill(out, n_shard * bulk + j * extra)

    shapes = [jax.ShapeDtypeStruct((n, columns), BF16) for _, _, n in cuts]
    shapes += [jax.ShapeDtypeStruct((extra, columns), BF16)] * (2 if extra else 0)
    packed = n_shard * bulk + 2 * extra
    return pl.pallas_call(
        kernel,
        grid=(1,),
        in_specs=[
            pl.BlockSpec((lines, LANES), lambda i: (lax.axis_index("shard"), 0)),
            pl.BlockSpec((rows, columns), lambda i: (0, lax.axis_index("rep"))),
        ],
        out_specs=[VMEM] * len(shapes),
        out_shape=shapes,
        scratch_shapes=[pltpu.VMEM((lines, LANES), I32)],
        cost_estimate=cost(2 * packed * rows * columns, 2 * (rows + packed) * columns),
        compiler_params=PARAMS,
        name="pack_rows",
    )(ids, train)


def partial_weights(matrix, chosen, block, depth, dtype, *addends, others=()):
    width, total = chosen.shape
    tile = 256 if depth % 256 == 0 else depth
    steps = depth // tile

    def kernel(block_ref, matrix_ref, chosen_ref, *rest):
        value = dot(matrix_ref[...], chosen_ref[...])
        for ref in rest[:len(addends)]:
            value = value + ref[...]
        rest[-1][...] = value.astype(dtype)

    rows = pl.BlockSpec((tile, total), lambda i, b: (i, 0))
    return pl.pallas_call(
        kernel,
        grid_spec=pltpu.PrefetchScalarGridSpec(
            num_scalar_prefetch=1,
            grid=(steps,),
            in_specs=[
                pl.BlockSpec((tile, width), lambda i, b: (b[0] * steps + i, 0)),
                pl.BlockSpec((width, total), lambda i, b: (0, 0)),
            ]
            + [rows] * len(addends)
            + [ANY] * len(others),
            out_specs=rows,
        ),
        out_shape=jax.ShapeDtypeStruct((depth, total), dtype),
        cost_estimate=cost(2 * depth * width * total, 2 * depth * width + 4 * depth * total),
        compiler_params=PARAMS,
        name="partial_weights",
    )(jnp.reshape(block, (1,)).astype(I32), matrix, chosen, *addends, *others)


def row_table(ids, lines, bulk, extra):
    n_shard = ids.shape[0] // lines

    def kernel(ids_ref, table_ref, flag_ref):
        me = lax.axis_index("shard")
        start = jnp.int32(0)
        most = jnp.int32(0)
        for s in range(n_shard):
            line = ids_ref[s * lines:(s + 1) * lines, :]

            def count(c):
                return jnp.sum((line == c).astype(I32))

            mine = count(me)
            before = jnp.int32(0)
            if extra:
                surplus = jnp.int32(0)
                for c in range(n_shard):
                    over = lax.div(jnp.maximum(count(c) - bulk, 0) + 15, jnp.int32(16)) * 16
                    before = before + jnp.where(c < me, over, 0)
                    surplus = surplus + over
                most = jnp.maximum(most, surplus)
            table_ref[s, 0] = start
            table_ref[s, 1] = jnp.minimum(mine, bulk)
            table_ref[s, 2] = lax.div(before, jnp.int32(16))
            table_ref[s, 3] = jnp.maximum(mine - bulk, 0)
            start = start + mine
        flag_ref[...] = jnp.full((8, LANES), (most > extra).astype(I32))

    return pl.pallas_call(
        kernel,
        in_specs=[VMEM],
        out_specs=[SMEM, VMEM],
        out_shape=[jax.ShapeDtypeStruct((n_shard, 4), I32), jax.ShapeDtypeStruct((8, LANES), I32)],
        cost_estimate=cost(0, 4 * ids.size),
        compiler_params=PARAMS,
        name="row_table",
    )(ids)


def put(acc, x, start, count=None):
    tiles, _, width = x.shape
    first, within = lax.div(start, jnp.int32(8)), lax.rem(start, jnp.int32(8))
    turned = pltpu.roll(x, within, 1)
    row = lax.broadcasted_iota(I32, (1, 8, width), 1)
    keep = row < within
    pieces = jnp.where(keep, jnp.concatenate([turned[:1], turned]), jnp.concatenate([turned, turned[-1:]]))
    if count is None:
        pieces = jnp.concatenate([jnp.where(keep, acc[pl.ds(first, 1)], turned[:1]), pieces[1:]])
    else:
        at = lax.broadcasted_iota(I32, (tiles + 1, 8, width), 0) * 8 + lax.broadcasted_iota(
            I32, (tiles + 1, 8, width), 1
        )
        pieces = jnp.where(
            (at >= within) & (at < within + count), pieces, acc[pl.ds(first, tiles + 1)]
        )
    acc[pl.ds(first, tiles + 1)] = pieces


def give(value, outs, rep, half):
    n_rep = len(outs)
    for r in range(n_rep):
        @pl.when(rep == r)
        def _():
            for d, out in enumerate(outs):
                at = ((r + d) % n_rep) * half
                out[...] = value(at)


def early_scores(own, others, pieces, firsts, seconds, table, rows, n_rep, n_shard, bulk):
    depth, width = own.shape
    half = width // n_rep
    n_other, n_piece = len(others), len(pieces)
    extra = firsts[0].shape[0] if firsts else 0
    last_hops = n_shard - 1

    def kernel(table_ref, *refs):
        own_ref, refs = refs[0], refs[1:]
        other_refs, refs = refs[:n_other], refs[n_other:]
        piece_refs, refs = refs[:n_piece], refs[n_piece:]
        first_refs, refs = refs[:len(firsts)], refs[len(firsts):]
        second_refs, refs = refs[:len(seconds)], refs[len(seconds):]
        high_ref, low_ref, outs, (scored, held, acc) = refs[0], refs[1], refs[2:2 + n_rep], refs[2 + n_rep:]
        me, rep = lax.axis_index("shard"), lax.axis_index("rep")
        weight = own_ref[...]
        for ref in other_refs:
            weight = weight + ref[...].astype(F32)
        high = weight.astype(BF16)
        high_ref[...] = high
        low_ref[...] = (weight - high.astype(F32)).astype(BF16)

        def score(x):
            y = dot(x, high_ref[...]) + dot(x, low_ref[...])
            return y.reshape(x.shape[0] // 8, 8, width)

        for hops, ref in enumerate(piece_refs):
            scored[lax.rem(me + (n_shard - hops), jnp.int32(n_shard))] = score(ref[...])
        last = lax.rem(me + (n_shard - last_hops), jnp.int32(n_shard))
        for s in range(n_shard):
            start = table_ref[s, 0]

            @pl.when(last != s)
            def _():
                put(acc, scored[s], start)

            if extra:
                @pl.when(table_ref[s, 3] > 0)
                def _():
                    apart = jnp.bitwise_xor(me, s)
                    for v in range(n_shard):
                        @pl.when(apart == v)
                        def _():
                            index = (v & 1) * 2 + v // 2
                            held[:extra, :] = first_refs[index][...]
                            held[extra:2 * extra, :] = second_refs[index][...]
                    x = held[pl.ds(pl.multiple_of(table_ref[s, 2] * 16, 16), extra), :]
                    put(acc, score(x), start + table_ref[s, 1])
        give(lambda at: acc[:rows // 8, :, at:at + half].reshape(rows, half), outs, rep, half)

    count = n_shard * bulk
    return pl.pallas_call(
        kernel,
        in_specs=[SMEM] + [VMEM] * (1 + n_other + n_piece + len(firsts) + len(seconds)),
        out_specs=[VMEM] * (2 + n_rep),
        out_shape=[jax.ShapeDtypeStruct((depth, width), BF16)] * 2
        + [jax.ShapeDtypeStruct((rows, half), F32)] * n_rep,
        scratch_shapes=[
            pltpu.VMEM((n_shard, bulk // 8, 8, width), F32),
            pltpu.VMEM((3 * extra + 16, depth), BF16),
            pltpu.VMEM(((rows + bulk + extra) // 8 + 2, 8, width), F32),
        ],
        cost_estimate=cost(4 * count * depth * width, 10 * depth * width + count * (2 * depth + 4 * width)),
        compiler_params=PARAMS,
        name="early_scores",
    )(table, own, *others, *pieces, *firsts, *seconds)


def late_scores(last, high, low, n_rep, *others):
    rows = last.shape[0]
    width = high.shape[1]
    half = width // n_rep

    def kernel(last_ref, high_ref, low_ref, *rest):
        outs, late = rest[len(others):-1], rest[-1]
        x = last_ref[...]
        late[...] = dot(x, high_ref[...]) + dot(x, low_ref[...])
        give(lambda at: late[:, at:at + half], outs, lax.axis_index("rep"), half)

    return pl.pallas_call(
        kernel,
        in_specs=[VMEM] * 3 + [ANY] * len(others),
        out_specs=[VMEM] * n_rep,
        out_shape=[jax.ShapeDtypeStruct((rows, half), F32)] * n_rep,
        scratch_shapes=[pltpu.VMEM((rows, width), F32)],
        cost_estimate=cost(4 * rows * high.shape[0] * width, 8 * rows * width),
        compiler_params=PARAMS,
        name="late_scores",
    )(last, high, low, *others)


def merge(table, early, late, n_shard):
    rows, width = early[0].shape
    last_rows = late[0].shape[0]
    last_hops = n_shard - 1

    def kernel(table_ref, *refs):
        early_refs, late_refs = refs[:len(early)], refs[len(early):-2]
        out_ref, acc = refs[-2:]
        source = lax.rem(lax.axis_index("shard") + (n_shard - last_hops), jnp.int32(n_shard))

        def total(parts):
            value = parts[0][...]
            for ref in parts[1:]:
                value = value + ref[...].astype(F32)
            return value.reshape(value.shape[0] // 8, 8, width)

        acc[:rows // 8] = total(early_refs)
        put(acc, total(late_refs), table_ref[source, 0], table_ref[source, 1])
        out_ref[...] = acc[:rows // 8].reshape(rows, width).T

    return pl.pallas_call(
        kernel,
        in_specs=[SMEM] + [VMEM] * (len(early) + len(late)),
        out_specs=VMEM,
        out_shape=jax.ShapeDtypeStruct((width, rows), F32),
        scratch_shapes=[pltpu.VMEM(((rows + last_rows) // 8 + 2, 8, width), F32)],
        cost_estimate=cost(0, 8 * rows * width),
        compiler_params=PARAMS,
        name="merge",
    )(table, *early, *late)


def body(train, cluster_ids, precond, query_store, block_slot, pattern):
    n_group, n_shard = lax.axis_size("groups"), lax.axis_size("shard")
    n_feat, n_rep = lax.axis_size("feat"), lax.axis_size("rep")
    feat, rep = lax.axis_index("feat"), lax.axis_index("rep")
    rows = train.shape[0]
    lines = rows // LANES
    base = rows // n_shard
    columns = train.shape[1] // n_rep
    extra = base // 2 if n_shard == 4 else 0
    bulk = base if extra else base + base // 2
    ids = cluster_ids.reshape(-1, LANES)

    me = lax.axis_index("shard")
    picked = pick_queries(query_store, block_slot, pattern, n_group)
    pieces = [picked[:1]]
    for d in range(1, n_shard):
        pieces.append(shift(picked[d:d + 1], "shard", n_shard, d))

    cuts = [(d, 0, bulk) for d in range(n_shard)]
    packed = pack_rows(train, ids, columns, bulk, extra, cuts)
    table, flag = row_table(ids, lines, bulk, extra)
    here = {0: packed[0]}
    last_hops = n_shard - 1

    def swap_far(x):
        return jnp.concatenate([x, swap(x, "shard", n_shard, 2)])

    def swap_near(x):
        return jnp.concatenate([x, swap(x, "shard", n_shard, 1)])

    before_join = []
    if extra:
        for d in range(1, n_group):
            flag = jnp.maximum(flag, shift(flag, "groups", n_group, d))
        second = lax.cond(
            flag[0, 0] > 0,
            lambda x: swap_near(swap_far(x)),
            lambda x: jnp.zeros((n_shard * extra, columns), BF16),
            packed[-1],
        )
        far = swap(packed[-2], "shard", n_shard, 2)
        before_join = [far, second]

    arrived = after(jnp.concatenate(pieces), packed[1], flag)
    parts = [arrived] + [shift(arrived, "groups", n_group, d) for d in range(1, n_group)]
    chosen = join_queries(parts, block_slot, pattern, query_store.shape[0], n_feat, n_rep, *before_join)
    here[1] = shift(after(packed[1], *before_join[:1]), "shard", n_shard, 1)

    matrix = precond[0]

    def weights(f, r, dtype, *addends, others=()):
        return partial_weights(matrix, chosen, f * n_rep + r, columns, dtype, *addends, others=others)

    def away(f, others=()):
        return [
            shift(weights(f, (rep + d) % n_rep, F32, others=others), "rep", n_rep, d) for d in range(1, n_rep)
        ]

    targets = [(feat + d) % n_feat for d in range(1, n_feat)]
    sends = [weights(f, rep, BF16, *x) for f, x in [(f, away(f)) for f in targets]]
    others = [shift(x, "feat", n_feat, d + 1) for d, x in enumerate(sends)]
    own = weights(feat, rep, F32, *away(feat, [here[1], *sends]))

    firsts, seconds = [], []
    if extra:
        first = swap_near(jnp.concatenate([packed[-2], far]))
        firsts = [first[j * extra:(j + 1) * extra] for j in range(n_shard)]
        seconds = [second[j * extra:(j + 1) * extra] for j in range(n_shard)]
    for d in range(2, last_hops):
        here[d] = shift(after(packed[d], *sends), "shard", n_shard, d)
    last = shift(after(packed[last_hops], here[last_hops - 1]), "shard", n_shard, last_hops)

    ready = [here[d] for d in range(last_hops)]
    high, low, *shares = early_scores(
        own, others, ready, firsts, seconds, table, rows, n_rep, n_shard, bulk
    )

    def over_rep(shares):
        total = shares[0]
        for d in range(1, n_rep):
            total = total + shift(shares[d], "rep", n_rep, d)
        return total

    def for_feat(total, d):
        share = total.shape[1] // n_feat
        return lax.dynamic_slice_in_dim(total, ((feat + d) % n_feat) * share, share, 1)

    early = over_rep(shares)
    early_sends = [for_feat(early, d).astype(BF16) for d in range(1, n_feat)]
    late = over_rep(late_scores(last, high, low, n_rep, *early_sends))
    late_sends = [for_feat(late, d).astype(BF16) for d in range(1, n_feat)]
    early_all = [for_feat(early, 0)] + [shift(x, "feat", n_feat, d + 1) for d, x in enumerate(early_sends)]
    late_all = [for_feat(late, 0)] + [shift(x, "feat", n_feat, d + 1) for d, x in enumerate(late_sends)]
    return merge(table, early_all, late_all, n_shard)[None]


def solution(mesh):
    return jax.shard_map(
        body,
        mesh=mesh,
        in_specs=(
            P(("groups", "shard"), "feat"),
            P("groups"),
            P(("groups", "shard"), None, ("feat", "rep")),
            P("shard", None, ("feat", "rep")),
            P(),
            P(),
        ),
        out_specs=P(("groups", "shard"), ("feat", "rep"), None),
        check_vma=False,
    )
```

```python
import functools

import jax
import jax.numpy as jnp
from jax import lax
from jax.experimental import pallas as pl
from jax.experimental.pallas import tpu as pltpu
from jax.sharding import PartitionSpec as P

F32, BF16, I32 = jnp.float32, jnp.bfloat16, jnp.int32
VMEM = pl.BlockSpec(memory_space=pltpu.VMEM)
ANY = pl.BlockSpec(memory_space=pl.ANY)
SMEM = pl.BlockSpec(memory_space=pltpu.SMEM)
PARAMS = pltpu.CompilerParams(vmem_limit_bytes=50 * 2**20)
FIRST = pltpu.CompilerParams(vmem_limit_bytes=60 * 2**20)
LANES = 128


def shift(x, axis, size, by):
    return lax.ppermute(x, axis, [(i, (i + by) % size) for i in range(size)])


def swap(x, axis, size, bit):
    return lax.ppermute(x, axis, [(i, i ^ bit) for i in range(size)])


def dot(a, b):
    return jnp.dot(a, b, preferred_element_type=F32)


def cost(flops, nbytes):
    return pl.CostEstimate(flops=1, bytes_accessed=1, transcendentals=0)


def after(x, *others):
    def kernel(*refs):
        pass

    return pl.pallas_call(
        kernel,
        in_specs=[ANY] * (1 + len(others)),
        out_specs=ANY,
        out_shape=jax.ShapeDtypeStruct(x.shape, x.dtype),
        input_output_aliases={0: 0},
        cost_estimate=cost(0, 0),
        compiler_params=PARAMS,
        name="after",
    )(x, *others)


def pick_queries(query_store, block_slot, pattern, n_group):
    local_blocks, block_rows, width = query_store.shape
    n_cluster, n_list = pattern.shape
    part = block_rows // n_group

    def kernel(pattern_ref, slot_ref, in_ref, *rest):
        outs, sem = rest[:-1], rest[-1]
        me, group = lax.axis_index("shard"), lax.axis_index("groups")
        copies = []
        for t, out in enumerate(outs):
            target = lax.rem(me + t, jnp.int32(n_cluster))
            found = jnp.int32(0)
            for k in range(n_list):
                slot = slot_ref[pattern_ref[target, k]]
                hit = (lax.div(slot, jnp.int32(local_blocks)) == me).astype(I32)
                found = found + hit * lax.rem(slot, jnp.int32(local_blocks))
            rows = pl.ds(pl.multiple_of(group * part, part), part)
            copies.append(pltpu.make_async_copy(in_ref.at[found, rows], out.at[0], sem.at[t]))
            copies[-1].start()
        for copy in copies:
            copy.wait()

    return pl.pallas_call(
        kernel,
        in_specs=[SMEM, SMEM, ANY],
        out_specs=[VMEM] * n_cluster,
        out_shape=[jax.ShapeDtypeStruct((1, part, width), BF16)] * n_cluster,
        scratch_shapes=[pltpu.SemaphoreType.DMA((n_cluster,))],
        cost_estimate=cost(0, 4 * n_cluster * part * width),
        compiler_params=FIRST,
        name="pick_queries",
    )(pattern, block_slot, query_store)


def join_queries(parts, block_slot, pattern, local_blocks, n_feat, n_rep, *others):
    n_group = len(parts)
    n_cluster, part, width = parts[0].shape
    n_list = pattern.shape[1]
    total = n_list * n_group * part
    share = total // (n_feat * n_rep)
    unit = min(share, part)

    def kernel(pattern_ref, slot_ref, *refs):
        outs, rows_ref = refs[-1 - n_rep:-1], refs[-1]
        me, group = lax.axis_index("shard"), lax.axis_index("groups")
        for k in range(n_list):
            owner = lax.div(slot_ref[pattern_ref[me, k]], jnp.int32(local_blocks))
            hops = lax.rem(me + (n_cluster - owner), jnp.int32(n_cluster))
            for d in range(n_group):
                origin = lax.rem(group + (n_group - d), jnp.int32(n_group))
                for u in range(part // unit):
                    first = (k * n_group + origin) * part + u * unit
                    chunk = lax.div(first, jnp.int32(share))
                    goal = lax.rem(chunk, jnp.int32(n_rep)) * n_feat + lax.div(chunk, jnp.int32(n_rep))
                    goal = goal * share + lax.rem(first, jnp.int32(share))
                    rows_ref[pl.ds(pl.multiple_of(goal, unit), unit), :] = refs[d][hops, u * unit:(u + 1) * unit, :]
        half = total // n_rep
        for r in range(n_rep):
            @pl.when(lax.axis_index("rep") == r)
            def _():
                for d, out in enumerate(outs):
                    at = ((r + d) % n_rep) * half
                    out[...] = rows_ref[at:at + half, :].T

    return pl.pallas_call(
        kernel,
        in_specs=[SMEM, SMEM] + [VMEM] * n_group + [ANY] * len(others),
        out_specs=[VMEM] * n_rep,
        out_shape=[jax.ShapeDtypeStruct((width, total // n_rep), BF16)] * n_rep,
        scratch_shapes=[pltpu.VMEM((total, width), BF16)],
        cost_estimate=cost(0, 4 * total * width),
        compiler_params=PARAMS,
        name="join_queries",
    )(pattern, block_slot, *parts, *others)


def select(goal_ref, train_ref, base, size):
    tile = 128 if size % 128 == 0 else size
    found = []
    for at in range(0, size, tile):
        index = lax.broadcasted_iota(I32, (tile, LANES), 0) + (base + at)
        pick = [(index == goal_ref[a:a + 1, :]).astype(F32).astype(BF16) for a in range(goal_ref.shape[0])]
        found.append(dot(jnp.concatenate(pick, axis=1), train_ref[...]).astype(BF16))
    return jnp.concatenate(found)


def own_rows(goal, train, bulk):
    def kernel(goal_ref, train_ref, out_ref):
        out_ref[...] = select(goal_ref, train_ref, lax.axis_index("shard") * bulk, bulk)

    return pl.pallas_call(
        kernel,
        in_specs=[VMEM] * 2,
        out_specs=VMEM,
        out_shape=jax.ShapeDtypeStruct((bulk, train.shape[1]), BF16),
        cost_estimate=cost(2 * bulk * train.size, 2 * train.size),
        compiler_params=PARAMS,
        name="own_rows",
    )(goal, train)


def pack_rows(train, ids, columns, bulk, extra, cuts):
    rows = train.shape[0]
    lines = rows // LANES
    n_shard = ids.shape[0] // lines

    def kernel(ids_ref, train_ref, *rest):
        outs, goal_ref = rest[:-1], rest[-1]
        me = lax.axis_index("shard")
        own = ids_ref[...]
        masks = [(own == c).astype(F32) for c in range(n_shard)]
        stacked = jnp.concatenate(masks, axis=0).astype(BF16)
        lane_from = lax.broadcasted_iota(I32, (LANES, LANES), 0)
        lane_to = lax.broadcasted_iota(I32, (LANES, LANES), 1)
        in_line = dot(stacked, (lane_from < lane_to).astype(F32).astype(BF16))
        line_sum = dot(stacked, jnp.ones((LANES, LANES), BF16)).astype(BF16)
        size = n_shard * lines
        to = lax.broadcasted_iota(I32, (size, size), 0)
        since = lax.broadcasted_iota(I32, (size, size), 1)
        same = (to // lines) == (since // lines)
        ahead = dot((same & (since < to)).astype(F32).astype(BF16), line_sum)
        whole = dot(same.astype(F32).astype(BF16), line_sum)
        rank = in_line + ahead
        goal = jnp.zeros((lines, LANES), F32)
        past = jnp.zeros((lines, LANES), F32)
        for c in range(n_shard):
            part = slice(c * lines, (c + 1) * lines)
            place = rank[part] + c * bulk
            if extra:
                surplus = n_shard * bulk + past + rank[part] - bulk
                place = jnp.where(rank[part] < bulk, place, surplus)
                past = past + jnp.floor((jnp.maximum(whole[part] - bulk, 0.0) + 15.0) * 0.0625) * 16.0
            goal = goal + masks[c] * place
        goal_ref[...] = goal.astype(I32)

        def fill(out, base):
            out[...] = select(goal_ref, train_ref, base, out.shape[0])

        for out, (hops, first, _) in zip(outs, cuts):
            fill(out, lax.rem(me + hops, jnp.int32(n_shard)) * bulk + first)
        for j, out in enumerate(outs[len(cuts):]):
            fill(out, n_shard * bulk + j * extra)

    shapes = [jax.ShapeDtypeStruct((n, columns), BF16) for _, _, n in cuts]
    shapes += [jax.ShapeDtypeStruct((extra, columns), BF16)] * (2 if extra else 0)
    shapes += [jax.ShapeDtypeStruct((lines, LANES), I32)]
    packed = n_shard * bulk + 2 * extra
    return pl.pallas_call(
        kernel,
        grid=(1,),
        in_specs=[
            pl.BlockSpec((lines, LANES), lambda i: (lax.axis_index("shard"), 0)),
            pl.BlockSpec((rows, columns), lambda i: (0, lax.axis_index("rep"))),
        ],
        out_specs=[VMEM] * len(shapes),
        out_shape=shapes,
        cost_estimate=cost(2 * packed * rows * columns, 2 * (rows + packed) * columns),
        compiler_params=PARAMS,
        name="pack_rows",
    )(ids, train)


def partial_weights(matrices, queries, block, depth, dtype, *others):
    width, total = queries[0].shape
    tile = 512 if depth % 512 == 0 else depth
    steps = depth // tile
    n = len(matrices)

    def kernel(block_ref, *refs):
        value = dot(refs[0][...], refs[n][...])
        for j in range(1, n):
            value = value + dot(refs[j][...], refs[n + j][...])
        refs[-1][...] = value.astype(dtype)

    return pl.pallas_call(
        kernel,
        grid_spec=pltpu.PrefetchScalarGridSpec(
            num_scalar_prefetch=1,
            grid=(steps,),
            in_specs=[pl.BlockSpec((tile, width), lambda i, b: (b[0] * steps + i, 0))] * n
            + [pl.BlockSpec((width, total), lambda i, b: (0, 0))] * n
            + [ANY] * len(others),
            out_specs=pl.BlockSpec((tile, total), lambda i, b: (i, 0)),
        ),
        out_shape=jax.ShapeDtypeStruct((depth, total), dtype),
        cost_estimate=cost(2 * n * depth * width * total, 2 * n * depth * width + 4 * depth * total),
        compiler_params=PARAMS,
        name="partial_weights",
    )(jnp.reshape(block, (1,)).astype(I32), *matrices, *queries, *others)


def row_table(ids, lines, bulk, extra):
    n_shard = ids.shape[0] // lines

    def kernel(ids_ref, table_ref, flag_ref):
        me = lax.axis_index("shard")
        start = jnp.int32(0)
        most = jnp.int32(0)
        for s in range(n_shard):
            line = ids_ref[s * lines:(s + 1) * lines, :]

            def count(c):
                return jnp.sum((line == c).astype(I32))

            mine = count(me)
            before = jnp.int32(0)
            if extra:
                surplus = jnp.int32(0)
                for c in range(n_shard):
                    over = lax.div(jnp.maximum(count(c) - bulk, 0) + 15, jnp.int32(16)) * 16
                    before = before + jnp.where(c < me, over, 0)
                    surplus = surplus + over
                most = jnp.maximum(most, surplus)
            table_ref[s, 0] = start
            table_ref[s, 1] = jnp.minimum(mine, bulk)
            table_ref[s, 2] = lax.div(before, jnp.int32(16))
            table_ref[s, 3] = jnp.maximum(mine - bulk, 0)
            start = start + mine
        flag_ref[...] = jnp.full((8, LANES), (most > extra).astype(I32))

    return pl.pallas_call(
        kernel,
        in_specs=[VMEM],
        out_specs=[SMEM, VMEM],
        out_shape=[jax.ShapeDtypeStruct((n_shard, 4), I32), jax.ShapeDtypeStruct((8, LANES), I32)],
        cost_estimate=cost(0, 4 * ids.size),
        compiler_params=PARAMS,
        name="row_table",
    )(ids)


def put(acc, x, start, count=None):
    tiles, _, width = x.shape
    first, within = lax.div(start, jnp.int32(8)), lax.rem(start, jnp.int32(8))
    turned = pltpu.roll(x, within, 1)
    row = lax.broadcasted_iota(I32, (1, 8, width), 1)
    keep = row < within
    pieces = jnp.where(keep, jnp.concatenate([turned[:1], turned]), jnp.concatenate([turned, turned[-1:]]))
    if count is None:
        pieces = jnp.concatenate([jnp.where(keep, acc[pl.ds(first, 1)], turned[:1]), pieces[1:]])
    else:
        at = lax.broadcasted_iota(I32, (tiles + 1, 8, width), 0) * 8 + lax.broadcasted_iota(
            I32, (tiles + 1, 8, width), 1
        )
        pieces = jnp.where(
            (at >= within) & (at < within + count), pieces, acc[pl.ds(first, tiles + 1)]
        )
    acc[pl.ds(first, tiles + 1)] = pieces


def score(high_ref, low_ref, parts, rep):
    total = None
    for d, x in enumerate(parts):
        depth = x.shape[1]
        block = pl.ds(pl.multiple_of(lax.rem(rep + (len(parts) - d), jnp.int32(len(parts))) * depth, depth), depth)
        value = dot(x, high_ref[block, :]) + dot(x, low_ref[block, :])
        total = value if total is None else total + value
    return total.reshape(total.shape[0] // 8, 8, total.shape[1])


def early_scores(own, others, mine, pieces, firsts, seconds, table, rows, n_rep, n_shard, bulk, extra):
    depth, width = own.shape
    columns = depth // n_rep
    n_other, n_piece = len(others), len(pieces)
    last_hops = n_shard - 1

    def kernel(table_ref, *refs):
        own_ref, refs = refs[0], refs[1:]
        other_refs, refs = refs[:n_other], refs[n_other:]
        mine_ref, refs = refs[0], refs[1:]
        piece_refs = [refs[j * n_rep:(j + 1) * n_rep] for j in range(n_piece)]
        refs = refs[n_piece * n_rep:]
        first_refs, second_refs = refs[:len(firsts)], refs[len(firsts):len(firsts) + len(seconds)]
        high_ref, low_ref, out_ref, scored, held, acc, sem = refs[len(firsts) + len(seconds):]
        me, rep = lax.axis_index("shard"), lax.axis_index("rep")
        weight = own_ref[...]
        for ref in other_refs:
            weight = weight + ref[...].astype(F32)
        high = weight.astype(BF16)
        high_ref[...] = high
        low_ref[...] = (weight - high.astype(F32)).astype(BF16)

        scored[me] = score(high_ref, low_ref, [mine_ref[...]], jnp.int32(0))
        for j, parts in enumerate(piece_refs):
            source = lax.rem(me + (n_shard - 1 - j), jnp.int32(n_shard))
            scored[source] = score(high_ref, low_ref, [p[...] for p in parts], rep)
        last = lax.rem(me + (n_shard - last_hops), jnp.int32(n_shard))
        for s in range(n_shard):
            start = table_ref[s, 0]

            @pl.when(last != s)
            def _():
                put(acc, scored[s], start)

            if extra:
                @pl.when(table_ref[s, 3] > 0)
                def _():
                    apart = jnp.bitwise_xor(me, s)
                    index = jnp.bitwise_and(apart, 1) * 2 + lax.div(apart, jnp.int32(2))
                    rows_in = pl.ds(pl.multiple_of(index * extra, extra), extra)
                    copies = []
                    for j, ref in enumerate([*first_refs, *second_refs]):
                        r, d = j // n_rep, j % n_rep
                        goal = held.at[d, r * extra:(r + 1) * extra]
                        copies.append(pltpu.make_async_copy(ref.at[rows_in], goal, sem.at[j]))
                    for copy in copies:
                        copy.start()
                    for copy in copies:
                        copy.wait()
                    some = pl.ds(pl.multiple_of(table_ref[s, 2] * 16, 16), extra)
                    x = [held[d, some, :] for d in range(n_rep)]
                    put(acc, score(high_ref, low_ref, x, rep), start + table_ref[s, 1])
        out_ref[...] = acc[:rows // 8].reshape(rows, width)

    count = n_shard * bulk
    return pl.pallas_call(
        kernel,
        in_specs=[SMEM] + [VMEM] * (2 + n_other + n_rep * n_piece) + [ANY] * (len(firsts) + len(seconds)),
        out_specs=[VMEM] * 3,
        out_shape=[jax.ShapeDtypeStruct((depth, width), BF16)] * 2 + [jax.ShapeDtypeStruct((rows, width), F32)],
        scratch_shapes=[
            pltpu.VMEM((n_shard, bulk // 8, 8, width), F32),
            pltpu.VMEM((n_rep, 3 * extra + 16, columns), BF16),
            pltpu.VMEM(((rows + bulk + extra) // 8 + 2, 8, width), F32),
            pltpu.SemaphoreType.DMA((2 * n_rep,)),
        ],
        cost_estimate=cost(4 * count * depth * width, 10 * depth * width + count * (2 * depth + 4 * width)),
        compiler_params=PARAMS,
        name="early_scores",
    )(table, own, *others, mine, *[p for parts in pieces for p in parts], *firsts, *seconds)


def late_scores(parts, high, low):
    rows = parts[0].shape[0]
    width = high.shape[1]

    def kernel(high_ref, low_ref, *refs):
        y = score(high_ref, low_ref, [ref[...] for ref in refs[:-1]], lax.axis_index("rep"))
        refs[-1][...] = y.reshape(rows, width)

    return pl.pallas_call(
        kernel,
        in_specs=[VMEM] * (2 + len(parts)),
        out_specs=VMEM,
        out_shape=jax.ShapeDtypeStruct((rows, width), F32),
        cost_estimate=cost(4 * rows * high.size, 8 * rows * width),
        compiler_params=PARAMS,
        name="late_scores",
    )(high, low, *parts)


def merge(table, early, late, n_shard):
    rows, width = early[0].shape
    last_rows = late[0].shape[0]
    last_hops = n_shard - 1

    def kernel(table_ref, *refs):
        early_refs, late_refs = refs[:len(early)], refs[len(early):-2]
        out_ref, acc = refs[-2:]
        source = lax.rem(lax.axis_index("shard") + (n_shard - last_hops), jnp.int32(n_shard))

        def total(parts):
            value = parts[0][...]
            for ref in parts[1:]:
                value = value + ref[...].astype(F32)
            return value.reshape(value.shape[0] // 8, 8, width)

        acc[:rows // 8] = total(early_refs)
        put(acc, total(late_refs), table_ref[source, 0], table_ref[source, 1])
        out_ref[...] = acc[:rows // 8].reshape(rows, width).T

    return pl.pallas_call(
        kernel,
        in_specs=[SMEM] + [VMEM] * (len(early) + len(late)),
        out_specs=VMEM,
        out_shape=jax.ShapeDtypeStruct((width, rows), F32),
        scratch_shapes=[pltpu.VMEM(((rows + last_rows) // 8 + 2, 8, width), F32)],
        cost_estimate=cost(0, 8 * rows * width),
        compiler_params=PARAMS,
        name="merge",
    )(table, *early, *late)


def body(train, cluster_ids, precond, query_store, block_slot, pattern):
    n_group, n_shard = lax.axis_size("groups"), lax.axis_size("shard")
    n_feat, n_rep = lax.axis_size("feat"), lax.axis_size("rep")
    feat, rep = lax.axis_index("feat"), lax.axis_index("rep")
    rows = train.shape[0]
    lines = rows // LANES
    base = rows // n_shard
    columns = train.shape[1] // n_rep
    extra = base // 2 if n_shard == 4 else 0
    bulk = base if extra else base + base // 2
    ids = cluster_ids.reshape(-1, LANES)

    last_hops = n_shard - 1

    def with_rep(x):
        return [x] + [shift(x, "rep", n_rep, d) for d in range(1, n_rep)]

    matrices = with_rep(precond[0])

    picked = pick_queries(query_store, block_slot, pattern, n_group)
    pieces = [picked[0]] + [shift(picked[d], "shard", n_shard, d) for d in range(1, n_shard)]

    *packed, goal = pack_rows(train, ids, columns, bulk, extra, [(d, 0, bulk) for d in range(1, n_shard)])
    sent = dict(zip(range(1, n_shard), packed))
    table, flag = row_table(ids, lines, bulk, extra)

    def swap_far(x):
        return jnp.concatenate([x, swap(x, "shard", n_shard, 2)])

    def swap_near(x):
        return jnp.concatenate([x, swap(x, "shard", n_shard, 1)])

    mine = own_rows(goal, train, bulk)
    before_join, firsts, seconds = [mine], [], []
    if extra:
        for d in range(1, n_group):
            flag = jnp.maximum(flag, shift(flag, "groups", n_group, d))
        seconds = lax.cond(
            flag[0, 0] > 0,
            lambda x: with_rep(swap_near(swap_far(x))),
            lambda x: [jnp.zeros((n_shard * extra, columns), BF16)] * n_rep,
            packed[-1],
        )
        far = swap(packed[-2], "shard", n_shard, 2)
        before_join = [far, mine, *seconds]
        firsts = with_rep(swap_near(jnp.concatenate([packed[-2], far])))

    arrived = after(jnp.concatenate(pieces), sent[1], flag)
    parts = [arrived] + [shift(arrived, "groups", n_group, d) for d in range(1, n_group)]
    chosen = join_queries(parts, block_slot, pattern, query_store.shape[0], n_feat, n_rep, *before_join)
    queries = [chosen[0]] + [shift(chosen[d], "rep", n_rep, d) for d in range(1, n_rep)]
    here = {1: shift(after(sent[1], *before_join[:1]), "shard", n_shard, 1)}

    def weights(f, dtype, *others):
        return partial_weights(matrices, queries, f, n_rep * columns, dtype, *others)

    sends = [weights((feat + d) % n_feat, BF16) for d in range(1, n_feat)]
    others = [shift(x, "feat", n_feat, d + 1) for d, x in enumerate(sends)]
    own = weights(feat, F32, *sends)

    for d in range(2, last_hops):
        here[d] = shift(after(sent[d], own), "shard", n_shard, d)
    last = shift(after(sent[last_hops], here[last_hops - 1]), "shard", n_shard, last_hops)

    ready = [with_rep(here[d]) for d in range(1, last_hops)]
    high, low, early = early_scores(
        own, others, mine, ready, firsts, seconds, table, rows, n_rep, n_shard, bulk, extra
    )

    def for_feat(total, d):
        share = total.shape[1] // n_feat
        return lax.dynamic_slice_in_dim(total, ((feat + d) % n_feat) * share, share, 1)

    def over_feat(total, sends):
        return [for_feat(total, 0)] + [shift(x, "feat", n_feat, d + 1) for d, x in enumerate(sends)]

    early_sends = [for_feat(early, d).astype(BF16) for d in range(1, n_feat)]
    late = late_scores(with_rep(after(last, *early_sends)), high, low)
    late_sends = [for_feat(late, d).astype(BF16) for d in range(1, n_feat)]
    return merge(table, over_feat(early, early_sends), over_feat(late, late_sends), n_shard)[None]


def solution(mesh):
    return jax.shard_map(
        body,
        mesh=mesh,
        in_specs=(
            P(("groups", "shard"), "feat"),
            P("groups"),
            P(("groups", "shard"), None, ("feat", "rep")),
            P("shard", None, ("feat", "rep")),
            P(),
            P(),
        ),
        out_specs=P(("groups", "shard"), ("feat", "rep"), None),
        check_vma=False,
    )
```

```python
import functools

import jax
import jax.numpy as jnp
from jax import lax
from jax.experimental import pallas as pl
from jax.experimental.pallas import tpu as pltpu
from jax.sharding import PartitionSpec as P

F32, BF16, I32 = jnp.float32, jnp.bfloat16, jnp.int32
VMEM = pl.BlockSpec(memory_space=pltpu.VMEM)
ANY = pl.BlockSpec(memory_space=pl.ANY)
SMEM = pl.BlockSpec(memory_space=pltpu.SMEM)
PARAMS = pltpu.CompilerParams(vmem_limit_bytes=24 * 2**20)
FIRST = pltpu.CompilerParams(vmem_limit_bytes=60 * 2**20)
LANES = 128


def shift(x, axis, size, by):
    return lax.ppermute(x, axis, [(i, (i + by) % size) for i in range(size)])


def swap(x, axis, size, bit):
    return lax.ppermute(x, axis, [(i, i ^ bit) for i in range(size)])


def dot(a, b):
    return jnp.dot(a, b, preferred_element_type=F32)


def cost(flops, nbytes):
    return pl.CostEstimate(flops=1, bytes_accessed=1, transcendentals=0)


def after(x, *others):
    def kernel(*refs):
        pass

    return pl.pallas_call(
        kernel,
        in_specs=[ANY] * (1 + len(others)),
        out_specs=ANY,
        out_shape=jax.ShapeDtypeStruct(x.shape, x.dtype),
        input_output_aliases={0: 0},
        cost_estimate=cost(0, 0),
        compiler_params=PARAMS,
        name="after",
    )(x, *others)


def stack(parts, *others):
    size, width = parts[0].shape
    n = len(parts)

    def kernel(*refs):
        out, sem = refs[-2:]
        copies = [
            pltpu.make_async_copy(refs[j], out.at[j * size:(j + 1) * size], sem.at[j]) for j in range(n)
        ]
        for copy in copies:
            copy.start()
        for copy in copies:
            copy.wait()

    return pl.pallas_call(
        kernel,
        in_specs=[ANY] * (n + len(others)),
        out_specs=ANY,
        out_shape=jax.ShapeDtypeStruct((n * size, width), parts[0].dtype),
        scratch_shapes=[pltpu.SemaphoreType.DMA((n,))],
        cost_estimate=cost(0, 0),
        compiler_params=PARAMS,
        name="stack",
    )(*parts, *others)


def pick_queries(query_store, block_slot, pattern, n_group):
    local_blocks, block_rows, width = query_store.shape
    n_cluster, n_list = pattern.shape
    part = block_rows // n_group

    def kernel(pattern_ref, slot_ref, in_ref, *rest):
        outs, sem = rest[:-1], rest[-1]
        me, group = lax.axis_index("shard"), lax.axis_index("groups")
        copies = []
        for t, out in enumerate(outs):
            target = lax.rem(me + t, jnp.int32(n_cluster))
            found = jnp.int32(0)
            for k in range(n_list):
                slot = slot_ref[pattern_ref[target, k]]
                hit = (lax.div(slot, jnp.int32(local_blocks)) == me).astype(I32)
                found = found + hit * lax.rem(slot, jnp.int32(local_blocks))
            rows = pl.ds(pl.multiple_of(group * part, part), part)
            copies.append(pltpu.make_async_copy(in_ref.at[found, rows], out.at[0], sem.at[t]))
            copies[-1].start()
        for copy in copies:
            copy.wait()

    return pl.pallas_call(
        kernel,
        in_specs=[SMEM, SMEM, ANY],
        out_specs=[VMEM] * n_cluster,
        out_shape=[jax.ShapeDtypeStruct((1, part, width), BF16)] * n_cluster,
        scratch_shapes=[pltpu.SemaphoreType.DMA((n_cluster,))],
        cost_estimate=cost(0, 4 * n_cluster * part * width),
        compiler_params=FIRST,
        name="pick_queries",
    )(pattern, block_slot, query_store)


def join_queries(parts, block_slot, pattern, local_blocks, n_feat, n_rep, *others):
    n_group, n_cluster = len(parts), len(parts[0])
    _, part, width = parts[0][0].shape
    n_list = pattern.shape[1]
    total = n_list * n_group * part
    share = total // (n_feat * n_rep)
    unit = min(share, part)
    half = total // n_rep

    def kernel(pattern_ref, slot_ref, *refs):
        outs, rows_ref = refs[-1 - n_rep:-1], refs[-1]
        me, group = lax.axis_index("shard"), lax.axis_index("groups")
        for k in range(n_list):
            owner = lax.div(slot_ref[pattern_ref[me, k]], jnp.int32(local_blocks))
            hops = lax.rem(me + (n_cluster - owner), jnp.int32(n_cluster))
            for d in range(n_group):
                origin = lax.rem(group + (n_group - d), jnp.int32(n_group))
                for h in range(n_cluster):
                    @pl.when(hops == h)
                    def _():
                        for u in range(part // unit):
                            first = (k * n_group + origin) * part + u * unit
                            chunk = lax.div(first, jnp.int32(share))
                            goal = lax.rem(chunk, jnp.int32(n_rep)) * n_feat + lax.div(chunk, jnp.int32(n_rep))
                            goal = pl.multiple_of(goal * share + lax.rem(first, jnp.int32(share)), unit)
                            rows_ref[pl.ds(goal, unit), :] = refs[d * n_cluster + h][0, u * unit:(u + 1) * unit, :]
        for r in range(n_rep):
            @pl.when(lax.axis_index("rep") == r)
            def _():
                for d, out in enumerate(outs):
                    at = ((r + d) % n_rep) * half
                    out[...] = rows_ref[at:at + half, :].T

    return pl.pallas_call(
        kernel,
        in_specs=[SMEM, SMEM] + [VMEM] * (n_group * n_cluster) + [ANY] * len(others),
        out_specs=[VMEM] * n_rep,
        out_shape=[jax.ShapeDtypeStruct((width, half), BF16)] * n_rep,
        scratch_shapes=[pltpu.VMEM((total, width), BF16)],
        cost_estimate=cost(0, 4 * total * width),
        compiler_params=PARAMS,
        name="join_queries",
    )(pattern, block_slot, *[x for line in parts for x in line], *others)


def select(goal_ref, train_ref, base, size):
    tile = 128 if size % 128 == 0 else size
    found = []
    for at in range(0, size, tile):
        index = lax.broadcasted_iota(I32, (tile, LANES), 0) + (base + at)
        pick = [(index == goal_ref[a:a + 1, :]).astype(F32).astype(BF16) for a in range(goal_ref.shape[0])]
        found.append(dot(jnp.concatenate(pick, axis=1), train_ref[...]).astype(BF16))
    return jnp.concatenate(found)


def own_rows(goal, train, bulk):
    def kernel(goal_ref, train_ref, out_ref):
        out_ref[...] = select(goal_ref, train_ref, lax.axis_index("shard") * bulk, bulk)

    return pl.pallas_call(
        kernel,
        in_specs=[VMEM] * 2,
        out_specs=VMEM,
        out_shape=jax.ShapeDtypeStruct((bulk, train.shape[1]), BF16),
        cost_estimate=cost(2 * bulk * train.size, 2 * train.size),
        compiler_params=PARAMS,
        name="own_rows",
    )(goal, train)


def pack_rows(train, ids, columns, bulk, extra, cuts):
    rows = train.shape[0]
    lines = rows // LANES
    n_shard = ids.shape[0] // lines

    def kernel(ids_ref, train_ref, *rest):
        outs, goal_ref = rest[:-1], rest[-1]
        me = lax.axis_index("shard")
        own = ids_ref[...]
        masks = [(own == c).astype(F32) for c in range(n_shard)]
        stacked = jnp.concatenate(masks, axis=0).astype(BF16)
        lane_from = lax.broadcasted_iota(I32, (LANES, LANES), 0)
        lane_to = lax.broadcasted_iota(I32, (LANES, LANES), 1)
        in_line = dot(stacked, (lane_from < lane_to).astype(F32).astype(BF16))
        line_sum = dot(stacked, jnp.ones((LANES, LANES), BF16)).astype(BF16)
        size = n_shard * lines
        to = lax.broadcasted_iota(I32, (size, size), 0)
        since = lax.broadcasted_iota(I32, (size, size), 1)
        same = (to // lines) == (since // lines)
        ahead = dot((same & (since < to)).astype(F32).astype(BF16), line_sum)
        whole = dot(same.astype(F32).astype(BF16), line_sum)
        rank = in_line + ahead
        goal = jnp.zeros((lines, LANES), F32)
        past = jnp.zeros((lines, LANES), F32)
        for c in range(n_shard):
            part = slice(c * lines, (c + 1) * lines)
            place = rank[part] + c * bulk
            if extra:
                surplus = n_shard * bulk + past + rank[part] - bulk
                place = jnp.where(rank[part] < bulk, place, surplus)
                past = past + jnp.floor((jnp.maximum(whole[part] - bulk, 0.0) + 15.0) * 0.0625) * 16.0
            goal = goal + masks[c] * place
        goal_ref[...] = goal.astype(I32)

        def fill(out, base):
            out[...] = select(goal_ref, train_ref, base, out.shape[0])

        for out, (hops, first, _) in zip(outs, cuts):
            fill(out, lax.rem(me + hops, jnp.int32(n_shard)) * bulk + first)
        for j, out in enumerate(outs[len(cuts):]):
            fill(out, n_shard * bulk + j * extra)

    shapes = [jax.ShapeDtypeStruct((n, columns), BF16) for _, _, n in cuts]
    shapes += [jax.ShapeDtypeStruct((extra, columns), BF16)] * (2 if extra else 0)
    shapes += [jax.ShapeDtypeStruct((lines, LANES), I32)]
    packed = n_shard * bulk + 2 * extra
    return pl.pallas_call(
        kernel,
        grid=(1,),
        in_specs=[
            pl.BlockSpec((lines, LANES), lambda i: (lax.axis_index("shard"), 0)),
            pl.BlockSpec((rows, columns), lambda i: (0, lax.axis_index("rep"))),
        ],
        out_specs=[VMEM] * len(shapes),
        out_shape=shapes,
        cost_estimate=cost(2 * packed * rows * columns, 2 * (rows + packed) * columns),
        compiler_params=PARAMS,
        name="pack_rows",
    )(ids, train)


def partial_weights(matrices, queries, block, depth, dtype, *others):
    width, total = queries[0].shape
    tile = 512 if depth % 512 == 0 else depth
    steps = depth // tile
    n = len(matrices)

    def kernel(block_ref, *refs):
        value = dot(refs[0][...], refs[n][...])
        for j in range(1, n):
            value = value + dot(refs[j][...], refs[n + j][...])
        refs[-1][...] = value.astype(dtype)

    return pl.pallas_call(
        kernel,
        grid_spec=pltpu.PrefetchScalarGridSpec(
            num_scalar_prefetch=1,
            grid=(steps,),
            in_specs=[pl.BlockSpec((tile, width), lambda i, b: (b[0] * steps + i, 0))] * n
            + [pl.BlockSpec((width, total), lambda i, b: (0, 0))] * n
            + [ANY] * len(others),
            out_specs=pl.BlockSpec((tile, total), lambda i, b: (i, 0)),
        ),
        out_shape=jax.ShapeDtypeStruct((depth, total), dtype),
        cost_estimate=cost(2 * n * depth * width * total, 2 * n * depth * width + 4 * depth * total),
        compiler_params=PARAMS,
        name="partial_weights",
    )(jnp.reshape(block, (1,)).astype(I32), *matrices, *queries, *others)


def row_table(ids, lines, bulk, extra):
    n_shard = ids.shape[0] // lines

    def kernel(ids_ref, table_ref, flag_ref):
        me = lax.axis_index("shard")
        start = jnp.int32(0)
        most = jnp.int32(0)
        for s in range(n_shard):
            line = ids_ref[s * lines:(s + 1) * lines, :]

            def count(c):
                return jnp.sum((line == c).astype(I32))

            mine = count(me)
            before = jnp.int32(0)
            if extra:
                surplus = jnp.int32(0)
                for c in range(n_shard):
                    over = lax.div(jnp.maximum(count(c) - bulk, 0) + 15, jnp.int32(16)) * 16
                    before = before + jnp.where(c < me, over, 0)
                    surplus = surplus + over
                most = jnp.maximum(most, surplus)
            table_ref[s, 0] = start
            table_ref[s, 1] = jnp.minimum(mine, bulk)
            table_ref[s, 2] = lax.div(before, jnp.int32(16))
            table_ref[s, 3] = jnp.maximum(mine - bulk, 0)
            start = start + mine
        flag_ref[...] = jnp.full((8, LANES), (most > extra).astype(I32))

    return pl.pallas_call(
        kernel,
        in_specs=[VMEM],
        out_specs=[SMEM, VMEM],
        out_shape=[jax.ShapeDtypeStruct((n_shard, 4), I32), jax.ShapeDtypeStruct((8, LANES), I32)],
        cost_estimate=cost(0, 4 * ids.size),
        compiler_params=PARAMS,
        name="row_table",
    )(ids)


def put(acc, x, start, count=None):
    tiles, _, width = x.shape
    first, within = lax.div(start, jnp.int32(8)), lax.rem(start, jnp.int32(8))
    turned = pltpu.roll(x, within, 1)
    row = lax.broadcasted_iota(I32, (1, 8, width), 1)
    keep = row < within
    pieces = jnp.where(keep, jnp.concatenate([turned[:1], turned]), jnp.concatenate([turned, turned[-1:]]))
    if count is None:
        pieces = jnp.concatenate([jnp.where(keep, acc[pl.ds(first, 1)], turned[:1]), pieces[1:]])
    else:
        at = lax.broadcasted_iota(I32, (tiles + 1, 8, width), 0) * 8 + lax.broadcasted_iota(
            I32, (tiles + 1, 8, width), 1
        )
        pieces = jnp.where(
            (at >= within) & (at < within + count), pieces, acc[pl.ds(first, tiles + 1)]
        )
    acc[pl.ds(first, tiles + 1)] = pieces


def score(high_ref, low_ref, parts, rep):
    total = None
    for d, x in enumerate(parts):
        depth = x.shape[1]
        block = pl.ds(pl.multiple_of(lax.rem(rep + (len(parts) - d), jnp.int32(len(parts))) * depth, depth), depth)
        value = dot(x, high_ref[block, :]) + dot(x, low_ref[block, :])
        total = value if total is None else total + value
    return total.reshape(total.shape[0] // 8, 8, total.shape[1])


def for_feats(value, outs):
    n = len(outs)
    share = outs[0].shape[1]
    for f in range(n):
        @pl.when(lax.axis_index("feat") == f)
        def _():
            for d, out in enumerate(outs):
                at = ((f + d) % n) * share
                out[...] = value(slice(at, at + share)).astype(out.dtype)


def feat_shapes(rows, width, n_feat):
    share = (rows, width // n_feat)
    return [jax.ShapeDtypeStruct(share, F32)] + [jax.ShapeDtypeStruct(share, BF16)] * (n_feat - 1)


def early_scores(own, others, mine, pieces, cuts, firsts, seconds, table, rows, n_feat, n_rep, n_shard, bulk, extra):
    depth, width = own.shape
    columns = depth // n_rep
    n_other, n_piece = len(others), len(pieces)
    n_first = len(firsts) * n_rep
    last_hops = n_shard - 1

    def kernel(table_ref, *refs):
        own_ref, refs = refs[0], refs[1:]
        other_refs, refs = refs[:n_other], refs[n_other:]
        mine_ref, refs = refs[0], refs[1:]
        piece_refs = [refs[j * n_rep:(j + 1) * n_rep] for j in range(n_piece)]
        refs = refs[n_piece * n_rep:]
        first_refs, second_refs, refs = refs[:n_first], refs[n_first:2 * n_first], refs[2 * n_first:]
        high_ref, low_ref, outs, (scored, held, acc, sem) = refs[0], refs[1], refs[2:-4], refs[-4:]
        me, rep = lax.axis_index("shard"), lax.axis_index("rep")
        weight = own_ref[...]
        for ref in other_refs:
            weight = weight + ref[...].astype(F32)
        high = weight.astype(BF16)
        high_ref[...] = high
        low_ref[...] = (weight - high.astype(F32)).astype(BF16)

        scored[me] = score(high_ref, low_ref, [mine_ref[...]], jnp.int32(0))
        for parts, (hops, first, size) in zip(piece_refs, cuts):
            source = lax.rem(me + (n_shard - hops), jnp.int32(n_shard))
            scored[source, first // 8:(first + size) // 8] = score(high_ref, low_ref, [p[...] for p in parts], rep)
        last = lax.rem(me + (n_shard - last_hops), jnp.int32(n_shard))
        for s in range(n_shard):
            start = table_ref[s, 0]

            @pl.when(last != s)
            def _():
                put(acc, scored[s], start)

            if extra:
                @pl.when(table_ref[s, 3] > 0)
                def _():
                    apart = jnp.bitwise_xor(me, s)
                    rows_in = pl.ds(pl.multiple_of(lax.div(apart, jnp.int32(2)) * extra, extra), extra)
                    for odd in range(2):
                        @pl.when(jnp.bitwise_and(apart, 1) == odd)
                        def _():
                            copies = []
                            for j, refs in enumerate([first_refs, second_refs]):
                                for d in range(n_rep):
                                    goal = held.at[d, j * extra:(j + 1) * extra]
                                    which = refs[odd * n_rep + d].at[rows_in]
                                    copies.append(pltpu.make_async_copy(which, goal, sem.at[j * n_rep + d]))
                            for copy in copies:
                                copy.start()
                            for copy in copies:
                                copy.wait()
                    some = pl.ds(pl.multiple_of(table_ref[s, 2] * 16, 16), extra)
                    x = [held[d, some, :] for d in range(n_rep)]
                    put(acc, score(high_ref, low_ref, x, rep), start + table_ref[s, 1])
        for_feats(lambda at: acc[:rows // 8, :, at].reshape(rows, width // n_feat), outs)

    count = n_shard * bulk
    surplus = [x for parts in [*firsts, *seconds] for x in parts]
    return pl.pallas_call(
        kernel,
        in_specs=[SMEM] + [VMEM] * (2 + n_other + n_rep * n_piece) + [ANY] * len(surplus),
        out_specs=[VMEM] * (2 + n_feat),
        out_shape=[jax.ShapeDtypeStruct((depth, width), BF16)] * 2 + feat_shapes(rows, width, n_feat),
        scratch_shapes=[
            pltpu.VMEM((n_shard, bulk // 8, 8, width), F32),
            pltpu.VMEM((n_rep, 3 * extra + 16, columns), BF16),
            pltpu.VMEM(((rows + bulk + extra) // 8 + 2, 8, width), F32),
            pltpu.SemaphoreType.DMA((2 * n_rep,)),
        ],
        cost_estimate=cost(4 * count * depth * width, 10 * depth * width + count * (2 * depth + 4 * width)),
        compiler_params=PARAMS,
        name="early_scores",
    )(table, own, *others, mine, *[p for parts in pieces for p in parts], *surplus)


def late_scores(parts, high, low, n_feat):
    rows = parts[0].shape[0]
    width = high.shape[1]

    def kernel(high_ref, low_ref, *refs):
        part_refs, outs, acc = refs[:len(parts)], refs[len(parts):-1], refs[-1]
        y = score(high_ref, low_ref, [ref[...] for ref in part_refs], lax.axis_index("rep"))
        acc[...] = y.reshape(rows, width)
        for_feats(lambda at: acc[:, at], outs)

    return pl.pallas_call(
        kernel,
        in_specs=[VMEM] * (2 + len(parts)),
        out_specs=[VMEM] * n_feat,
        out_shape=feat_shapes(rows, width, n_feat),
        scratch_shapes=[pltpu.VMEM((rows, width), F32)],
        cost_estimate=cost(4 * rows * high.size, 8 * rows * width),
        compiler_params=PARAMS,
        name="late_scores",
    )(high, low, *parts)


def merge(table, early, late, n_shard):
    rows, width = early[0].shape
    last_rows = late[0].shape[0]
    last_hops = n_shard - 1

    def kernel(table_ref, *refs):
        early_refs, late_refs = refs[:len(early)], refs[len(early):-2]
        out_ref, acc = refs[-2:]
        source = lax.rem(lax.axis_index("shard") + (n_shard - last_hops), jnp.int32(n_shard))

        def total(parts):
            value = parts[0][...]
            for ref in parts[1:]:
                value = value + ref[...].astype(F32)
            return value.reshape(value.shape[0] // 8, 8, width)

        acc[:rows // 8] = total(early_refs)
        put(acc, total(late_refs), table_ref[source, 0], table_ref[source, 1])
        out_ref[...] = acc[:rows // 8].reshape(rows, width).T

    return pl.pallas_call(
        kernel,
        in_specs=[SMEM] + [VMEM] * (len(early) + len(late)),
        out_specs=VMEM,
        out_shape=jax.ShapeDtypeStruct((width, rows), F32),
        scratch_shapes=[pltpu.VMEM(((rows + last_rows) // 8 + 2, 8, width), F32)],
        cost_estimate=cost(0, 8 * rows * width),
        compiler_params=PARAMS,
        name="merge",
    )(table, *early, *late)


def body(train, cluster_ids, precond, query_store, block_slot, pattern):
    n_group, n_shard = lax.axis_size("groups"), lax.axis_size("shard")
    n_feat, n_rep = lax.axis_size("feat"), lax.axis_size("rep")
    feat, rep = lax.axis_index("feat"), lax.axis_index("rep")
    rows = train.shape[0]
    lines = rows // LANES
    base = rows // n_shard
    columns = train.shape[1] // n_rep
    extra = base // 2 if n_shard == 4 else 0
    bulk = base if extra else base + base // 2
    ids = cluster_ids.reshape(-1, LANES)

    last_hops = n_shard - 1

    def with_rep(x):
        return [x] + [shift(x, "rep", n_rep, d) for d in range(1, n_rep)]

    matrices = with_rep(precond[0])

    picked = pick_queries(query_store, block_slot, pattern, n_group)
    pieces = [picked[0]] + [shift(picked[d], "shard", n_shard, d) for d in range(1, n_shard)]

    middle = [(d, 0, bulk) for d in range(1, last_hops)]
    if extra:
        middle = middle[:-1] + [(last_hops - 1, j * bulk // 2, bulk // 2) for j in range(2)]
    *packed, goal = pack_rows(train, ids, columns, bulk, extra, middle + [(last_hops, 0, bulk)])
    table, flag = row_table(ids, lines, bulk, extra)
    mine = own_rows(goal, train, bulk)
    before_join, firsts, seconds = [mine], [], []
    if extra:
        for d in range(1, n_group):
            flag = jnp.maximum(flag, shift(flag, "groups", n_group, d))

        def second_round(x):
            pair = jnp.concatenate([x, swap(x, "shard", n_shard, 2)])
            return [with_rep(pair), with_rep(swap(pair, "shard", n_shard, 1))]

        def no_round(x):
            return [[jnp.zeros((2 * extra, columns), BF16)] * n_rep] * 2

        seconds = lax.cond(flag[0, 0] > 0, second_round, no_round, packed[-1])
        far = swap(packed[-2], "shard", n_shard, 2)
        before_join += [far] + [x for parts in seconds for x in parts]

    final = after(pieces[n_shard // 2], packed[0], flag, *[x for d, x in enumerate(pieces) if d != n_shard // 2])
    pieces = [final if d == n_shard // 2 else x for d, x in enumerate(pieces)]
    parts = [pieces] + [[shift(x, "groups", n_group, d) for x in pieces] for d in range(1, n_group)]
    chosen = join_queries(parts, block_slot, pattern, query_store.shape[0], n_feat, n_rep, *before_join)
    queries = [chosen[0]] + [shift(chosen[d], "rep", n_rep, d) for d in range(1, n_rep)]
    here = [shift(after(packed[0], *before_join[1:2]), "shard", n_shard, 1)]

    def weights(f, dtype, *others):
        return partial_weights(matrices, queries, f, n_rep * columns, dtype, *others)

    sends = [weights((feat + d) % n_feat, BF16) for d in range(1, n_feat)]
    others = [shift(x, "feat", n_feat, d + 1) for d, x in enumerate(sends)]
    own = weights(feat, F32, *sends)

    for (hops, _, _), x in zip(middle[1:], packed[1:]):
        here.append(shift(after(x, own), "shard", n_shard, hops))
    last = shift(after(packed[len(middle)], *here[1:]), "shard", n_shard, last_hops)
    if extra:
        pair = stack([packed[-2], far], chosen[0])
        firsts = [with_rep(pair), with_rep(swap(pair, "shard", n_shard, 1))]

    ready = [with_rep(after(x, own)) for x in here[:1]] + [with_rep(x) for x in here[1:]]
    high, low, *early = early_scores(
        own, others, mine, ready, middle, firsts, seconds, table, rows, n_feat, n_rep, n_shard, bulk, extra
    )

    def over_feat(shares):
        return [shares[0]] + [shift(shares[d], "feat", n_feat, d) for d in range(1, n_feat)]

    late = late_scores(with_rep(after(last, *early[1:])), high, low, n_feat)
    return merge(table, over_feat(early), over_feat(late), n_shard)[None]


def solution(mesh):
    return jax.shard_map(
        body,
        mesh=mesh,
        in_specs=(
            P(("groups", "shard"), "feat"),
            P("groups"),
            P(("groups", "shard"), None, ("feat", "rep")),
            P("shard", None, ("feat", "rep")),
            P(),
            P(),
        ),
        out_specs=P(("groups", "shard"), ("feat", "rep"), None),
        check_vma=False,
    )
```

```python
import functools

import jax
import jax.numpy as jnp
from jax import lax
from jax.experimental import pallas as pl
from jax.experimental.pallas import tpu as pltpu
from jax.sharding import PartitionSpec as P

F32, BF16, I32 = jnp.float32, jnp.bfloat16, jnp.int32
VMEM = pl.BlockSpec(memory_space=pltpu.VMEM)
ANY = pl.BlockSpec(memory_space=pl.ANY)
SMEM = pl.BlockSpec(memory_space=pltpu.SMEM)
PARAMS = pltpu.CompilerParams(vmem_limit_bytes=24 * 2**20)
FIRST = pltpu.CompilerParams(vmem_limit_bytes=60 * 2**20)
LANES = 128


def shift(x, axis, size, by):
    return lax.ppermute(x, axis, [(i, (i + by) % size) for i in range(size)])


def swap(x, axis, size, bit):
    return lax.ppermute(x, axis, [(i, i ^ bit) for i in range(size)])


def dot(a, b):
    return jnp.dot(a, b, preferred_element_type=F32)


def cost(flops, nbytes):
    return pl.CostEstimate(flops=1, bytes_accessed=1, transcendentals=0)


def after(x, *others):
    def kernel(*refs):
        pass

    return pl.pallas_call(
        kernel,
        in_specs=[ANY] * (1 + len(others)),
        out_specs=ANY,
        out_shape=jax.ShapeDtypeStruct(x.shape, x.dtype),
        input_output_aliases={0: 0},
        cost_estimate=cost(0, 0),
        compiler_params=PARAMS,
        name="after",
    )(x, *others)


def stack(parts, *others):
    size, width = parts[0].shape
    n = len(parts)

    def kernel(*refs):
        for j in range(n):
            refs[-1][j * size:(j + 1) * size, :] = refs[j][...]

    return pl.pallas_call(
        kernel,
        in_specs=[VMEM] * n + [ANY] * len(others),
        out_specs=VMEM,
        out_shape=jax.ShapeDtypeStruct((n * size, width), parts[0].dtype),
        cost_estimate=cost(0, 0),
        compiler_params=PARAMS,
        name="stack",
    )(*parts, *others)


def pick_queries(query_store, block_slot, pattern, n_group):
    local_blocks, block_rows, width = query_store.shape
    n_cluster, n_list = pattern.shape
    part = block_rows // n_group

    def kernel(pattern_ref, slot_ref, in_ref, *rest):
        outs, sem = rest[:-1], rest[-1]
        me, group = lax.axis_index("shard"), lax.axis_index("groups")
        copies = []
        for t, out in enumerate(outs):
            target = lax.rem(me + t, jnp.int32(n_cluster))
            found = jnp.int32(0)
            for k in range(n_list):
                slot = slot_ref[pattern_ref[target, k]]
                hit = (lax.div(slot, jnp.int32(local_blocks)) == me).astype(I32)
                found = found + hit * lax.rem(slot, jnp.int32(local_blocks))
            rows = pl.ds(pl.multiple_of(group * part, part), part)
            copies.append(pltpu.make_async_copy(in_ref.at[found, rows], out.at[0], sem.at[t]))
            copies[-1].start()
        for copy in copies:
            copy.wait()

    return pl.pallas_call(
        kernel,
        in_specs=[SMEM, SMEM, ANY],
        out_specs=[VMEM] * n_cluster,
        out_shape=[jax.ShapeDtypeStruct((1, part, width), BF16)] * n_cluster,
        scratch_shapes=[pltpu.SemaphoreType.DMA((n_cluster,))],
        cost_estimate=cost(0, 4 * n_cluster * part * width),
        compiler_params=FIRST,
        name="pick_queries",
    )(pattern, block_slot, query_store)


def join_queries(parts, block_slot, pattern, local_blocks, n_feat, n_rep, *others):
    n_group, n_cluster = len(parts), len(parts[0])
    _, part, width = parts[0][0].shape
    n_list = pattern.shape[1]
    total = n_list * n_group * part
    share = total // (n_feat * n_rep)
    unit = min(share, part)
    half = total // n_rep

    def kernel(pattern_ref, slot_ref, *refs):
        outs, rows_ref = refs[-1 - n_rep:-1], refs[-1]
        me, group = lax.axis_index("shard"), lax.axis_index("groups")
        for k in range(n_list):
            owner = lax.div(slot_ref[pattern_ref[me, k]], jnp.int32(local_blocks))
            hops = lax.rem(me + (n_cluster - owner), jnp.int32(n_cluster))
            for d in range(n_group):
                origin = lax.rem(group + (n_group - d), jnp.int32(n_group))
                for h in range(n_cluster):
                    @pl.when(hops == h)
                    def _():
                        for u in range(part // unit):
                            first = (k * n_group + origin) * part + u * unit
                            chunk = lax.div(first, jnp.int32(share))
                            goal = lax.rem(chunk, jnp.int32(n_rep)) * n_feat + lax.div(chunk, jnp.int32(n_rep))
                            goal = pl.multiple_of(goal * share + lax.rem(first, jnp.int32(share)), unit)
                            rows_ref[pl.ds(goal, unit), :] = refs[d * n_cluster + h][0, u * unit:(u + 1) * unit, :]
        for r in range(n_rep):
            @pl.when(lax.axis_index("rep") == r)
            def _():
                for d, out in enumerate(outs):
                    at = ((r + d) % n_rep) * half
                    out[...] = rows_ref[at:at + half, :].T

    return pl.pallas_call(
        kernel,
        in_specs=[SMEM, SMEM] + [VMEM] * (n_group * n_cluster) + [ANY] * len(others),
        out_specs=[VMEM] * n_rep,
        out_shape=[jax.ShapeDtypeStruct((width, half), BF16)] * n_rep,
        scratch_shapes=[pltpu.VMEM((total, width), BF16)],
        cost_estimate=cost(0, 4 * total * width),
        compiler_params=PARAMS,
        name="join_queries",
    )(pattern, block_slot, *[x for line in parts for x in line], *others)


def select(goal_ref, train_ref, base, size):
    tile = 128 if size % 128 == 0 else size
    found = []
    for at in range(0, size, tile):
        index = lax.broadcasted_iota(I32, (tile, LANES), 0) + (base + at)
        pick = [(index == goal_ref[a:a + 1, :]).astype(F32).astype(BF16) for a in range(goal_ref.shape[0])]
        found.append(dot(jnp.concatenate(pick, axis=1), train_ref[...]).astype(BF16))
    return jnp.concatenate(found)


def own_rows(goal, train, bulk):
    def kernel(goal_ref, train_ref, out_ref):
        out_ref[...] = select(goal_ref, train_ref, lax.axis_index("shard") * bulk, bulk)

    return pl.pallas_call(
        kernel,
        in_specs=[VMEM] * 2,
        out_specs=VMEM,
        out_shape=jax.ShapeDtypeStruct((bulk, train.shape[1]), BF16),
        cost_estimate=cost(2 * bulk * train.size, 2 * train.size),
        compiler_params=FIRST,
        name="own_rows",
    )(goal, train)


def pack_rows(train, ids, columns, bulk, extra, cuts):
    rows = train.shape[0]
    lines = rows // LANES
    n_shard = ids.shape[0] // lines

    def kernel(ids_ref, train_ref, *rest):
        outs, goal_ref = rest[:-1], rest[-1]
        me = lax.axis_index("shard")
        own = ids_ref[...]
        masks = [(own == c).astype(F32) for c in range(n_shard)]
        stacked = jnp.concatenate(masks, axis=0).astype(BF16)
        lane_from = lax.broadcasted_iota(I32, (LANES, LANES), 0)
        lane_to = lax.broadcasted_iota(I32, (LANES, LANES), 1)
        in_line = dot(stacked, (lane_from < lane_to).astype(F32).astype(BF16))
        line_sum = dot(stacked, jnp.ones((LANES, LANES), BF16)).astype(BF16)
        size = n_shard * lines
        to = lax.broadcasted_iota(I32, (size, size), 0)
        since = lax.broadcasted_iota(I32, (size, size), 1)
        same = (to // lines) == (since // lines)
        ahead = dot((same & (since < to)).astype(F32).astype(BF16), line_sum)
        whole = dot(same.astype(F32).astype(BF16), line_sum)
        rank = in_line + ahead
        goal = jnp.zeros((lines, LANES), F32)
        past = jnp.zeros((lines, LANES), F32)
        for c in range(n_shard):
            part = slice(c * lines, (c + 1) * lines)
            place = rank[part] + c * bulk
            if extra:
                surplus = n_shard * bulk + past + rank[part] - bulk
                place = jnp.where(rank[part] < bulk, place, surplus)
                past = past + jnp.floor((jnp.maximum(whole[part] - bulk, 0.0) + 15.0) * 0.0625) * 16.0
            goal = goal + masks[c] * place
        goal_ref[...] = goal.astype(I32)

        def fill(out, base):
            out[...] = select(goal_ref, train_ref, base, out.shape[0])

        for out, (hops, first, _) in zip(outs, cuts):
            fill(out, lax.rem(me + hops, jnp.int32(n_shard)) * bulk + first)
        for j, out in enumerate(outs[len(cuts):]):
            fill(out, n_shard * bulk + j * extra)

    shapes = [jax.ShapeDtypeStruct((n, columns), BF16) for _, _, n in cuts]
    shapes += [jax.ShapeDtypeStruct((extra, columns), BF16)] * (2 if extra else 0)
    shapes += [jax.ShapeDtypeStruct((lines, LANES), I32)]
    packed = n_shard * bulk + 2 * extra
    return pl.pallas_call(
        kernel,
        grid=(1,),
        in_specs=[
            pl.BlockSpec((lines, LANES), lambda i: (lax.axis_index("shard"), 0)),
            pl.BlockSpec((rows, columns), lambda i: (0, lax.axis_index("rep"))),
        ],
        out_specs=[VMEM] * len(shapes),
        out_shape=shapes,
        cost_estimate=cost(2 * packed * rows * columns, 2 * (rows + packed) * columns),
        compiler_params=FIRST,
        name="pack_rows",
    )(ids, train)


def partial_weights(matrices, queries, block, depth, dtype, *others):
    width, total = queries[0].shape
    tile = 512 if depth % 512 == 0 else depth
    steps = depth // tile
    n = len(matrices)

    def kernel(block_ref, *refs):
        value = dot(refs[0][...], refs[n][...])
        for j in range(1, n):
            value = value + dot(refs[j][...], refs[n + j][...])
        refs[-1][...] = value.astype(dtype)

    return pl.pallas_call(
        kernel,
        grid_spec=pltpu.PrefetchScalarGridSpec(
            num_scalar_prefetch=1,
            grid=(steps,),
            in_specs=[pl.BlockSpec((tile, width), lambda i, b: (b[0] * steps + i, 0))] * n
            + [pl.BlockSpec((width, total), lambda i, b: (0, 0))] * n
            + [ANY] * len(others),
            out_specs=pl.BlockSpec((tile, total), lambda i, b: (i, 0)),
        ),
        out_shape=jax.ShapeDtypeStruct((depth, total), dtype),
        cost_estimate=cost(2 * n * depth * width * total, 2 * n * depth * width + 4 * depth * total),
        compiler_params=FIRST,
        name="partial_weights",
    )(jnp.reshape(block, (1,)).astype(I32), *matrices, *queries, *others)


def row_table(ids, lines, bulk, extra):
    n_shard = ids.shape[0] // lines

    def kernel(ids_ref, table_ref, flag_ref):
        me = lax.axis_index("shard")
        start = jnp.int32(0)
        most = jnp.int32(0)
        for s in range(n_shard):
            line = ids_ref[s * lines:(s + 1) * lines, :]

            def count(c):
                return jnp.sum((line == c).astype(I32))

            mine = count(me)
            before = jnp.int32(0)
            if extra:
                surplus = jnp.int32(0)
                for c in range(n_shard):
                    over = lax.div(jnp.maximum(count(c) - bulk, 0) + 15, jnp.int32(16)) * 16
                    before = before + jnp.where(c < me, over, 0)
                    surplus = surplus + over
                most = jnp.maximum(most, surplus)
            table_ref[s, 0] = start
            table_ref[s, 1] = jnp.minimum(mine, bulk)
            table_ref[s, 2] = lax.div(before, jnp.int32(16))
            table_ref[s, 3] = jnp.maximum(mine - bulk, 0)
            start = start + mine
        flag_ref[...] = jnp.full((8, LANES), (most > extra).astype(I32))

    return pl.pallas_call(
        kernel,
        in_specs=[VMEM],
        out_specs=[SMEM, VMEM],
        out_shape=[jax.ShapeDtypeStruct((n_shard, 4), I32), jax.ShapeDtypeStruct((8, LANES), I32)],
        cost_estimate=cost(0, 4 * ids.size),
        compiler_params=FIRST,
        name="row_table",
    )(ids)


def put(acc, x, start, count=None):
    tiles, _, width = x.shape
    first, within = lax.div(start, jnp.int32(8)), lax.rem(start, jnp.int32(8))
    turned = pltpu.roll(x, within, 1)
    row = lax.broadcasted_iota(I32, (1, 8, width), 1)
    keep = row < within
    pieces = jnp.where(keep, jnp.concatenate([turned[:1], turned]), jnp.concatenate([turned, turned[-1:]]))
    if count is None:
        pieces = jnp.concatenate([jnp.where(keep, acc[pl.ds(first, 1)], turned[:1]), pieces[1:]])
    else:
        at = lax.broadcasted_iota(I32, (tiles + 1, 8, width), 0) * 8 + lax.broadcasted_iota(
            I32, (tiles + 1, 8, width), 1
        )
        pieces = jnp.where(
            (at >= within) & (at < within + count), pieces, acc[pl.ds(first, tiles + 1)]
        )
    acc[pl.ds(first, tiles + 1)] = pieces


def score(high_ref, low_ref, parts, rep):
    total = None
    for d, x in enumerate(parts):
        depth = x.shape[1]
        block = pl.ds(pl.multiple_of(lax.rem(rep + (len(parts) - d), jnp.int32(len(parts))) * depth, depth), depth)
        value = dot(x, high_ref[block, :]) + dot(x, low_ref[block, :])
        total = value if total is None else total + value
    return total.reshape(total.shape[0] // 8, 8, total.shape[1])


def for_feats(value, outs):
    n = len(outs)
    share = outs[0].shape[1]
    for f in range(n):
        @pl.when(lax.axis_index("feat") == f)
        def _():
            for d, out in enumerate(outs):
                at = ((f + d) % n) * share
                out[...] = value(slice(at, at + share)).astype(out.dtype)


def feat_shapes(rows, width, n_feat):
    share = (rows, width // n_feat)
    return [jax.ShapeDtypeStruct(share, F32)] + [jax.ShapeDtypeStruct(share, BF16)] * (n_feat - 1)


def early_scores(own, others, mine, pieces, cuts, firsts, seconds, table, rows, n_feat, n_rep, n_shard, bulk, extra):
    depth, width = own.shape
    columns = depth // n_rep
    n_other, n_piece = len(others), len(pieces)
    n_first = len(firsts) * n_rep
    last_hops = n_shard - 1

    def kernel(table_ref, *refs):
        own_ref, refs = refs[0], refs[1:]
        other_refs, refs = refs[:n_other], refs[n_other:]
        mine_ref, refs = refs[0], refs[1:]
        piece_refs = [refs[j * n_rep:(j + 1) * n_rep] for j in range(n_piece)]
        refs = refs[n_piece * n_rep:]
        first_refs, second_refs, refs = refs[:n_first], refs[n_first:2 * n_first], refs[2 * n_first:]
        high_ref, low_ref, outs, (scored, held, acc, sem) = refs[0], refs[1], refs[2:-4], refs[-4:]
        me, rep = lax.axis_index("shard"), lax.axis_index("rep")
        weight = own_ref[...]
        for ref in other_refs:
            weight = weight + ref[...].astype(F32)
        high = weight.astype(BF16)
        high_ref[...] = high
        low_ref[...] = (weight - high.astype(F32)).astype(BF16)

        scored[me] = score(high_ref, low_ref, [mine_ref[...]], jnp.int32(0))
        for parts, (hops, first, size) in zip(piece_refs, cuts):
            source = lax.rem(me + (n_shard - hops), jnp.int32(n_shard))
            scored[source, first // 8:(first + size) // 8] = score(high_ref, low_ref, [p[...] for p in parts], rep)
        last = lax.rem(me + (n_shard - last_hops), jnp.int32(n_shard))
        for s in range(n_shard):
            start = table_ref[s, 0]

            @pl.when(last != s)
            def _():
                put(acc, scored[s], start)

            if extra:
                @pl.when(table_ref[s, 3] > 0)
                def _():
                    apart = jnp.bitwise_xor(me, s)
                    rows_in = pl.ds(pl.multiple_of(lax.div(apart, jnp.int32(2)) * extra, extra), extra)
                    for odd in range(2):
                        @pl.when(jnp.bitwise_and(apart, 1) == odd)
                        def _():
                            copies = []
                            for j, refs in enumerate([first_refs, second_refs]):
                                for d in range(n_rep):
                                    goal = held.at[d, j * extra:(j + 1) * extra]
                                    which = refs[odd * n_rep + d].at[rows_in]
                                    copies.append(pltpu.make_async_copy(which, goal, sem.at[j * n_rep + d]))
                            for copy in copies:
                                copy.start()
                            for copy in copies:
                                copy.wait()
                    some = pl.ds(pl.multiple_of(table_ref[s, 2] * 16, 16), extra)
                    x = [held[d, some, :] for d in range(n_rep)]
                    put(acc, score(high_ref, low_ref, x, rep), start + table_ref[s, 1])
        for_feats(lambda at: acc[:rows // 8, :, at].reshape(rows, width // n_feat), outs)

    count = n_shard * bulk
    surplus = [x for parts in [*firsts, *seconds] for x in parts]
    return pl.pallas_call(
        kernel,
        in_specs=[SMEM] + [VMEM] * (2 + n_other + n_rep * n_piece) + [ANY] * len(surplus),
        out_specs=[VMEM] * (2 + n_feat),
        out_shape=[jax.ShapeDtypeStruct((depth, width), BF16)] * 2 + feat_shapes(rows, width, n_feat),
        scratch_shapes=[
            pltpu.VMEM((n_shard, bulk // 8, 8, width), F32),
            pltpu.VMEM((n_rep, 3 * extra + 16, columns), BF16),
            pltpu.VMEM(((rows + bulk + extra) // 8 + 2, 8, width), F32),
            pltpu.SemaphoreType.DMA((2 * n_rep,)),
        ],
        cost_estimate=cost(4 * count * depth * width, 10 * depth * width + count * (2 * depth + 4 * width)),
        compiler_params=PARAMS,
        name="early_scores",
    )(table, own, *others, mine, *[p for parts in pieces for p in parts], *surplus)


def late_scores(pieces, high, low, n_feat):
    n, n_rep = len(pieces), len(pieces[0])
    size = pieces[0][0].shape[0]
    rows = n * size
    width = high.shape[1]

    def kernel(high_ref, low_ref, *refs):
        part_refs, outs, acc = refs[:n * n_rep], refs[n * n_rep:-1], refs[-1]
        parts = [jnp.concatenate([part_refs[j * n_rep + d][...] for j in range(n)]) for d in range(n_rep)]
        y = score(high_ref, low_ref, parts, lax.axis_index("rep"))
        acc[...] = y.reshape(rows, width)
        for_feats(lambda at: acc[:, at], outs)

    return pl.pallas_call(
        kernel,
        in_specs=[VMEM] * (2 + n * n_rep),
        out_specs=[VMEM] * n_feat,
        out_shape=feat_shapes(rows, width, n_feat),
        scratch_shapes=[pltpu.VMEM((rows, width), F32)],
        cost_estimate=cost(4 * rows * high.size, 8 * rows * width),
        compiler_params=PARAMS,
        name="late_scores",
    )(high, low, *[p for parts in pieces for p in parts])


def merge(table, early, late, n_shard):
    rows, width = early[0].shape
    last_rows = late[0].shape[0]
    last_hops = n_shard - 1

    def kernel(table_ref, *refs):
        early_refs, late_refs = refs[:len(early)], refs[len(early):-2]
        out_ref, acc = refs[-2:]
        source = lax.rem(lax.axis_index("shard") + (n_shard - last_hops), jnp.int32(n_shard))

        def total(parts):
            value = parts[0][...]
            for ref in parts[1:]:
                value = value + ref[...].astype(F32)
            return value.reshape(value.shape[0] // 8, 8, width)

        acc[:rows // 8] = total(early_refs)
        put(acc, total(late_refs), table_ref[source, 0], table_ref[source, 1])
        out_ref[...] = acc[:rows // 8].reshape(rows, width).T

    return pl.pallas_call(
        kernel,
        in_specs=[SMEM] + [VMEM] * (len(early) + len(late)),
        out_specs=VMEM,
        out_shape=jax.ShapeDtypeStruct((width, rows), F32),
        scratch_shapes=[pltpu.VMEM(((rows + last_rows) // 8 + 2, 8, width), F32)],
        cost_estimate=cost(0, 8 * rows * width),
        compiler_params=PARAMS,
        name="merge",
    )(table, *early, *late)


def body(train, cluster_ids, precond, query_store, block_slot, pattern):
    n_group, n_shard = lax.axis_size("groups"), lax.axis_size("shard")
    n_feat, n_rep = lax.axis_size("feat"), lax.axis_size("rep")
    feat, rep = lax.axis_index("feat"), lax.axis_index("rep")
    rows = train.shape[0]
    lines = rows // LANES
    base = rows // n_shard
    columns = train.shape[1] // n_rep
    extra = base // 2 if n_shard == 4 else 0
    bulk = base if extra else base + base // 2
    ids = cluster_ids.reshape(-1, LANES)

    last_hops = n_shard - 1

    def with_rep(x):
        return [x] + [shift(x, "rep", n_rep, d) for d in range(1, n_rep)]

    matrices = with_rep(precond[0])

    picked = pick_queries(query_store, block_slot, pattern, n_group)
    pieces = [picked[0]] + [shift(picked[d], "shard", n_shard, d) for d in range(1, n_shard)]

    middle = [(d, 0, bulk) for d in range(1, last_hops)]
    part = 64 if bulk % 64 == 0 else bulk
    final = [(last_hops, at, part) for at in range(0, bulk, part)]
    *packed, goal = pack_rows(train, ids, columns, bulk, extra, middle + final)
    table, flag = row_table(ids, lines, bulk, extra)
    mine = own_rows(goal, train, bulk)
    before_join, firsts, seconds = [mine], [], []
    if extra:
        for d in range(1, n_group):
            flag = jnp.maximum(flag, shift(flag, "groups", n_group, d))

        def second_round(x):
            pair = jnp.concatenate([x, swap(x, "shard", n_shard, 2)])
            return [with_rep(pair), with_rep(swap(pair, "shard", n_shard, 1))]

        def no_round(x):
            return [[jnp.zeros((2 * extra, columns), BF16)] * n_rep] * 2

        seconds = lax.cond(flag[0, 0] > 0, second_round, no_round, after(packed[-1], *pieces[1:]))
        far = swap(after(packed[-2], *pieces[1:]), "shard", n_shard, 2)
        before_join += [far] + [x for parts in seconds for x in parts]

    parts = [pieces] + [[shift(x, "groups", n_group, d) for x in pieces] for d in range(1, n_group)]
    chosen = join_queries(parts, block_slot, pattern, query_store.shape[0], n_feat, n_rep, *before_join)
    queries = [chosen[0]] + [shift(chosen[d], "rep", n_rep, d) for d in range(1, n_rep)]
    here = [shift(after(packed[0], *before_join[1:2]), "shard", n_shard, 1)]

    def weights(f, dtype, *others):
        return partial_weights(matrices, queries, f, n_rep * columns, dtype, *others)

    sends = [weights((feat + d) % n_feat, BF16) for d in range(1, n_feat)]
    others = [shift(x, "feat", n_feat, d + 1) for d, x in enumerate(sends)]
    own = weights(feat, F32, *sends)

    for (hops, _, _), x in zip(middle[1:], packed[1:]):
        here.append(shift(after(x, here[-1], *sends), "shard", n_shard, hops))
    last = [
        shift(after(packed[len(middle) + j], here[-1], own), "shard", n_shard, last_hops) for j in range(len(final))
    ]
    if extra:
        pair = stack([packed[-2], far], *sends)
        firsts = [with_rep(pair), with_rep(swap(pair, "shard", n_shard, 1))]

    mark = shift(after(jnp.zeros((8, LANES), I32), own), "rep", n_rep, 1)
    ready = [with_rep(after(x, mark)) for x in here]
    high, low, *early = early_scores(
        own, others, mine, ready, middle, firsts, seconds, table, rows, n_feat, n_rep, n_shard, bulk, extra
    )

    def over_feat(shares):
        return [shares[0]] + [shift(shares[d], "feat", n_feat, d) for d in range(1, n_feat)]

    late = late_scores([with_rep(after(x, *early[1:])) for x in last], high, low, n_feat)
    return merge(table, over_feat(early), over_feat(late), n_shard)[None]


def solution(mesh):
    return jax.shard_map(
        body,
        mesh=mesh,
        in_specs=(
            P(("groups", "shard"), "feat"),
            P("groups"),
            P(("groups", "shard"), None, ("feat", "rep")),
            P("shard", None, ("feat", "rep")),
            P(),
            P(),
        ),
        out_specs=P(("groups", "shard"), ("feat", "rep"), None),
        check_vma=False,
    )
```

```python
import functools

import jax
import jax.numpy as jnp
from jax import lax
from jax.experimental import pallas as pl
from jax.experimental.pallas import tpu as pltpu
from jax.sharding import PartitionSpec as P

F32, BF16, I32 = jnp.float32, jnp.bfloat16, jnp.int32
VMEM = pl.BlockSpec(memory_space=pltpu.VMEM)
ANY = pl.BlockSpec(memory_space=pl.ANY)
SMEM = pl.BlockSpec(memory_space=pltpu.SMEM)
PARAMS = pltpu.CompilerParams(vmem_limit_bytes=24 * 2**20)
FIRST = pltpu.CompilerParams(vmem_limit_bytes=60 * 2**20)
LANES = 128


def shift(x, axis, size, by):
    return lax.ppermute(x, axis, [(i, (i + by) % size) for i in range(size)])


def swap(x, axis, size, bit):
    return lax.ppermute(x, axis, [(i, i ^ bit) for i in range(size)])


def dot(a, b):
    return jnp.dot(a, b, preferred_element_type=F32)


def cost(flops, nbytes):
    return pl.CostEstimate(flops=1, bytes_accessed=1, transcendentals=0)


def after(x, *others):
    def kernel(*refs):
        pass

    return pl.pallas_call(
        kernel,
        in_specs=[ANY] * (1 + len(others)),
        out_specs=ANY,
        out_shape=jax.ShapeDtypeStruct(x.shape, x.dtype),
        input_output_aliases={0: 0},
        cost_estimate=cost(0, 0),
        compiler_params=PARAMS,
        name="after",
    )(x, *others)


def stack(parts, *others):
    size, width = parts[0].shape
    n = len(parts)

    def kernel(*refs):
        for j in range(n):
            refs[-1][j * size:(j + 1) * size, :] = refs[j][...]

    return pl.pallas_call(
        kernel,
        in_specs=[VMEM] * n + [ANY] * len(others),
        out_specs=VMEM,
        out_shape=jax.ShapeDtypeStruct((n * size, width), parts[0].dtype),
        cost_estimate=cost(0, 0),
        compiler_params=PARAMS,
        name="stack",
    )(*parts, *others)


def pick_queries(query_store, block_slot, pattern, n_group):
    local_blocks, block_rows, width = query_store.shape
    n_cluster, n_list = pattern.shape
    part = block_rows // n_group

    def kernel(pattern_ref, slot_ref, in_ref, *rest):
        outs, sem = rest[:-1], rest[-1]
        me, group = lax.axis_index("shard"), lax.axis_index("groups")
        copies = []
        for t, out in enumerate(outs):
            target = lax.rem(me + t, jnp.int32(n_cluster))
            found = jnp.int32(0)
            for k in range(n_list):
                slot = slot_ref[pattern_ref[target, k]]
                hit = (lax.div(slot, jnp.int32(local_blocks)) == me).astype(I32)
                found = found + hit * lax.rem(slot, jnp.int32(local_blocks))
            rows = pl.ds(pl.multiple_of(group * part, part), part)
            copies.append(pltpu.make_async_copy(in_ref.at[found, rows], out.at[0], sem.at[t]))
            copies[-1].start()
        for copy in copies:
            copy.wait()

    return pl.pallas_call(
        kernel,
        in_specs=[SMEM, SMEM, ANY],
        out_specs=[VMEM] * n_cluster,
        out_shape=[jax.ShapeDtypeStruct((1, part, width), BF16)] * n_cluster,
        scratch_shapes=[pltpu.SemaphoreType.DMA((n_cluster,))],
        cost_estimate=cost(0, 4 * n_cluster * part * width),
        compiler_params=FIRST,
        name="pick_queries",
    )(pattern, block_slot, query_store)


def join_queries(parts, block_slot, pattern, local_blocks, n_feat, n_rep, *others):
    n_group, n_cluster = len(parts), len(parts[0])
    _, part, width = parts[0][0].shape
    n_list = pattern.shape[1]
    total = n_list * n_group * part
    share = total // (n_feat * n_rep)
    unit = min(share, part)
    half = total // n_rep

    def kernel(pattern_ref, slot_ref, *refs):
        outs, rows_ref = refs[-1 - n_rep:-1], refs[-1]
        me, group = lax.axis_index("shard"), lax.axis_index("groups")
        for k in range(n_list):
            owner = lax.div(slot_ref[pattern_ref[me, k]], jnp.int32(local_blocks))
            hops = lax.rem(me + (n_cluster - owner), jnp.int32(n_cluster))
            for d in range(n_group):
                origin = lax.rem(group + (n_group - d), jnp.int32(n_group))
                for h in range(n_cluster):
                    @pl.when(hops == h)
                    def _():
                        for u in range(part // unit):
                            first = (k * n_group + origin) * part + u * unit
                            chunk = lax.div(first, jnp.int32(share))
                            goal = lax.rem(chunk, jnp.int32(n_rep)) * n_feat + lax.div(chunk, jnp.int32(n_rep))
                            goal = pl.multiple_of(goal * share + lax.rem(first, jnp.int32(share)), unit)
                            rows_ref[pl.ds(goal, unit), :] = refs[d * n_cluster + h][0, u * unit:(u + 1) * unit, :]
        for r in range(n_rep):
            @pl.when(lax.axis_index("rep") == r)
            def _():
                for d, out in enumerate(outs):
                    at = ((r + d) % n_rep) * half
                    out[...] = rows_ref[at:at + half, :].T

    return pl.pallas_call(
        kernel,
        in_specs=[SMEM, SMEM] + [VMEM] * (n_group * n_cluster) + [ANY] * len(others),
        out_specs=[VMEM] * n_rep,
        out_shape=[jax.ShapeDtypeStruct((width, half), BF16)] * n_rep,
        scratch_shapes=[pltpu.VMEM((total, width), BF16)],
        cost_estimate=cost(0, 4 * total * width),
        compiler_params=PARAMS,
        name="join_queries",
    )(pattern, block_slot, *[x for line in parts for x in line], *others)


def select(goal_ref, train_ref, base, size):
    tile = 128 if size % 128 == 0 else size
    found = []
    for at in range(0, size, tile):
        index = lax.broadcasted_iota(I32, (tile, LANES), 0) + (base + at)
        pick = [(index == goal_ref[a:a + 1, :]).astype(F32).astype(BF16) for a in range(goal_ref.shape[0])]
        found.append(dot(jnp.concatenate(pick, axis=1), train_ref[...]).astype(BF16))
    return jnp.concatenate(found)


def own_rows(goal, train, bulk, *others):
    def kernel(goal_ref, train_ref, *rest):
        rest[-1][...] = select(goal_ref, train_ref, lax.axis_index("shard") * bulk, bulk)

    return pl.pallas_call(
        kernel,
        in_specs=[VMEM] * 2 + [ANY] * len(others),
        out_specs=VMEM,
        out_shape=jax.ShapeDtypeStruct((bulk, train.shape[1]), BF16),
        cost_estimate=cost(2 * bulk * train.size, 2 * train.size),
        compiler_params=FIRST,
        name="own_rows",
    )(goal, train, *others)


def pack_rows(train, ids, columns, bulk, extra, cuts):
    rows = train.shape[0]
    lines = rows // LANES
    n_shard = ids.shape[0] // lines

    def kernel(ids_ref, train_ref, *rest):
        outs, goal_ref = rest[:-1], rest[-1]
        me = lax.axis_index("shard")
        own = ids_ref[...]
        masks = [(own == c).astype(F32) for c in range(n_shard)]
        stacked = jnp.concatenate(masks, axis=0).astype(BF16)
        lane_from = lax.broadcasted_iota(I32, (LANES, LANES), 0)
        lane_to = lax.broadcasted_iota(I32, (LANES, LANES), 1)
        in_line = dot(stacked, (lane_from < lane_to).astype(F32).astype(BF16))
        line_sum = dot(stacked, jnp.ones((LANES, LANES), BF16)).astype(BF16)
        size = n_shard * lines
        to = lax.broadcasted_iota(I32, (size, size), 0)
        since = lax.broadcasted_iota(I32, (size, size), 1)
        same = (to // lines) == (since // lines)
        ahead = dot((same & (since < to)).astype(F32).astype(BF16), line_sum)
        whole = dot(same.astype(F32).astype(BF16), line_sum)
        rank = in_line + ahead
        goal = jnp.zeros((lines, LANES), F32)
        past = jnp.zeros((lines, LANES), F32)
        for c in range(n_shard):
            part = slice(c * lines, (c + 1) * lines)
            place = rank[part] + c * bulk
            if extra:
                surplus = n_shard * bulk + past + rank[part] - bulk
                place = jnp.where(rank[part] < bulk, place, surplus)
                past = past + jnp.floor((jnp.maximum(whole[part] - bulk, 0.0) + 15.0) * 0.0625) * 16.0
            goal = goal + masks[c] * place
        goal_ref[...] = goal.astype(I32)

        def fill(out, base):
            out[...] = select(goal_ref, train_ref, base, out.shape[0])

        for out, (hops, first, _) in zip(outs, cuts):
            fill(out, lax.rem(me + hops, jnp.int32(n_shard)) * bulk + first)
        for j, out in enumerate(outs[len(cuts):]):
            fill(out, n_shard * bulk + max(j - 1, 0) * extra)

    shapes = [jax.ShapeDtypeStruct((n, columns), BF16) for _, _, n in cuts]
    shapes += [jax.ShapeDtypeStruct((extra, columns), BF16)] * (3 if extra else 0)
    shapes += [jax.ShapeDtypeStruct((lines, LANES), I32)]
    packed = n_shard * bulk + 2 * extra
    return pl.pallas_call(
        kernel,
        grid=(1,),
        in_specs=[
            pl.BlockSpec((lines, LANES), lambda i: (lax.axis_index("shard"), 0)),
            pl.BlockSpec((rows, columns), lambda i: (0, lax.axis_index("rep"))),
        ],
        out_specs=[VMEM] * len(shapes),
        out_shape=shapes,
        cost_estimate=cost(2 * packed * rows * columns, 2 * (rows + packed) * columns),
        compiler_params=FIRST,
        name="pack_rows",
    )(ids, train)


def partial_weights(matrices, queries, block, depth, dtype, *others):
    width, total = queries[0].shape
    tile = 512 if depth % 512 == 0 else depth
    steps = depth // tile
    n = len(matrices)

    def kernel(block_ref, *refs):
        value = dot(refs[0][...], refs[n][...])
        for j in range(1, n):
            value = value + dot(refs[j][...], refs[n + j][...])
        refs[-1][...] = value.astype(dtype)

    return pl.pallas_call(
        kernel,
        grid_spec=pltpu.PrefetchScalarGridSpec(
            num_scalar_prefetch=1,
            grid=(steps,),
            in_specs=[pl.BlockSpec((tile, width), lambda i, b: (b[0] * steps + i, 0))] * n
            + [pl.BlockSpec((width, total), lambda i, b: (0, 0))] * n
            + [ANY] * len(others),
            out_specs=pl.BlockSpec((tile, total), lambda i, b: (i, 0)),
        ),
        out_shape=jax.ShapeDtypeStruct((depth, total), dtype),
        cost_estimate=cost(2 * n * depth * width * total, 2 * n * depth * width + 4 * depth * total),
        compiler_params=FIRST,
        name="partial_weights",
    )(jnp.reshape(block, (1,)).astype(I32), *matrices, *queries, *others)


def fetch(matrices, block, depth, *others):
    width = matrices[0].shape[1]
    n = len(matrices)
    cuts = 4

    def kernel(block_ref, *refs):
        outs, sem = refs[-1 - n:-1], refs[-1]
        first = pl.multiple_of(block_ref[0] * depth, depth)
        copies = []
        for j in range(n):
            for c in range(cuts):
                size = depth // cuts
                source = refs[j].at[pl.ds(first + c * size, size)]
                copies.append(
                    pltpu.make_async_copy(source, outs[j].at[c * size:(c + 1) * size], sem.at[j * cuts + c])
                )
        for copy in copies:
            copy.start()
        for copy in copies:
            copy.wait()

    return pl.pallas_call(
        kernel,
        in_specs=[SMEM] + [ANY] * (n + len(others)),
        out_specs=[VMEM] * n,
        out_shape=[jax.ShapeDtypeStruct((depth, width), BF16)] * n,
        scratch_shapes=[pltpu.SemaphoreType.DMA((n * cuts,))],
        cost_estimate=cost(0, 2 * n * depth * width),
        compiler_params=PARAMS,
        name="fetch",
    )(jnp.reshape(block, (1,)).astype(I32), *matrices, *others)


def fetched_weights(matrices, queries, dtype):
    depth = matrices[0].shape[0]
    total = queries[0].shape[1]
    tile = 512 if depth % 512 == 0 else depth
    n = len(matrices)

    def kernel(*refs):
        for at in range(0, depth, tile):
            value = dot(refs[0][at:at + tile, :], refs[n][...])
            for j in range(1, n):
                value = value + dot(refs[j][at:at + tile, :], refs[n + j][...])
            refs[-1][at:at + tile, :] = value.astype(dtype)

    return pl.pallas_call(
        kernel,
        in_specs=[VMEM] * (2 * n),
        out_specs=VMEM,
        out_shape=jax.ShapeDtypeStruct((depth, total), dtype),
        cost_estimate=cost(2 * n * matrices[0].size * total, 2 * n * matrices[0].size),
        compiler_params=PARAMS,
        name="fetched_weights",
    )(*matrices, *queries)


def row_table(ids, lines, bulk, extra, *others):
    n_shard = ids.shape[0] // lines

    def kernel(ids_ref, *rest):
        table_ref, flag_ref = rest[-2:]
        me = lax.axis_index("shard")
        start = jnp.int32(0)
        most = jnp.int32(0)
        for s in range(n_shard):
            line = ids_ref[s * lines:(s + 1) * lines, :]

            def count(c):
                return jnp.sum((line == c).astype(I32))

            mine = count(me)
            before = jnp.int32(0)
            if extra:
                surplus = jnp.int32(0)
                for c in range(n_shard):
                    over = lax.div(jnp.maximum(count(c) - bulk, 0) + 15, jnp.int32(16)) * 16
                    before = before + jnp.where(c < me, over, 0)
                    surplus = surplus + over
                most = jnp.maximum(most, surplus)
            table_ref[s, 0] = start
            table_ref[s, 1] = jnp.minimum(mine, bulk)
            table_ref[s, 2] = lax.div(before, jnp.int32(16))
            table_ref[s, 3] = jnp.maximum(mine - bulk, 0)
            start = start + mine
        flag_ref[...] = jnp.full((8, LANES), (most > extra).astype(I32))

    return pl.pallas_call(
        kernel,
        in_specs=[VMEM] + [ANY] * len(others),
        out_specs=[SMEM, VMEM],
        out_shape=[jax.ShapeDtypeStruct((n_shard, 4), I32), jax.ShapeDtypeStruct((8, LANES), I32)],
        cost_estimate=cost(0, 4 * ids.size),
        compiler_params=FIRST,
        name="row_table",
    )(ids, *others)


def put(acc, x, start, count=None):
    tiles, _, width = x.shape
    first, within = lax.div(start, jnp.int32(8)), lax.rem(start, jnp.int32(8))
    turned = pltpu.roll(x, within, 1)
    row = lax.broadcasted_iota(I32, (1, 8, width), 1)
    keep = row < within
    pieces = jnp.where(keep, jnp.concatenate([turned[:1], turned]), jnp.concatenate([turned, turned[-1:]]))
    if count is None:
        pieces = jnp.concatenate([jnp.where(keep, acc[pl.ds(first, 1)], turned[:1]), pieces[1:]])
    else:
        at = lax.broadcasted_iota(I32, (tiles + 1, 8, width), 0) * 8 + lax.broadcasted_iota(
            I32, (tiles + 1, 8, width), 1
        )
        pieces = jnp.where(
            (at >= within) & (at < within + count), pieces, acc[pl.ds(first, tiles + 1)]
        )
    acc[pl.ds(first, tiles + 1)] = pieces


def score(high_ref, low_ref, parts, rep):
    total = None
    for d, x in enumerate(parts):
        depth = x.shape[1]
        block = pl.ds(pl.multiple_of(lax.rem(rep + (len(parts) - d), jnp.int32(len(parts))) * depth, depth), depth)
        value = dot(x, high_ref[block, :]) + dot(x, low_ref[block, :])
        total = value if total is None else total + value
    return total.reshape(total.shape[0] // 8, 8, total.shape[1])


def for_feats(value, outs):
    n = len(outs)
    share = outs[0].shape[1]
    for f in range(n):
        @pl.when(lax.axis_index("feat") == f)
        def _():
            for d, out in enumerate(outs):
                at = ((f + d) % n) * share
                out[...] = value(slice(at, at + share)).astype(out.dtype)


def feat_shapes(rows, width, n_feat):
    share = (rows, width // n_feat)
    return [jax.ShapeDtypeStruct(share, F32)] + [jax.ShapeDtypeStruct(share, BF16)] * (n_feat - 1)


def early_scores(own, others, mine, pieces, cuts, firsts, seconds, table, rows, n_feat, n_rep, n_shard, bulk, extra):
    depth, width = own.shape
    columns = depth // n_rep
    n_other, n_piece = len(others), len(pieces)
    n_first = len(firsts) * n_rep
    last_hops = n_shard - 1

    def kernel(table_ref, *refs):
        own_ref, refs = refs[0], refs[1:]
        other_refs, refs = refs[:n_other], refs[n_other:]
        mine_ref, refs = refs[0], refs[1:]
        piece_refs = [refs[j * n_rep:(j + 1) * n_rep] for j in range(n_piece)]
        refs = refs[n_piece * n_rep:]
        first_refs, second_refs, refs = refs[:n_first], refs[n_first:2 * n_first], refs[2 * n_first:]
        high_ref, low_ref, outs, (scored, held, acc, sem) = refs[0], refs[1], refs[2:-4], refs[-4:]
        me, rep = lax.axis_index("shard"), lax.axis_index("rep")
        weight = own_ref[...]
        for ref in other_refs:
            weight = weight + ref[...].astype(F32)
        high = weight.astype(BF16)
        high_ref[...] = high
        low_ref[...] = (weight - high.astype(F32)).astype(BF16)

        scored[me] = score(high_ref, low_ref, [mine_ref[...]], jnp.int32(0))
        for parts, (hops, first, size) in zip(piece_refs, cuts):
            source = lax.rem(me + (n_shard - hops), jnp.int32(n_shard))
            scored[source, first // 8:(first + size) // 8] = score(high_ref, low_ref, [p[...] for p in parts], rep)
        last = lax.rem(me + (n_shard - last_hops), jnp.int32(n_shard))
        for s in range(n_shard):
            start = table_ref[s, 0]

            @pl.when(last != s)
            def _():
                put(acc, scored[s], start)

            if extra:
                @pl.when(table_ref[s, 3] > 0)
                def _():
                    apart = jnp.bitwise_xor(me, s)
                    rows_in = pl.ds(pl.multiple_of(lax.div(apart, jnp.int32(2)) * extra, extra), extra)
                    for odd in range(2):
                        @pl.when(jnp.bitwise_and(apart, 1) == odd)
                        def _():
                            copies = []
                            for j, refs in enumerate([first_refs, second_refs]):
                                for d in range(n_rep):
                                    goal = held.at[d, j * extra:(j + 1) * extra]
                                    which = refs[odd * n_rep + d].at[rows_in]
                                    copies.append(pltpu.make_async_copy(which, goal, sem.at[j * n_rep + d]))
                            for copy in copies:
                                copy.start()
                            for copy in copies:
                                copy.wait()
                    some = pl.ds(pl.multiple_of(table_ref[s, 2] * 16, 16), extra)
                    x = [held[d, some, :] for d in range(n_rep)]
                    put(acc, score(high_ref, low_ref, x, rep), start + table_ref[s, 1])
        for_feats(lambda at: acc[:rows // 8, :, at].reshape(rows, width // n_feat), outs)

    count = n_shard * bulk
    surplus = [x for parts in [*firsts, *seconds] for x in parts]
    return pl.pallas_call(
        kernel,
        in_specs=[SMEM] + [VMEM] * (2 + n_other + n_rep * n_piece) + [ANY] * len(surplus),
        out_specs=[VMEM] * (2 + n_feat),
        out_shape=[jax.ShapeDtypeStruct((depth, width), BF16)] * 2 + feat_shapes(rows, width, n_feat),
        scratch_shapes=[
            pltpu.VMEM((n_shard, bulk // 8, 8, width), F32),
            pltpu.VMEM((n_rep, 3 * extra + 16, columns), BF16),
            pltpu.VMEM(((rows + bulk + extra) // 8 + 2, 8, width), F32),
            pltpu.SemaphoreType.DMA((2 * n_rep,)),
        ],
        cost_estimate=cost(4 * count * depth * width, 10 * depth * width + count * (2 * depth + 4 * width)),
        compiler_params=PARAMS,
        name="early_scores",
    )(table, own, *others, mine, *[p for parts in pieces for p in parts], *surplus)


def late_scores(pieces, high, low, n_feat):
    n, n_rep = len(pieces), len(pieces[0])
    size = pieces[0][0].shape[0]
    rows = n * size
    width = high.shape[1]

    def kernel(high_ref, low_ref, *refs):
        part_refs, outs, acc = refs[:n * n_rep], refs[n * n_rep:-1], refs[-1]
        parts = [jnp.concatenate([part_refs[j * n_rep + d][...] for j in range(n)]) for d in range(n_rep)]
        y = score(high_ref, low_ref, parts, lax.axis_index("rep"))
        acc[...] = y.reshape(rows, width)
        for_feats(lambda at: acc[:, at], outs)

    return pl.pallas_call(
        kernel,
        in_specs=[VMEM] * (2 + n * n_rep),
        out_specs=[VMEM] * n_feat,
        out_shape=feat_shapes(rows, width, n_feat),
        scratch_shapes=[pltpu.VMEM((rows, width), F32)],
        cost_estimate=cost(4 * rows * high.size, 8 * rows * width),
        compiler_params=PARAMS,
        name="late_scores",
    )(high, low, *[p for parts in pieces for p in parts])


def merge(table, early, late, n_shard):
    rows, width = early[0].shape
    last_rows = late[0].shape[0]
    last_hops = n_shard - 1

    def kernel(table_ref, *refs):
        early_refs, late_refs = refs[:len(early)], refs[len(early):-2]
        out_ref, acc = refs[-2:]
        source = lax.rem(lax.axis_index("shard") + (n_shard - last_hops), jnp.int32(n_shard))

        def total(parts):
            value = parts[0][...]
            for ref in parts[1:]:
                value = value + ref[...].astype(F32)
            return value.reshape(value.shape[0] // 8, 8, width)

        acc[:rows // 8] = total(early_refs)
        put(acc, total(late_refs), table_ref[source, 0], table_ref[source, 1])
        out_ref[...] = acc[:rows // 8].reshape(rows, width).T

    return pl.pallas_call(
        kernel,
        in_specs=[SMEM] + [VMEM] * (len(early) + len(late)),
        out_specs=VMEM,
        out_shape=jax.ShapeDtypeStruct((width, rows), F32),
        scratch_shapes=[pltpu.VMEM(((rows + last_rows) // 8 + 2, 8, width), F32)],
        cost_estimate=cost(0, 8 * rows * width),
        compiler_params=PARAMS,
        name="merge",
    )(table, *early, *late)


def body(train, cluster_ids, precond, query_store, block_slot, pattern):
    n_group, n_shard = lax.axis_size("groups"), lax.axis_size("shard")
    n_feat, n_rep = lax.axis_size("feat"), lax.axis_size("rep")
    feat, rep = lax.axis_index("feat"), lax.axis_index("rep")
    rows = train.shape[0]
    lines = rows // LANES
    base = rows // n_shard
    columns = train.shape[1] // n_rep
    extra = base // 2 if n_shard == 4 else 0
    bulk = base if extra else base + base // 2
    ids = cluster_ids.reshape(-1, LANES)

    last_hops = n_shard - 1

    def with_rep(x):
        return [x] + [shift(x, "rep", n_rep, d) for d in range(1, n_rep)]

    matrices = with_rep(precond[0])

    picked = pick_queries(query_store, block_slot, pattern, n_group)
    pieces = [picked[0]] + [shift(picked[d], "shard", n_shard, d) for d in range(1, n_shard)]

    middle = [(d, 0, bulk) for d in range(1, last_hops)]
    part = 64 if bulk % 64 == 0 else bulk
    final = [(last_hops, at, part) for at in range(0, bulk, part)]
    *packed, goal = pack_rows(train, ids, columns, bulk, extra, middle + final)
    before_join, firsts, seconds = [], [], []
    if extra:
        far = swap(after(packed[-2], *pieces[1:]), "shard", n_shard, 2)
        before_join = [far]
    depth = n_rep * columns
    targets = [(feat + d) % n_feat for d in range(1, n_feat)]
    near_chip = fetch(matrices, targets[0], depth, *pieces[1:])

    parts = [pieces] + [[shift(x, "groups", n_group, d) for x in pieces] for d in range(1, n_group)]
    chosen = join_queries(
        parts, block_slot, pattern, query_store.shape[0], n_feat, n_rep, *before_join, *near_chip
    )
    queries = [chosen[0]] + [shift(chosen[d], "rep", n_rep, d) for d in range(1, n_rep)]
    here = [shift(after(packed[0], *before_join), "shard", n_shard, 1)]

    sends = [fetched_weights(near_chip, queries, BF16)]
    sends += [partial_weights(matrices, queries, f, depth, BF16) for f in targets[1:]]
    others = [shift(x, "feat", n_feat, d + 1) for d, x in enumerate(sends)]
    own = partial_weights(matrices, queries, feat, depth, F32, *sends)

    for (hops, _, _), x in zip(middle[1:], packed[1:]):
        here.append(shift(after(x, here[-1], *sends), "shard", n_shard, hops))
    last = [
        shift(after(packed[len(middle) + j], here[-1], own), "shard", n_shard, last_hops) for j in range(len(final))
    ]

    mine = own_rows(goal, train, bulk, own)
    table, flag = row_table(ids, lines, bulk, extra, own)
    marks = [own, mine]
    if extra:
        for d in range(1, n_group):
            flag = jnp.maximum(flag, shift(flag, "groups", n_group, d))

        def second_round(x):
            pair = jnp.concatenate([x, swap(x, "shard", n_shard, 2)])
            return [with_rep(pair), with_rep(swap(pair, "shard", n_shard, 1))]

        def no_round(x):
            return [[jnp.zeros((2 * extra, columns), BF16)] * n_rep] * 2

        seconds = lax.cond(flag[0, 0] > 0, second_round, no_round, packed[-1])
        pair = stack([packed[-3], far], *sends)
        near = swap(pair, "shard", n_shard, 1)
        firsts = [with_rep(pair), with_rep(near)]
        marks += [seconds[0][0], near]

    mark = shift(after(jnp.zeros((8, LANES), I32), *marks), "rep", n_rep, 1)
    ready = [with_rep(after(x, mark)) for x in here]
    high, low, *early = early_scores(
        own, others, mine, ready, middle, firsts, seconds, table, rows, n_feat, n_rep, n_shard, bulk, extra
    )

    def over_feat(shares):
        return [shares[0]] + [shift(shares[d], "feat", n_feat, d) for d in range(1, n_feat)]

    late = late_scores([with_rep(after(x, *early[1:])) for x in last], high, low, n_feat)
    return merge(table, over_feat(early), over_feat(late), n_shard)[None]


def solution(mesh):
    return jax.shard_map(
        body,
        mesh=mesh,
        in_specs=(
            P(("groups", "shard"), "feat"),
            P("groups"),
            P(("groups", "shard"), None, ("feat", "rep")),
            P("shard", None, ("feat", "rep")),
            P(),
            P(),
        ),
        out_specs=P(("groups", "shard"), ("feat", "rep"), None),
        check_vma=False,
    )
```

```python
import functools

import jax
import jax.numpy as jnp
from jax import lax
from jax.experimental import pallas as pl
from jax.experimental.pallas import tpu as pltpu
from jax.sharding import PartitionSpec as P

F32, BF16, I32 = jnp.float32, jnp.bfloat16, jnp.int32
VMEM = pl.BlockSpec(memory_space=pltpu.VMEM)
ANY = pl.BlockSpec(memory_space=pl.ANY)
SMEM = pl.BlockSpec(memory_space=pltpu.SMEM)
PARAMS = pltpu.CompilerParams(vmem_limit_bytes=24 * 2**20)
MIDDLE = pltpu.CompilerParams(vmem_limit_bytes=48 * 2**20)
FIRST = pltpu.CompilerParams(vmem_limit_bytes=60 * 2**20)
LANES = 128


def shift(x, axis, size, by):
    return lax.ppermute(x, axis, [(i, (i + by) % size) for i in range(size)])


def swap(x, axis, size, bit):
    return lax.ppermute(x, axis, [(i, i ^ bit) for i in range(size)])


def dot(a, b):
    return jnp.dot(a, b, preferred_element_type=F32)


def cost(flops, nbytes):
    return pl.CostEstimate(flops=1, bytes_accessed=1, transcendentals=0)


def after(x, *others):
    def kernel(*refs):
        pass

    return pl.pallas_call(
        kernel,
        in_specs=[ANY] * (1 + len(others)),
        out_specs=ANY,
        out_shape=jax.ShapeDtypeStruct(x.shape, x.dtype),
        input_output_aliases={0: 0},
        cost_estimate=cost(0, 0),
        compiler_params=PARAMS,
        name="after",
    )(x, *others)


def stack(parts, *others):
    size, width = parts[0].shape
    n = len(parts)

    def kernel(*refs):
        for j in range(n):
            refs[-1][j * size:(j + 1) * size, :] = refs[j][...]

    return pl.pallas_call(
        kernel,
        in_specs=[VMEM] * n + [ANY] * len(others),
        out_specs=VMEM,
        out_shape=jax.ShapeDtypeStruct((n * size, width), parts[0].dtype),
        cost_estimate=cost(0, 0),
        compiler_params=PARAMS,
        name="stack",
    )(*parts, *others)


def pick_queries(query_store, block_slot, pattern, n_group):
    local_blocks, block_rows, width = query_store.shape
    n_cluster, n_list = pattern.shape
    part = block_rows // n_group

    def kernel(pattern_ref, slot_ref, in_ref, *rest):
        outs, sem = rest[:-1], rest[-1]
        me, group = lax.axis_index("shard"), lax.axis_index("groups")
        copies = []
        for t, out in enumerate(outs):
            target = lax.rem(me + t, jnp.int32(n_cluster))
            found = jnp.int32(0)
            for k in range(n_list):
                slot = slot_ref[pattern_ref[target, k]]
                hit = (lax.div(slot, jnp.int32(local_blocks)) == me).astype(I32)
                found = found + hit * lax.rem(slot, jnp.int32(local_blocks))
            rows = pl.ds(pl.multiple_of(group * part, part), part)
            copies.append(pltpu.make_async_copy(in_ref.at[found, rows], out.at[0], sem.at[t]))
            copies[-1].start()
        for copy in copies:
            copy.wait()

    return pl.pallas_call(
        kernel,
        in_specs=[SMEM, SMEM, ANY],
        out_specs=[VMEM] * n_cluster,
        out_shape=[jax.ShapeDtypeStruct((1, part, width), BF16)] * n_cluster,
        scratch_shapes=[pltpu.SemaphoreType.DMA((n_cluster,))],
        cost_estimate=cost(0, 4 * n_cluster * part * width),
        compiler_params=FIRST,
        name="pick_queries",
    )(pattern, block_slot, query_store)


def join_queries(parts, block_slot, pattern, local_blocks, n_feat, n_rep, *others):
    n_group, n_cluster = len(parts), len(parts[0])
    _, part, width = parts[0][0].shape
    n_list = pattern.shape[1]
    total = n_list * n_group * part
    share = total // (n_feat * n_rep)
    unit = min(share, part)
    half = total // n_rep

    def kernel(pattern_ref, slot_ref, *refs):
        outs, rows_ref = refs[-1 - n_rep:-1], refs[-1]
        me, group = lax.axis_index("shard"), lax.axis_index("groups")
        for k in range(n_list):
            owner = lax.div(slot_ref[pattern_ref[me, k]], jnp.int32(local_blocks))
            hops = lax.rem(me + (n_cluster - owner), jnp.int32(n_cluster))
            for d in range(n_group):
                origin = lax.rem(group + (n_group - d), jnp.int32(n_group))
                for h in range(n_cluster):
                    @pl.when(hops == h)
                    def _():
                        for u in range(part // unit):
                            first = (k * n_group + origin) * part + u * unit
                            chunk = lax.div(first, jnp.int32(share))
                            goal = lax.rem(chunk, jnp.int32(n_rep)) * n_feat + lax.div(chunk, jnp.int32(n_rep))
                            goal = pl.multiple_of(goal * share + lax.rem(first, jnp.int32(share)), unit)
                            rows_ref[pl.ds(goal, unit), :] = refs[d * n_cluster + h][0, u * unit:(u + 1) * unit, :]
        for r in range(n_rep):
            @pl.when(lax.axis_index("rep") == r)
            def _():
                for d, out in enumerate(outs):
                    at = ((r + d) % n_rep) * half
                    out[...] = rows_ref[at:at + half, :].T

    return pl.pallas_call(
        kernel,
        in_specs=[SMEM, SMEM] + [VMEM] * (n_group * n_cluster) + [ANY] * len(others),
        out_specs=[VMEM] * n_rep,
        out_shape=[jax.ShapeDtypeStruct((width, half), BF16)] * n_rep,
        scratch_shapes=[pltpu.VMEM((total, width), BF16)],
        cost_estimate=cost(0, 4 * total * width),
        compiler_params=PARAMS,
        name="join_queries",
    )(pattern, block_slot, *[x for line in parts for x in line], *others)


def select(goal_ref, train_ref, base, size):
    tile = 128 if size % 128 == 0 else size
    found = []
    for at in range(0, size, tile):
        index = lax.broadcasted_iota(I32, (tile, LANES), 0) + (base + at)
        pick = [(index == goal_ref[a:a + 1, :]).astype(F32).astype(BF16) for a in range(goal_ref.shape[0])]
        found.append(dot(jnp.concatenate(pick, axis=1), train_ref[...]).astype(BF16))
    return jnp.concatenate(found)


def own_rows(goal, train, bulk, *others):
    def kernel(goal_ref, train_ref, *rest):
        rest[-1][...] = select(goal_ref, train_ref, lax.axis_index("shard") * bulk, bulk)

    return pl.pallas_call(
        kernel,
        in_specs=[VMEM] * 2 + [ANY] * len(others),
        out_specs=VMEM,
        out_shape=jax.ShapeDtypeStruct((bulk, train.shape[1]), BF16),
        cost_estimate=cost(2 * bulk * train.size, 2 * train.size),
        compiler_params=FIRST,
        name="own_rows",
    )(goal, train, *others)


def pack_rows(train, ids, columns, bulk, extra, cuts):
    rows = train.shape[0]
    lines = rows // LANES
    n_shard = ids.shape[0] // lines

    def kernel(ids_ref, train_ref, *rest):
        outs, goal_ref = rest[:-1], rest[-1]
        me = lax.axis_index("shard")
        own = ids_ref[...]
        masks = [(own == c).astype(F32) for c in range(n_shard)]
        stacked = jnp.concatenate(masks, axis=0).astype(BF16)
        lane_from = lax.broadcasted_iota(I32, (LANES, LANES), 0)
        lane_to = lax.broadcasted_iota(I32, (LANES, LANES), 1)
        in_line = dot(stacked, (lane_from < lane_to).astype(F32).astype(BF16))
        line_sum = dot(stacked, jnp.ones((LANES, LANES), BF16)).astype(BF16)
        size = n_shard * lines
        to = lax.broadcasted_iota(I32, (size, size), 0)
        since = lax.broadcasted_iota(I32, (size, size), 1)
        same = (to // lines) == (since // lines)
        ahead = dot((same & (since < to)).astype(F32).astype(BF16), line_sum)
        whole = dot(same.astype(F32).astype(BF16), line_sum)
        rank = in_line + ahead
        goal = jnp.zeros((lines, LANES), F32)
        past = jnp.zeros((lines, LANES), F32)
        for c in range(n_shard):
            part = slice(c * lines, (c + 1) * lines)
            place = rank[part] + c * bulk
            if extra:
                surplus = n_shard * bulk + past + rank[part] - bulk
                place = jnp.where(rank[part] < bulk, place, surplus)
                past = past + jnp.floor((jnp.maximum(whole[part] - bulk, 0.0) + 15.0) * 0.0625) * 16.0
            goal = goal + masks[c] * place
        goal_ref[...] = goal.astype(I32)

        def fill(out, base):
            out[...] = select(goal_ref, train_ref, base, out.shape[0])

        for out, (hops, first, _) in zip(outs, cuts):
            fill(out, lax.rem(me + hops, jnp.int32(n_shard)) * bulk + first)
        for j, out in enumerate(outs[len(cuts):]):
            fill(out, n_shard * bulk + max(j - 1, 0) * extra)

    shapes = [jax.ShapeDtypeStruct((n, columns), BF16) for _, _, n in cuts]
    shapes += [jax.ShapeDtypeStruct((extra, columns), BF16)] * (3 if extra else 0)
    shapes += [jax.ShapeDtypeStruct((lines, LANES), I32)]
    packed = n_shard * bulk + 2 * extra
    return pl.pallas_call(
        kernel,
        grid=(1,),
        in_specs=[
            pl.BlockSpec((lines, LANES), lambda i: (lax.axis_index("shard"), 0)),
            pl.BlockSpec((rows, columns), lambda i: (0, lax.axis_index("rep"))),
        ],
        out_specs=[VMEM] * len(shapes),
        out_shape=shapes,
        cost_estimate=cost(2 * packed * rows * columns, 2 * (rows + packed) * columns),
        compiler_params=FIRST,
        name="pack_rows",
    )(ids, train)


def partial_weights(matrices, queries, block, depth, dtype, *others):
    width, total = queries[0].shape
    tile = 512 if depth % 512 == 0 else depth
    steps = depth // tile
    n = len(matrices)

    def kernel(block_ref, *refs):
        value = dot(refs[0][...], refs[n][...])
        for j in range(1, n):
            value = value + dot(refs[j][...], refs[n + j][...])
        refs[-1][...] = value.astype(dtype)

    return pl.pallas_call(
        kernel,
        grid_spec=pltpu.PrefetchScalarGridSpec(
            num_scalar_prefetch=1,
            grid=(steps,),
            in_specs=[pl.BlockSpec((tile, width), lambda i, b: (b[0] * steps + i, 0))] * n
            + [pl.BlockSpec((width, total), lambda i, b: (0, 0))] * n
            + [ANY] * len(others),
            out_specs=pl.BlockSpec((tile, total), lambda i, b: (i, 0)),
        ),
        out_shape=jax.ShapeDtypeStruct((depth, total), dtype),
        cost_estimate=cost(2 * n * depth * width * total, 2 * n * depth * width + 4 * depth * total),
        compiler_params=FIRST,
        name="partial_weights",
    )(jnp.reshape(block, (1,)).astype(I32), *matrices, *queries, *others)


def fetch(matrices, block, depth, *others):
    width = matrices[0].shape[1]
    n = len(matrices)
    cuts = 4

    def kernel(block_ref, *refs):
        outs, sem = refs[-1 - n:-1], refs[-1]
        first = pl.multiple_of(block_ref[0] * depth, depth)
        copies = []
        for j in range(n):
            for c in range(cuts):
                size = depth // cuts
                source = refs[j].at[pl.ds(first + c * size, size)]
                copies.append(
                    pltpu.make_async_copy(source, outs[j].at[c * size:(c + 1) * size], sem.at[j * cuts + c])
                )
        for copy in copies:
            copy.start()
        for copy in copies:
            copy.wait()

    return pl.pallas_call(
        kernel,
        in_specs=[SMEM] + [ANY] * (n + len(others)),
        out_specs=[VMEM] * n,
        out_shape=[jax.ShapeDtypeStruct((depth, width), BF16)] * n,
        scratch_shapes=[pltpu.SemaphoreType.DMA((n * cuts,))],
        cost_estimate=cost(0, 2 * n * depth * width),
        compiler_params=MIDDLE,
        name="fetch",
    )(jnp.reshape(block, (1,)).astype(I32), *matrices, *others)


def fetched_weights(matrices, queries, dtype):
    depth = matrices[0].shape[0]
    total = queries[0].shape[1]
    tile = 512 if depth % 512 == 0 else depth
    n = len(matrices)

    def kernel(*refs):
        for at in range(0, depth, tile):
            value = dot(refs[0][at:at + tile, :], refs[n][...])
            for j in range(1, n):
                value = value + dot(refs[j][at:at + tile, :], refs[n + j][...])
            refs[-1][at:at + tile, :] = value.astype(dtype)

    return pl.pallas_call(
        kernel,
        in_specs=[VMEM] * (2 * n),
        out_specs=VMEM,
        out_shape=jax.ShapeDtypeStruct((depth, total), dtype),
        cost_estimate=cost(2 * n * matrices[0].size * total, 2 * n * matrices[0].size),
        compiler_params=PARAMS,
        name="fetched_weights",
    )(*matrices, *queries)


def row_table(ids, lines, bulk, extra, *others):
    n_shard = ids.shape[0] // lines

    def kernel(ids_ref, *rest):
        table_ref, flag_ref = rest[-2:]
        me = lax.axis_index("shard")
        start = jnp.int32(0)
        most = jnp.int32(0)
        for s in range(n_shard):
            line = ids_ref[s * lines:(s + 1) * lines, :]

            def count(c):
                return jnp.sum((line == c).astype(I32))

            mine = count(me)
            before = jnp.int32(0)
            if extra:
                surplus = jnp.int32(0)
                for c in range(n_shard):
                    over = lax.div(jnp.maximum(count(c) - bulk, 0) + 15, jnp.int32(16)) * 16
                    before = before + jnp.where(c < me, over, 0)
                    surplus = surplus + over
                most = jnp.maximum(most, surplus)
            table_ref[s, 0] = start
            table_ref[s, 1] = jnp.minimum(mine, bulk)
            table_ref[s, 2] = lax.div(before, jnp.int32(16))
            table_ref[s, 3] = jnp.maximum(mine - bulk, 0)
            start = start + mine
        flag_ref[...] = jnp.full((8, LANES), (most > extra).astype(I32))

    return pl.pallas_call(
        kernel,
        in_specs=[VMEM] + [ANY] * len(others),
        out_specs=[SMEM, VMEM],
        out_shape=[jax.ShapeDtypeStruct((n_shard, 4), I32), jax.ShapeDtypeStruct((8, LANES), I32)],
        cost_estimate=cost(0, 4 * ids.size),
        compiler_params=FIRST,
        name="row_table",
    )(ids, *others)


def put(acc, x, start, count=None):
    tiles, _, width = x.shape
    first, within = lax.div(start, jnp.int32(8)), lax.rem(start, jnp.int32(8))
    turned = pltpu.roll(x, within, 1)
    row = lax.broadcasted_iota(I32, (1, 8, width), 1)
    keep = row < within
    pieces = jnp.where(keep, jnp.concatenate([turned[:1], turned]), jnp.concatenate([turned, turned[-1:]]))
    if count is None:
        pieces = jnp.concatenate([jnp.where(keep, acc[pl.ds(first, 1)], turned[:1]), pieces[1:]])
    else:
        at = lax.broadcasted_iota(I32, (tiles + 1, 8, width), 0) * 8 + lax.broadcasted_iota(
            I32, (tiles + 1, 8, width), 1
        )
        pieces = jnp.where(
            (at >= within) & (at < within + count), pieces, acc[pl.ds(first, tiles + 1)]
        )
    acc[pl.ds(first, tiles + 1)] = pieces


def score(high_ref, low_ref, parts, rep):
    total = None
    for d, x in enumerate(parts):
        depth = x.shape[1]
        block = pl.ds(pl.multiple_of(lax.rem(rep + (len(parts) - d), jnp.int32(len(parts))) * depth, depth), depth)
        value = dot(x, high_ref[block, :]) + dot(x, low_ref[block, :])
        total = value if total is None else total + value
    return total.reshape(total.shape[0] // 8, 8, total.shape[1])


def for_feats(value, outs):
    n = len(outs)
    share = outs[0].shape[1]
    for f in range(n):
        @pl.when(lax.axis_index("feat") == f)
        def _():
            for d, out in enumerate(outs):
                at = ((f + d) % n) * share
                out[...] = value(slice(at, at + share)).astype(out.dtype)


def feat_shapes(rows, width, n_feat):
    share = (rows, width // n_feat)
    return [jax.ShapeDtypeStruct(share, F32)] + [jax.ShapeDtypeStruct(share, BF16)] * (n_feat - 1)


def early_scores(own, others, mine, pieces, cuts, firsts, seconds, table, rows, n_feat, n_rep, n_shard, bulk, extra):
    depth, width = own.shape
    columns = depth // n_rep
    n_other, n_piece = len(others), len(pieces)
    n_first = len(firsts) * n_rep
    last_hops = n_shard - 1

    def kernel(table_ref, *refs):
        own_ref, refs = refs[0], refs[1:]
        other_refs, refs = refs[:n_other], refs[n_other:]
        mine_ref, refs = refs[0], refs[1:]
        piece_refs = [refs[j * n_rep:(j + 1) * n_rep] for j in range(n_piece)]
        refs = refs[n_piece * n_rep:]
        first_refs, second_refs, refs = refs[:n_first], refs[n_first:2 * n_first], refs[2 * n_first:]
        high_ref, low_ref, outs, (scored, held, acc, sem) = refs[0], refs[1], refs[2:-4], refs[-4:]
        me, rep = lax.axis_index("shard"), lax.axis_index("rep")
        weight = own_ref[...]
        for ref in other_refs:
            weight = weight + ref[...].astype(F32)
        high = weight.astype(BF16)
        high_ref[...] = high
        low_ref[...] = (weight - high.astype(F32)).astype(BF16)

        scored[me] = score(high_ref, low_ref, [mine_ref[...]], jnp.int32(0))
        for parts, (hops, first, size) in zip(piece_refs, cuts):
            source = lax.rem(me + (n_shard - hops), jnp.int32(n_shard))
            scored[source, first // 8:(first + size) // 8] = score(high_ref, low_ref, [p[...] for p in parts], rep)
        last = lax.rem(me + (n_shard - last_hops), jnp.int32(n_shard))
        for s in range(n_shard):
            start = table_ref[s, 0]

            @pl.when(last != s)
            def _():
                put(acc, scored[s], start)

            if extra:
                @pl.when(table_ref[s, 3] > 0)
                def _():
                    apart = jnp.bitwise_xor(me, s)
                    rows_in = pl.ds(pl.multiple_of(lax.div(apart, jnp.int32(2)) * extra, extra), extra)
                    for odd in range(2):
                        @pl.when(jnp.bitwise_and(apart, 1) == odd)
                        def _():
                            copies = []
                            for j, refs in enumerate([first_refs, second_refs]):
                                for d in range(n_rep):
                                    goal = held.at[d, j * extra:(j + 1) * extra]
                                    which = refs[odd * n_rep + d].at[rows_in]
                                    copies.append(pltpu.make_async_copy(which, goal, sem.at[j * n_rep + d]))
                            for copy in copies:
                                copy.start()
                            for copy in copies:
                                copy.wait()
                    some = pl.ds(pl.multiple_of(table_ref[s, 2] * 16, 16), extra)
                    x = [held[d, some, :] for d in range(n_rep)]
                    put(acc, score(high_ref, low_ref, x, rep), start + table_ref[s, 1])
        for_feats(lambda at: acc[:rows // 8, :, at].reshape(rows, width // n_feat), outs)

    count = n_shard * bulk
    surplus = [x for parts in [*firsts, *seconds] for x in parts]
    return pl.pallas_call(
        kernel,
        in_specs=[SMEM] + [VMEM] * (2 + n_other + n_rep * n_piece) + [ANY] * len(surplus),
        out_specs=[VMEM] * (2 + n_feat),
        out_shape=[jax.ShapeDtypeStruct((depth, width), BF16)] * 2 + feat_shapes(rows, width, n_feat),
        scratch_shapes=[
            pltpu.VMEM((n_shard, bulk // 8, 8, width), F32),
            pltpu.VMEM((n_rep, 3 * extra + 16, columns), BF16),
            pltpu.VMEM(((rows + bulk + extra) // 8 + 2, 8, width), F32),
            pltpu.SemaphoreType.DMA((2 * n_rep,)),
        ],
        cost_estimate=cost(4 * count * depth * width, 10 * depth * width + count * (2 * depth + 4 * width)),
        compiler_params=PARAMS,
        name="early_scores",
    )(table, own, *others, mine, *[p for parts in pieces for p in parts], *surplus)


def late_scores(pieces, high, low, n_feat):
    n, n_rep = len(pieces), len(pieces[0])
    size = pieces[0][0].shape[0]
    rows = n * size
    width = high.shape[1]

    def kernel(high_ref, low_ref, *refs):
        part_refs, outs, acc = refs[:n * n_rep], refs[n * n_rep:-1], refs[-1]
        parts = [jnp.concatenate([part_refs[j * n_rep + d][...] for j in range(n)]) for d in range(n_rep)]
        y = score(high_ref, low_ref, parts, lax.axis_index("rep"))
        acc[...] = y.reshape(rows, width)
        for_feats(lambda at: acc[:, at], outs)

    return pl.pallas_call(
        kernel,
        in_specs=[VMEM] * (2 + n * n_rep),
        out_specs=[VMEM] * n_feat,
        out_shape=feat_shapes(rows, width, n_feat),
        scratch_shapes=[pltpu.VMEM((rows, width), F32)],
        cost_estimate=cost(4 * rows * high.size, 8 * rows * width),
        compiler_params=PARAMS,
        name="late_scores",
    )(high, low, *[p for parts in pieces for p in parts])


def merge(table, early, late, n_shard):
    rows, width = early[0].shape
    last_rows = late[0].shape[0]
    last_hops = n_shard - 1

    def kernel(table_ref, *refs):
        early_refs, late_refs = refs[:len(early)], refs[len(early):-2]
        out_ref, acc = refs[-2:]
        source = lax.rem(lax.axis_index("shard") + (n_shard - last_hops), jnp.int32(n_shard))

        def total(parts):
            value = parts[0][...]
            for ref in parts[1:]:
                value = value + ref[...].astype(F32)
            return value.reshape(value.shape[0] // 8, 8, width)

        acc[:rows // 8] = total(early_refs)
        put(acc, total(late_refs), table_ref[source, 0], table_ref[source, 1])
        out_ref[...] = acc[:rows // 8].reshape(rows, width).T

    return pl.pallas_call(
        kernel,
        in_specs=[SMEM] + [VMEM] * (len(early) + len(late)),
        out_specs=VMEM,
        out_shape=jax.ShapeDtypeStruct((width, rows), F32),
        scratch_shapes=[pltpu.VMEM(((rows + last_rows) // 8 + 2, 8, width), F32)],
        cost_estimate=cost(0, 8 * rows * width),
        compiler_params=PARAMS,
        name="merge",
    )(table, *early, *late)


def body(train, cluster_ids, precond, query_store, block_slot, pattern):
    n_group, n_shard = lax.axis_size("groups"), lax.axis_size("shard")
    n_feat, n_rep = lax.axis_size("feat"), lax.axis_size("rep")
    feat, rep = lax.axis_index("feat"), lax.axis_index("rep")
    rows = train.shape[0]
    lines = rows // LANES
    base = rows // n_shard
    columns = train.shape[1] // n_rep
    extra = base // 2 if n_shard == 4 else 0
    bulk = base if extra else base + base // 2
    ids = cluster_ids.reshape(-1, LANES)

    last_hops = n_shard - 1

    def with_rep(x):
        return [x] + [shift(x, "rep", n_rep, d) for d in range(1, n_rep)]

    matrices = with_rep(precond[0])

    picked = pick_queries(query_store, block_slot, pattern, n_group)
    pieces = [picked[0]] + [shift(picked[d], "shard", n_shard, d) for d in range(1, n_shard)]

    middle = [(d, 0, bulk) for d in range(1, last_hops)]
    part = 64 if bulk % 64 == 0 else bulk
    final = [(last_hops, at, part) for at in range(0, bulk, part)]
    *packed, goal = pack_rows(train, ids, columns, bulk, extra, middle + final)
    firsts, seconds = [], []
    parts = [pieces] + [[shift(x, "groups", n_group, d) for x in pieces] for d in range(1, n_group)]
    first_cut = packed[0]
    if extra:
        far = swap(after(packed[-2], *pieces[1:], *[x[0] for x in parts[1:]]), "shard", n_shard, 2)
        first_cut = after(first_cut, far)
    depth = n_rep * columns
    targets = [(feat + d) % n_feat for d in range(1, n_feat)]
    near_chip = fetch(matrices, targets[0], depth, *pieces[1:])

    chosen = join_queries(parts, block_slot, pattern, query_store.shape[0], n_feat, n_rep, *near_chip)
    queries = [chosen[0]] + [shift(chosen[d], "rep", n_rep, d) for d in range(1, n_rep)]
    here = [shift(first_cut, "shard", n_shard, 1)]

    sends = [fetched_weights(near_chip, queries, BF16)]
    sends += [partial_weights(matrices, queries, f, depth, BF16) for f in targets[1:]]
    others = [shift(x, "feat", n_feat, d + 1) for d, x in enumerate(sends)]
    own = partial_weights(matrices, queries, feat, depth, F32, *sends)

    for (hops, _, _), x in zip(middle[1:], packed[1:]):
        here.append(shift(after(x, here[-1], *sends), "shard", n_shard, hops))
    last = [
        shift(after(packed[len(middle) + j], here[-1], own), "shard", n_shard, last_hops) for j in range(len(final))
    ]

    mine = own_rows(goal, train, bulk, own)
    table, flag = row_table(ids, lines, bulk, extra, own)
    marks = [own, mine]
    if extra:
        for d in range(1, n_group):
            flag = jnp.maximum(flag, shift(flag, "groups", n_group, d))

        def second_round(x):
            pair = jnp.concatenate([x, swap(x, "shard", n_shard, 2)])
            return [with_rep(pair), with_rep(swap(pair, "shard", n_shard, 1))]

        def no_round(x):
            return [[jnp.zeros((2 * extra, columns), BF16)] * n_rep] * 2

        seconds = lax.cond(flag[0, 0] > 0, second_round, no_round, packed[-1])
        pair = stack([packed[-3], far], here[0], *sends)
        near = swap(pair, "shard", n_shard, 1)
        firsts = [with_rep(pair), with_rep(near)]
        marks += [seconds[0][0], near]

    mark = shift(after(jnp.zeros((8, LANES), I32), *marks), "rep", n_rep, 1)
    ready = [with_rep(after(x, mark)) for x in here]
    high, low, *early = early_scores(
        own, others, mine, ready, middle, firsts, seconds, table, rows, n_feat, n_rep, n_shard, bulk, extra
    )

    def over_feat(shares):
        return [shares[0]] + [shift(shares[d], "feat", n_feat, d) for d in range(1, n_feat)]

    late = late_scores([with_rep(after(x, *early[1:])) for x in last], high, low, n_feat)
    return merge(table, over_feat(early), over_feat(late), n_shard)[None]


def solution(mesh):
    return jax.shard_map(
        body,
        mesh=mesh,
        in_specs=(
            P(("groups", "shard"), "feat"),
            P("groups"),
            P(("groups", "shard"), None, ("feat", "rep")),
            P("shard", None, ("feat", "rep")),
            P(),
            P(),
        ),
        out_specs=P(("groups", "shard"), ("feat", "rep"), None),
        check_vma=False,
    )
```

```python
import functools

import jax
import jax.numpy as jnp
from jax import lax
from jax.experimental import pallas as pl
from jax.experimental.pallas import tpu as pltpu
from jax.sharding import PartitionSpec as P

F32, BF16, I32 = jnp.float32, jnp.bfloat16, jnp.int32
VMEM = pl.BlockSpec(memory_space=pltpu.VMEM)
ANY = pl.BlockSpec(memory_space=pl.ANY)
SMEM = pl.BlockSpec(memory_space=pltpu.SMEM)
PARAMS = pltpu.CompilerParams(vmem_limit_bytes=24 * 2**20)
MIDDLE = pltpu.CompilerParams(vmem_limit_bytes=48 * 2**20)
FIRST = pltpu.CompilerParams(vmem_limit_bytes=60 * 2**20)
LANES = 128


def shift(x, axis, size, by):
    return lax.ppermute(x, axis, [(i, (i + by) % size) for i in range(size)])


def swap(x, axis, size, bit):
    return lax.ppermute(x, axis, [(i, i ^ bit) for i in range(size)])


def dot(a, b):
    return jnp.dot(a, b, preferred_element_type=F32)


def cost(flops, nbytes):
    return pl.CostEstimate(flops=1, bytes_accessed=1, transcendentals=0)


def after(x, *others):
    def kernel(*refs):
        pass

    return pl.pallas_call(
        kernel,
        in_specs=[ANY] * (1 + len(others)),
        out_specs=ANY,
        out_shape=jax.ShapeDtypeStruct(x.shape, x.dtype),
        input_output_aliases={0: 0},
        cost_estimate=cost(0, 0),
        compiler_params=PARAMS,
        name="after",
    )(x, *others)


def stack(parts, *others):
    size, width = parts[0].shape
    n = len(parts)

    def kernel(*refs):
        for j in range(n):
            refs[-1][j * size:(j + 1) * size, :] = refs[j][...]

    return pl.pallas_call(
        kernel,
        in_specs=[VMEM] * n + [ANY] * len(others),
        out_specs=VMEM,
        out_shape=jax.ShapeDtypeStruct((n * size, width), parts[0].dtype),
        cost_estimate=cost(0, 0),
        compiler_params=PARAMS,
        name="stack",
    )(*parts, *others)


def pick_queries(query_store, block_slot, pattern, n_group):
    local_blocks, block_rows, width = query_store.shape
    n_cluster, n_list = pattern.shape
    part = block_rows // n_group

    def kernel(pattern_ref, slot_ref, in_ref, *rest):
        outs, sem = rest[:-1], rest[-1]
        me, group = lax.axis_index("shard"), lax.axis_index("groups")
        copies = []
        for t, out in enumerate(outs):
            target = lax.rem(me + t, jnp.int32(n_cluster))
            found = jnp.int32(0)
            for k in range(n_list):
                slot = slot_ref[pattern_ref[target, k]]
                hit = (lax.div(slot, jnp.int32(local_blocks)) == me).astype(I32)
                found = found + hit * lax.rem(slot, jnp.int32(local_blocks))
            rows = pl.ds(pl.multiple_of(group * part, part), part)
            copies.append(pltpu.make_async_copy(in_ref.at[found, rows], out.at[0], sem.at[t]))
            copies[-1].start()
        for copy in copies:
            copy.wait()

    return pl.pallas_call(
        kernel,
        in_specs=[SMEM, SMEM, ANY],
        out_specs=[VMEM] * n_cluster,
        out_shape=[jax.ShapeDtypeStruct((1, part, width), BF16)] * n_cluster,
        scratch_shapes=[pltpu.SemaphoreType.DMA((n_cluster,))],
        cost_estimate=cost(0, 4 * n_cluster * part * width),
        compiler_params=FIRST,
        name="pick_queries",
    )(pattern, block_slot, query_store)


def join_queries(parts, block_slot, pattern, local_blocks, n_feat, n_rep, *others):
    n_group, n_cluster = len(parts), len(parts[0])
    _, part, width = parts[0][0].shape
    n_list = pattern.shape[1]
    total = n_list * n_group * part
    share = total // (n_feat * n_rep)
    unit = min(share, part)
    half = total // n_rep

    def kernel(pattern_ref, slot_ref, *refs):
        outs, rows_ref = refs[-1 - 2 * n_rep:-1], refs[-1]
        me, group = lax.axis_index("shard"), lax.axis_index("groups")
        for k in range(n_list):
            owner = lax.div(slot_ref[pattern_ref[me, k]], jnp.int32(local_blocks))
            hops = lax.rem(me + (n_cluster - owner), jnp.int32(n_cluster))
            for d in range(n_group):
                origin = lax.rem(group + (n_group - d), jnp.int32(n_group))
                for h in range(n_cluster):
                    @pl.when(hops == h)
                    def _():
                        for u in range(part // unit):
                            first = (k * n_group + origin) * part + u * unit
                            chunk = lax.div(first, jnp.int32(share))
                            goal = lax.rem(chunk, jnp.int32(n_rep)) * n_feat + lax.div(chunk, jnp.int32(n_rep))
                            goal = pl.multiple_of(goal * share + lax.rem(first, jnp.int32(share)), unit)
                            rows_ref[pl.ds(goal, unit), :] = refs[d * n_cluster + h][0, u * unit:(u + 1) * unit, :]
        for r in range(n_rep):
            @pl.when(lax.axis_index("rep") == r)
            def _():
                for j, out in enumerate(outs):
                    at, first = ((r + j // 2) % n_rep) * half, (j % 2) * (width // 2)
                    out[...] = rows_ref[at:at + half, first:first + width // 2].T

    return pl.pallas_call(
        kernel,
        in_specs=[SMEM, SMEM] + [VMEM] * (n_group * n_cluster) + [ANY] * len(others),
        out_specs=[VMEM] * (2 * n_rep),
        out_shape=[jax.ShapeDtypeStruct((width // 2, half), BF16)] * (2 * n_rep),
        scratch_shapes=[pltpu.VMEM((total, width), BF16)],
        cost_estimate=cost(0, 4 * total * width),
        compiler_params=PARAMS,
        name="join_queries",
    )(pattern, block_slot, *[x for line in parts for x in line], *others)


def select(goal_ref, train_ref, base, size):
    tile = 128 if size % 128 == 0 else size
    found = []
    for at in range(0, size, tile):
        index = lax.broadcasted_iota(I32, (tile, LANES), 0) + (base + at)
        pick = [(index == goal_ref[a:a + 1, :]).astype(F32).astype(BF16) for a in range(goal_ref.shape[0])]
        found.append(dot(jnp.concatenate(pick, axis=1), train_ref[...]).astype(BF16))
    return jnp.concatenate(found)


def own_rows(goal, train, bulk, *others):
    def kernel(goal_ref, train_ref, *rest):
        rest[-1][...] = select(goal_ref, train_ref, lax.axis_index("shard") * bulk, bulk)

    return pl.pallas_call(
        kernel,
        in_specs=[VMEM] * 2 + [ANY] * len(others),
        out_specs=VMEM,
        out_shape=jax.ShapeDtypeStruct((bulk, train.shape[1]), BF16),
        cost_estimate=cost(2 * bulk * train.size, 2 * train.size),
        compiler_params=FIRST,
        name="own_rows",
    )(goal, train, *others)


def pack_rows(train, ids, columns, bulk, extra, cuts):
    rows = train.shape[0]
    lines = rows // LANES
    n_shard = ids.shape[0] // lines

    def kernel(ids_ref, train_ref, *rest):
        outs, goal_ref = rest[:-1], rest[-1]
        me = lax.axis_index("shard")
        own = ids_ref[...]
        masks = [(own == c).astype(F32) for c in range(n_shard)]
        stacked = jnp.concatenate(masks, axis=0).astype(BF16)
        lane_from = lax.broadcasted_iota(I32, (LANES, LANES), 0)
        lane_to = lax.broadcasted_iota(I32, (LANES, LANES), 1)
        in_line = dot(stacked, (lane_from < lane_to).astype(F32).astype(BF16))
        line_sum = dot(stacked, jnp.ones((LANES, LANES), BF16)).astype(BF16)
        size = n_shard * lines
        to = lax.broadcasted_iota(I32, (size, size), 0)
        since = lax.broadcasted_iota(I32, (size, size), 1)
        same = (to // lines) == (since // lines)
        ahead = dot((same & (since < to)).astype(F32).astype(BF16), line_sum)
        whole = dot(same.astype(F32).astype(BF16), line_sum)
        rank = in_line + ahead
        goal = jnp.zeros((lines, LANES), F32)
        past = jnp.zeros((lines, LANES), F32)
        for c in range(n_shard):
            part = slice(c * lines, (c + 1) * lines)
            place = rank[part] + c * bulk
            if extra:
                surplus = n_shard * bulk + past + rank[part] - bulk
                place = jnp.where(rank[part] < bulk, place, surplus)
                past = past + jnp.floor((jnp.maximum(whole[part] - bulk, 0.0) + 15.0) * 0.0625) * 16.0
            goal = goal + masks[c] * place
        goal_ref[...] = goal.astype(I32)

        def fill(out, base):
            out[...] = select(goal_ref, train_ref, base, out.shape[0])

        for out, (hops, first, _) in zip(outs, cuts):
            fill(out, lax.rem(me + hops, jnp.int32(n_shard)) * bulk + first)
        for j, out in enumerate(outs[len(cuts):]):
            fill(out, n_shard * bulk + max(j - 1, 0) * extra)

    shapes = [jax.ShapeDtypeStruct((n, columns), BF16) for _, _, n in cuts]
    shapes += [jax.ShapeDtypeStruct((extra, columns), BF16)] * (3 if extra else 0)
    shapes += [jax.ShapeDtypeStruct((lines, LANES), I32)]
    packed = n_shard * bulk + 2 * extra
    return pl.pallas_call(
        kernel,
        grid=(1,),
        in_specs=[
            pl.BlockSpec((lines, LANES), lambda i: (lax.axis_index("shard"), 0)),
            pl.BlockSpec((rows, columns), lambda i: (0, lax.axis_index("rep"))),
        ],
        out_specs=[VMEM] * len(shapes),
        out_shape=shapes,
        cost_estimate=cost(2 * packed * rows * columns, 2 * (rows + packed) * columns),
        compiler_params=FIRST,
        name="pack_rows",
    )(ids, train)


def partial_weights(matrices, queries, block, depth, dtype, *others):
    width, total = matrices[0].shape[1], queries[0].shape[1]
    tile = 512 if depth % 512 == 0 else depth
    steps = depth // tile
    n = len(matrices)

    def kernel(block_ref, *refs):
        value = None
        for j in range(n):
            part = dot(refs[j][...], jnp.concatenate([refs[n + 2 * j][...], refs[n + 2 * j + 1][...]]))
            value = part if value is None else value + part
        refs[-1][...] = value.astype(dtype)

    return pl.pallas_call(
        kernel,
        grid_spec=pltpu.PrefetchScalarGridSpec(
            num_scalar_prefetch=1,
            grid=(steps,),
            in_specs=[pl.BlockSpec((tile, width), lambda i, b: (b[0] * steps + i, 0))] * n
            + [pl.BlockSpec((width // 2, total), lambda i, b: (0, 0))] * (2 * n)
            + [ANY] * len(others),
            out_specs=pl.BlockSpec((tile, total), lambda i, b: (i, 0)),
        ),
        out_shape=jax.ShapeDtypeStruct((depth, total), dtype),
        cost_estimate=cost(2 * n * depth * width * total, 2 * n * depth * width + 4 * depth * total),
        compiler_params=FIRST,
        name="partial_weights",
    )(jnp.reshape(block, (1,)).astype(I32), *matrices, *queries, *others)


def fetch(matrices, block, depth, *others):
    width = matrices[0].shape[1]
    n = len(matrices)
    cuts = 4

    def kernel(block_ref, *refs):
        outs, sem = refs[-1 - n:-1], refs[-1]
        first = pl.multiple_of(block_ref[0] * depth, depth)
        copies = []
        for j in range(n):
            for c in range(cuts):
                size = depth // cuts
                source = refs[j].at[pl.ds(first + c * size, size)]
                copies.append(
                    pltpu.make_async_copy(source, outs[j].at[c * size:(c + 1) * size], sem.at[j * cuts + c])
                )
        for copy in copies:
            copy.start()
        for copy in copies:
            copy.wait()

    return pl.pallas_call(
        kernel,
        in_specs=[SMEM] + [ANY] * (n + len(others)),
        out_specs=[VMEM] * n,
        out_shape=[jax.ShapeDtypeStruct((depth, width), BF16)] * n,
        scratch_shapes=[pltpu.SemaphoreType.DMA((n * cuts,))],
        cost_estimate=cost(0, 2 * n * depth * width),
        compiler_params=MIDDLE,
        name="fetch",
    )(jnp.reshape(block, (1,)).astype(I32), *matrices, *others)


def fetched_weights(matrices, queries, dtype):
    depth = matrices[0].shape[0]
    total = queries[0].shape[1]
    tile = 512 if depth % 512 == 0 else depth
    n = len(matrices)

    def kernel(*refs):
        parts = [jnp.concatenate([refs[n + 2 * j][...], refs[n + 2 * j + 1][...]]) for j in range(n)]
        for at in range(0, depth, tile):
            value = None
            for j in range(n):
                part = dot(refs[j][at:at + tile, :], parts[j])
                value = part if value is None else value + part
            refs[-1][at:at + tile, :] = value.astype(dtype)

    return pl.pallas_call(
        kernel,
        in_specs=[VMEM] * (3 * n),
        out_specs=VMEM,
        out_shape=jax.ShapeDtypeStruct((depth, total), dtype),
        cost_estimate=cost(2 * n * matrices[0].size * total, 2 * n * matrices[0].size),
        compiler_params=PARAMS,
        name="fetched_weights",
    )(*matrices, *queries)


def row_table(ids, lines, bulk, extra, *others):
    n_shard = ids.shape[0] // lines

    def kernel(ids_ref, *rest):
        table_ref, flag_ref = rest[-2:]
        me = lax.axis_index("shard")
        start = jnp.int32(0)
        most = jnp.int32(0)
        for s in range(n_shard):
            line = ids_ref[s * lines:(s + 1) * lines, :]

            def count(c):
                return jnp.sum((line == c).astype(I32))

            mine = count(me)
            before = jnp.int32(0)
            if extra:
                surplus = jnp.int32(0)
                for c in range(n_shard):
                    over = lax.div(jnp.maximum(count(c) - bulk, 0) + 15, jnp.int32(16)) * 16
                    before = before + jnp.where(c < me, over, 0)
                    surplus = surplus + over
                most = jnp.maximum(most, surplus)
            table_ref[s, 0] = start
            table_ref[s, 1] = jnp.minimum(mine, bulk)
            table_ref[s, 2] = lax.div(before, jnp.int32(16))
            table_ref[s, 3] = jnp.maximum(mine - bulk, 0)
            start = start + mine
        flag_ref[...] = jnp.full((8, LANES), (most > extra).astype(I32))

    return pl.pallas_call(
        kernel,
        in_specs=[VMEM] + [ANY] * len(others),
        out_specs=[SMEM, VMEM],
        out_shape=[jax.ShapeDtypeStruct((n_shard, 4), I32), jax.ShapeDtypeStruct((8, LANES), I32)],
        cost_estimate=cost(0, 4 * ids.size),
        compiler_params=FIRST,
        name="row_table",
    )(ids, *others)


def put(acc, x, start, count=None):
    tiles, _, width = x.shape
    first, within = lax.div(start, jnp.int32(8)), lax.rem(start, jnp.int32(8))
    turned = pltpu.roll(x, within, 1)
    row = lax.broadcasted_iota(I32, (1, 8, width), 1)
    keep = row < within
    pieces = jnp.where(keep, jnp.concatenate([turned[:1], turned]), jnp.concatenate([turned, turned[-1:]]))
    if count is None:
        pieces = jnp.concatenate([jnp.where(keep, acc[pl.ds(first, 1)], turned[:1]), pieces[1:]])
    else:
        at = lax.broadcasted_iota(I32, (tiles + 1, 8, width), 0) * 8 + lax.broadcasted_iota(
            I32, (tiles + 1, 8, width), 1
        )
        pieces = jnp.where(
            (at >= within) & (at < within + count), pieces, acc[pl.ds(first, tiles + 1)]
        )
    acc[pl.ds(first, tiles + 1)] = pieces


def score(high_ref, low_ref, parts, rep):
    total = None
    for d, x in enumerate(parts):
        depth = x.shape[1]
        block = pl.ds(pl.multiple_of(lax.rem(rep + (len(parts) - d), jnp.int32(len(parts))) * depth, depth), depth)
        value = dot(x, high_ref[block, :]) + dot(x, low_ref[block, :])
        total = value if total is None else total + value
    return total.reshape(total.shape[0] // 8, 8, total.shape[1])


def for_feats(value, outs):
    n = len(outs)
    share = outs[0].shape[1]
    for f in range(n):
        @pl.when(lax.axis_index("feat") == f)
        def _():
            for d, out in enumerate(outs):
                at = ((f + d) % n) * share
                out[...] = value(slice(at, at + share)).astype(out.dtype)


def feat_shapes(rows, width, n_feat):
    share = (rows, width // n_feat)
    return [jax.ShapeDtypeStruct(share, F32)] + [jax.ShapeDtypeStruct(share, BF16)] * (n_feat - 1)


def early_scores(own, others, mine, pieces, cuts, firsts, seconds, table, rows, n_feat, n_rep, n_shard, bulk, extra):
    depth, width = own.shape
    columns = depth // n_rep
    n_other, n_piece = len(others), len(pieces)
    n_first = len(firsts) * n_rep
    last_hops = n_shard - 1

    def kernel(table_ref, *refs):
        own_ref, refs = refs[0], refs[1:]
        other_refs, refs = refs[:n_other], refs[n_other:]
        mine_ref, refs = refs[0], refs[1:]
        piece_refs = [refs[j * n_rep:(j + 1) * n_rep] for j in range(n_piece)]
        refs = refs[n_piece * n_rep:]
        first_refs, second_refs, refs = refs[:n_first], refs[n_first:2 * n_first], refs[2 * n_first:]
        high_ref, low_ref, outs, (scored, held, acc, sem) = refs[0], refs[1], refs[2:-4], refs[-4:]
        me, rep = lax.axis_index("shard"), lax.axis_index("rep")
        weight = own_ref[...]
        for ref in other_refs:
            weight = weight + ref[...].astype(F32)
        high = weight.astype(BF16)
        high_ref[...] = high
        low_ref[...] = (weight - high.astype(F32)).astype(BF16)

        scored[me] = score(high_ref, low_ref, [mine_ref[...]], jnp.int32(0))
        for parts, (hops, first, size) in zip(piece_refs, cuts):
            source = lax.rem(me + (n_shard - hops), jnp.int32(n_shard))
            scored[source, first // 8:(first + size) // 8] = score(high_ref, low_ref, [p[...] for p in parts], rep)
        last = lax.rem(me + (n_shard - last_hops), jnp.int32(n_shard))
        for s in range(n_shard):
            start = table_ref[s, 0]

            @pl.when(last != s)
            def _():
                put(acc, scored[s], start)

            if extra:
                @pl.when(table_ref[s, 3] > 0)
                def _():
                    apart = jnp.bitwise_xor(me, s)
                    rows_in = pl.ds(pl.multiple_of(lax.div(apart, jnp.int32(2)) * extra, extra), extra)
                    for odd in range(2):
                        @pl.when(jnp.bitwise_and(apart, 1) == odd)
                        def _():
                            copies = []
                            for j, refs in enumerate([first_refs, second_refs]):
                                for d in range(n_rep):
                                    goal = held.at[d, j * extra:(j + 1) * extra]
                                    which = refs[odd * n_rep + d].at[rows_in]
                                    copies.append(pltpu.make_async_copy(which, goal, sem.at[j * n_rep + d]))
                            for copy in copies:
                                copy.start()
                            for copy in copies:
                                copy.wait()
                    some = pl.ds(pl.multiple_of(table_ref[s, 2] * 16, 16), extra)
                    x = [held[d, some, :] for d in range(n_rep)]
                    put(acc, score(high_ref, low_ref, x, rep), start + table_ref[s, 1])
        for_feats(lambda at: acc[:rows // 8, :, at].reshape(rows, width // n_feat), outs)

    count = n_shard * bulk
    surplus = [x for parts in [*firsts, *seconds] for x in parts]
    return pl.pallas_call(
        kernel,
        in_specs=[SMEM] + [VMEM] * (2 + n_other + n_rep * n_piece) + [ANY] * len(surplus),
        out_specs=[VMEM] * (2 + n_feat),
        out_shape=[jax.ShapeDtypeStruct((depth, width), BF16)] * 2 + feat_shapes(rows, width, n_feat),
        scratch_shapes=[
            pltpu.VMEM((n_shard, bulk // 8, 8, width), F32),
            pltpu.VMEM((n_rep, 3 * extra + 16, columns), BF16),
            pltpu.VMEM(((rows + bulk + extra) // 8 + 2, 8, width), F32),
            pltpu.SemaphoreType.DMA((2 * n_rep,)),
        ],
        cost_estimate=cost(4 * count * depth * width, 10 * depth * width + count * (2 * depth + 4 * width)),
        compiler_params=PARAMS,
        name="early_scores",
    )(table, own, *others, mine, *[p for parts in pieces for p in parts], *surplus)


def late_scores(pieces, high, low, n_feat):
    n, n_rep = len(pieces), len(pieces[0])
    size = pieces[0][0].shape[0]
    rows = n * size
    width = high.shape[1]

    def kernel(high_ref, low_ref, *refs):
        part_refs, outs, acc = refs[:n * n_rep], refs[n * n_rep:-1], refs[-1]
        parts = [jnp.concatenate([part_refs[j * n_rep + d][...] for j in range(n)]) for d in range(n_rep)]
        y = score(high_ref, low_ref, parts, lax.axis_index("rep"))
        acc[...] = y.reshape(rows, width)
        for_feats(lambda at: acc[:, at], outs)

    return pl.pallas_call(
        kernel,
        in_specs=[VMEM] * (2 + n * n_rep),
        out_specs=[VMEM] * n_feat,
        out_shape=feat_shapes(rows, width, n_feat),
        scratch_shapes=[pltpu.VMEM((rows, width), F32)],
        cost_estimate=cost(4 * rows * high.size, 8 * rows * width),
        compiler_params=PARAMS,
        name="late_scores",
    )(high, low, *[p for parts in pieces for p in parts])


def merge(table, early, late, n_shard):
    rows, width = early[0].shape
    last_rows = late[0].shape[0]
    last_hops = n_shard - 1

    def kernel(table_ref, *refs):
        early_refs, late_refs = refs[:len(early)], refs[len(early):-2]
        out_ref, acc = refs[-2:]
        source = lax.rem(lax.axis_index("shard") + (n_shard - last_hops), jnp.int32(n_shard))

        def total(parts):
            value = parts[0][...]
            for ref in parts[1:]:
                value = value + ref[...].astype(F32)
            return value.reshape(value.shape[0] // 8, 8, width)

        acc[:rows // 8] = total(early_refs)
        put(acc, total(late_refs), table_ref[source, 0], table_ref[source, 1])
        out_ref[...] = acc[:rows // 8].reshape(rows, width).T

    return pl.pallas_call(
        kernel,
        in_specs=[SMEM] + [VMEM] * (len(early) + len(late)),
        out_specs=VMEM,
        out_shape=jax.ShapeDtypeStruct((width, rows), F32),
        scratch_shapes=[pltpu.VMEM(((rows + last_rows) // 8 + 2, 8, width), F32)],
        cost_estimate=cost(0, 8 * rows * width),
        compiler_params=PARAMS,
        name="merge",
    )(table, *early, *late)


def body(train, cluster_ids, precond, query_store, block_slot, pattern):
    n_group, n_shard = lax.axis_size("groups"), lax.axis_size("shard")
    n_feat, n_rep = lax.axis_size("feat"), lax.axis_size("rep")
    feat, rep = lax.axis_index("feat"), lax.axis_index("rep")
    rows = train.shape[0]
    lines = rows // LANES
    base = rows // n_shard
    columns = train.shape[1] // n_rep
    extra = base // 2 if n_shard == 4 else 0
    bulk = base if extra else base + base // 2
    ids = cluster_ids.reshape(-1, LANES)

    last_hops = n_shard - 1

    def with_rep(x):
        return [x] + [shift(x, "rep", n_rep, d) for d in range(1, n_rep)]

    matrices = with_rep(precond[0])

    picked = pick_queries(query_store, block_slot, pattern, n_group)
    pieces = [picked[0]] + [shift(picked[d], "shard", n_shard, d) for d in range(1, n_shard)]

    middle = [(d, 0, bulk) for d in range(1, last_hops)]
    part = 64 if bulk % 64 == 0 else bulk
    final = [(last_hops, at, part) for at in range(0, bulk, part)]
    *packed, goal = pack_rows(train, ids, columns, bulk, extra, middle + final)
    firsts, seconds = [], []
    parts = [pieces] + [[shift(x, "groups", n_group, d) for x in pieces] for d in range(1, n_group)]
    here = [shift(after(packed[0], *pieces[1:]), "shard", n_shard, 1)]
    urgent = [here[0]]
    if extra:
        far = swap(after(packed[-2], *pieces[1:]), "shard", n_shard, 2)
        far_all = with_rep(far)
        urgent += far_all[1:]
    depth = n_rep * columns
    targets = [(feat + d) % n_feat for d in range(1, n_feat)]
    near_chip = fetch(matrices, targets[0], depth, *pieces[1:])

    chosen = join_queries(parts, block_slot, pattern, query_store.shape[0], n_feat, n_rep, *near_chip)
    queries = [*chosen[:2]] + [shift(chosen[j], "rep", n_rep, j // 2) for j in range(2, 2 * n_rep)]

    sends = [fetched_weights(near_chip, queries, BF16)]
    sends += [partial_weights(matrices, queries, f, depth, BF16) for f in targets[1:]]
    others = [shift(x, "feat", n_feat, d + 1) for d, x in enumerate(sends)]
    own = partial_weights(matrices, queries, feat, depth, F32, *sends)

    for (hops, _, _), x in zip(middle[1:], packed[1:]):
        here.append(shift(after(x, *urgent, *sends), "shard", n_shard, hops))
        urgent = [here[-1]]
    last = [
        shift(after(packed[len(middle) + j], here[-1], own), "shard", n_shard, last_hops) for j in range(len(final))
    ]

    mine = own_rows(goal, train, bulk, own)
    table, flag = row_table(ids, lines, bulk, extra, own)
    marks = [own, mine]
    if extra:
        for d in range(1, n_group):
            flag = jnp.maximum(flag, shift(flag, "groups", n_group, d))

        def second_round(x):
            pair = jnp.concatenate([x, swap(x, "shard", n_shard, 2)])
            return [with_rep(pair), with_rep(swap(pair, "shard", n_shard, 1))]

        def no_round(x):
            return [[jnp.zeros((2 * extra, columns), BF16)] * n_rep] * 2

        seconds = lax.cond(flag[0, 0] > 0, second_round, no_round, packed[-1])
        near = swap(stack([packed[-3], far], *sends), "shard", n_shard, 1)
        pairs = [stack([x, y], own) for x, y in zip(with_rep(packed[-3]), far_all)]
        firsts = [pairs, with_rep(after(near, own))]
        marks += [seconds[0][0], near, *pairs]

    mark = shift(after(jnp.zeros((8, LANES), I32), *marks), "rep", n_rep, 1)
    ready = [with_rep(after(x, mark)) for x in here]
    high, low, *early = early_scores(
        own, others, mine, ready, middle, firsts, seconds, table, rows, n_feat, n_rep, n_shard, bulk, extra
    )

    def over_feat(shares):
        return [shares[0]] + [shift(shares[d], "feat", n_feat, d) for d in range(1, n_feat)]

    late = late_scores([with_rep(after(x, *early[1:])) for x in last], high, low, n_feat)
    return merge(table, over_feat(early), over_feat(late), n_shard)[None]


def solution(mesh):
    return jax.shard_map(
        body,
        mesh=mesh,
        in_specs=(
            P(("groups", "shard"), "feat"),
            P("groups"),
            P(("groups", "shard"), None, ("feat", "rep")),
            P("shard", None, ("feat", "rep")),
            P(),
            P(),
        ),
        out_specs=P(("groups", "shard"), ("feat", "rep"), None),
        check_vma=False,
    )
```

```python
import functools

import jax
import jax.numpy as jnp
from jax import lax
from jax.experimental import pallas as pl
from jax.experimental.pallas import tpu as pltpu
from jax.sharding import PartitionSpec as P

F32, BF16, I32 = jnp.float32, jnp.bfloat16, jnp.int32
VMEM = pl.BlockSpec(memory_space=pltpu.VMEM)
ANY = pl.BlockSpec(memory_space=pl.ANY)
SMEM = pl.BlockSpec(memory_space=pltpu.SMEM)
PARAMS = pltpu.CompilerParams(vmem_limit_bytes=24 * 2**20)
MIDDLE = pltpu.CompilerParams(vmem_limit_bytes=48 * 2**20)
FIRST = pltpu.CompilerParams(vmem_limit_bytes=60 * 2**20)
LANES = 128
CUTS = 8


def shift(x, axis, size, by):
    return lax.ppermute(x, axis, [(i, (i + by) % size) for i in range(size)])


def swap(x, axis, size, bit):
    return lax.ppermute(x, axis, [(i, i ^ bit) for i in range(size)])


def dot(a, b):
    return jnp.dot(a, b, preferred_element_type=F32)


def cost(flops, nbytes):
    return pl.CostEstimate(flops=1, bytes_accessed=1, transcendentals=0)


def after(x, *others):
    def kernel(*refs):
        pass

    return pl.pallas_call(
        kernel,
        in_specs=[ANY] * (1 + len(others)),
        out_specs=ANY,
        out_shape=jax.ShapeDtypeStruct(x.shape, x.dtype),
        input_output_aliases={0: 0},
        cost_estimate=cost(0, 0),
        compiler_params=PARAMS,
        name="after",
    )(x, *others)


def unwritten(shape, n):
    def kernel(*refs):
        pass

    return pl.pallas_call(
        kernel,
        out_specs=[ANY] * n,
        out_shape=[jax.ShapeDtypeStruct(shape, BF16)] * n,
        cost_estimate=cost(0, 0),
        compiler_params=PARAMS,
        name="unwritten",
    )()


def stack(parts, *others):
    size, width = parts[0].shape
    n = len(parts)

    def kernel(*refs):
        for j in range(n):
            refs[-1][j * size:(j + 1) * size, :] = refs[j][...]

    return pl.pallas_call(
        kernel,
        in_specs=[VMEM] * n + [ANY] * len(others),
        out_specs=VMEM,
        out_shape=jax.ShapeDtypeStruct((n * size, width), parts[0].dtype),
        cost_estimate=cost(0, 0),
        compiler_params=PARAMS,
        name="stack",
    )(*parts, *others)


def pick_queries(query_store, block_slot, pattern, n_group):
    local_blocks, block_rows, width = query_store.shape
    n_cluster, n_list = pattern.shape
    part = block_rows // n_group

    def kernel(pattern_ref, slot_ref, in_ref, *rest):
        outs, sem = rest[:-1], rest[-1]
        me, group = lax.axis_index("shard"), lax.axis_index("groups")
        copies = []
        for t, out in enumerate(outs):
            target = lax.rem(me + t, jnp.int32(n_cluster))
            found = jnp.int32(0)
            for k in range(n_list):
                slot = slot_ref[pattern_ref[target, k]]
                hit = (lax.div(slot, jnp.int32(local_blocks)) == me).astype(I32)
                found = found + hit * lax.rem(slot, jnp.int32(local_blocks))
            rows = pl.ds(pl.multiple_of(group * part, part), part)
            copies.append(pltpu.make_async_copy(in_ref.at[found, rows], out.at[0], sem.at[t]))
            copies[-1].start()
        for copy in copies:
            copy.wait()

    return pl.pallas_call(
        kernel,
        in_specs=[SMEM, SMEM, ANY],
        out_specs=[VMEM] * n_cluster,
        out_shape=[jax.ShapeDtypeStruct((1, part, width), BF16)] * n_cluster,
        scratch_shapes=[pltpu.SemaphoreType.DMA((n_cluster,))],
        cost_estimate=cost(0, 4 * n_cluster * part * width),
        compiler_params=FIRST,
        name="pick_queries",
    )(pattern, block_slot, query_store)


def join_queries(parts, block_slot, pattern, local_blocks, n_feat, n_rep, *others):
    n_group, n_cluster = len(parts), len(parts[0])
    _, part, width = parts[0][0].shape
    n_list = pattern.shape[1]
    total = n_list * n_group * part
    share = total // (n_feat * n_rep)
    unit = min(share, part)
    half = total // n_rep

    def kernel(pattern_ref, slot_ref, *refs):
        outs, rows_ref = refs[-1 - CUTS * n_rep:-1], refs[-1]
        me, group = lax.axis_index("shard"), lax.axis_index("groups")
        for k in range(n_list):
            owner = lax.div(slot_ref[pattern_ref[me, k]], jnp.int32(local_blocks))
            hops = lax.rem(me + (n_cluster - owner), jnp.int32(n_cluster))
            for d in range(n_group):
                origin = lax.rem(group + (n_group - d), jnp.int32(n_group))
                for h in range(n_cluster):
                    @pl.when(hops == h)
                    def _():
                        for u in range(part // unit):
                            first = (k * n_group + origin) * part + u * unit
                            chunk = lax.div(first, jnp.int32(share))
                            goal = lax.rem(chunk, jnp.int32(n_rep)) * n_feat + lax.div(chunk, jnp.int32(n_rep))
                            goal = pl.multiple_of(goal * share + lax.rem(first, jnp.int32(share)), unit)
                            rows_ref[pl.ds(goal, unit), :] = refs[d * n_cluster + h][0, u * unit:(u + 1) * unit, :]
        for r in range(n_rep):
            @pl.when(lax.axis_index("rep") == r)
            def _():
                for j, out in enumerate(outs):
                    at, first = ((r + j // CUTS) % n_rep) * half, (j % CUTS) * (width // CUTS)
                    out[...] = rows_ref[at:at + half, first:first + width // CUTS].T

    return pl.pallas_call(
        kernel,
        in_specs=[SMEM, SMEM] + [VMEM] * (n_group * n_cluster) + [ANY] * len(others),
        out_specs=[VMEM] * (CUTS * n_rep),
        out_shape=[jax.ShapeDtypeStruct((width // CUTS, half), BF16)] * (CUTS * n_rep),
        scratch_shapes=[pltpu.VMEM((total, width), BF16)],
        cost_estimate=cost(0, 4 * total * width),
        compiler_params=PARAMS,
        name="join_queries",
    )(pattern, block_slot, *[x for line in parts for x in line], *others)


def select(goal_ref, train_ref, base, size):
    tile = 128 if size % 128 == 0 else size
    found = []
    for at in range(0, size, tile):
        index = lax.broadcasted_iota(I32, (tile, LANES), 0) + (base + at)
        pick = [(index == goal_ref[a:a + 1, :]).astype(F32).astype(BF16) for a in range(goal_ref.shape[0])]
        found.append(dot(jnp.concatenate(pick, axis=1), train_ref[...]).astype(BF16))
    return jnp.concatenate(found)


def own_rows(goal, train, bulk, *others):
    def kernel(goal_ref, train_ref, *rest):
        rest[-1][...] = select(goal_ref, train_ref, lax.axis_index("shard") * bulk, bulk)

    return pl.pallas_call(
        kernel,
        in_specs=[VMEM] * 2 + [ANY] * len(others),
        out_specs=VMEM,
        out_shape=jax.ShapeDtypeStruct((bulk, train.shape[1]), BF16),
        cost_estimate=cost(2 * bulk * train.size, 2 * train.size),
        compiler_params=FIRST,
        name="own_rows",
    )(goal, train, *others)


def pack_rows(train, ids, columns, bulk, extra, cuts):
    rows = train.shape[0]
    lines = rows // LANES
    n_shard = ids.shape[0] // lines

    def kernel(ids_ref, train_ref, *rest):
        outs, goal_ref = rest[:-1], rest[-1]
        me = lax.axis_index("shard")
        own = ids_ref[...]
        masks = [(own == c).astype(F32) for c in range(n_shard)]
        stacked = jnp.concatenate(masks, axis=0).astype(BF16)
        lane_from = lax.broadcasted_iota(I32, (LANES, LANES), 0)
        lane_to = lax.broadcasted_iota(I32, (LANES, LANES), 1)
        in_line = dot(stacked, (lane_from < lane_to).astype(F32).astype(BF16))
        line_sum = dot(stacked, jnp.ones((LANES, LANES), BF16)).astype(BF16)
        size = n_shard * lines
        to = lax.broadcasted_iota(I32, (size, size), 0)
        since = lax.broadcasted_iota(I32, (size, size), 1)
        same = (to // lines) == (since // lines)
        ahead = dot((same & (since < to)).astype(F32).astype(BF16), line_sum)
        whole = dot(same.astype(F32).astype(BF16), line_sum)
        rank = in_line + ahead
        goal = jnp.zeros((lines, LANES), F32)
        past = jnp.zeros((lines, LANES), F32)
        for c in range(n_shard):
            part = slice(c * lines, (c + 1) * lines)
            place = rank[part] + c * bulk
            if extra:
                surplus = n_shard * bulk + past + rank[part] - bulk
                place = jnp.where(rank[part] < bulk, place, surplus)
                past = past + jnp.floor((jnp.maximum(whole[part] - bulk, 0.0) + 15.0) * 0.0625) * 16.0
            goal = goal + masks[c] * place
        goal_ref[...] = goal.astype(I32)

        def fill(out, base):
            out[...] = select(goal_ref, train_ref, base, out.shape[0])

        for out, (hops, first, _) in zip(outs, cuts):
            fill(out, lax.rem(me + hops, jnp.int32(n_shard)) * bulk + first)
        for j, out in enumerate(outs[len(cuts):]):
            fill(out, n_shard * bulk + max(j - 1, 0) * extra)

    shapes = [jax.ShapeDtypeStruct((n, columns), BF16) for _, _, n in cuts]
    shapes += [jax.ShapeDtypeStruct((extra, columns), BF16)] * (3 if extra else 0)
    shapes += [jax.ShapeDtypeStruct((lines, LANES), I32)]
    packed = n_shard * bulk + 2 * extra
    return pl.pallas_call(
        kernel,
        grid=(1,),
        in_specs=[
            pl.BlockSpec((lines, LANES), lambda i: (lax.axis_index("shard"), 0)),
            pl.BlockSpec((rows, columns), lambda i: (0, lax.axis_index("rep"))),
        ],
        out_specs=[VMEM] * len(shapes),
        out_shape=shapes,
        cost_estimate=cost(2 * packed * rows * columns, 2 * (rows + packed) * columns),
        compiler_params=FIRST,
        name="pack_rows",
    )(ids, train)


def partial_weights(matrices, queries, block, depth, dtype, *others):
    width, total = matrices[0].shape[1], queries[0].shape[1]
    tile = 512 if depth % 512 == 0 else depth
    steps = depth // tile
    n = len(matrices)

    def kernel(block_ref, *refs):
        value = None
        for j in range(n):
            part = dot(refs[j][...], jnp.concatenate([r[...] for r in refs[n + CUTS * j:n + CUTS * (j + 1)]]))
            value = part if value is None else value + part
        refs[-1][...] = value.astype(dtype)

    return pl.pallas_call(
        kernel,
        grid_spec=pltpu.PrefetchScalarGridSpec(
            num_scalar_prefetch=1,
            grid=(steps,),
            in_specs=[pl.BlockSpec((tile, width), lambda i, b: (b[0] * steps + i, 0))] * n
            + [pl.BlockSpec((width // CUTS, total), lambda i, b: (0, 0))] * (CUTS * n)
            + [ANY] * len(others),
            out_specs=pl.BlockSpec((tile, total), lambda i, b: (i, 0)),
        ),
        out_shape=jax.ShapeDtypeStruct((depth, total), dtype),
        cost_estimate=cost(2 * n * depth * width * total, 2 * n * depth * width + 4 * depth * total),
        compiler_params=FIRST,
        name="partial_weights",
    )(jnp.reshape(block, (1,)).astype(I32), *matrices, *queries, *others)


def fetch(matrices, block, depth, *others):
    width = matrices[0].shape[1]
    n = len(matrices)
    cuts = 4

    def kernel(block_ref, *refs):
        outs, sem = refs[-1 - n:-1], refs[-1]
        first = pl.multiple_of(block_ref[0] * depth, depth)
        copies = []
        for j in range(n):
            for c in range(cuts):
                size = depth // cuts
                source = refs[j].at[pl.ds(first + c * size, size)]
                copies.append(
                    pltpu.make_async_copy(source, outs[j].at[c * size:(c + 1) * size], sem.at[j * cuts + c])
                )
        for copy in copies:
            copy.start()
        for copy in copies:
            copy.wait()

    return pl.pallas_call(
        kernel,
        in_specs=[SMEM] + [ANY] * (n + len(others)),
        out_specs=[VMEM] * n,
        out_shape=[jax.ShapeDtypeStruct((depth, width), BF16)] * n,
        scratch_shapes=[pltpu.SemaphoreType.DMA((n * cuts,))],
        cost_estimate=cost(0, 2 * n * depth * width),
        compiler_params=MIDDLE,
        name="fetch",
    )(jnp.reshape(block, (1,)).astype(I32), *matrices, *others)


def fetched_weights(matrices, queries, dtype):
    depth = matrices[0].shape[0]
    total = queries[0].shape[1]
    tile = 512 if depth % 512 == 0 else depth
    n = len(matrices)

    def kernel(*refs):
        parts = [jnp.concatenate([r[...] for r in refs[n + CUTS * j:n + CUTS * (j + 1)]]) for j in range(n)]
        for at in range(0, depth, tile):
            value = None
            for j in range(n):
                part = dot(refs[j][at:at + tile, :], parts[j])
                value = part if value is None else value + part
            refs[-1][at:at + tile, :] = value.astype(dtype)

    return pl.pallas_call(
        kernel,
        in_specs=[VMEM] * ((1 + CUTS) * n),
        out_specs=VMEM,
        out_shape=jax.ShapeDtypeStruct((depth, total), dtype),
        cost_estimate=cost(2 * n * matrices[0].size * total, 2 * n * matrices[0].size),
        compiler_params=PARAMS,
        name="fetched_weights",
    )(*matrices, *queries)


def row_table(ids, lines, bulk, extra, *others):
    n_shard = ids.shape[0] // lines

    def kernel(ids_ref, *rest):
        table_ref, flag_ref = rest[-2:]
        me = lax.axis_index("shard")
        start = jnp.int32(0)
        most = jnp.int32(0)
        for s in range(n_shard):
            line = ids_ref[s * lines:(s + 1) * lines, :]

            def count(c):
                return jnp.sum((line == c).astype(I32))

            mine = count(me)
            before = jnp.int32(0)
            if extra:
                surplus = jnp.int32(0)
                for c in range(n_shard):
                    over = lax.div(jnp.maximum(count(c) - bulk, 0) + 15, jnp.int32(16)) * 16
                    before = before + jnp.where(c < me, over, 0)
                    surplus = surplus + over
                most = jnp.maximum(most, surplus)
            table_ref[s, 0] = start
            table_ref[s, 1] = jnp.minimum(mine, bulk)
            table_ref[s, 2] = lax.div(before, jnp.int32(16))
            table_ref[s, 3] = jnp.maximum(mine - bulk, 0)
            start = start + mine
        flag_ref[...] = jnp.full((8, LANES), (most > extra).astype(I32))

    return pl.pallas_call(
        kernel,
        in_specs=[VMEM] + [ANY] * len(others),
        out_specs=[SMEM, VMEM],
        out_shape=[jax.ShapeDtypeStruct((n_shard, 4), I32), jax.ShapeDtypeStruct((8, LANES), I32)],
        cost_estimate=cost(0, 4 * ids.size),
        compiler_params=FIRST,
        name="row_table",
    )(ids, *others)


def put(acc, x, start, count=None):
    tiles, _, width = x.shape
    first, within = lax.div(start, jnp.int32(8)), lax.rem(start, jnp.int32(8))
    turned = pltpu.roll(x, within, 1)
    row = lax.broadcasted_iota(I32, (1, 8, width), 1)
    keep = row < within
    pieces = jnp.where(keep, jnp.concatenate([turned[:1], turned]), jnp.concatenate([turned, turned[-1:]]))
    if count is None:
        pieces = jnp.concatenate([jnp.where(keep, acc[pl.ds(first, 1)], turned[:1]), pieces[1:]])
    else:
        at = lax.broadcasted_iota(I32, (tiles + 1, 8, width), 0) * 8 + lax.broadcasted_iota(
            I32, (tiles + 1, 8, width), 1
        )
        pieces = jnp.where(
            (at >= within) & (at < within + count), pieces, acc[pl.ds(first, tiles + 1)]
        )
    acc[pl.ds(first, tiles + 1)] = pieces


def score(high_ref, low_ref, parts, rep):
    total = None
    for d, x in enumerate(parts):
        depth = x.shape[1]
        block = pl.ds(pl.multiple_of(lax.rem(rep + (len(parts) - d), jnp.int32(len(parts))) * depth, depth), depth)
        value = dot(x, high_ref[block, :]) + dot(x, low_ref[block, :])
        total = value if total is None else total + value
    return total.reshape(total.shape[0] // 8, 8, total.shape[1])


def for_feats(value, outs):
    n = len(outs)
    share = outs[0].shape[1]
    for f in range(n):
        @pl.when(lax.axis_index("feat") == f)
        def _():
            for d, out in enumerate(outs):
                at = ((f + d) % n) * share
                out[...] = value(slice(at, at + share)).astype(out.dtype)


def feat_shapes(rows, width, n_feat):
    share = (rows, width // n_feat)
    return [jax.ShapeDtypeStruct(share, F32)] + [jax.ShapeDtypeStruct(share, BF16)] * (n_feat - 1)


def early_scores(own, others, mine, pieces, cuts, firsts, seconds, table, rows, n_feat, n_rep, n_shard, bulk, extra):
    depth, width = own.shape
    columns = depth // n_rep
    n_other, n_piece = len(others), len(pieces)
    n_first = len(firsts) * n_rep
    last_hops = n_shard - 1

    def kernel(table_ref, *refs):
        own_ref, refs = refs[0], refs[1:]
        other_refs, refs = refs[:n_other], refs[n_other:]
        mine_ref, refs = refs[0], refs[1:]
        piece_refs = [refs[j * n_rep:(j + 1) * n_rep] for j in range(n_piece)]
        refs = refs[n_piece * n_rep:]
        first_refs, second_refs, refs = refs[:n_first], refs[n_first:2 * n_first], refs[2 * n_first:]
        high_ref, low_ref, outs, (scored, held, acc, sem) = refs[0], refs[1], refs[2:-4], refs[-4:]
        me, rep = lax.axis_index("shard"), lax.axis_index("rep")
        weight = own_ref[...]
        for ref in other_refs:
            weight = weight + ref[...].astype(F32)
        high = weight.astype(BF16)
        high_ref[...] = high
        low_ref[...] = (weight - high.astype(F32)).astype(BF16)

        scored[me] = score(high_ref, low_ref, [mine_ref[...]], jnp.int32(0))
        for parts, (hops, first, size) in zip(piece_refs, cuts):
            source = lax.rem(me + (n_shard - hops), jnp.int32(n_shard))
            scored[source, first // 8:(first + size) // 8] = score(high_ref, low_ref, [p[...] for p in parts], rep)
        last = lax.rem(me + (n_shard - last_hops), jnp.int32(n_shard))
        for s in range(n_shard):
            start = table_ref[s, 0]

            @pl.when(last != s)
            def _():
                put(acc, scored[s], start)

            if extra:
                @pl.when(table_ref[s, 3] > 0)
                def _():
                    apart = jnp.bitwise_xor(me, s)
                    rows_in = pl.ds(pl.multiple_of(lax.div(apart, jnp.int32(2)) * extra, extra), extra)
                    for odd in range(2):
                        @pl.when(jnp.bitwise_and(apart, 1) == odd)
                        def _():
                            copies = []
                            for j, refs in enumerate([first_refs, second_refs]):
                                for d in range(n_rep):
                                    goal = held.at[d, j * extra:(j + 1) * extra]
                                    which = refs[odd * n_rep + d].at[rows_in]
                                    copies.append(pltpu.make_async_copy(which, goal, sem.at[j * n_rep + d]))
                            for copy in copies:
                                copy.start()
                            for copy in copies:
                                copy.wait()
                    some = pl.ds(pl.multiple_of(table_ref[s, 2] * 16, 16), extra)
                    x = [held[d, some, :] for d in range(n_rep)]
                    put(acc, score(high_ref, low_ref, x, rep), start + table_ref[s, 1])
        for_feats(lambda at: acc[:rows // 8, :, at].reshape(rows, width // n_feat), outs)

    count = n_shard * bulk
    surplus = [x for parts in [*firsts, *seconds] for x in parts]
    return pl.pallas_call(
        kernel,
        in_specs=[SMEM] + [VMEM] * (2 + n_other + n_rep * n_piece) + [ANY] * len(surplus),
        out_specs=[VMEM] * (2 + n_feat),
        out_shape=[jax.ShapeDtypeStruct((depth, width), BF16)] * 2 + feat_shapes(rows, width, n_feat),
        scratch_shapes=[
            pltpu.VMEM((n_shard, bulk // 8, 8, width), F32),
            pltpu.VMEM((n_rep, 3 * extra + 16, columns), BF16),
            pltpu.VMEM(((rows + bulk + extra) // 8 + 2, 8, width), F32),
            pltpu.SemaphoreType.DMA((2 * n_rep,)),
        ],
        cost_estimate=cost(4 * count * depth * width, 10 * depth * width + count * (2 * depth + 4 * width)),
        compiler_params=PARAMS,
        name="early_scores",
    )(table, own, *others, mine, *[p for parts in pieces for p in parts], *surplus)


def late_scores(pieces, high, low, n_feat):
    n, n_rep = len(pieces), len(pieces[0])
    size = pieces[0][0].shape[0]
    rows = n * size
    width = high.shape[1]

    def kernel(high_ref, low_ref, *refs):
        part_refs, outs, acc = refs[:n * n_rep], refs[n * n_rep:-1], refs[-1]
        parts = [jnp.concatenate([part_refs[j * n_rep + d][...] for j in range(n)]) for d in range(n_rep)]
        y = score(high_ref, low_ref, parts, lax.axis_index("rep"))
        acc[...] = y.reshape(rows, width)
        for_feats(lambda at: acc[:, at], outs)

    return pl.pallas_call(
        kernel,
        in_specs=[VMEM] * (2 + n * n_rep),
        out_specs=[VMEM] * n_feat,
        out_shape=feat_shapes(rows, width, n_feat),
        scratch_shapes=[pltpu.VMEM((rows, width), F32)],
        cost_estimate=cost(4 * rows * high.size, 8 * rows * width),
        compiler_params=PARAMS,
        name="late_scores",
    )(high, low, *[p for parts in pieces for p in parts])


def merge(table, early, late, n_shard):
    rows, width = early[0].shape
    last_rows = late[0].shape[0]
    last_hops = n_shard - 1

    def kernel(table_ref, *refs):
        early_refs, late_refs = refs[:len(early)], refs[len(early):-2]
        out_ref, acc = refs[-2:]
        source = lax.rem(lax.axis_index("shard") + (n_shard - last_hops), jnp.int32(n_shard))

        def total(parts):
            value = parts[0][...]
            for ref in parts[1:]:
                value = value + ref[...].astype(F32)
            return value.reshape(value.shape[0] // 8, 8, width)

        acc[:rows // 8] = total(early_refs)
        put(acc, total(late_refs), table_ref[source, 0], table_ref[source, 1])
        out_ref[...] = acc[:rows // 8].reshape(rows, width).T

    return pl.pallas_call(
        kernel,
        in_specs=[SMEM] + [VMEM] * (len(early) + len(late)),
        out_specs=VMEM,
        out_shape=jax.ShapeDtypeStruct((width, rows), F32),
        scratch_shapes=[pltpu.VMEM(((rows + last_rows) // 8 + 2, 8, width), F32)],
        cost_estimate=cost(0, 8 * rows * width),
        compiler_params=PARAMS,
        name="merge",
    )(table, *early, *late)


def body(train, cluster_ids, precond, query_store, block_slot, pattern):
    n_group, n_shard = lax.axis_size("groups"), lax.axis_size("shard")
    n_feat, n_rep = lax.axis_size("feat"), lax.axis_size("rep")
    feat, rep = lax.axis_index("feat"), lax.axis_index("rep")
    rows = train.shape[0]
    lines = rows // LANES
    base = rows // n_shard
    columns = train.shape[1] // n_rep
    extra = base // 2 if n_shard == 4 else 0
    bulk = base if extra else base + base // 2
    ids = cluster_ids.reshape(-1, LANES)

    last_hops = n_shard - 1

    def with_rep(x):
        return [x] + [shift(x, "rep", n_rep, d) for d in range(1, n_rep)]

    matrices = with_rep(precond[0])

    picked = pick_queries(query_store, block_slot, pattern, n_group)
    pieces = [picked[0]] + [shift(picked[d], "shard", n_shard, d) for d in range(1, n_shard)]

    middle = [(d, 0, bulk) for d in range(1, last_hops)]
    part = 64 if bulk % 64 == 0 else bulk
    final = [(last_hops, at, part) for at in range(0, bulk, part)]
    *packed, goal = pack_rows(train, ids, columns, bulk, extra, middle + final)
    firsts, seconds = [], []
    parts = [pieces] + [[shift(x, "groups", n_group, d) for x in pieces] for d in range(1, n_group)]
    here = [shift(after(packed[0], *pieces[1:]), "shard", n_shard, 1)]
    urgent = [here[0]]
    if extra:
        far = swap(after(packed[-2], *pieces[1:]), "shard", n_shard, 2)
        urgent.append(far)
    depth = n_rep * columns
    targets = [(feat + d) % n_feat for d in range(1, n_feat)]
    near_chip = fetch(matrices, targets[0], depth, *pieces[1:])

    mine = own_rows(goal, train, bulk, *pieces[1:])
    table, flag = row_table(ids, lines, bulk, extra, *pieces[1:])
    chosen = join_queries(
        parts, block_slot, pattern, query_store.shape[0], n_feat, n_rep, *near_chip, mine, flag
    )
    queries = [*chosen[:CUTS]] + [shift(chosen[j], "rep", n_rep, j // CUTS) for j in range(CUTS, CUTS * n_rep)]

    sends = [fetched_weights(near_chip, queries, BF16)]
    sends += [partial_weights(matrices, queries, f, depth, BF16) for f in targets[1:]]
    others = [shift(x, "feat", n_feat, d + 1) for d, x in enumerate(sends)]
    own = partial_weights(matrices, queries, feat, depth, F32, *sends)

    for (hops, _, _), x in zip(middle[1:], packed[1:]):
        here.append(shift(after(x, *urgent, *sends), "shard", n_shard, hops))
        urgent = [here[-1]]
    last = [
        shift(after(packed[len(middle) + j], here[-1], own), "shard", n_shard, last_hops) for j in range(len(final))
    ]

    marks = [own]
    if extra:
        for d in range(1, n_group):
            flag = jnp.maximum(flag, shift(flag, "groups", n_group, d))

        def second_round(x):
            pair = jnp.concatenate([x, swap(x, "shard", n_shard, 2)])
            return [with_rep(pair), with_rep(swap(pair, "shard", n_shard, 1))]

        def no_round(x):
            empty = unwritten((2 * extra, columns), 2 * n_rep)
            return [[*empty[:n_rep]], [*empty[n_rep:]]]

        seconds = lax.cond(flag[0, 0] > 0, second_round, no_round, after(packed[-1], own))
        near = swap(stack([packed[-3], far], *sends), "shard", n_shard, 1)
        pairs = [stack([x, y], own) for x, y in zip(with_rep(packed[-3]), with_rep(after(far, own)))]
        firsts = [pairs, with_rep(after(near, own))]
        marks += [seconds[0][0], near, *pairs]

    mark = shift(after(jnp.zeros((8, LANES), I32), *marks), "rep", n_rep, 1)
    ready = [with_rep(after(x, mark)) for x in here]
    high, low, *early = early_scores(
        own, others, mine, ready, middle, firsts, seconds, table, rows, n_feat, n_rep, n_shard, bulk, extra
    )

    def over_feat(shares):
        return [shares[0]] + [shift(shares[d], "feat", n_feat, d) for d in range(1, n_feat)]

    late = late_scores([with_rep(after(x, *early[1:])) for x in last], high, low, n_feat)
    return merge(table, over_feat(early), over_feat(late), n_shard)[None]


def solution(mesh):
    return jax.shard_map(
        body,
        mesh=mesh,
        in_specs=(
            P(("groups", "shard"), "feat"),
            P("groups"),
            P(("groups", "shard"), None, ("feat", "rep")),
            P("shard", None, ("feat", "rep")),
            P(),
            P(),
        ),
        out_specs=P(("groups", "shard"), ("feat", "rep"), None),
        check_vma=False,
    )
```

```python
import functools

import jax
import jax.numpy as jnp
from jax import lax
from jax.experimental import pallas as pl
from jax.experimental.pallas import tpu as pltpu
from jax.sharding import PartitionSpec as P

F32, BF16, I32 = jnp.float32, jnp.bfloat16, jnp.int32
VMEM = pl.BlockSpec(memory_space=pltpu.VMEM)
ANY = pl.BlockSpec(memory_space=pl.ANY)
HBM = pl.BlockSpec(memory_space=pltpu.HBM)
SMEM = pl.BlockSpec(memory_space=pltpu.SMEM)
PARAMS = pltpu.CompilerParams(vmem_limit_bytes=24 * 2**20)
FIRST = pltpu.CompilerParams(vmem_limit_bytes=60 * 2**20)
LANES = 128
CUTS = 8


def shift(x, axis, size, by):
    return lax.ppermute(x, axis, [(i, (i + by) % size) for i in range(size)])


def swap(x, axis, size, bit):
    return lax.ppermute(x, axis, [(i, i ^ bit) for i in range(size)])


def dot(a, b):
    return jnp.dot(a, b, preferred_element_type=F32)


def cost(flops, nbytes):
    return pl.CostEstimate(flops=1, bytes_accessed=1, transcendentals=0)


def after(x, *others):
    def kernel(*refs):
        pass

    return pl.pallas_call(
        kernel,
        in_specs=[ANY] * (1 + len(others)),
        out_specs=ANY,
        out_shape=jax.ShapeDtypeStruct(x.shape, x.dtype),
        input_output_aliases={0: 0},
        cost_estimate=cost(0, 0),
        compiler_params=PARAMS,
        name="after",
    )(x, *others)


def unwritten(shape, n):
    def kernel(*refs):
        pass

    return pl.pallas_call(
        kernel,
        out_specs=[ANY] * n,
        out_shape=[jax.ShapeDtypeStruct(shape, BF16)] * n,
        cost_estimate=cost(0, 0),
        compiler_params=PARAMS,
        name="unwritten",
    )()


def stack(parts, *others):
    size, width = parts[0].shape
    n = len(parts)

    def kernel(*refs):
        for j in range(n):
            refs[-1][j * size:(j + 1) * size, :] = refs[j][...]

    return pl.pallas_call(
        kernel,
        in_specs=[VMEM] * n + [ANY] * len(others),
        out_specs=VMEM,
        out_shape=jax.ShapeDtypeStruct((n * size, width), parts[0].dtype),
        cost_estimate=cost(0, 0),
        compiler_params=PARAMS,
        name="stack",
    )(*parts, *others)


def pick_queries(query_store, block_slot, pattern, n_group):
    local_blocks, block_rows, width = query_store.shape
    n_cluster, n_list = pattern.shape
    part = block_rows // n_group

    def kernel(pattern_ref, slot_ref, in_ref, *rest):
        outs, sem = rest[:-1], rest[-1]
        me, group = lax.axis_index("shard"), lax.axis_index("groups")
        copies = []
        for t, out in enumerate(outs):
            target = lax.rem(me + t, jnp.int32(n_cluster))
            found = jnp.int32(0)
            for k in range(n_list):
                slot = slot_ref[pattern_ref[target, k]]
                hit = (lax.div(slot, jnp.int32(local_blocks)) == me).astype(I32)
                found = found + hit * lax.rem(slot, jnp.int32(local_blocks))
            rows = pl.ds(pl.multiple_of(group * part, part), part)
            copies.append(pltpu.make_async_copy(in_ref.at[found, rows], out.at[0], sem.at[t]))
            copies[-1].start()
        for copy in copies:
            copy.wait()

    return pl.pallas_call(
        kernel,
        in_specs=[SMEM, SMEM, ANY],
        out_specs=[VMEM] * n_cluster,
        out_shape=[jax.ShapeDtypeStruct((1, part, width), BF16)] * n_cluster,
        scratch_shapes=[pltpu.SemaphoreType.DMA((n_cluster,))],
        cost_estimate=cost(0, 4 * n_cluster * part * width),
        compiler_params=FIRST,
        name="pick_queries",
    )(pattern, block_slot, query_store)


def join_queries(parts, block_slot, pattern, local_blocks, n_feat, n_rep, *others):
    n_group, n_cluster = len(parts), len(parts[0])
    _, part, width = parts[0][0].shape
    n_list = pattern.shape[1]
    total = n_list * n_group * part
    share = total // (n_feat * n_rep)
    unit = min(share, part)
    half = total // n_rep

    def kernel(pattern_ref, slot_ref, *refs):
        outs, rows_ref = refs[-1 - CUTS * n_rep:-1], refs[-1]
        me, group = lax.axis_index("shard"), lax.axis_index("groups")
        for k in range(n_list):
            owner = lax.div(slot_ref[pattern_ref[me, k]], jnp.int32(local_blocks))
            hops = lax.rem(me + (n_cluster - owner), jnp.int32(n_cluster))
            for d in range(n_group):
                origin = lax.rem(group + (n_group - d), jnp.int32(n_group))
                for h in range(n_cluster):
                    @pl.when(hops == h)
                    def _():
                        for u in range(part // unit):
                            first = (k * n_group + origin) * part + u * unit
                            chunk = lax.div(first, jnp.int32(share))
                            goal = lax.rem(chunk, jnp.int32(n_rep)) * n_feat + lax.div(chunk, jnp.int32(n_rep))
                            goal = pl.multiple_of(goal * share + lax.rem(first, jnp.int32(share)), unit)
                            rows_ref[pl.ds(goal, unit), :] = refs[d * n_cluster + h][0, u * unit:(u + 1) * unit, :]
        for r in range(n_rep):
            @pl.when(lax.axis_index("rep") == r)
            def _():
                for j, out in enumerate(outs):
                    at, first = ((r + j // CUTS) % n_rep) * half, (j % CUTS) * (width // CUTS)
                    out[...] = rows_ref[at:at + half, first:first + width // CUTS].T

    return pl.pallas_call(
        kernel,
        in_specs=[SMEM, SMEM] + [VMEM] * (n_group * n_cluster) + [ANY] * len(others),
        out_specs=[VMEM] * (CUTS * n_rep),
        out_shape=[jax.ShapeDtypeStruct((width // CUTS, half), BF16)] * (CUTS * n_rep),
        scratch_shapes=[pltpu.VMEM((total, width), BF16)],
        cost_estimate=cost(0, 4 * total * width),
        compiler_params=PARAMS,
        name="join_queries",
    )(pattern, block_slot, *[x for line in parts for x in line], *others)


def one_hot(goal_ref, base, size):
    index = lax.broadcasted_iota(I32, (size, LANES), 0) + base
    lines = range(goal_ref.shape[0])
    return jnp.concatenate([(index == goal_ref[a:a + 1, :]).astype(F32).astype(BF16) for a in lines], axis=1)


def select(goal_ref, train_ref, base, size):
    tile = 128 if size % 128 == 0 else size
    found = [dot(one_hot(goal_ref, base + at, tile), train_ref[...]).astype(BF16) for at in range(0, size, tile)]
    return jnp.concatenate(found)


def own_rows(goal, train, bulk, *others):
    rows, width = train.shape
    cuts = 4
    part = width // cuts

    def kernel(goal_ref, train_ref, *rest):
        out_ref, held, sem = rest[-3:]
        copies = [
            pltpu.make_async_copy(train_ref.at[:, c * part:(c + 1) * part], held.at[c], sem.at[c]) for c in range(cuts)
        ]
        for copy in copies:
            copy.start()
        pick = one_hot(goal_ref, lax.axis_index("shard") * bulk, bulk)
        for c, copy in enumerate(copies):
            copy.wait()
            out_ref[:, c * part:(c + 1) * part] = dot(pick, held[c]).astype(BF16)

    return pl.pallas_call(
        kernel,
        in_specs=[VMEM, HBM] + [ANY] * len(others),
        out_specs=VMEM,
        out_shape=jax.ShapeDtypeStruct((bulk, width), BF16),
        scratch_shapes=[pltpu.VMEM((cuts, rows, part), BF16), pltpu.SemaphoreType.DMA((cuts,))],
        cost_estimate=cost(2 * bulk * train.size, 2 * train.size),
        compiler_params=PARAMS,
        name="own_rows",
    )(goal, train, *others)


def pack_rows(train, ids, columns, bulk, extra, cuts):
    rows = train.shape[0]
    lines = rows // LANES
    n_shard = ids.shape[0] // lines

    def kernel(ids_ref, train_ref, *rest):
        outs, goal_ref = rest[:-1], rest[-1]
        me = lax.axis_index("shard")
        own = ids_ref[...]
        masks = [(own == c).astype(F32) for c in range(n_shard)]
        stacked = jnp.concatenate(masks, axis=0).astype(BF16)
        lane_from = lax.broadcasted_iota(I32, (LANES, LANES), 0)
        lane_to = lax.broadcasted_iota(I32, (LANES, LANES), 1)
        in_line = dot(stacked, (lane_from < lane_to).astype(F32).astype(BF16))
        line_sum = dot(stacked, jnp.ones((LANES, LANES), BF16)).astype(BF16)
        size = n_shard * lines
        to = lax.broadcasted_iota(I32, (size, size), 0)
        since = lax.broadcasted_iota(I32, (size, size), 1)
        same = (to // lines) == (since // lines)
        ahead = dot((same & (since < to)).astype(F32).astype(BF16), line_sum)
        whole = dot(same.astype(F32).astype(BF16), line_sum)
        rank = in_line + ahead
        goal = jnp.zeros((lines, LANES), F32)
        past = jnp.zeros((lines, LANES), F32)
        for c in range(n_shard):
            part = slice(c * lines, (c + 1) * lines)
            place = rank[part] + c * bulk
            if extra:
                surplus = n_shard * bulk + past + rank[part] - bulk
                place = jnp.where(rank[part] < bulk, place, surplus)
                past = past + jnp.floor((jnp.maximum(whole[part] - bulk, 0.0) + 15.0) * 0.0625) * 16.0
            goal = goal + masks[c] * place
        goal_ref[...] = goal.astype(I32)

        def fill(out, base):
            out[...] = select(goal_ref, train_ref, base, out.shape[0])

        for out, (hops, first, _) in zip(outs, cuts):
            fill(out, lax.rem(me + hops, jnp.int32(n_shard)) * bulk + first)
        for j, out in enumerate(outs[len(cuts):]):
            fill(out, n_shard * bulk + max(j - 1, 0) * extra)

    shapes = [jax.ShapeDtypeStruct((n, columns), BF16) for _, _, n in cuts]
    shapes += [jax.ShapeDtypeStruct((extra, columns), BF16)] * (3 if extra else 0)
    shapes += [jax.ShapeDtypeStruct((lines, LANES), I32)]
    packed = n_shard * bulk + 2 * extra
    return pl.pallas_call(
        kernel,
        grid=(1,),
        in_specs=[
            pl.BlockSpec((lines, LANES), lambda i: (lax.axis_index("shard"), 0)),
            pl.BlockSpec((rows, columns), lambda i: (0, lax.axis_index("rep"))),
        ],
        out_specs=[VMEM] * len(shapes),
        out_shape=shapes,
        cost_estimate=cost(2 * packed * rows * columns, 2 * (rows + packed) * columns),
        compiler_params=FIRST,
        name="pack_rows",
    )(ids, train)


def partial_weights(matrices, queries, block, depth, dtype, *others):
    width, total = matrices[0].shape[1], queries[0].shape[1]
    tile = 512 if depth % 512 == 0 else depth
    steps = depth // tile
    n = len(matrices)

    def kernel(block_ref, *refs):
        out_ref, held, sem = refs[-3:]
        first = pl.multiple_of(block_ref[0] * depth, depth)
        copies = []
        for i in range(steps):
            for j in range(n):
                source = refs[j].at[pl.ds(first + i * tile, tile)]
                copies.append(pltpu.make_async_copy(source, held.at[j, i], sem.at[i * n + j]))
        for copy in copies:
            copy.start()
        parts = [jnp.concatenate([r[...] for r in refs[n + CUTS * j:n + CUTS * (j + 1)]]) for j in range(n)]
        for i in range(steps):
            value = None
            for j in range(n):
                copies[i * n + j].wait()
                part = dot(held[j, i], parts[j])
                value = part if value is None else value + part
            out_ref[i * tile:(i + 1) * tile, :] = value.astype(dtype)

    return pl.pallas_call(
        kernel,
        in_specs=[SMEM] + [HBM] * n + [VMEM] * (CUTS * n) + [ANY] * len(others),
        out_specs=VMEM,
        out_shape=jax.ShapeDtypeStruct((depth, total), dtype),
        scratch_shapes=[pltpu.VMEM((n, steps, tile, width), BF16), pltpu.SemaphoreType.DMA((steps * n,))],
        cost_estimate=cost(2 * n * depth * width * total, 2 * n * depth * width + 4 * depth * total),
        compiler_params=PARAMS,
        name="partial_weights",
    )(jnp.reshape(block, (1,)).astype(I32), *matrices, *queries, *others)


def fetch(matrices, block, depth, *others):
    width = matrices[0].shape[1]
    n = len(matrices)
    cuts = 4

    def kernel(block_ref, *refs):
        outs, sem = refs[-1 - n:-1], refs[-1]
        first = pl.multiple_of(block_ref[0] * depth, depth)
        copies = []
        for j in range(n):
            for c in range(cuts):
                size = depth // cuts
                source = refs[j].at[pl.ds(first + c * size, size)]
                copies.append(
                    pltpu.make_async_copy(source, outs[j].at[c * size:(c + 1) * size], sem.at[j * cuts + c])
                )
        for copy in copies:
            copy.start()
        for copy in copies:
            copy.wait()

    return pl.pallas_call(
        kernel,
        in_specs=[SMEM] + [HBM] * n + [ANY] * len(others),
        out_specs=[VMEM] * n,
        out_shape=[jax.ShapeDtypeStruct((depth, width), BF16)] * n,
        scratch_shapes=[pltpu.SemaphoreType.DMA((n * cuts,))],
        cost_estimate=cost(0, 2 * n * depth * width),
        compiler_params=PARAMS,
        name="fetch",
    )(jnp.reshape(block, (1,)).astype(I32), *matrices, *others)


def fetched_weights(matrices, queries, dtype):
    depth = matrices[0].shape[0]
    total = queries[0].shape[1]
    tile = 512 if depth % 512 == 0 else depth
    n = len(matrices)

    def kernel(*refs):
        parts = [jnp.concatenate([r[...] for r in refs[n + CUTS * j:n + CUTS * (j + 1)]]) for j in range(n)]
        for at in range(0, depth, tile):
            value = None
            for j in range(n):
                part = dot(refs[j][at:at + tile, :], parts[j])
                value = part if value is None else value + part
            refs[-1][at:at + tile, :] = value.astype(dtype)

    return pl.pallas_call(
        kernel,
        in_specs=[VMEM] * ((1 + CUTS) * n),
        out_specs=VMEM,
        out_shape=jax.ShapeDtypeStruct((depth, total), dtype),
        cost_estimate=cost(2 * n * matrices[0].size * total, 2 * n * matrices[0].size),
        compiler_params=PARAMS,
        name="fetched_weights",
    )(*matrices, *queries)


def row_table(ids, lines, bulk, extra, *others):
    n_shard = ids.shape[0] // lines

    def kernel(ids_ref, *rest):
        table_ref, flag_ref = rest[-2:]
        me = lax.axis_index("shard")
        start = jnp.int32(0)
        most = jnp.int32(0)
        for s in range(n_shard):
            line = ids_ref[s * lines:(s + 1) * lines, :]

            def count(c):
                return jnp.sum((line == c).astype(I32))

            mine = count(me)
            before = jnp.int32(0)
            if extra:
                surplus = jnp.int32(0)
                for c in range(n_shard):
                    over = lax.div(jnp.maximum(count(c) - bulk, 0) + 15, jnp.int32(16)) * 16
                    before = before + jnp.where(c < me, over, 0)
                    surplus = surplus + over
                most = jnp.maximum(most, surplus)
            table_ref[s, 0] = start
            table_ref[s, 1] = jnp.minimum(mine, bulk)
            table_ref[s, 2] = lax.div(before, jnp.int32(16))
            table_ref[s, 3] = jnp.maximum(mine - bulk, 0)
            start = start + mine
        flag_ref[...] = jnp.full((8, LANES), (most > extra).astype(I32))

    return pl.pallas_call(
        kernel,
        in_specs=[VMEM] + [ANY] * len(others),
        out_specs=[SMEM, VMEM],
        out_shape=[jax.ShapeDtypeStruct((n_shard, 4), I32), jax.ShapeDtypeStruct((8, LANES), I32)],
        cost_estimate=cost(0, 4 * ids.size),
        compiler_params=PARAMS,
        name="row_table",
    )(ids, *others)


def put(acc, x, start, count=None):
    tiles, _, width = x.shape
    first, within = lax.div(start, jnp.int32(8)), lax.rem(start, jnp.int32(8))
    turned = pltpu.roll(x, within, 1)
    row = lax.broadcasted_iota(I32, (1, 8, width), 1)
    keep = row < within
    pieces = jnp.where(keep, jnp.concatenate([turned[:1], turned]), jnp.concatenate([turned, turned[-1:]]))
    if count is None:
        pieces = jnp.concatenate([jnp.where(keep, acc[pl.ds(first, 1)], turned[:1]), pieces[1:]])
    else:
        at = lax.broadcasted_iota(I32, (tiles + 1, 8, width), 0) * 8 + lax.broadcasted_iota(
            I32, (tiles + 1, 8, width), 1
        )
        pieces = jnp.where(
            (at >= within) & (at < within + count), pieces, acc[pl.ds(first, tiles + 1)]
        )
    acc[pl.ds(first, tiles + 1)] = pieces


def score(high_ref, low_ref, parts, rep):
    total = None
    for d, x in enumerate(parts):
        depth = x.shape[1]
        block = pl.ds(pl.multiple_of(lax.rem(rep + (len(parts) - d), jnp.int32(len(parts))) * depth, depth), depth)
        value = dot(x, high_ref[block, :]) + dot(x, low_ref[block, :])
        total = value if total is None else total + value
    return total.reshape(total.shape[0] // 8, 8, total.shape[1])


def for_feats(value, outs):
    n = len(outs)
    share = outs[0].shape[1]
    for f in range(n):
        @pl.when(lax.axis_index("feat") == f)
        def _():
            for d, out in enumerate(outs):
                at = ((f + d) % n) * share
                out[...] = value(slice(at, at + share)).astype(out.dtype)


def feat_shapes(rows, width, n_feat):
    share = (rows, width // n_feat)
    return [jax.ShapeDtypeStruct(share, F32)] + [jax.ShapeDtypeStruct(share, BF16)] * (n_feat - 1)


def early_scores(own, others, mine, pieces, cuts, firsts, seconds, table, rows, n_feat, n_rep, n_shard, bulk, extra):
    depth, width = own.shape
    columns = depth // n_rep
    n_other, n_piece = len(others), len(pieces)
    n_first = len(firsts) * n_rep
    last_hops = n_shard - 1

    def kernel(table_ref, *refs):
        own_ref, refs = refs[0], refs[1:]
        other_refs, refs = refs[:n_other], refs[n_other:]
        mine_ref, refs = refs[0], refs[1:]
        piece_refs = [refs[j * n_rep:(j + 1) * n_rep] for j in range(n_piece)]
        refs = refs[n_piece * n_rep:]
        first_refs, second_refs, refs = refs[:n_first], refs[n_first:2 * n_first], refs[2 * n_first:]
        high_ref, low_ref, outs, (scored, held, acc, sem) = refs[0], refs[1], refs[2:-4], refs[-4:]
        me, rep = lax.axis_index("shard"), lax.axis_index("rep")
        weight = own_ref[...]
        for ref in other_refs:
            weight = weight + ref[...].astype(F32)
        high = weight.astype(BF16)
        high_ref[...] = high
        low_ref[...] = (weight - high.astype(F32)).astype(BF16)

        scored[me] = score(high_ref, low_ref, [mine_ref[...]], jnp.int32(0))
        for parts, (hops, first, size) in zip(piece_refs, cuts):
            source = lax.rem(me + (n_shard - hops), jnp.int32(n_shard))
            scored[source, first // 8:(first + size) // 8] = score(high_ref, low_ref, [p[...] for p in parts], rep)
        last = lax.rem(me + (n_shard - last_hops), jnp.int32(n_shard))
        for s in range(n_shard):
            start = table_ref[s, 0]

            @pl.when(last != s)
            def _():
                put(acc, scored[s], start)

            if extra:
                @pl.when(table_ref[s, 3] > 0)
                def _():
                    apart = jnp.bitwise_xor(me, s)
                    rows_in = pl.ds(pl.multiple_of(lax.div(apart, jnp.int32(2)) * extra, extra), extra)
                    for odd in range(2):
                        @pl.when(jnp.bitwise_and(apart, 1) == odd)
                        def _():
                            copies = []
                            for j, refs in enumerate([first_refs, second_refs]):
                                for d in range(n_rep):
                                    goal = held.at[d, j * extra:(j + 1) * extra]
                                    which = refs[odd * n_rep + d].at[rows_in]
                                    copies.append(pltpu.make_async_copy(which, goal, sem.at[j * n_rep + d]))
                            for copy in copies:
                                copy.start()
                            for copy in copies:
                                copy.wait()
                    some = pl.ds(pl.multiple_of(table_ref[s, 2] * 16, 16), extra)
                    x = [held[d, some, :] for d in range(n_rep)]
                    put(acc, score(high_ref, low_ref, x, rep), start + table_ref[s, 1])
        for_feats(lambda at: acc[:rows // 8, :, at].reshape(rows, width // n_feat), outs)

    count = n_shard * bulk
    surplus = [x for parts in [*firsts, *seconds] for x in parts]
    return pl.pallas_call(
        kernel,
        in_specs=[SMEM] + [VMEM] * (2 + n_other + n_rep * n_piece) + [ANY] * len(surplus),
        out_specs=[VMEM] * (2 + n_feat),
        out_shape=[jax.ShapeDtypeStruct((depth, width), BF16)] * 2 + feat_shapes(rows, width, n_feat),
        scratch_shapes=[
            pltpu.VMEM((n_shard, bulk // 8, 8, width), F32),
            pltpu.VMEM((n_rep, 3 * extra + 16, columns), BF16),
            pltpu.VMEM(((rows + bulk + extra) // 8 + 2, 8, width), F32),
            pltpu.SemaphoreType.DMA((2 * n_rep,)),
        ],
        cost_estimate=cost(4 * count * depth * width, 10 * depth * width + count * (2 * depth + 4 * width)),
        compiler_params=PARAMS,
        name="early_scores",
    )(table, own, *others, mine, *[p for parts in pieces for p in parts], *surplus)


def late_scores(pieces, high, low, n_feat):
    n, n_rep = len(pieces), len(pieces[0])
    size = pieces[0][0].shape[0]
    rows = n * size
    width = high.shape[1]

    def kernel(high_ref, low_ref, *refs):
        part_refs, outs, acc = refs[:n * n_rep], refs[n * n_rep:-1], refs[-1]
        parts = [jnp.concatenate([part_refs[j * n_rep + d][...] for j in range(n)]) for d in range(n_rep)]
        y = score(high_ref, low_ref, parts, lax.axis_index("rep"))
        acc[...] = y.reshape(rows, width)
        for_feats(lambda at: acc[:, at], outs)

    return pl.pallas_call(
        kernel,
        in_specs=[VMEM] * (2 + n * n_rep),
        out_specs=[VMEM] * n_feat,
        out_shape=feat_shapes(rows, width, n_feat),
        scratch_shapes=[pltpu.VMEM((rows, width), F32)],
        cost_estimate=cost(4 * rows * high.size, 8 * rows * width),
        compiler_params=PARAMS,
        name="late_scores",
    )(high, low, *[p for parts in pieces for p in parts])


def merge(table, early, late, n_shard):
    rows, width = early[0].shape
    last_rows = late[0].shape[0]
    last_hops = n_shard - 1

    def kernel(table_ref, *refs):
        early_refs, late_refs = refs[:len(early)], refs[len(early):-2]
        out_ref, acc = refs[-2:]
        source = lax.rem(lax.axis_index("shard") + (n_shard - last_hops), jnp.int32(n_shard))

        def total(parts):
            value = parts[0][...]
            for ref in parts[1:]:
                value = value + ref[...].astype(F32)
            return value.reshape(value.shape[0] // 8, 8, width)

        acc[:rows // 8] = total(early_refs)
        put(acc, total(late_refs), table_ref[source, 0], table_ref[source, 1])
        out_ref[...] = acc[:rows // 8].reshape(rows, width).T

    return pl.pallas_call(
        kernel,
        in_specs=[SMEM] + [VMEM] * (len(early) + len(late)),
        out_specs=VMEM,
        out_shape=jax.ShapeDtypeStruct((width, rows), F32),
        scratch_shapes=[pltpu.VMEM(((rows + last_rows) // 8 + 2, 8, width), F32)],
        cost_estimate=cost(0, 8 * rows * width),
        compiler_params=PARAMS,
        name="merge",
    )(table, *early, *late)


def body(train, cluster_ids, precond, query_store, block_slot, pattern):
    n_group, n_shard = lax.axis_size("groups"), lax.axis_size("shard")
    n_feat, n_rep = lax.axis_size("feat"), lax.axis_size("rep")
    feat, rep = lax.axis_index("feat"), lax.axis_index("rep")
    rows = train.shape[0]
    lines = rows // LANES
    base = rows // n_shard
    columns = train.shape[1] // n_rep
    extra = base // 2 if n_shard == 4 else 0
    bulk = base if extra else base + base // 2
    ids = cluster_ids.reshape(-1, LANES)

    last_hops = n_shard - 1

    def with_rep(x):
        return [x] + [shift(x, "rep", n_rep, d) for d in range(1, n_rep)]

    matrices = with_rep(precond[0])

    picked = pick_queries(query_store, block_slot, pattern, n_group)
    pieces = [picked[0]] + [shift(picked[d], "shard", n_shard, d) for d in range(1, n_shard)]

    middle = [(d, 0, bulk) for d in range(1, last_hops)]
    part = 64 if bulk % 64 == 0 else bulk
    final = [(last_hops, at, part) for at in range(0, bulk, part)]
    *packed, goal = pack_rows(train, ids, columns, bulk, extra, middle + final)
    firsts, seconds = [], []
    parts = [pieces] + [[shift(x, "groups", n_group, d) for x in pieces] for d in range(1, n_group)]
    here = [shift(after(packed[0], *pieces[1:]), "shard", n_shard, 1)]
    urgent = [here[0]]
    if extra:
        far = swap(after(packed[-2], *pieces[1:]), "shard", n_shard, 2)
        urgent.append(far)
    depth = n_rep * columns
    targets = [(feat + d) % n_feat for d in range(1, n_feat)]
    near_chip = fetch(matrices, targets[0], depth, *pieces[1:])

    table, flag = row_table(ids, lines, bulk, extra, *pieces[1:])
    chosen = join_queries(
        parts, block_slot, pattern, query_store.shape[0], n_feat, n_rep, *near_chip, flag
    )
    queries = [*chosen[:CUTS]] + [shift(chosen[j], "rep", n_rep, j // CUTS) for j in range(CUTS, CUTS * n_rep)]

    sends = [fetched_weights(near_chip, queries, BF16)]
    sends += [partial_weights(matrices, queries, f, depth, BF16) for f in targets[1:]]
    others = [shift(x, "feat", n_feat, d + 1) for d, x in enumerate(sends)]
    own = partial_weights(matrices, queries, feat, depth, F32, *sends)

    for (hops, _, _), x in zip(middle[1:], packed[1:]):
        here.append(shift(after(x, *urgent, *sends), "shard", n_shard, hops))
        urgent = [here[-1]]
    last = [
        shift(after(packed[len(middle) + j], here[-1], own), "shard", n_shard, last_hops) for j in range(len(final))
    ]

    mine = own_rows(goal, train, bulk, own)
    marks = [own, mine]
    if extra:
        for d in range(1, n_group):
            flag = jnp.maximum(flag, shift(flag, "groups", n_group, d))

        def second_round(x):
            pair = jnp.concatenate([x, swap(x, "shard", n_shard, 2)])
            return [with_rep(pair), with_rep(swap(pair, "shard", n_shard, 1))]

        def no_round(x):
            empty = unwritten((2 * extra, columns), 2 * n_rep)
            return [[*empty[:n_rep]], [*empty[n_rep:]]]

        seconds = lax.cond(flag[0, 0] > 0, second_round, no_round, after(packed[-1], own))
        near = swap(stack([packed[-3], far], *sends), "shard", n_shard, 1)
        pairs = [stack([x, y], own) for x, y in zip(with_rep(packed[-3]), with_rep(after(far, own)))]
        firsts = [pairs, with_rep(after(near, own))]
        marks += [seconds[0][0], near, *pairs]

    mark = shift(after(jnp.zeros((8, LANES), I32), *marks), "rep", n_rep, 1)
    ready = [with_rep(after(x, mark)) for x in here]
    high, low, *early = early_scores(
        own, others, mine, ready, middle, firsts, seconds, table, rows, n_feat, n_rep, n_shard, bulk, extra
    )

    def over_feat(shares):
        return [shares[0]] + [shift(shares[d], "feat", n_feat, d) for d in range(1, n_feat)]

    late = late_scores([with_rep(after(x, *early[1:])) for x in last], high, low, n_feat)
    return merge(table, over_feat(early), over_feat(late), n_shard)[None]


def solution(mesh):
    return jax.shard_map(
        body,
        mesh=mesh,
        in_specs=(
            P(("groups", "shard"), "feat"),
            P("groups"),
            P(("groups", "shard"), None, ("feat", "rep")),
            P("shard", None, ("feat", "rep")),
            P(),
            P(),
        ),
        out_specs=P(("groups", "shard"), ("feat", "rep"), None),
        check_vma=False,
    )
```

```python
import functools

import jax
import jax.numpy as jnp
from jax import lax
from jax.experimental import pallas as pl
from jax.experimental.pallas import tpu as pltpu
from jax.sharding import PartitionSpec as P

F32, BF16, I32 = jnp.float32, jnp.bfloat16, jnp.int32
VMEM = pl.BlockSpec(memory_space=pltpu.VMEM)
ANY = pl.BlockSpec(memory_space=pl.ANY)
HBM = pl.BlockSpec(memory_space=pltpu.HBM)
SMEM = pl.BlockSpec(memory_space=pltpu.SMEM)
PARAMS = pltpu.CompilerParams(vmem_limit_bytes=24 * 2**20)
FIRST = pltpu.CompilerParams(vmem_limit_bytes=60 * 2**20)
LANES = 128
CUTS = 8


def shift(x, axis, size, by):
    return lax.ppermute(x, axis, [(i, (i + by) % size) for i in range(size)])


def swap(x, axis, size, bit):
    return lax.ppermute(x, axis, [(i, i ^ bit) for i in range(size)])


def dot(a, b):
    return jnp.dot(a, b, preferred_element_type=F32)


def cost(flops, nbytes):
    return pl.CostEstimate(flops=1, bytes_accessed=1, transcendentals=0)


def after(x, *others):
    def kernel(*refs):
        pass

    return pl.pallas_call(
        kernel,
        in_specs=[ANY] * (1 + len(others)),
        out_specs=ANY,
        out_shape=jax.ShapeDtypeStruct(x.shape, x.dtype),
        input_output_aliases={0: 0},
        cost_estimate=cost(0, 0),
        compiler_params=PARAMS,
        name="after",
    )(x, *others)


def unwritten(shape, n):
    def kernel(*refs):
        pass

    return pl.pallas_call(
        kernel,
        out_specs=[ANY] * n,
        out_shape=[jax.ShapeDtypeStruct(shape, BF16)] * n,
        cost_estimate=cost(0, 0),
        compiler_params=PARAMS,
        name="unwritten",
    )()


def stack(parts, *others):
    size, width = parts[0].shape
    n = len(parts)

    def kernel(*refs):
        for j in range(n):
            refs[-1][j * size:(j + 1) * size, :] = refs[j][...]

    return pl.pallas_call(
        kernel,
        in_specs=[VMEM] * n + [ANY] * len(others),
        out_specs=VMEM,
        out_shape=jax.ShapeDtypeStruct((n * size, width), parts[0].dtype),
        cost_estimate=cost(0, 0),
        compiler_params=PARAMS,
        name="stack",
    )(*parts, *others)


def pick_queries(query_store, block_slot, pattern, n_group):
    local_blocks, block_rows, width = query_store.shape
    n_cluster, n_list = pattern.shape
    part = block_rows // n_group

    def kernel(pattern_ref, slot_ref, in_ref, *rest):
        outs, sem = rest[:-1], rest[-1]
        me, group = lax.axis_index("shard"), lax.axis_index("groups")
        copies = []
        for t, out in enumerate(outs):
            target = lax.rem(me + t, jnp.int32(n_cluster))
            found = jnp.int32(0)
            for k in range(n_list):
                slot = slot_ref[pattern_ref[target, k]]
                hit = (lax.div(slot, jnp.int32(local_blocks)) == me).astype(I32)
                found = found + hit * lax.rem(slot, jnp.int32(local_blocks))
            rows = pl.ds(pl.multiple_of(group * part, part), part)
            copies.append(pltpu.make_async_copy(in_ref.at[found, rows], out.at[0], sem.at[t]))
            copies[-1].start()
        for copy in copies:
            copy.wait()

    return pl.pallas_call(
        kernel,
        in_specs=[SMEM, SMEM, ANY],
        out_specs=[VMEM] * n_cluster,
        out_shape=[jax.ShapeDtypeStruct((1, part, width), BF16)] * n_cluster,
        scratch_shapes=[pltpu.SemaphoreType.DMA((n_cluster,))],
        cost_estimate=cost(0, 4 * n_cluster * part * width),
        compiler_params=FIRST,
        name="pick_queries",
    )(pattern, block_slot, query_store)


def join_queries(parts, block_slot, pattern, local_blocks, n_feat, n_rep, *others):
    n_group, n_cluster = len(parts), len(parts[0])
    _, part, width = parts[0][0].shape
    n_list = pattern.shape[1]
    total = n_list * n_group * part
    share = total // (n_feat * n_rep)
    unit = min(share, part)
    half = total // n_rep

    def kernel(pattern_ref, slot_ref, *refs):
        outs, rows_ref = refs[-1 - CUTS * n_rep:-1], refs[-1]
        me, group = lax.axis_index("shard"), lax.axis_index("groups")
        for k in range(n_list):
            owner = lax.div(slot_ref[pattern_ref[me, k]], jnp.int32(local_blocks))
            hops = lax.rem(me + (n_cluster - owner), jnp.int32(n_cluster))
            for d in range(n_group):
                origin = lax.rem(group + (n_group - d), jnp.int32(n_group))
                for h in range(n_cluster):
                    @pl.when(hops == h)
                    def _():
                        for u in range(part // unit):
                            first = (k * n_group + origin) * part + u * unit
                            chunk = lax.div(first, jnp.int32(share))
                            goal = lax.rem(chunk, jnp.int32(n_rep)) * n_feat + lax.div(chunk, jnp.int32(n_rep))
                            goal = pl.multiple_of(goal * share + lax.rem(first, jnp.int32(share)), unit)
                            rows_ref[pl.ds(goal, unit), :] = refs[d * n_cluster + h][0, u * unit:(u + 1) * unit, :]
        for r in range(n_rep):
            @pl.when(lax.axis_index("rep") == r)
            def _():
                for j, out in enumerate(outs):
                    at, first = ((r + j // CUTS) % n_rep) * half, (j % CUTS) * (width // CUTS)
                    out[...] = rows_ref[at:at + half, first:first + width // CUTS].T

    return pl.pallas_call(
        kernel,
        in_specs=[SMEM, SMEM] + [VMEM] * (n_group * n_cluster) + [ANY] * len(others),
        out_specs=[VMEM] * (CUTS * n_rep),
        out_shape=[jax.ShapeDtypeStruct((width // CUTS, half), BF16)] * (CUTS * n_rep),
        scratch_shapes=[pltpu.VMEM((total, width), BF16)],
        cost_estimate=cost(0, 4 * total * width),
        compiler_params=PARAMS,
        name="join_queries",
    )(pattern, block_slot, *[x for line in parts for x in line], *others)


def one_hot(goal_ref, base, size):
    index = lax.broadcasted_iota(I32, (size, LANES), 0) + base
    lines = range(goal_ref.shape[0])
    return jnp.concatenate([(index == goal_ref[a:a + 1, :]).astype(F32).astype(BF16) for a in lines], axis=1)


def select(goal_ref, train_ref, base, size):
    tile = 128 if size % 128 == 0 else size
    found = [dot(one_hot(goal_ref, base + at, tile), train_ref[...]).astype(BF16) for at in range(0, size, tile)]
    return jnp.concatenate(found)


def own_rows(goal, train, bulk, *others):
    rows, width = train.shape
    cuts = 4
    part = width // cuts

    def kernel(goal_ref, train_ref, *rest):
        out_ref, held, sem = rest[-3:]
        copies = [
            pltpu.make_async_copy(train_ref.at[:, c * part:(c + 1) * part], held.at[c], sem.at[c]) for c in range(cuts)
        ]
        for copy in copies:
            copy.start()
        pick = one_hot(goal_ref, lax.axis_index("shard") * bulk, bulk)
        for c, copy in enumerate(copies):
            copy.wait()
            out_ref[:, c * part:(c + 1) * part] = dot(pick, held[c]).astype(BF16)

    return pl.pallas_call(
        kernel,
        in_specs=[VMEM, HBM] + [ANY] * len(others),
        out_specs=VMEM,
        out_shape=jax.ShapeDtypeStruct((bulk, width), BF16),
        scratch_shapes=[pltpu.VMEM((cuts, rows, part), BF16), pltpu.SemaphoreType.DMA((cuts,))],
        cost_estimate=cost(2 * bulk * train.size, 2 * train.size),
        compiler_params=PARAMS,
        name="own_rows",
    )(goal, train, *others)


def pack_rows(train, ids, columns, bulk, extra, cuts):
    rows = train.shape[0]
    lines = rows // LANES
    n_shard = ids.shape[0] // lines

    def kernel(ids_ref, train_ref, *rest):
        outs, goal_ref = rest[:-1], rest[-1]
        me = lax.axis_index("shard")
        own = ids_ref[...]
        masks = [(own == c).astype(F32) for c in range(n_shard)]
        stacked = jnp.concatenate(masks, axis=0).astype(BF16)
        lane_from = lax.broadcasted_iota(I32, (LANES, LANES), 0)
        lane_to = lax.broadcasted_iota(I32, (LANES, LANES), 1)
        in_line = dot(stacked, (lane_from < lane_to).astype(F32).astype(BF16))
        line_sum = dot(stacked, jnp.ones((LANES, LANES), BF16)).astype(BF16)
        size = n_shard * lines
        to = lax.broadcasted_iota(I32, (size, size), 0)
        since = lax.broadcasted_iota(I32, (size, size), 1)
        same = (to // lines) == (since // lines)
        ahead = dot((same & (since < to)).astype(F32).astype(BF16), line_sum)
        whole = dot(same.astype(F32).astype(BF16), line_sum)
        rank = in_line + ahead
        goal = jnp.zeros((lines, LANES), F32)
        past = jnp.zeros((lines, LANES), F32)
        for c in range(n_shard):
            part = slice(c * lines, (c + 1) * lines)
            place = rank[part] + c * bulk
            if extra:
                surplus = n_shard * bulk + past + rank[part] - bulk
                place = jnp.where(rank[part] < bulk, place, surplus)
                past = past + jnp.floor((jnp.maximum(whole[part] - bulk, 0.0) + 15.0) * 0.0625) * 16.0
            goal = goal + masks[c] * place
        goal_ref[...] = goal.astype(I32)

        def fill(out, base):
            out[...] = select(goal_ref, train_ref, base, out.shape[0])

        for out, (hops, first, _) in zip(outs, cuts):
            fill(out, lax.rem(me + hops, jnp.int32(n_shard)) * bulk + first)
        for j, out in enumerate(outs[len(cuts):]):
            fill(out, n_shard * bulk + max(j - 1, 0) * extra)

    shapes = [jax.ShapeDtypeStruct((n, columns), BF16) for _, _, n in cuts]
    shapes += [jax.ShapeDtypeStruct((extra, columns), BF16)] * (3 if extra else 0)
    shapes += [jax.ShapeDtypeStruct((lines, LANES), I32)]
    packed = n_shard * bulk + 2 * extra
    return pl.pallas_call(
        kernel,
        grid=(1,),
        in_specs=[
            pl.BlockSpec((lines, LANES), lambda i: (lax.axis_index("shard"), 0)),
            pl.BlockSpec((rows, columns), lambda i: (0, lax.axis_index("rep"))),
        ],
        out_specs=[VMEM] * len(shapes),
        out_shape=shapes,
        cost_estimate=cost(2 * packed * rows * columns, 2 * (rows + packed) * columns),
        compiler_params=FIRST,
        name="pack_rows",
    )(ids, train)


def partial_weights(matrices, queries, block, depth, dtype, *others):
    width, total = matrices[0].shape[1], queries[0].shape[1]
    tile = 512 if depth % 512 == 0 else depth
    steps = depth // tile
    n = len(matrices)

    def kernel(block_ref, *refs):
        out_ref, held, sem = refs[-3:]
        first = pl.multiple_of(block_ref[0] * depth, depth)
        copies = []
        for i in range(steps):
            for j in range(n):
                source = refs[j].at[pl.ds(first + i * tile, tile)]
                copies.append(pltpu.make_async_copy(source, held.at[j, i], sem.at[i * n + j]))
        for copy in copies:
            copy.start()
        parts = [jnp.concatenate([r[...] for r in refs[n + CUTS * j:n + CUTS * (j + 1)]]) for j in range(n)]
        for i in range(steps):
            value = None
            for j in range(n):
                copies[i * n + j].wait()
                part = dot(held[j, i], parts[j])
                value = part if value is None else value + part
            out_ref[i * tile:(i + 1) * tile, :] = value.astype(dtype)

    return pl.pallas_call(
        kernel,
        in_specs=[SMEM] + [HBM] * n + [VMEM] * (CUTS * n) + [ANY] * len(others),
        out_specs=VMEM,
        out_shape=jax.ShapeDtypeStruct((depth, total), dtype),
        scratch_shapes=[pltpu.VMEM((n, steps, tile, width), BF16), pltpu.SemaphoreType.DMA((steps * n,))],
        cost_estimate=cost(2 * n * depth * width * total, 2 * n * depth * width + 4 * depth * total),
        compiler_params=PARAMS,
        name="partial_weights",
    )(jnp.reshape(block, (1,)).astype(I32), *matrices, *queries, *others)


def fetch(matrices, block, depth, *others):
    width = matrices[0].shape[1]
    n = len(matrices)
    cuts = 4

    def kernel(block_ref, *refs):
        outs, sem = refs[-1 - n:-1], refs[-1]
        first = pl.multiple_of(block_ref[0] * depth, depth)
        copies = []
        for j in range(n):
            for c in range(cuts):
                size = depth // cuts
                source = refs[j].at[pl.ds(first + c * size, size)]
                copies.append(
                    pltpu.make_async_copy(source, outs[j].at[c * size:(c + 1) * size], sem.at[j * cuts + c])
                )
        for copy in copies:
            copy.start()
        for copy in copies:
            copy.wait()

    return pl.pallas_call(
        kernel,
        in_specs=[SMEM] + [HBM] * n + [ANY] * len(others),
        out_specs=[VMEM] * n,
        out_shape=[jax.ShapeDtypeStruct((depth, width), BF16)] * n,
        scratch_shapes=[pltpu.SemaphoreType.DMA((n * cuts,))],
        cost_estimate=cost(0, 2 * n * depth * width),
        compiler_params=PARAMS,
        name="fetch",
    )(jnp.reshape(block, (1,)).astype(I32), *matrices, *others)


def fetched_weights(matrices, queries, dtype):
    depth = matrices[0].shape[0]
    total = queries[0].shape[1]
    tile = 512 if depth % 512 == 0 else depth
    n = len(matrices)

    def kernel(*refs):
        parts = [jnp.concatenate([r[...] for r in refs[n + CUTS * j:n + CUTS * (j + 1)]]) for j in range(n)]
        for at in range(0, depth, tile):
            value = None
            for j in range(n):
                part = dot(refs[j][at:at + tile, :], parts[j])
                value = part if value is None else value + part
            refs[-1][at:at + tile, :] = value.astype(dtype)

    return pl.pallas_call(
        kernel,
        in_specs=[VMEM] * ((1 + CUTS) * n),
        out_specs=VMEM,
        out_shape=jax.ShapeDtypeStruct((depth, total), dtype),
        cost_estimate=cost(2 * n * matrices[0].size * total, 2 * n * matrices[0].size),
        compiler_params=PARAMS,
        name="fetched_weights",
    )(*matrices, *queries)


def row_table(ids, lines, bulk, extra, *others):
    n_shard = ids.shape[0] // lines

    def kernel(ids_ref, *rest):
        table_ref, flag_ref = rest[-2:]
        me = lax.axis_index("shard")
        start = jnp.int32(0)
        most = jnp.int32(0)
        for s in range(n_shard):
            line = ids_ref[s * lines:(s + 1) * lines, :]

            def count(c):
                return jnp.sum((line == c).astype(I32))

            mine = count(me)
            before = jnp.int32(0)
            if extra:
                surplus = jnp.int32(0)
                for c in range(n_shard):
                    over = lax.div(jnp.maximum(count(c) - bulk, 0) + 15, jnp.int32(16)) * 16
                    before = before + jnp.where(c < me, over, 0)
                    surplus = surplus + over
                most = jnp.maximum(most, surplus)
            table_ref[s, 0] = start
            table_ref[s, 1] = jnp.minimum(mine, bulk)
            table_ref[s, 2] = lax.div(before, jnp.int32(16))
            table_ref[s, 3] = jnp.maximum(mine - bulk, 0)
            start = start + mine
        flag_ref[...] = jnp.full((8, LANES), (most > extra).astype(I32))

    return pl.pallas_call(
        kernel,
        in_specs=[VMEM] + [ANY] * len(others),
        out_specs=[SMEM, VMEM],
        out_shape=[jax.ShapeDtypeStruct((n_shard, 4), I32), jax.ShapeDtypeStruct((8, LANES), I32)],
        cost_estimate=cost(0, 4 * ids.size),
        compiler_params=PARAMS,
        name="row_table",
    )(ids, *others)


def put(acc, x, start, count=None):
    tiles, _, width = x.shape
    first, within = lax.div(start, jnp.int32(8)), lax.rem(start, jnp.int32(8))
    turned = pltpu.roll(x, within, 1)
    row = lax.broadcasted_iota(I32, (1, 8, width), 1)
    keep = row < within
    pieces = jnp.where(keep, jnp.concatenate([turned[:1], turned]), jnp.concatenate([turned, turned[-1:]]))
    if count is None:
        pieces = jnp.concatenate([jnp.where(keep, acc[pl.ds(first, 1)], turned[:1]), pieces[1:]])
    else:
        at = lax.broadcasted_iota(I32, (tiles + 1, 8, width), 0) * 8 + lax.broadcasted_iota(
            I32, (tiles + 1, 8, width), 1
        )
        pieces = jnp.where(
            (at >= within) & (at < within + count), pieces, acc[pl.ds(first, tiles + 1)]
        )
    acc[pl.ds(first, tiles + 1)] = pieces


def score(high_ref, low_ref, parts, rep):
    total = None
    for d, x in enumerate(parts):
        depth = x.shape[1]
        block = pl.ds(pl.multiple_of(lax.rem(rep + (len(parts) - d), jnp.int32(len(parts))) * depth, depth), depth)
        value = dot(x, high_ref[block, :]) + dot(x, low_ref[block, :])
        total = value if total is None else total + value
    return total.reshape(total.shape[0] // 8, 8, total.shape[1])


def for_feats(value, outs):
    n = len(outs)
    share = outs[0].shape[1]
    for f in range(n):
        @pl.when(lax.axis_index("feat") == f)
        def _():
            for d, out in enumerate(outs):
                at = ((f + d) % n) * share
                out[...] = value(slice(at, at + share)).astype(out.dtype)


def feat_shapes(rows, width, n_feat):
    share = (rows, width // n_feat)
    return [jax.ShapeDtypeStruct(share, F32)] + [jax.ShapeDtypeStruct(share, BF16)] * (n_feat - 1)


def early_scores(own, others, mine, pieces, cuts, firsts, seconds, table, rows, n_feat, n_rep, n_shard, bulk, extra):
    depth, width = own.shape
    columns = depth // n_rep
    n_other, n_piece = len(others), len(pieces)
    n_first = len(firsts) * n_rep
    last_hops = n_shard - 1

    def kernel(table_ref, *refs):
        own_ref, refs = refs[0], refs[1:]
        other_refs, refs = refs[:n_other], refs[n_other:]
        mine_ref, refs = refs[0], refs[1:]
        piece_refs = [refs[j * n_rep:(j + 1) * n_rep] for j in range(n_piece)]
        refs = refs[n_piece * n_rep:]
        first_refs, second_refs, refs = refs[:n_first], refs[n_first:2 * n_first], refs[2 * n_first:]
        high_ref, low_ref, outs, (scored, held, acc, sem) = refs[0], refs[1], refs[2:-4], refs[-4:]
        me, rep = lax.axis_index("shard"), lax.axis_index("rep")
        weight = own_ref[...]
        for ref in other_refs:
            weight = weight + ref[...].astype(F32)
        high = weight.astype(BF16)
        high_ref[...] = high
        low_ref[...] = (weight - high.astype(F32)).astype(BF16)

        scored[me] = score(high_ref, low_ref, [mine_ref[...]], jnp.int32(0))
        for parts, (hops, first, size) in zip(piece_refs, cuts):
            source = lax.rem(me + (n_shard - hops), jnp.int32(n_shard))
            scored[source, first // 8:(first + size) // 8] = score(high_ref, low_ref, [p[...] for p in parts], rep)
        last = lax.rem(me + (n_shard - last_hops), jnp.int32(n_shard))
        for s in range(n_shard):
            start = table_ref[s, 0]

            @pl.when(last != s)
            def _():
                put(acc, scored[s], start)

            if extra:
                @pl.when(table_ref[s, 3] > 0)
                def _():
                    apart = jnp.bitwise_xor(me, s)
                    rows_in = pl.ds(pl.multiple_of(lax.div(apart, jnp.int32(2)) * extra, extra), extra)
                    for odd in range(2):
                        @pl.when(jnp.bitwise_and(apart, 1) == odd)
                        def _():
                            copies = []
                            for j, refs in enumerate([first_refs, second_refs]):
                                for d in range(n_rep):
                                    goal = held.at[d, j * extra:(j + 1) * extra]
                                    which = refs[odd * n_rep + d].at[rows_in]
                                    copies.append(pltpu.make_async_copy(which, goal, sem.at[j * n_rep + d]))
                            for copy in copies:
                                copy.start()
                            for copy in copies:
                                copy.wait()
                    some = pl.ds(pl.multiple_of(table_ref[s, 2] * 16, 16), extra)
                    x = [held[d, some, :] for d in range(n_rep)]
                    put(acc, score(high_ref, low_ref, x, rep), start + table_ref[s, 1])
        for_feats(lambda at: acc[:rows // 8, :, at].reshape(rows, width // n_feat), outs)

    count = n_shard * bulk
    surplus = [x for parts in [*firsts, *seconds] for x in parts]
    return pl.pallas_call(
        kernel,
        in_specs=[SMEM] + [VMEM] * (2 + n_other + n_rep * n_piece) + [ANY] * len(surplus),
        out_specs=[VMEM] * (2 + n_feat),
        out_shape=[jax.ShapeDtypeStruct((depth, width), BF16)] * 2 + feat_shapes(rows, width, n_feat),
        scratch_shapes=[
            pltpu.VMEM((n_shard, bulk // 8, 8, width), F32),
            pltpu.VMEM((n_rep, 3 * extra + 16, columns), BF16),
            pltpu.VMEM(((rows + bulk + extra) // 8 + 2, 8, width), F32),
            pltpu.SemaphoreType.DMA((2 * n_rep,)),
        ],
        cost_estimate=cost(4 * count * depth * width, 10 * depth * width + count * (2 * depth + 4 * width)),
        compiler_params=PARAMS,
        name="early_scores",
    )(table, own, *others, mine, *[p for parts in pieces for p in parts], *surplus)


def late_scores(pieces, high, low, n_feat):
    n, n_rep = len(pieces), len(pieces[0])
    size = pieces[0][0].shape[0]
    rows = n * size
    width = high.shape[1]

    def kernel(high_ref, low_ref, *refs):
        part_refs, outs, acc = refs[:n * n_rep], refs[n * n_rep:-1], refs[-1]
        parts = [jnp.concatenate([part_refs[j * n_rep + d][...] for j in range(n)]) for d in range(n_rep)]
        y = score(high_ref, low_ref, parts, lax.axis_index("rep"))
        acc[...] = y.reshape(rows, width)
        for_feats(lambda at: acc[:, at], outs)

    return pl.pallas_call(
        kernel,
        in_specs=[VMEM] * (2 + n * n_rep),
        out_specs=[VMEM] * n_feat,
        out_shape=feat_shapes(rows, width, n_feat),
        scratch_shapes=[pltpu.VMEM((rows, width), F32)],
        cost_estimate=cost(4 * rows * high.size, 8 * rows * width),
        compiler_params=PARAMS,
        name="late_scores",
    )(high, low, *[p for parts in pieces for p in parts])


def merge(table, early, late, n_shard):
    rows, width = early[0].shape
    last_rows = late[0].shape[0]
    last_hops = n_shard - 1

    def kernel(table_ref, *refs):
        early_refs, late_refs = refs[:len(early)], refs[len(early):-2]
        out_ref, acc = refs[-2:]
        source = lax.rem(lax.axis_index("shard") + (n_shard - last_hops), jnp.int32(n_shard))

        def total(parts):
            value = parts[0][...]
            for ref in parts[1:]:
                value = value + ref[...].astype(F32)
            return value.reshape(value.shape[0] // 8, 8, width)

        acc[:rows // 8] = total(early_refs)
        put(acc, total(late_refs), table_ref[source, 0], table_ref[source, 1])
        out_ref[...] = acc[:rows // 8].reshape(rows, width).T

    return pl.pallas_call(
        kernel,
        in_specs=[SMEM] + [VMEM] * (len(early) + len(late)),
        out_specs=VMEM,
        out_shape=jax.ShapeDtypeStruct((width, rows), F32),
        scratch_shapes=[pltpu.VMEM(((rows + last_rows) // 8 + 2, 8, width), F32)],
        cost_estimate=cost(0, 8 * rows * width),
        compiler_params=PARAMS,
        name="merge",
    )(table, *early, *late)


def body(train, cluster_ids, precond, query_store, block_slot, pattern):
    n_group, n_shard = lax.axis_size("groups"), lax.axis_size("shard")
    n_feat, n_rep = lax.axis_size("feat"), lax.axis_size("rep")
    feat, rep = lax.axis_index("feat"), lax.axis_index("rep")
    rows = train.shape[0]
    lines = rows // LANES
    base = rows // n_shard
    columns = train.shape[1] // n_rep
    extra = base // 2 if n_shard == 4 else 0
    bulk = base if extra else base + base // 2
    ids = cluster_ids.reshape(-1, LANES)

    last_hops = n_shard - 1

    def with_rep(x):
        return [x] + [shift(x, "rep", n_rep, d) for d in range(1, n_rep)]

    matrices = with_rep(precond[0])

    picked = pick_queries(query_store, block_slot, pattern, n_group)
    pieces = [picked[0]] + [shift(picked[d], "shard", n_shard, d) for d in range(1, n_shard)]

    middle = [(d, 0, bulk) for d in range(1, last_hops)]
    part = 64 if bulk % 64 == 0 else bulk
    final = [(last_hops, at, part) for at in range(0, bulk, part)]
    *packed, goal = pack_rows(train, ids, columns, bulk, extra, middle + final)
    firsts, seconds = [], []
    parts = [pieces] + [[shift(x, "groups", n_group, d) for x in pieces] for d in range(1, n_group)]
    here = [shift(after(packed[0], *pieces[1:]), "shard", n_shard, 1)]
    urgent = [here[0]]
    if extra:
        far = swap(after(packed[-2], *pieces[1:]), "shard", n_shard, 2)
        urgent.append(far)
    depth = n_rep * columns
    targets = [(feat + d) % n_feat for d in range(1, n_feat)]
    near_chip = fetch(matrices, targets[0], depth, *pieces[1:])

    table, flag = row_table(ids, lines, bulk, extra, *pieces[1:])
    chosen = join_queries(
        parts, block_slot, pattern, query_store.shape[0], n_feat, n_rep, *near_chip, flag
    )
    queries = [*chosen[:CUTS]] + [shift(chosen[j], "rep", n_rep, j // CUTS) for j in range(CUTS, CUTS * n_rep)]

    sends = [fetched_weights(near_chip, queries, BF16)]
    sends += [partial_weights(matrices, queries, f, depth, BF16) for f in targets[1:]]
    others = [shift(x, "feat", n_feat, d + 1) for d, x in enumerate(sends)]
    own = partial_weights(matrices, queries, feat, depth, F32, *sends)

    for (hops, _, _), x in zip(middle[1:], packed[1:]):
        here.append(shift(after(x, *urgent, *sends), "shard", n_shard, hops))
        urgent = [here[-1]]
    last = [after(x, own) for x in packed[len(middle):len(middle) + len(final)]]

    mine = own_rows(goal, train, bulk, own)
    marks = [own, mine, *last]
    if extra:
        for d in range(1, n_group):
            flag = jnp.maximum(flag, shift(flag, "groups", n_group, d))

        def second_round(x):
            pair = jnp.concatenate([x, swap(x, "shard", n_shard, 2)])
            return [with_rep(pair), with_rep(swap(pair, "shard", n_shard, 1))]

        def no_round(x):
            empty = unwritten((2 * extra, columns), 2 * n_rep)
            return [[*empty[:n_rep]], [*empty[n_rep:]]]

        seconds = lax.cond(flag[0, 0] > 0, second_round, no_round, after(packed[-1], own))
        near = swap(stack([packed[-3], far], *sends), "shard", n_shard, 1)
        pairs = [stack([x, y], own) for x, y in zip(with_rep(packed[-3]), with_rep(after(far, own)))]
        firsts = [pairs, with_rep(after(near, own))]
        marks += [seconds[0][0], near, *pairs]

    mark = shift(after(jnp.zeros((8, LANES), I32), *marks), "rep", n_rep, 1)
    last = [shift(x, "shard", n_shard, last_hops) for x in last]
    ready = [with_rep(after(x, mark)) for x in here]
    high, low, *early = early_scores(
        own, others, mine, ready, middle, firsts, seconds, table, rows, n_feat, n_rep, n_shard, bulk, extra
    )

    def over_feat(shares):
        return [shares[0]] + [shift(shares[d], "feat", n_feat, d) for d in range(1, n_feat)]

    late = late_scores([with_rep(after(x, *early[1:])) for x in last], high, low, n_feat)
    return merge(table, over_feat(early), over_feat(late), n_shard)[None]


def solution(mesh):
    return jax.shard_map(
        body,
        mesh=mesh,
        in_specs=(
            P(("groups", "shard"), "feat"),
            P("groups"),
            P(("groups", "shard"), None, ("feat", "rep")),
            P("shard", None, ("feat", "rep")),
            P(),
            P(),
        ),
        out_specs=P(("groups", "shard"), ("feat", "rep"), None),
        check_vma=False,
    )
```

```python
import functools

import jax
import jax.numpy as jnp
from jax import lax
from jax.experimental import pallas as pl
from jax.experimental.pallas import tpu as pltpu
from jax.sharding import PartitionSpec as P

F32, BF16, I32 = jnp.float32, jnp.bfloat16, jnp.int32
VMEM = pl.BlockSpec(memory_space=pltpu.VMEM)
ANY = pl.BlockSpec(memory_space=pl.ANY)
HBM = pl.BlockSpec(memory_space=pltpu.HBM)
SMEM = pl.BlockSpec(memory_space=pltpu.SMEM)
PARAMS = pltpu.CompilerParams(vmem_limit_bytes=24 * 2**20)
FIRST = pltpu.CompilerParams(vmem_limit_bytes=60 * 2**20)
LANES = 128
CUTS = 8


def shift(x, axis, size, by):
    return lax.ppermute(x, axis, [(i, (i + by) % size) for i in range(size)])


def swap(x, axis, size, bit):
    return lax.ppermute(x, axis, [(i, i ^ bit) for i in range(size)])


def dot(a, b):
    return jnp.dot(a, b, preferred_element_type=F32)


def cost(flops, nbytes):
    return pl.CostEstimate(flops=1, bytes_accessed=1, transcendentals=0)


def after(x, *others):
    def kernel(*refs):
        pass

    return pl.pallas_call(
        kernel,
        in_specs=[ANY] * (1 + len(others)),
        out_specs=ANY,
        out_shape=jax.ShapeDtypeStruct(x.shape, x.dtype),
        input_output_aliases={0: 0},
        cost_estimate=cost(0, 0),
        compiler_params=PARAMS,
        name="after",
    )(x, *others)


def unwritten(shape, n):
    def kernel(*refs):
        pass

    return pl.pallas_call(
        kernel,
        out_specs=[ANY] * n,
        out_shape=[jax.ShapeDtypeStruct(shape, BF16)] * n,
        cost_estimate=cost(0, 0),
        compiler_params=PARAMS,
        name="unwritten",
    )()


def stack(parts, *others):
    size, width = parts[0].shape
    n = len(parts)

    def kernel(*refs):
        for j in range(n):
            refs[-1][j * size:(j + 1) * size, :] = refs[j][...]

    return pl.pallas_call(
        kernel,
        in_specs=[VMEM] * n + [ANY] * len(others),
        out_specs=VMEM,
        out_shape=jax.ShapeDtypeStruct((n * size, width), parts[0].dtype),
        cost_estimate=cost(0, 0),
        compiler_params=PARAMS,
        name="stack",
    )(*parts, *others)


def pick_queries(query_store, block_slot, pattern, n_group):
    local_blocks, block_rows, width = query_store.shape
    n_cluster, n_list = pattern.shape
    part = block_rows // n_group

    def kernel(pattern_ref, slot_ref, in_ref, *rest):
        outs, sem = rest[:-1], rest[-1]
        me, group = lax.axis_index("shard"), lax.axis_index("groups")
        copies = []
        for t, out in enumerate(outs):
            target = lax.rem(me + t, jnp.int32(n_cluster))
            found = jnp.int32(0)
            for k in range(n_list):
                slot = slot_ref[pattern_ref[target, k]]
                hit = (lax.div(slot, jnp.int32(local_blocks)) == me).astype(I32)
                found = found + hit * lax.rem(slot, jnp.int32(local_blocks))
            rows = pl.ds(pl.multiple_of(group * part, part), part)
            copies.append(pltpu.make_async_copy(in_ref.at[found, rows], out.at[0], sem.at[t]))
            copies[-1].start()
        for copy in copies:
            copy.wait()

    return pl.pallas_call(
        kernel,
        in_specs=[SMEM, SMEM, ANY],
        out_specs=[VMEM] * n_cluster,
        out_shape=[jax.ShapeDtypeStruct((1, part, width), BF16)] * n_cluster,
        scratch_shapes=[pltpu.SemaphoreType.DMA((n_cluster,))],
        cost_estimate=cost(0, 4 * n_cluster * part * width),
        compiler_params=FIRST,
        name="pick_queries",
    )(pattern, block_slot, query_store)


def join_queries(parts, block_slot, pattern, local_blocks, n_feat, n_rep, *others):
    n_group, n_cluster = len(parts), len(parts[0])
    _, part, width = parts[0][0].shape
    n_list = pattern.shape[1]
    total = n_list * n_group * part
    share = total // (n_feat * n_rep)
    unit = min(share, part)
    half = total // n_rep

    def kernel(pattern_ref, slot_ref, *refs):
        outs, rows_ref = refs[-1 - CUTS * n_rep:-1], refs[-1]
        me, group = lax.axis_index("shard"), lax.axis_index("groups")
        for k in range(n_list):
            owner = lax.div(slot_ref[pattern_ref[me, k]], jnp.int32(local_blocks))
            hops = lax.rem(me + (n_cluster - owner), jnp.int32(n_cluster))
            for d in range(n_group):
                origin = lax.rem(group + (n_group - d), jnp.int32(n_group))
                for h in range(n_cluster):
                    @pl.when(hops == h)
                    def _():
                        for u in range(part // unit):
                            first = (k * n_group + origin) * part + u * unit
                            chunk = lax.div(first, jnp.int32(share))
                            goal = lax.rem(chunk, jnp.int32(n_rep)) * n_feat + lax.div(chunk, jnp.int32(n_rep))
                            goal = pl.multiple_of(goal * share + lax.rem(first, jnp.int32(share)), unit)
                            rows_ref[pl.ds(goal, unit), :] = refs[d * n_cluster + h][0, u * unit:(u + 1) * unit, :]
        for r in range(n_rep):
            @pl.when(lax.axis_index("rep") == r)
            def _():
                for j, out in enumerate(outs):
                    at, first = ((r + j // CUTS) % n_rep) * half, (j % CUTS) * (width // CUTS)
                    out[...] = rows_ref[at:at + half, first:first + width // CUTS].T

    return pl.pallas_call(
        kernel,
        in_specs=[SMEM, SMEM] + [VMEM] * (n_group * n_cluster) + [ANY] * len(others),
        out_specs=[VMEM] * (CUTS * n_rep),
        out_shape=[jax.ShapeDtypeStruct((width // CUTS, half), BF16)] * (CUTS * n_rep),
        scratch_shapes=[pltpu.VMEM((total, width), BF16)],
        cost_estimate=cost(0, 4 * total * width),
        compiler_params=PARAMS,
        name="join_queries",
    )(pattern, block_slot, *[x for line in parts for x in line], *others)


def one_hot(goal_ref, base, size):
    index = lax.broadcasted_iota(I32, (size, LANES), 0) + base
    lines = range(goal_ref.shape[0])
    return jnp.concatenate([(index == goal_ref[a:a + 1, :]).astype(F32).astype(BF16) for a in lines], axis=1)


def select(goal_ref, train_ref, base, size):
    tile = 128 if size % 128 == 0 else size
    found = [dot(one_hot(goal_ref, base + at, tile), train_ref[...]).astype(BF16) for at in range(0, size, tile)]
    return jnp.concatenate(found)


def own_rows(goal, train, bulk, *others):
    rows, width = train.shape
    cuts = 4
    part = width // cuts

    def kernel(goal_ref, train_ref, *rest):
        out_ref, held, sem = rest[-3:]
        copies = [
            pltpu.make_async_copy(train_ref.at[:, c * part:(c + 1) * part], held.at[c], sem.at[c]) for c in range(cuts)
        ]
        for copy in copies:
            copy.start()
        pick = one_hot(goal_ref, lax.axis_index("shard") * bulk, bulk)
        for c, copy in enumerate(copies):
            copy.wait()
            out_ref[:, c * part:(c + 1) * part] = dot(pick, held[c]).astype(BF16)

    return pl.pallas_call(
        kernel,
        in_specs=[VMEM, HBM] + [ANY] * len(others),
        out_specs=VMEM,
        out_shape=jax.ShapeDtypeStruct((bulk, width), BF16),
        scratch_shapes=[pltpu.VMEM((cuts, rows, part), BF16), pltpu.SemaphoreType.DMA((cuts,))],
        cost_estimate=cost(2 * bulk * train.size, 2 * train.size),
        compiler_params=PARAMS,
        name="own_rows",
    )(goal, train, *others)


def pack_rows(train, ids, columns, bulk, extra, cuts):
    rows = train.shape[0]
    lines = rows // LANES
    n_shard = ids.shape[0] // lines

    def kernel(ids_ref, train_ref, *rest):
        outs, goal_ref = rest[:-1], rest[-1]
        me = lax.axis_index("shard")
        own = ids_ref[...]
        masks = [(own == c).astype(F32) for c in range(n_shard)]
        stacked = jnp.concatenate(masks, axis=0).astype(BF16)
        lane_from = lax.broadcasted_iota(I32, (LANES, LANES), 0)
        lane_to = lax.broadcasted_iota(I32, (LANES, LANES), 1)
        in_line = dot(stacked, (lane_from < lane_to).astype(F32).astype(BF16))
        line_sum = dot(stacked, jnp.ones((LANES, LANES), BF16)).astype(BF16)
        size = n_shard * lines
        to = lax.broadcasted_iota(I32, (size, size), 0)
        since = lax.broadcasted_iota(I32, (size, size), 1)
        same = (to // lines) == (since // lines)
        ahead = dot((same & (since < to)).astype(F32).astype(BF16), line_sum)
        whole = dot(same.astype(F32).astype(BF16), line_sum)
        rank = in_line + ahead
        goal = jnp.zeros((lines, LANES), F32)
        past = jnp.zeros((lines, LANES), F32)
        for c in range(n_shard):
            part = slice(c * lines, (c + 1) * lines)
            place = rank[part] + c * bulk
            if extra:
                surplus = n_shard * bulk + past + rank[part] - bulk
                place = jnp.where(rank[part] < bulk, place, surplus)
                past = past + jnp.floor((jnp.maximum(whole[part] - bulk, 0.0) + 15.0) * 0.0625) * 16.0
            goal = goal + masks[c] * place
        goal_ref[...] = goal.astype(I32)

        def fill(out, base):
            out[...] = select(goal_ref, train_ref, base, out.shape[0])

        for out, (hops, first, _) in zip(outs, cuts):
            fill(out, lax.rem(me + hops, jnp.int32(n_shard)) * bulk + first)
        for j, out in enumerate(outs[len(cuts):]):
            fill(out, n_shard * bulk + max(j - 1, 0) * extra)

    shapes = [jax.ShapeDtypeStruct((n, columns), BF16) for _, _, n in cuts]
    shapes += [jax.ShapeDtypeStruct((extra, columns), BF16)] * (3 if extra else 0)
    shapes += [jax.ShapeDtypeStruct((lines, LANES), I32)]
    packed = n_shard * bulk + 2 * extra
    return pl.pallas_call(
        kernel,
        grid=(1,),
        in_specs=[
            pl.BlockSpec((lines, LANES), lambda i: (lax.axis_index("shard"), 0)),
            pl.BlockSpec((rows, columns), lambda i: (0, lax.axis_index("rep"))),
        ],
        out_specs=[VMEM] * len(shapes),
        out_shape=shapes,
        cost_estimate=cost(2 * packed * rows * columns, 2 * (rows + packed) * columns),
        compiler_params=FIRST,
        name="pack_rows",
    )(ids, train)


def partial_weights(matrices, queries, block, depth, dtype, *others):
    width, total = matrices[0].shape[1], queries[0].shape[1]
    tile = 512 if depth % 512 == 0 else depth
    steps = depth // tile
    n = len(matrices)

    def kernel(block_ref, *refs):
        out_ref, held, sem = refs[-3:]
        first = pl.multiple_of(block_ref[0] * depth, depth)
        copies = []
        for i in range(steps):
            for j in range(n):
                source = refs[j].at[pl.ds(first + i * tile, tile)]
                copies.append(pltpu.make_async_copy(source, held.at[j, i], sem.at[i * n + j]))
        for copy in copies:
            copy.start()
        parts = [jnp.concatenate([r[...] for r in refs[n + CUTS * j:n + CUTS * (j + 1)]]) for j in range(n)]
        for i in range(steps):
            value = None
            for j in range(n):
                copies[i * n + j].wait()
                part = dot(held[j, i], parts[j])
                value = part if value is None else value + part
            out_ref[i * tile:(i + 1) * tile, :] = value.astype(dtype)

    return pl.pallas_call(
        kernel,
        in_specs=[SMEM] + [HBM] * n + [VMEM] * (CUTS * n) + [ANY] * len(others),
        out_specs=VMEM,
        out_shape=jax.ShapeDtypeStruct((depth, total), dtype),
        scratch_shapes=[pltpu.VMEM((n, steps, tile, width), BF16), pltpu.SemaphoreType.DMA((steps * n,))],
        cost_estimate=cost(2 * n * depth * width * total, 2 * n * depth * width + 4 * depth * total),
        compiler_params=PARAMS,
        name="partial_weights",
    )(jnp.reshape(block, (1,)).astype(I32), *matrices, *queries, *others)


def fetch(matrices, block, depth, *others):
    width = matrices[0].shape[1]
    n = len(matrices)
    cuts = 4

    def kernel(block_ref, *refs):
        outs, sem = refs[-1 - n:-1], refs[-1]
        first = pl.multiple_of(block_ref[0] * depth, depth)
        copies = []
        for j in range(n):
            for c in range(cuts):
                size = depth // cuts
                source = refs[j].at[pl.ds(first + c * size, size)]
                copies.append(
                    pltpu.make_async_copy(source, outs[j].at[c * size:(c + 1) * size], sem.at[j * cuts + c])
                )
        for copy in copies:
            copy.start()
        for copy in copies:
            copy.wait()

    return pl.pallas_call(
        kernel,
        in_specs=[SMEM] + [HBM] * n + [ANY] * len(others),
        out_specs=[VMEM] * n,
        out_shape=[jax.ShapeDtypeStruct((depth, width), BF16)] * n,
        scratch_shapes=[pltpu.SemaphoreType.DMA((n * cuts,))],
        cost_estimate=cost(0, 2 * n * depth * width),
        compiler_params=PARAMS,
        name="fetch",
    )(jnp.reshape(block, (1,)).astype(I32), *matrices, *others)


def fetched_weights(matrices, queries, dtype):
    depth = matrices[0].shape[0]
    total = queries[0].shape[1]
    tile = 512 if depth % 512 == 0 else depth
    n = len(matrices)

    def kernel(*refs):
        parts = [jnp.concatenate([r[...] for r in refs[n + CUTS * j:n + CUTS * (j + 1)]]) for j in range(n)]
        for at in range(0, depth, tile):
            value = None
            for j in range(n):
                part = dot(refs[j][at:at + tile, :], parts[j])
                value = part if value is None else value + part
            refs[-1][at:at + tile, :] = value.astype(dtype)

    return pl.pallas_call(
        kernel,
        in_specs=[VMEM] * ((1 + CUTS) * n),
        out_specs=VMEM,
        out_shape=jax.ShapeDtypeStruct((depth, total), dtype),
        cost_estimate=cost(2 * n * matrices[0].size * total, 2 * n * matrices[0].size),
        compiler_params=PARAMS,
        name="fetched_weights",
    )(*matrices, *queries)


def row_table(ids, lines, bulk, extra, *others):
    n_shard = ids.shape[0] // lines

    def kernel(ids_ref, *rest):
        table_ref, flag_ref = rest[-2:]
        me = lax.axis_index("shard")
        start = jnp.int32(0)
        most = jnp.int32(0)
        for s in range(n_shard):
            line = ids_ref[s * lines:(s + 1) * lines, :]

            def count(c):
                return jnp.sum((line == c).astype(I32))

            mine = count(me)
            before = jnp.int32(0)
            if extra:
                surplus = jnp.int32(0)
                for c in range(n_shard):
                    over = lax.div(jnp.maximum(count(c) - bulk, 0) + 15, jnp.int32(16)) * 16
                    before = before + jnp.where(c < me, over, 0)
                    surplus = surplus + over
                most = jnp.maximum(most, surplus)
            table_ref[s, 0] = start
            table_ref[s, 1] = jnp.minimum(mine, bulk)
            table_ref[s, 2] = lax.div(before, jnp.int32(16))
            table_ref[s, 3] = jnp.maximum(mine - bulk, 0)
            start = start + mine
        flag_ref[...] = jnp.full((8, LANES), (most > extra).astype(I32))

    return pl.pallas_call(
        kernel,
        in_specs=[VMEM] + [ANY] * len(others),
        out_specs=[SMEM, VMEM],
        out_shape=[jax.ShapeDtypeStruct((n_shard, 4), I32), jax.ShapeDtypeStruct((8, LANES), I32)],
        cost_estimate=cost(0, 4 * ids.size),
        compiler_params=PARAMS,
        name="row_table",
    )(ids, *others)


def put(acc, x, start, count=None):
    tiles, _, width = x.shape
    first, within = lax.div(start, jnp.int32(8)), lax.rem(start, jnp.int32(8))
    turned = pltpu.roll(x, within, 1)
    row = lax.broadcasted_iota(I32, (1, 8, width), 1)
    keep = row < within
    pieces = jnp.where(keep, jnp.concatenate([turned[:1], turned]), jnp.concatenate([turned, turned[-1:]]))
    if count is None:
        pieces = jnp.concatenate([jnp.where(keep, acc[pl.ds(first, 1)], turned[:1]), pieces[1:]])
    else:
        at = lax.broadcasted_iota(I32, (tiles + 1, 8, width), 0) * 8 + lax.broadcasted_iota(
            I32, (tiles + 1, 8, width), 1
        )
        pieces = jnp.where(
            (at >= within) & (at < within + count), pieces, acc[pl.ds(first, tiles + 1)]
        )
    acc[pl.ds(first, tiles + 1)] = pieces


def score(high_ref, low_ref, parts, rep):
    total = None
    for d, x in enumerate(parts):
        depth = x.shape[1]
        block = pl.ds(pl.multiple_of(lax.rem(rep + (len(parts) - d), jnp.int32(len(parts))) * depth, depth), depth)
        value = dot(x, high_ref[block, :]) + dot(x, low_ref[block, :])
        total = value if total is None else total + value
    return total.reshape(total.shape[0] // 8, 8, total.shape[1])


def for_feats(value, outs):
    n = len(outs)
    share = outs[0].shape[1]
    for f in range(n):
        @pl.when(lax.axis_index("feat") == f)
        def _():
            for d, out in enumerate(outs):
                at = ((f + d) % n) * share
                out[...] = value(slice(at, at + share)).astype(out.dtype)


def feat_shapes(rows, width, n_feat):
    share = (rows, width // n_feat)
    return [jax.ShapeDtypeStruct(share, F32)] + [jax.ShapeDtypeStruct(share, BF16)] * (n_feat - 1)


def early_scores(own, others, mine, pieces, cuts, firsts, seconds, table, rows, n_feat, n_rep, n_shard, bulk, extra):
    depth, width = own.shape
    columns = depth // n_rep
    n_other, n_piece = len(others), len(pieces)
    n_first = len(firsts) * n_rep
    last_hops = n_shard - 1

    def kernel(table_ref, *refs):
        own_ref, refs = refs[0], refs[1:]
        other_refs, refs = refs[:n_other], refs[n_other:]
        mine_ref, refs = refs[0], refs[1:]
        piece_refs = [refs[j * n_rep:(j + 1) * n_rep] for j in range(n_piece)]
        refs = refs[n_piece * n_rep:]
        first_refs, second_refs, refs = refs[:n_first], refs[n_first:2 * n_first], refs[2 * n_first:]
        high_ref, low_ref, outs, (scored, held, acc, sem) = refs[0], refs[1], refs[2:-4], refs[-4:]
        me, rep = lax.axis_index("shard"), lax.axis_index("rep")
        weight = own_ref[...]
        for ref in other_refs:
            weight = weight + ref[...].astype(F32)
        high = weight.astype(BF16)
        high_ref[...] = high
        low_ref[...] = (weight - high.astype(F32)).astype(BF16)

        scored[me] = score(high_ref, low_ref, [mine_ref[...]], jnp.int32(0))
        for parts, (hops, first, size) in zip(piece_refs, cuts):
            source = lax.rem(me + (n_shard - hops), jnp.int32(n_shard))
            scored[source, first // 8:(first + size) // 8] = score(high_ref, low_ref, [p[...] for p in parts], rep)
        last = lax.rem(me + (n_shard - last_hops), jnp.int32(n_shard))
        for s in range(n_shard):
            start = table_ref[s, 0]

            @pl.when(last != s)
            def _():
                put(acc, scored[s], start)

            if extra:
                @pl.when(table_ref[s, 3] > 0)
                def _():
                    apart = jnp.bitwise_xor(me, s)
                    rows_in = pl.ds(pl.multiple_of(lax.div(apart, jnp.int32(2)) * extra, extra), extra)
                    for odd in range(2):
                        @pl.when(jnp.bitwise_and(apart, 1) == odd)
                        def _():
                            copies = []
                            for j, refs in enumerate([first_refs, second_refs]):
                                for d in range(n_rep):
                                    goal = held.at[d, j * extra:(j + 1) * extra]
                                    which = refs[odd * n_rep + d].at[rows_in]
                                    copies.append(pltpu.make_async_copy(which, goal, sem.at[j * n_rep + d]))
                            for copy in copies:
                                copy.start()
                            for copy in copies:
                                copy.wait()
                    some = pl.ds(pl.multiple_of(table_ref[s, 2] * 16, 16), extra)
                    x = [held[d, some, :] for d in range(n_rep)]
                    put(acc, score(high_ref, low_ref, x, rep), start + table_ref[s, 1])
        for_feats(lambda at: acc[:rows // 8, :, at].reshape(rows, width // n_feat), outs)

    count = n_shard * bulk
    surplus = [x for parts in [*firsts, *seconds] for x in parts]
    return pl.pallas_call(
        kernel,
        in_specs=[SMEM] + [VMEM] * (2 + n_other + n_rep * n_piece) + [ANY] * len(surplus),
        out_specs=[VMEM] * (2 + n_feat),
        out_shape=[jax.ShapeDtypeStruct((depth, width), BF16)] * 2 + feat_shapes(rows, width, n_feat),
        scratch_shapes=[
            pltpu.VMEM((n_shard, bulk // 8, 8, width), F32),
            pltpu.VMEM((n_rep, 3 * extra + 16, columns), BF16),
            pltpu.VMEM(((rows + bulk + extra) // 8 + 2, 8, width), F32),
            pltpu.SemaphoreType.DMA((2 * n_rep,)),
        ],
        cost_estimate=cost(4 * count * depth * width, 10 * depth * width + count * (2 * depth + 4 * width)),
        compiler_params=PARAMS,
        name="early_scores",
    )(table, own, *others, mine, *[p for parts in pieces for p in parts], *surplus)


def late_scores(pieces, high, low, n_feat):
    n, n_rep = len(pieces), len(pieces[0])
    size = pieces[0][0].shape[0]
    rows = n * size
    width = high.shape[1]

    def kernel(high_ref, low_ref, *refs):
        part_refs, outs, acc = refs[:n * n_rep], refs[n * n_rep:-1], refs[-1]
        parts = [jnp.concatenate([part_refs[j * n_rep + d][...] for j in range(n)]) for d in range(n_rep)]
        y = score(high_ref, low_ref, parts, lax.axis_index("rep"))
        acc[...] = y.reshape(rows, width)
        for_feats(lambda at: acc[:, at], outs)

    return pl.pallas_call(
        kernel,
        in_specs=[VMEM] * (2 + n * n_rep),
        out_specs=[VMEM] * n_feat,
        out_shape=feat_shapes(rows, width, n_feat),
        scratch_shapes=[pltpu.VMEM((rows, width), F32)],
        cost_estimate=cost(4 * rows * high.size, 8 * rows * width),
        compiler_params=PARAMS,
        name="late_scores",
    )(high, low, *[p for parts in pieces for p in parts])


def merge(table, early, late, n_shard):
    rows, width = early[0].shape
    last_rows = late[0].shape[0]
    last_hops = n_shard - 1

    def kernel(table_ref, *refs):
        early_refs, late_refs = refs[:len(early)], refs[len(early):-2]
        out_ref, acc = refs[-2:]
        source = lax.rem(lax.axis_index("shard") + (n_shard - last_hops), jnp.int32(n_shard))

        def total(parts):
            value = parts[0][...]
            for ref in parts[1:]:
                value = value + ref[...].astype(F32)
            return value.reshape(value.shape[0] // 8, 8, width)

        acc[:rows // 8] = total(early_refs)
        put(acc, total(late_refs), table_ref[source, 0], table_ref[source, 1])
        out_ref[...] = acc[:rows // 8].reshape(rows, width).T

    return pl.pallas_call(
        kernel,
        in_specs=[SMEM] + [VMEM] * (len(early) + len(late)),
        out_specs=VMEM,
        out_shape=jax.ShapeDtypeStruct((width, rows), F32),
        scratch_shapes=[pltpu.VMEM(((rows + last_rows) // 8 + 2, 8, width), F32)],
        cost_estimate=cost(0, 8 * rows * width),
        compiler_params=PARAMS,
        name="merge",
    )(table, *early, *late)


def body(train, cluster_ids, precond, query_store, block_slot, pattern):
    n_group, n_shard = lax.axis_size("groups"), lax.axis_size("shard")
    n_feat, n_rep = lax.axis_size("feat"), lax.axis_size("rep")
    feat, rep = lax.axis_index("feat"), lax.axis_index("rep")
    rows = train.shape[0]
    lines = rows // LANES
    base = rows // n_shard
    columns = train.shape[1] // n_rep
    extra = base // 2 if n_shard == 4 else 0
    bulk = base if extra else base + base // 2
    ids = cluster_ids.reshape(-1, LANES)

    last_hops = n_shard - 1

    def with_rep(x):
        return [x] + [shift(x, "rep", n_rep, d) for d in range(1, n_rep)]

    matrices = with_rep(precond[0])

    picked = pick_queries(query_store, block_slot, pattern, n_group)
    pieces = [picked[0]] + [shift(picked[d], "shard", n_shard, d) for d in range(1, n_shard)]

    middle = [(d, 0, bulk) for d in range(1, last_hops)]
    part = 64 if bulk % 64 == 0 else bulk
    final = [(last_hops, at, part) for at in range(0, bulk, part)]
    *packed, goal = pack_rows(train, ids, columns, bulk, extra, middle + final)
    firsts, seconds = [], []
    parts = [pieces] + [[shift(x, "groups", n_group, d) for x in pieces] for d in range(1, n_group)]
    here = [shift(after(packed[0], *pieces[1:]), "shard", n_shard, 1)]
    urgent = [here[0]]
    if extra:
        far = swap(after(packed[-2], *pieces[1:]), "shard", n_shard, 2)
        urgent.append(far)
    sent_last = packed[len(middle):len(middle) + len(final)]
    last = [shift(after(sent_last[0], *pieces[1:]), "shard", n_shard, last_hops)]
    urgent.append(last[0])
    depth = n_rep * columns
    targets = [(feat + d) % n_feat for d in range(1, n_feat)]
    near_chip = fetch(matrices, targets[0], depth, *pieces[1:])

    table, flag = row_table(ids, lines, bulk, extra, *pieces[1:])
    chosen = join_queries(
        parts, block_slot, pattern, query_store.shape[0], n_feat, n_rep, *near_chip, flag
    )
    queries = [*chosen[:CUTS]] + [shift(chosen[j], "rep", n_rep, j // CUTS) for j in range(CUTS, CUTS * n_rep)]

    sends = [fetched_weights(near_chip, queries, BF16)]
    sends += [partial_weights(matrices, queries, f, depth, BF16) for f in targets[1:]]
    others = [shift(x, "feat", n_feat, d + 1) for d, x in enumerate(sends)]
    own = partial_weights(matrices, queries, feat, depth, F32, *sends)

    for (hops, _, _), x in zip(middle[1:], packed[1:]):
        here.append(shift(after(x, *urgent, *sends), "shard", n_shard, hops))
        urgent = [here[-1]]
    sent_last = [after(x, own) for x in sent_last[1:]]
    last_all = [with_rep(after(last[0], own))]

    mine = own_rows(goal, train, bulk, own)
    marks = [own, mine, *sent_last, *last_all[0][1:]]
    if extra:
        for d in range(1, n_group):
            flag = jnp.maximum(flag, shift(flag, "groups", n_group, d))

        def second_round(x):
            pair = jnp.concatenate([x, swap(x, "shard", n_shard, 2)])
            return [with_rep(pair), with_rep(swap(pair, "shard", n_shard, 1))]

        def no_round(x):
            empty = unwritten((2 * extra, columns), 2 * n_rep)
            return [[*empty[:n_rep]], [*empty[n_rep:]]]

        seconds = lax.cond(flag[0, 0] > 0, second_round, no_round, after(packed[-1], own))
        near = swap(stack([packed[-3], far], *sends), "shard", n_shard, 1)
        pairs = [stack([x, y], own) for x, y in zip(with_rep(packed[-3]), with_rep(after(far, own)))]
        firsts = [pairs, with_rep(after(near, own))]
        marks += [seconds[0][0], near, *pairs]

    mark = shift(after(jnp.zeros((8, LANES), I32), *marks), "rep", n_rep, 1)
    last += [shift(x, "shard", n_shard, last_hops) for x in sent_last]
    ready = [with_rep(after(x, mark)) for x in here]
    high, low, *early = early_scores(
        own, others, mine, ready, middle, firsts, seconds, table, rows, n_feat, n_rep, n_shard, bulk, extra
    )

    def over_feat(shares):
        return [shares[0]] + [shift(shares[d], "feat", n_feat, d) for d in range(1, n_feat)]

    last_all += [with_rep(after(x, *early[1:])) for x in last[1:]]
    late = late_scores(last_all, high, low, n_feat)
    return merge(table, over_feat(early), over_feat(late), n_shard)[None]


def solution(mesh):
    return jax.shard_map(
        body,
        mesh=mesh,
        in_specs=(
            P(("groups", "shard"), "feat"),
            P("groups"),
            P(("groups", "shard"), None, ("feat", "rep")),
            P("shard", None, ("feat", "rep")),
            P(),
            P(),
        ),
        out_specs=P(("groups", "shard"), ("feat", "rep"), None),
        check_vma=False,
    )
```

```python
import functools

import jax
import jax.numpy as jnp
from jax import lax
from jax.experimental import pallas as pl
from jax.experimental.pallas import tpu as pltpu
from jax.sharding import PartitionSpec as P

F32, BF16, I32 = jnp.float32, jnp.bfloat16, jnp.int32
VMEM = pl.BlockSpec(memory_space=pltpu.VMEM)
ANY = pl.BlockSpec(memory_space=pl.ANY)
HBM = pl.BlockSpec(memory_space=pltpu.HBM)
SMEM = pl.BlockSpec(memory_space=pltpu.SMEM)
PARAMS = pltpu.CompilerParams(vmem_limit_bytes=24 * 2**20)
FIRST = pltpu.CompilerParams(vmem_limit_bytes=60 * 2**20)
LANES = 128
CUTS = 8


def shift(x, axis, size, by):
    return lax.ppermute(x, axis, [(i, (i + by) % size) for i in range(size)])


def swap(x, axis, size, bit):
    return lax.ppermute(x, axis, [(i, i ^ bit) for i in range(size)])


def dot(a, b):
    return jnp.dot(a, b, preferred_element_type=F32)


def cost(flops, nbytes):
    return pl.CostEstimate(flops=1, bytes_accessed=1, transcendentals=0)


def after(x, *others):
    def kernel(*refs):
        pass

    return pl.pallas_call(
        kernel,
        in_specs=[ANY] * (1 + len(others)),
        out_specs=ANY,
        out_shape=jax.ShapeDtypeStruct(x.shape, x.dtype),
        input_output_aliases={0: 0},
        cost_estimate=cost(0, 0),
        compiler_params=PARAMS,
        name="after",
    )(x, *others)


def unwritten(shape, n):
    def kernel(*refs):
        pass

    return pl.pallas_call(
        kernel,
        out_specs=[ANY] * n,
        out_shape=[jax.ShapeDtypeStruct(shape, BF16)] * n,
        cost_estimate=cost(0, 0),
        compiler_params=PARAMS,
        name="unwritten",
    )()


def stack(parts, *others):
    size, width = parts[0].shape
    n = len(parts)

    def kernel(*refs):
        for j in range(n):
            refs[-1][j * size:(j + 1) * size, :] = refs[j][...]

    return pl.pallas_call(
        kernel,
        in_specs=[VMEM] * n + [ANY] * len(others),
        out_specs=VMEM,
        out_shape=jax.ShapeDtypeStruct((n * size, width), parts[0].dtype),
        cost_estimate=cost(0, 0),
        compiler_params=PARAMS,
        name="stack",
    )(*parts, *others)


def pick_queries(query_store, block_slot, pattern, n_group):
    local_blocks, block_rows, width = query_store.shape
    n_cluster, n_list = pattern.shape
    part = block_rows // n_group

    def kernel(pattern_ref, slot_ref, in_ref, *rest):
        outs, sem = rest[:-1], rest[-1]
        me, group = lax.axis_index("shard"), lax.axis_index("groups")
        copies = []
        for t, out in enumerate(outs):
            target = lax.rem(me + t, jnp.int32(n_cluster))
            found = jnp.int32(0)
            for k in range(n_list):
                slot = slot_ref[pattern_ref[target, k]]
                hit = (lax.div(slot, jnp.int32(local_blocks)) == me).astype(I32)
                found = found + hit * lax.rem(slot, jnp.int32(local_blocks))
            rows = pl.ds(pl.multiple_of(group * part, part), part)
            copies.append(pltpu.make_async_copy(in_ref.at[found, rows], out.at[0], sem.at[t]))
            copies[-1].start()
        for copy in copies:
            copy.wait()

    return pl.pallas_call(
        kernel,
        in_specs=[SMEM, SMEM, ANY],
        out_specs=[VMEM] * n_cluster,
        out_shape=[jax.ShapeDtypeStruct((1, part, width), BF16)] * n_cluster,
        scratch_shapes=[pltpu.SemaphoreType.DMA((n_cluster,))],
        cost_estimate=cost(0, 4 * n_cluster * part * width),
        compiler_params=FIRST,
        name="pick_queries",
    )(pattern, block_slot, query_store)


def join_queries(parts, block_slot, pattern, local_blocks, n_feat, n_rep, *others):
    n_group, n_cluster = len(parts), len(parts[0])
    _, part, width = parts[0][0].shape
    n_list = pattern.shape[1]
    total = n_list * n_group * part
    share = total // (n_feat * n_rep)
    unit = min(share, part)
    half = total // n_rep

    def kernel(pattern_ref, slot_ref, *refs):
        outs, rows_ref = refs[-1 - CUTS * n_rep:-1], refs[-1]
        me, group = lax.axis_index("shard"), lax.axis_index("groups")
        for k in range(n_list):
            owner = lax.div(slot_ref[pattern_ref[me, k]], jnp.int32(local_blocks))
            hops = lax.rem(me + (n_cluster - owner), jnp.int32(n_cluster))
            for d in range(n_group):
                origin = lax.rem(group + (n_group - d), jnp.int32(n_group))
                for h in range(n_cluster):
                    @pl.when(hops == h)
                    def _():
                        for u in range(part // unit):
                            first = (k * n_group + origin) * part + u * unit
                            chunk = lax.div(first, jnp.int32(share))
                            goal = lax.rem(chunk, jnp.int32(n_rep)) * n_feat + lax.div(chunk, jnp.int32(n_rep))
                            goal = pl.multiple_of(goal * share + lax.rem(first, jnp.int32(share)), unit)
                            rows_ref[pl.ds(goal, unit), :] = refs[d * n_cluster + h][0, u * unit:(u + 1) * unit, :]
        for r in range(n_rep):
            @pl.when(lax.axis_index("rep") == r)
            def _():
                for j, out in enumerate(outs):
                    at, first = ((r + j // CUTS) % n_rep) * half, (j % CUTS) * (width // CUTS)
                    out[...] = rows_ref[at:at + half, first:first + width // CUTS].T

    return pl.pallas_call(
        kernel,
        in_specs=[SMEM, SMEM] + [VMEM] * (n_group * n_cluster) + [ANY] * len(others),
        out_specs=[VMEM] * (CUTS * n_rep),
        out_shape=[jax.ShapeDtypeStruct((width // CUTS, half), BF16)] * (CUTS * n_rep),
        scratch_shapes=[pltpu.VMEM((total, width), BF16)],
        cost_estimate=cost(0, 4 * total * width),
        compiler_params=PARAMS,
        name="join_queries",
    )(pattern, block_slot, *[x for line in parts for x in line], *others)


def one_hot(goal_ref, base, size):
    index = lax.broadcasted_iota(I32, (size, LANES), 0) + base
    lines = range(goal_ref.shape[0])
    return jnp.concatenate([(index == goal_ref[a:a + 1, :]).astype(F32).astype(BF16) for a in lines], axis=1)


def select(goal_ref, train_ref, base, size):
    tile = 128 if size % 128 == 0 else size
    found = [dot(one_hot(goal_ref, base + at, tile), train_ref[...]).astype(BF16) for at in range(0, size, tile)]
    return jnp.concatenate(found)


def own_rows(goal, train, bulk, *others):
    rows, width = train.shape
    cuts = 4
    part = width // cuts

    def kernel(goal_ref, train_ref, *rest):
        out_ref, held, sem = rest[-3:]
        copies = [
            pltpu.make_async_copy(train_ref.at[:, c * part:(c + 1) * part], held.at[c], sem.at[c]) for c in range(cuts)
        ]
        for copy in copies:
            copy.start()
        pick = one_hot(goal_ref, lax.axis_index("shard") * bulk, bulk)
        for c, copy in enumerate(copies):
            copy.wait()
            out_ref[:, c * part:(c + 1) * part] = dot(pick, held[c]).astype(BF16)

    return pl.pallas_call(
        kernel,
        in_specs=[VMEM, HBM] + [ANY] * len(others),
        out_specs=VMEM,
        out_shape=jax.ShapeDtypeStruct((bulk, width), BF16),
        scratch_shapes=[pltpu.VMEM((cuts, rows, part), BF16), pltpu.SemaphoreType.DMA((cuts,))],
        cost_estimate=cost(2 * bulk * train.size, 2 * train.size),
        compiler_params=PARAMS,
        name="own_rows",
    )(goal, train, *others)


def pack_rows(train, ids, columns, bulk, extra, cuts):
    rows = train.shape[0]
    lines = rows // LANES
    n_shard = ids.shape[0] // lines

    def kernel(ids_ref, train_ref, *rest):
        outs, goal_ref = rest[:-1], rest[-1]
        me = lax.axis_index("shard")
        own = ids_ref[...]
        masks = [(own == c).astype(F32) for c in range(n_shard)]
        stacked = jnp.concatenate(masks, axis=0).astype(BF16)
        lane_from = lax.broadcasted_iota(I32, (LANES, LANES), 0)
        lane_to = lax.broadcasted_iota(I32, (LANES, LANES), 1)
        in_line = dot(stacked, (lane_from < lane_to).astype(F32).astype(BF16))
        line_sum = dot(stacked, jnp.ones((LANES, LANES), BF16)).astype(BF16)
        size = n_shard * lines
        to = lax.broadcasted_iota(I32, (size, size), 0)
        since = lax.broadcasted_iota(I32, (size, size), 1)
        same = (to // lines) == (since // lines)
        ahead = dot((same & (since < to)).astype(F32).astype(BF16), line_sum)
        whole = dot(same.astype(F32).astype(BF16), line_sum)
        rank = in_line + ahead
        goal = jnp.zeros((lines, LANES), F32)
        past = jnp.zeros((lines, LANES), F32)
        for c in range(n_shard):
            part = slice(c * lines, (c + 1) * lines)
            place = rank[part] + c * bulk
            if extra:
                surplus = n_shard * bulk + past + rank[part] - bulk
                place = jnp.where(rank[part] < bulk, place, surplus)
                past = past + jnp.floor((jnp.maximum(whole[part] - bulk, 0.0) + 15.0) * 0.0625) * 16.0
            goal = goal + masks[c] * place
        goal_ref[...] = goal.astype(I32)

        def fill(out, base):
            out[...] = select(goal_ref, train_ref, base, out.shape[0])

        for out, (hops, first, _) in zip(outs, cuts):
            fill(out, lax.rem(me + hops, jnp.int32(n_shard)) * bulk + first)
        for j, out in enumerate(outs[len(cuts):]):
            fill(out, n_shard * bulk + max(j - 1, 0) * extra)

    shapes = [jax.ShapeDtypeStruct((n, columns), BF16) for _, _, n in cuts]
    shapes += [jax.ShapeDtypeStruct((extra, columns), BF16)] * (3 if extra else 0)
    shapes += [jax.ShapeDtypeStruct((lines, LANES), I32)]
    packed = n_shard * bulk + 2 * extra
    return pl.pallas_call(
        kernel,
        grid=(1,),
        in_specs=[
            pl.BlockSpec((lines, LANES), lambda i: (lax.axis_index("shard"), 0)),
            pl.BlockSpec((rows, columns), lambda i: (0, lax.axis_index("rep"))),
        ],
        out_specs=[VMEM] * len(shapes),
        out_shape=shapes,
        cost_estimate=cost(2 * packed * rows * columns, 2 * (rows + packed) * columns),
        compiler_params=FIRST,
        name="pack_rows",
    )(ids, train)


def partial_weights(matrices, queries, block, depth, dtype, *others):
    width, total = matrices[0].shape[1], queries[0].shape[1]
    tile = 512 if depth % 512 == 0 else depth
    steps = depth // tile
    n = len(matrices)

    def kernel(block_ref, *refs):
        out_ref, held, sem = refs[-3:]
        first = pl.multiple_of(block_ref[0] * depth, depth)
        copies = []
        for i in range(steps):
            for j in range(n):
                source = refs[j].at[pl.ds(first + i * tile, tile)]
                copies.append(pltpu.make_async_copy(source, held.at[j, i], sem.at[i * n + j]))
        for copy in copies:
            copy.start()
        parts = [jnp.concatenate([r[...] for r in refs[n + CUTS * j:n + CUTS * (j + 1)]]) for j in range(n)]
        for i in range(steps):
            value = None
            for j in range(n):
                copies[i * n + j].wait()
                part = dot(held[j, i], parts[j])
                value = part if value is None else value + part
            out_ref[i * tile:(i + 1) * tile, :] = value.astype(dtype)

    return pl.pallas_call(
        kernel,
        in_specs=[SMEM] + [HBM] * n + [VMEM] * (CUTS * n) + [ANY] * len(others),
        out_specs=VMEM,
        out_shape=jax.ShapeDtypeStruct((depth, total), dtype),
        scratch_shapes=[pltpu.VMEM((n, steps, tile, width), BF16), pltpu.SemaphoreType.DMA((steps * n,))],
        cost_estimate=cost(2 * n * depth * width * total, 2 * n * depth * width + 4 * depth * total),
        compiler_params=PARAMS,
        name="partial_weights",
    )(jnp.reshape(block, (1,)).astype(I32), *matrices, *queries, *others)


def fetch(matrices, block, depth, *others):
    width = matrices[0].shape[1]
    n = len(matrices)
    cuts = 4

    def kernel(block_ref, *refs):
        outs, sem = refs[-1 - n:-1], refs[-1]
        first = pl.multiple_of(block_ref[0] * depth, depth)
        copies = []
        for j in range(n):
            for c in range(cuts):
                size = depth // cuts
                source = refs[j].at[pl.ds(first + c * size, size)]
                copies.append(
                    pltpu.make_async_copy(source, outs[j].at[c * size:(c + 1) * size], sem.at[j * cuts + c])
                )
        for copy in copies:
            copy.start()
        for copy in copies:
            copy.wait()

    return pl.pallas_call(
        kernel,
        in_specs=[SMEM] + [HBM] * n + [ANY] * len(others),
        out_specs=[VMEM] * n,
        out_shape=[jax.ShapeDtypeStruct((depth, width), BF16)] * n,
        scratch_shapes=[pltpu.SemaphoreType.DMA((n * cuts,))],
        cost_estimate=cost(0, 2 * n * depth * width),
        compiler_params=PARAMS,
        name="fetch",
    )(jnp.reshape(block, (1,)).astype(I32), *matrices, *others)


def fetched_weights(matrices, queries, dtype):
    depth = matrices[0].shape[0]
    total = queries[0].shape[1]
    tile = 512 if depth % 512 == 0 else depth
    n = len(matrices)

    def kernel(*refs):
        parts = [jnp.concatenate([r[...] for r in refs[n + CUTS * j:n + CUTS * (j + 1)]]) for j in range(n)]
        for at in range(0, depth, tile):
            value = None
            for j in range(n):
                part = dot(refs[j][at:at + tile, :], parts[j])
                value = part if value is None else value + part
            refs[-1][at:at + tile, :] = value.astype(dtype)

    return pl.pallas_call(
        kernel,
        in_specs=[VMEM] * ((1 + CUTS) * n),
        out_specs=VMEM,
        out_shape=jax.ShapeDtypeStruct((depth, total), dtype),
        cost_estimate=cost(2 * n * matrices[0].size * total, 2 * n * matrices[0].size),
        compiler_params=PARAMS,
        name="fetched_weights",
    )(*matrices, *queries)


def row_table(ids, lines, bulk, extra, *others):
    n_shard = ids.shape[0] // lines

    def kernel(ids_ref, *rest):
        table_ref, flag_ref = rest[-2:]
        me = lax.axis_index("shard")
        start = jnp.int32(0)
        most = jnp.int32(0)
        for s in range(n_shard):
            line = ids_ref[s * lines:(s + 1) * lines, :]

            def count(c):
                return jnp.sum((line == c).astype(I32))

            mine = count(me)
            before = jnp.int32(0)
            if extra:
                surplus = jnp.int32(0)
                for c in range(n_shard):
                    over = lax.div(jnp.maximum(count(c) - bulk, 0) + 15, jnp.int32(16)) * 16
                    before = before + jnp.where(c < me, over, 0)
                    surplus = surplus + over
                most = jnp.maximum(most, surplus)
            table_ref[s, 0] = start
            table_ref[s, 1] = jnp.minimum(mine, bulk)
            table_ref[s, 2] = lax.div(before, jnp.int32(16))
            table_ref[s, 3] = jnp.maximum(mine - bulk, 0)
            start = start + mine
        flag_ref[...] = jnp.full((8, LANES), (most > extra).astype(I32))

    return pl.pallas_call(
        kernel,
        in_specs=[VMEM] + [ANY] * len(others),
        out_specs=[SMEM, VMEM],
        out_shape=[jax.ShapeDtypeStruct((n_shard, 4), I32), jax.ShapeDtypeStruct((8, LANES), I32)],
        cost_estimate=cost(0, 4 * ids.size),
        compiler_params=PARAMS,
        name="row_table",
    )(ids, *others)


def put(acc, x, start, count=None):
    tiles, _, width = x.shape
    first, within = lax.div(start, jnp.int32(8)), lax.rem(start, jnp.int32(8))
    turned = pltpu.roll(x, within, 1)
    row = lax.broadcasted_iota(I32, (1, 8, width), 1)
    keep = row < within
    pieces = jnp.where(keep, jnp.concatenate([turned[:1], turned]), jnp.concatenate([turned, turned[-1:]]))
    if count is None:
        pieces = jnp.concatenate([jnp.where(keep, acc[pl.ds(first, 1)], turned[:1]), pieces[1:]])
    else:
        at = lax.broadcasted_iota(I32, (tiles + 1, 8, width), 0) * 8 + lax.broadcasted_iota(
            I32, (tiles + 1, 8, width), 1
        )
        pieces = jnp.where(
            (at >= within) & (at < within + count), pieces, acc[pl.ds(first, tiles + 1)]
        )
    acc[pl.ds(first, tiles + 1)] = pieces


def score(weight_ref, parts, rep):
    total = None
    for d, x in enumerate(parts):
        depth = x.shape[1]
        block = pl.ds(pl.multiple_of(lax.rem(rep + (len(parts) - d), jnp.int32(len(parts))) * depth, depth), depth)
        value = dot(x, weight_ref[block, :])
        total = value if total is None else total + value
    width = total.shape[1] // 2
    total = total[:, :width] + total[:, width:]
    return total.reshape(total.shape[0] // 8, 8, width)


def for_feats(value, outs):
    n = len(outs)
    share = outs[0].shape[1]
    for f in range(n):
        @pl.when(lax.axis_index("feat") == f)
        def _():
            for d, out in enumerate(outs):
                at = ((f + d) % n) * share
                out[...] = value(slice(at, at + share)).astype(out.dtype)


def feat_shapes(rows, width, n_feat):
    share = (rows, width // n_feat)
    return [jax.ShapeDtypeStruct(share, F32)] + [jax.ShapeDtypeStruct(share, BF16)] * (n_feat - 1)


def early_scores(own, others, mine, pieces, cuts, firsts, seconds, table, rows, n_feat, n_rep, n_shard, bulk, extra):
    depth, width = own.shape
    columns = depth // n_rep
    n_other, n_piece = len(others), len(pieces)
    n_first = len(firsts) * n_rep
    last_hops = n_shard - 1

    def kernel(table_ref, *refs):
        own_ref, refs = refs[0], refs[1:]
        other_refs, refs = refs[:n_other], refs[n_other:]
        mine_ref, refs = refs[0], refs[1:]
        piece_refs = [refs[j * n_rep:(j + 1) * n_rep] for j in range(n_piece)]
        refs = refs[n_piece * n_rep:]
        first_refs, second_refs, refs = refs[:n_first], refs[n_first:2 * n_first], refs[2 * n_first:]
        weight_ref, outs, (scored, held, acc, sem) = refs[0], refs[1:-4], refs[-4:]
        me, rep = lax.axis_index("shard"), lax.axis_index("rep")
        weight = own_ref[...]
        for ref in other_refs:
            weight = weight + ref[...].astype(F32)
        high = weight.astype(BF16)
        weight_ref[:, :width] = high
        weight_ref[:, width:] = (weight - high.astype(F32)).astype(BF16)

        scored[me] = score(weight_ref, [mine_ref[...]], jnp.int32(0))
        for parts, (hops, first, size) in zip(piece_refs, cuts):
            source = lax.rem(me + (n_shard - hops), jnp.int32(n_shard))
            scored[source, first // 8:(first + size) // 8] = score(weight_ref, [p[...] for p in parts], rep)
        last = lax.rem(me + (n_shard - last_hops), jnp.int32(n_shard))
        for s in range(n_shard):
            start = table_ref[s, 0]

            @pl.when(last != s)
            def _():
                put(acc, scored[s], start)

            if extra:
                @pl.when(table_ref[s, 3] > 0)
                def _():
                    apart = jnp.bitwise_xor(me, s)
                    rows_in = pl.ds(pl.multiple_of(lax.div(apart, jnp.int32(2)) * extra, extra), extra)
                    for odd in range(2):
                        @pl.when(jnp.bitwise_and(apart, 1) == odd)
                        def _():
                            copies = []
                            for j, refs in enumerate([first_refs, second_refs]):
                                for d in range(n_rep):
                                    goal = held.at[d, j * extra:(j + 1) * extra]
                                    which = refs[odd * n_rep + d].at[rows_in]
                                    copies.append(pltpu.make_async_copy(which, goal, sem.at[j * n_rep + d]))
                            for copy in copies:
                                copy.start()
                            for copy in copies:
                                copy.wait()
                    some = pl.ds(pl.multiple_of(table_ref[s, 2] * 16, 16), extra)
                    x = [held[d, some, :] for d in range(n_rep)]
                    put(acc, score(weight_ref, x, rep), start + table_ref[s, 1])
        for_feats(lambda at: acc[:rows // 8, :, at].reshape(rows, width // n_feat), outs)

    count = n_shard * bulk
    surplus = [x for parts in [*firsts, *seconds] for x in parts]
    return pl.pallas_call(
        kernel,
        in_specs=[SMEM] + [VMEM] * (2 + n_other + n_rep * n_piece) + [ANY] * len(surplus),
        out_specs=[VMEM] * (1 + n_feat),
        out_shape=[jax.ShapeDtypeStruct((depth, 2 * width), BF16)] + feat_shapes(rows, width, n_feat),
        scratch_shapes=[
            pltpu.VMEM((n_shard, bulk // 8, 8, width), F32),
            pltpu.VMEM((n_rep, 3 * extra + 16, columns), BF16),
            pltpu.VMEM(((rows + bulk + extra) // 8 + 2, 8, width), F32),
            pltpu.SemaphoreType.DMA((2 * n_rep,)),
        ],
        cost_estimate=cost(4 * count * depth * width, 10 * depth * width + count * (2 * depth + 4 * width)),
        compiler_params=PARAMS,
        name="early_scores",
    )(table, own, *others, mine, *[p for parts in pieces for p in parts], *surplus)


def late_scores(pieces, weight, n_feat):
    n, n_rep = len(pieces), len(pieces[0])
    rows = sum(parts[0].shape[0] for parts in pieces)
    width = weight.shape[1] // 2

    def kernel(weight_ref, *refs):
        part_refs, outs, acc = refs[:n * n_rep], refs[n * n_rep:-1], refs[-1]
        parts = [jnp.concatenate([part_refs[j * n_rep + d][...] for j in range(n)]) for d in range(n_rep)]
        acc[...] = score(weight_ref, parts, lax.axis_index("rep")).reshape(rows, width)
        for_feats(lambda at: acc[:, at], outs)

    return pl.pallas_call(
        kernel,
        in_specs=[VMEM] * (1 + n * n_rep),
        out_specs=[VMEM] * n_feat,
        out_shape=feat_shapes(rows, width, n_feat),
        scratch_shapes=[pltpu.VMEM((rows, width), F32)],
        cost_estimate=cost(4 * rows * weight.size, 8 * rows * width),
        compiler_params=PARAMS,
        name="late_scores",
    )(weight, *[p for parts in pieces for p in parts])


def merge(table, early, late, n_shard):
    rows, width = early[0].shape
    last_rows = late[0].shape[0]
    last_hops = n_shard - 1

    def kernel(table_ref, *refs):
        early_refs, late_refs = refs[:len(early)], refs[len(early):-2]
        out_ref, acc = refs[-2:]
        source = lax.rem(lax.axis_index("shard") + (n_shard - last_hops), jnp.int32(n_shard))

        def total(parts):
            value = parts[0][...]
            for ref in parts[1:]:
                value = value + ref[...].astype(F32)
            return value.reshape(value.shape[0] // 8, 8, width)

        acc[:rows // 8] = total(early_refs)
        put(acc, total(late_refs), table_ref[source, 0], table_ref[source, 1])
        out_ref[...] = acc[:rows // 8].reshape(rows, width).T

    return pl.pallas_call(
        kernel,
        in_specs=[SMEM] + [VMEM] * (len(early) + len(late)),
        out_specs=VMEM,
        out_shape=jax.ShapeDtypeStruct((width, rows), F32),
        scratch_shapes=[pltpu.VMEM(((rows + last_rows) // 8 + 2, 8, width), F32)],
        cost_estimate=cost(0, 8 * rows * width),
        compiler_params=PARAMS,
        name="merge",
    )(table, *early, *late)


def body(train, cluster_ids, precond, query_store, block_slot, pattern):
    n_group, n_shard = lax.axis_size("groups"), lax.axis_size("shard")
    n_feat, n_rep = lax.axis_size("feat"), lax.axis_size("rep")
    feat, rep = lax.axis_index("feat"), lax.axis_index("rep")
    rows = train.shape[0]
    lines = rows // LANES
    base = rows // n_shard
    columns = train.shape[1] // n_rep
    extra = base // 2 if n_shard == 4 else 0
    bulk = base if extra else base + base // 2
    ids = cluster_ids.reshape(-1, LANES)

    last_hops = n_shard - 1

    def with_rep(x):
        return [x] + [shift(x, "rep", n_rep, d) for d in range(1, n_rep)]

    matrices = with_rep(precond[0])

    picked = pick_queries(query_store, block_slot, pattern, n_group)
    pieces = [picked[0]] + [shift(picked[d], "shard", n_shard, d) for d in range(1, n_shard)]

    middle = [(d, 0, bulk) for d in range(1, last_hops)]
    part = 64 if bulk % 64 == 0 else bulk // 2
    final = [(last_hops, at, part) for at in range(0, bulk, part)]
    *packed, goal = pack_rows(train, ids, columns, bulk, extra, middle + final)
    firsts, seconds = [], []
    parts = [pieces] + [[shift(x, "groups", n_group, d) for x in pieces] for d in range(1, n_group)]
    here = [shift(after(packed[0], *pieces[1:]), "shard", n_shard, 1)]
    urgent = [here[0]]
    if extra:
        far = swap(after(packed[-2], *pieces[1:]), "shard", n_shard, 2)
        urgent.append(far)
    sent_last = packed[len(middle):len(middle) + len(final)]
    last = [shift(after(sent_last[0], *pieces[1:]), "shard", n_shard, last_hops)]
    urgent.append(last[0])
    depth = n_rep * columns
    targets = [(feat + d) % n_feat for d in range(1, n_feat)]
    near_chip = fetch(matrices, targets[0], depth, *pieces[1:])

    table, flag = row_table(ids, lines, bulk, extra, *pieces[1:])
    chosen = join_queries(
        parts, block_slot, pattern, query_store.shape[0], n_feat, n_rep, *near_chip, flag
    )
    queries = [*chosen[:CUTS]] + [shift(chosen[j], "rep", n_rep, j // CUTS) for j in range(CUTS, CUTS * n_rep)]

    sends = [fetched_weights(near_chip, queries, BF16)]
    sends += [partial_weights(matrices, queries, f, depth, BF16) for f in targets[1:]]
    others = [shift(x, "feat", n_feat, d + 1) for d, x in enumerate(sends)]
    own = partial_weights(matrices, queries, feat, depth, F32, *sends)

    for (hops, _, _), x in zip(middle[1:], packed[1:]):
        here.append(shift(after(x, *urgent, *sends), "shard", n_shard, hops))
        urgent = [here[-1]]
    sent_last = [after(x, own) for x in sent_last[1:]]
    last_all = [with_rep(after(last[0], own))]

    mine = own_rows(goal, train, bulk, own)
    marks = [own, mine, *sent_last, *last_all[0][1:]]
    if extra:
        for d in range(1, n_group):
            flag = jnp.maximum(flag, shift(flag, "groups", n_group, d))

        def second_round(x):
            pair = jnp.concatenate([x, swap(x, "shard", n_shard, 2)])
            return [with_rep(pair), with_rep(swap(pair, "shard", n_shard, 1))]

        def no_round(x):
            empty = unwritten((2 * extra, columns), 2 * n_rep)
            return [[*empty[:n_rep]], [*empty[n_rep:]]]

        seconds = lax.cond(flag[0, 0] > 0, second_round, no_round, after(packed[-1], own))
        near = swap(stack([packed[-3], far], *sends), "shard", n_shard, 1)
        pairs = [stack([x, y], own) for x, y in zip(with_rep(packed[-3]), with_rep(after(far, own)))]
        firsts = [pairs, with_rep(after(near, own))]
        marks += [seconds[0][0], near, *pairs]

    mark = shift(after(jnp.zeros((8, LANES), I32), *marks), "rep", n_rep, 1)
    last += [shift(x, "shard", n_shard, last_hops) for x in sent_last]
    ready = [with_rep(after(x, mark)) for x in here]
    weight, *early = early_scores(
        own, others, mine, ready, middle, firsts, seconds, table, rows, n_feat, n_rep, n_shard, bulk, extra
    )

    def over_feat(shares):
        return [shares[0]] + [shift(shares[d], "feat", n_feat, d) for d in range(1, n_feat)]

    last_all += [with_rep(after(x, *early[1:])) for x in last[1:]]
    late = late_scores(last_all, weight, n_feat)
    return merge(table, over_feat(early), over_feat(late), n_shard)[None]


def solution(mesh):
    return jax.shard_map(
        body,
        mesh=mesh,
        in_specs=(
            P(("groups", "shard"), "feat"),
            P("groups"),
            P(("groups", "shard"), None, ("feat", "rep")),
            P("shard", None, ("feat", "rep")),
            P(),
            P(),
        ),
        out_specs=P(("groups", "shard"), ("feat", "rep"), None),
        check_vma=False,
    )
```

```python
import functools

import jax
import jax.numpy as jnp
from jax import lax
from jax.experimental import pallas as pl
from jax.experimental.pallas import tpu as pltpu
from jax.sharding import PartitionSpec as P

F32, BF16, I32 = jnp.float32, jnp.bfloat16, jnp.int32
VMEM = pl.BlockSpec(memory_space=pltpu.VMEM)
ANY = pl.BlockSpec(memory_space=pl.ANY)
HBM = pl.BlockSpec(memory_space=pltpu.HBM)
SMEM = pl.BlockSpec(memory_space=pltpu.SMEM)
PARAMS = pltpu.CompilerParams(vmem_limit_bytes=24 * 2**20)
WIDE = pltpu.CompilerParams(vmem_limit_bytes=32 * 2**20)
FIRST = pltpu.CompilerParams(vmem_limit_bytes=60 * 2**20)
LANES = 128
CUTS = 8


def shift(x, axis, size, by):
    return lax.ppermute(x, axis, [(i, (i + by) % size) for i in range(size)])


def swap(x, axis, size, bit):
    return lax.ppermute(x, axis, [(i, i ^ bit) for i in range(size)])


def dot(a, b):
    return jnp.dot(a, b, preferred_element_type=F32)


def cost(flops, nbytes):
    return pl.CostEstimate(flops=1, bytes_accessed=1, transcendentals=0)


def after(x, *others):
    def kernel(*refs):
        pass

    return pl.pallas_call(
        kernel,
        in_specs=[ANY] * (1 + len(others)),
        out_specs=ANY,
        out_shape=jax.ShapeDtypeStruct(x.shape, x.dtype),
        input_output_aliases={0: 0},
        cost_estimate=cost(0, 0),
        compiler_params=PARAMS,
        name="after",
    )(x, *others)


def unwritten(shape, n):
    def kernel(*refs):
        pass

    return pl.pallas_call(
        kernel,
        out_specs=[ANY] * n,
        out_shape=[jax.ShapeDtypeStruct(shape, BF16)] * n,
        cost_estimate=cost(0, 0),
        compiler_params=PARAMS,
        name="unwritten",
    )()


def stack(parts, *others):
    size, width = parts[0].shape
    n = len(parts)

    def kernel(*refs):
        for j in range(n):
            refs[-1][j * size:(j + 1) * size, :] = refs[j][...]

    return pl.pallas_call(
        kernel,
        in_specs=[VMEM] * n + [ANY] * len(others),
        out_specs=VMEM,
        out_shape=jax.ShapeDtypeStruct((n * size, width), parts[0].dtype),
        cost_estimate=cost(0, 0),
        compiler_params=PARAMS,
        name="stack",
    )(*parts, *others)


def pick_queries(query_store, block_slot, pattern, n_group):
    local_blocks, block_rows, width = query_store.shape
    n_cluster, n_list = pattern.shape
    part = block_rows // n_group

    def kernel(pattern_ref, slot_ref, in_ref, *rest):
        outs, sem = rest[:-1], rest[-1]
        me, group = lax.axis_index("shard"), lax.axis_index("groups")
        copies = []
        for t, out in enumerate(outs):
            target = lax.rem(me + t, jnp.int32(n_cluster))
            found = jnp.int32(0)
            for k in range(n_list):
                slot = slot_ref[pattern_ref[target, k]]
                hit = (lax.div(slot, jnp.int32(local_blocks)) == me).astype(I32)
                found = found + hit * lax.rem(slot, jnp.int32(local_blocks))
            rows = pl.ds(pl.multiple_of(group * part, part), part)
            copies.append(pltpu.make_async_copy(in_ref.at[found, rows], out.at[0], sem.at[t]))
            copies[-1].start()
        for copy in copies:
            copy.wait()

    return pl.pallas_call(
        kernel,
        in_specs=[SMEM, SMEM, ANY],
        out_specs=[VMEM] * n_cluster,
        out_shape=[jax.ShapeDtypeStruct((1, part, width), BF16)] * n_cluster,
        scratch_shapes=[pltpu.SemaphoreType.DMA((n_cluster,))],
        cost_estimate=cost(0, 4 * n_cluster * part * width),
        compiler_params=FIRST,
        name="pick_queries",
    )(pattern, block_slot, query_store)


def join_queries(parts, block_slot, pattern, local_blocks, n_feat, n_rep, *others):
    n_group, n_cluster = len(parts), len(parts[0])
    _, part, width = parts[0][0].shape
    n_list = pattern.shape[1]
    total = n_list * n_group * part
    share = total // (n_feat * n_rep)
    unit = min(share, part)
    half = total // n_rep

    def kernel(pattern_ref, slot_ref, *refs):
        outs, rows_ref = refs[-1 - CUTS * n_rep:-1], refs[-1]
        me, group = lax.axis_index("shard"), lax.axis_index("groups")
        for k in range(n_list):
            owner = lax.div(slot_ref[pattern_ref[me, k]], jnp.int32(local_blocks))
            hops = lax.rem(me + (n_cluster - owner), jnp.int32(n_cluster))
            for d in range(n_group):
                origin = lax.rem(group + (n_group - d), jnp.int32(n_group))
                for h in range(n_cluster):
                    @pl.when(hops == h)
                    def _():
                        for u in range(part // unit):
                            first = (k * n_group + origin) * part + u * unit
                            chunk = lax.div(first, jnp.int32(share))
                            goal = lax.rem(chunk, jnp.int32(n_rep)) * n_feat + lax.div(chunk, jnp.int32(n_rep))
                            goal = pl.multiple_of(goal * share + lax.rem(first, jnp.int32(share)), unit)
                            rows_ref[pl.ds(goal, unit), :] = refs[d * n_cluster + h][0, u * unit:(u + 1) * unit, :]
        for r in range(n_rep):
            @pl.when(lax.axis_index("rep") == r)
            def _():
                for j, out in enumerate(outs):
                    at, first = ((r + j // CUTS) % n_rep) * half, (j % CUTS) * (width // CUTS)
                    out[...] = rows_ref[at:at + half, first:first + width // CUTS].T

    return pl.pallas_call(
        kernel,
        in_specs=[SMEM, SMEM] + [VMEM] * (n_group * n_cluster) + [ANY] * len(others),
        out_specs=[VMEM] * (CUTS * n_rep),
        out_shape=[jax.ShapeDtypeStruct((width // CUTS, half), BF16)] * (CUTS * n_rep),
        scratch_shapes=[pltpu.VMEM((total, width), BF16)],
        cost_estimate=cost(0, 4 * total * width),
        compiler_params=PARAMS,
        name="join_queries",
    )(pattern, block_slot, *[x for line in parts for x in line], *others)


def one_hot(goal_ref, base, size):
    index = lax.broadcasted_iota(I32, (size, LANES), 0) + base
    lines = range(goal_ref.shape[0])
    return jnp.concatenate([(index == goal_ref[a:a + 1, :]).astype(F32).astype(BF16) for a in lines], axis=1)


def select(goal_ref, train_ref, base, size):
    tile = 128 if size % 128 == 0 else size
    found = [dot(one_hot(goal_ref, base + at, tile), train_ref[...]).astype(BF16) for at in range(0, size, tile)]
    return jnp.concatenate(found)


def own_rows(goal, train, bulk, *others):
    rows, width = train.shape
    cuts = 4
    part = width // cuts

    def kernel(goal_ref, train_ref, *rest):
        out_ref, held, sem = rest[-3:]
        copies = [
            pltpu.make_async_copy(train_ref.at[:, c * part:(c + 1) * part], held.at[c], sem.at[c]) for c in range(cuts)
        ]
        for copy in copies:
            copy.start()
        pick = one_hot(goal_ref, lax.axis_index("shard") * bulk, bulk)
        for c, copy in enumerate(copies):
            copy.wait()
            out_ref[:, c * part:(c + 1) * part] = dot(pick, held[c]).astype(BF16)

    return pl.pallas_call(
        kernel,
        in_specs=[VMEM, HBM] + [ANY] * len(others),
        out_specs=VMEM,
        out_shape=jax.ShapeDtypeStruct((bulk, width), BF16),
        scratch_shapes=[pltpu.VMEM((cuts, rows, part), BF16), pltpu.SemaphoreType.DMA((cuts,))],
        cost_estimate=cost(2 * bulk * train.size, 2 * train.size),
        compiler_params=PARAMS,
        name="own_rows",
    )(goal, train, *others)


def pack_rows(train, ids, columns, bulk, extra, cuts):
    rows = train.shape[0]
    lines = rows // LANES
    n_shard = ids.shape[0] // lines

    def kernel(ids_ref, train_ref, *rest):
        outs, goal_ref = rest[:-1], rest[-1]
        me = lax.axis_index("shard")
        own = ids_ref[...]
        masks = [(own == c).astype(F32) for c in range(n_shard)]
        stacked = jnp.concatenate(masks, axis=0).astype(BF16)
        lane_from = lax.broadcasted_iota(I32, (LANES, LANES), 0)
        lane_to = lax.broadcasted_iota(I32, (LANES, LANES), 1)
        in_line = dot(stacked, (lane_from < lane_to).astype(F32).astype(BF16))
        line_sum = dot(stacked, jnp.ones((LANES, LANES), BF16)).astype(BF16)
        size = n_shard * lines
        to = lax.broadcasted_iota(I32, (size, size), 0)
        since = lax.broadcasted_iota(I32, (size, size), 1)
        same = (to // lines) == (since // lines)
        ahead = dot((same & (since < to)).astype(F32).astype(BF16), line_sum)
        whole = dot(same.astype(F32).astype(BF16), line_sum)
        rank = in_line + ahead
        goal = jnp.zeros((lines, LANES), F32)
        past = jnp.zeros((lines, LANES), F32)
        for c in range(n_shard):
            part = slice(c * lines, (c + 1) * lines)
            place = rank[part] + c * bulk
            if extra:
                surplus = n_shard * bulk + past + rank[part] - bulk
                place = jnp.where(rank[part] < bulk, place, surplus)
                past = past + jnp.floor((jnp.maximum(whole[part] - bulk, 0.0) + 15.0) * 0.0625) * 16.0
            goal = goal + masks[c] * place
        goal_ref[...] = goal.astype(I32)

        def fill(out, base):
            out[...] = select(goal_ref, train_ref, base, out.shape[0])

        for out, (hops, first, _) in zip(outs, cuts):
            fill(out, lax.rem(me + hops, jnp.int32(n_shard)) * bulk + first)
        for j, out in enumerate(outs[len(cuts):]):
            fill(out, n_shard * bulk + max(j - 1, 0) * extra)

    shapes = [jax.ShapeDtypeStruct((n, columns), BF16) for _, _, n in cuts]
    shapes += [jax.ShapeDtypeStruct((extra, columns), BF16)] * (3 if extra else 0)
    shapes += [jax.ShapeDtypeStruct((lines, LANES), I32)]
    packed = n_shard * bulk + 2 * extra
    return pl.pallas_call(
        kernel,
        grid=(1,),
        in_specs=[
            pl.BlockSpec((lines, LANES), lambda i: (lax.axis_index("shard"), 0)),
            pl.BlockSpec((rows, columns), lambda i: (0, lax.axis_index("rep"))),
        ],
        out_specs=[VMEM] * len(shapes),
        out_shape=shapes,
        cost_estimate=cost(2 * packed * rows * columns, 2 * (rows + packed) * columns),
        compiler_params=FIRST,
        name="pack_rows",
    )(ids, train)


def partial_weights(matrices, queries, block, depth, dtype, *others):
    width, total = matrices[0].shape[1], queries[0].shape[1]
    tile = 512 if depth % 512 == 0 else depth
    steps = depth // tile
    n = len(matrices)

    def kernel(block_ref, *refs):
        out_ref, held, sem = refs[-3:]
        first = pl.multiple_of(block_ref[0] * depth, depth)
        copies = []
        for i in range(steps):
            for j in range(n):
                source = refs[j].at[pl.ds(first + i * tile, tile)]
                copies.append(pltpu.make_async_copy(source, held.at[j, i], sem.at[i * n + j]))
        for copy in copies:
            copy.start()
        parts = [jnp.concatenate([r[...] for r in refs[n + CUTS * j:n + CUTS * (j + 1)]]) for j in range(n)]
        for i in range(steps):
            value = None
            for j in range(n):
                copies[i * n + j].wait()
                part = dot(held[j, i], parts[j])
                value = part if value is None else value + part
            out_ref[i * tile:(i + 1) * tile, :] = value.astype(dtype)

    return pl.pallas_call(
        kernel,
        in_specs=[SMEM] + [HBM] * n + [VMEM] * (CUTS * n) + [ANY] * len(others),
        out_specs=VMEM,
        out_shape=jax.ShapeDtypeStruct((depth, total), dtype),
        scratch_shapes=[pltpu.VMEM((n, steps, tile, width), BF16), pltpu.SemaphoreType.DMA((steps * n,))],
        cost_estimate=cost(2 * n * depth * width * total, 2 * n * depth * width + 4 * depth * total),
        compiler_params=PARAMS,
        name="partial_weights",
    )(jnp.reshape(block, (1,)).astype(I32), *matrices, *queries, *others)


def fetch(matrices, block, depth, *others):
    width = matrices[0].shape[1]
    n = len(matrices)
    cuts = 4

    def kernel(block_ref, *refs):
        outs, sem = refs[-1 - n:-1], refs[-1]
        first = pl.multiple_of(block_ref[0] * depth, depth)
        copies = []
        for j in range(n):
            for c in range(cuts):
                size = depth // cuts
                source = refs[j].at[pl.ds(first + c * size, size)]
                copies.append(
                    pltpu.make_async_copy(source, outs[j].at[c * size:(c + 1) * size], sem.at[j * cuts + c])
                )
        for copy in copies:
            copy.start()
        for copy in copies:
            copy.wait()

    return pl.pallas_call(
        kernel,
        in_specs=[SMEM] + [HBM] * n + [ANY] * len(others),
        out_specs=[VMEM] * n,
        out_shape=[jax.ShapeDtypeStruct((depth, width), BF16)] * n,
        scratch_shapes=[pltpu.SemaphoreType.DMA((n * cuts,))],
        cost_estimate=cost(0, 2 * n * depth * width),
        compiler_params=PARAMS,
        name="fetch",
    )(jnp.reshape(block, (1,)).astype(I32), *matrices, *others)


def fetched_weights(matrices, queries, dtype):
    depth = matrices[0].shape[0]
    total = queries[0].shape[1]
    tile = 512 if depth % 512 == 0 else depth
    n = len(matrices)

    def kernel(*refs):
        parts = [jnp.concatenate([r[...] for r in refs[n + CUTS * j:n + CUTS * (j + 1)]]) for j in range(n)]
        for at in range(0, depth, tile):
            value = None
            for j in range(n):
                part = dot(refs[j][at:at + tile, :], parts[j])
                value = part if value is None else value + part
            refs[-1][at:at + tile, :] = value.astype(dtype)

    return pl.pallas_call(
        kernel,
        in_specs=[VMEM] * ((1 + CUTS) * n),
        out_specs=VMEM,
        out_shape=jax.ShapeDtypeStruct((depth, total), dtype),
        cost_estimate=cost(2 * n * matrices[0].size * total, 2 * n * matrices[0].size),
        compiler_params=PARAMS,
        name="fetched_weights",
    )(*matrices, *queries)


def row_table(ids, lines, bulk, extra, *others):
    n_shard = ids.shape[0] // lines

    def kernel(ids_ref, *rest):
        table_ref, flag_ref = rest[-2:]
        me = lax.axis_index("shard")
        start = jnp.int32(0)
        most = jnp.int32(0)
        for s in range(n_shard):
            line = ids_ref[s * lines:(s + 1) * lines, :]

            def count(c):
                return jnp.sum((line == c).astype(I32))

            mine = count(me)
            before = jnp.int32(0)
            if extra:
                surplus = jnp.int32(0)
                for c in range(n_shard):
                    over = lax.div(jnp.maximum(count(c) - bulk, 0) + 15, jnp.int32(16)) * 16
                    before = before + jnp.where(c < me, over, 0)
                    surplus = surplus + over
                most = jnp.maximum(most, surplus)
            table_ref[s, 0] = start
            table_ref[s, 1] = jnp.minimum(mine, bulk)
            table_ref[s, 2] = lax.div(before, jnp.int32(16))
            table_ref[s, 3] = jnp.maximum(mine - bulk, 0)
            start = start + mine
        flag_ref[...] = jnp.full((8, LANES), (most > extra).astype(I32))

    return pl.pallas_call(
        kernel,
        in_specs=[VMEM] + [ANY] * len(others),
        out_specs=[SMEM, VMEM],
        out_shape=[jax.ShapeDtypeStruct((n_shard, 4), I32), jax.ShapeDtypeStruct((8, LANES), I32)],
        cost_estimate=cost(0, 4 * ids.size),
        compiler_params=PARAMS,
        name="row_table",
    )(ids, *others)


def put(acc, x, start, count=None):
    tiles, _, width = x.shape
    first, within = lax.div(start, jnp.int32(8)), lax.rem(start, jnp.int32(8))
    turned = pltpu.roll(x, within, 1)
    row = lax.broadcasted_iota(I32, (1, 8, width), 1)
    keep = row < within
    pieces = jnp.where(keep, jnp.concatenate([turned[:1], turned]), jnp.concatenate([turned, turned[-1:]]))
    if count is None:
        pieces = jnp.concatenate([jnp.where(keep, acc[pl.ds(first, 1)], turned[:1]), pieces[1:]])
    else:
        at = lax.broadcasted_iota(I32, (tiles + 1, 8, width), 0) * 8 + lax.broadcasted_iota(
            I32, (tiles + 1, 8, width), 1
        )
        pieces = jnp.where(
            (at >= within) & (at < within + count), pieces, acc[pl.ds(first, tiles + 1)]
        )
    acc[pl.ds(first, tiles + 1)] = pieces


def score(weight_ref, parts, rep):
    total = None
    for d, x in enumerate(parts):
        depth = x.shape[1]
        block = pl.ds(pl.multiple_of(lax.rem(rep + (len(parts) - d), jnp.int32(len(parts))) * depth, depth), depth)
        value = dot(x, weight_ref[block, :])
        total = value if total is None else total + value
    width = total.shape[1] // 2
    total = total[:, :width] + total[:, width:]
    return total.reshape(total.shape[0] // 8, 8, width)


def for_feats(value, outs):
    n = len(outs)
    share = outs[0].shape[1]
    for f in range(n):
        @pl.when(lax.axis_index("feat") == f)
        def _():
            for d, out in enumerate(outs):
                at = ((f + d) % n) * share
                out[...] = value(slice(at, at + share)).astype(out.dtype)


def feat_shapes(rows, width, n_feat):
    share = (rows, width // n_feat)
    return [jax.ShapeDtypeStruct(share, F32)] + [jax.ShapeDtypeStruct(share, BF16)] * (n_feat - 1)


def early_scores(own, others, mine, pieces, cuts, firsts, seconds, table, rows, n_feat, n_rep, n_shard, bulk, extra):
    depth, width = own.shape
    columns = depth // n_rep
    n_other, n_piece = len(others), len(pieces)
    n_first = len(firsts) * n_rep
    last_hops = n_shard - 1

    def kernel(table_ref, *refs):
        own_ref, refs = refs[0], refs[1:]
        other_refs, refs = refs[:n_other], refs[n_other:]
        mine_ref, refs = refs[0], refs[1:]
        piece_refs = [refs[j * n_rep:(j + 1) * n_rep] for j in range(n_piece)]
        refs = refs[n_piece * n_rep:]
        first_refs, second_refs, refs = refs[:n_first], refs[n_first:2 * n_first], refs[2 * n_first:]
        weight_ref, outs, (scored, held, acc, sem) = refs[0], refs[1:-4], refs[-4:]
        me, rep = lax.axis_index("shard"), lax.axis_index("rep")
        weight = own_ref[...]
        for ref in other_refs:
            weight = weight + ref[...].astype(F32)
        high = weight.astype(BF16)
        weight_ref[:, :width] = high
        weight_ref[:, width:] = (weight - high.astype(F32)).astype(BF16)

        total = None
        for d in range(n_rep):
            block = lax.rem(rep + (n_rep - d), jnp.int32(n_rep)) * columns
            block = pl.ds(pl.multiple_of(block, columns), columns)
            x = jnp.concatenate([mine_ref[:, block], *[parts[d][...] for parts in piece_refs]])
            value = dot(x, weight_ref[block, :])
            total = value if total is None else total + value
        total = total[:, :width] + total[:, width:]
        total = total.reshape(total.shape[0] // 8, 8, width)
        scored[me] = total[:bulk // 8]
        at = bulk // 8
        for hops, first, size in cuts:
            source = lax.rem(me + (n_shard - hops), jnp.int32(n_shard))
            scored[source, first // 8:(first + size) // 8] = total[at:at + size // 8]
            at += size // 8
        last = lax.rem(me + (n_shard - last_hops), jnp.int32(n_shard))
        for s in range(n_shard):
            start = table_ref[s, 0]

            @pl.when(last != s)
            def _():
                put(acc, scored[s], start)

            if extra:
                @pl.when(table_ref[s, 3] > 0)
                def _():
                    apart = jnp.bitwise_xor(me, s)
                    rows_in = pl.ds(pl.multiple_of(lax.div(apart, jnp.int32(2)) * extra, extra), extra)
                    for odd in range(2):
                        @pl.when(jnp.bitwise_and(apart, 1) == odd)
                        def _():
                            copies = []
                            for j, refs in enumerate([first_refs, second_refs]):
                                for d in range(n_rep):
                                    goal = held.at[d, j * extra:(j + 1) * extra]
                                    which = refs[odd * n_rep + d].at[rows_in]
                                    copies.append(pltpu.make_async_copy(which, goal, sem.at[j * n_rep + d]))
                            for copy in copies:
                                copy.start()
                            for copy in copies:
                                copy.wait()
                    some = pl.ds(pl.multiple_of(table_ref[s, 2] * 16, 16), extra)
                    x = [held[d, some, :] for d in range(n_rep)]
                    put(acc, score(weight_ref, x, rep), start + table_ref[s, 1])
        for_feats(lambda at: acc[:rows // 8, :, at].reshape(rows, width // n_feat), outs)

    count = n_shard * bulk
    surplus = [x for parts in [*firsts, *seconds] for x in parts]
    return pl.pallas_call(
        kernel,
        in_specs=[SMEM] + [VMEM] * (2 + n_other + n_rep * n_piece) + [ANY] * len(surplus),
        out_specs=[VMEM] * (1 + n_feat),
        out_shape=[jax.ShapeDtypeStruct((depth, 2 * width), BF16)] + feat_shapes(rows, width, n_feat),
        scratch_shapes=[
            pltpu.VMEM((n_shard, bulk // 8, 8, width), F32),
            pltpu.VMEM((n_rep, 3 * extra + 16, columns), BF16),
            pltpu.VMEM(((rows + bulk + extra) // 8 + 2, 8, width), F32),
            pltpu.SemaphoreType.DMA((2 * n_rep,)),
        ],
        cost_estimate=cost(4 * count * depth * width, 10 * depth * width + count * (2 * depth + 4 * width)),
        compiler_params=WIDE,
        name="early_scores",
    )(table, own, *others, mine, *[p for parts in pieces for p in parts], *surplus)


def late_scores(pieces, weight, n_feat):
    n, n_rep = len(pieces), len(pieces[0])
    rows = sum(parts[0].shape[0] for parts in pieces)
    width = weight.shape[1] // 2

    def kernel(weight_ref, *refs):
        part_refs, outs, acc = refs[:n * n_rep], refs[n * n_rep:-1], refs[-1]
        parts = [jnp.concatenate([part_refs[j * n_rep + d][...] for j in range(n)]) for d in range(n_rep)]
        acc[...] = score(weight_ref, parts, lax.axis_index("rep")).reshape(rows, width)
        for_feats(lambda at: acc[:, at], outs)

    return pl.pallas_call(
        kernel,
        in_specs=[VMEM] * (1 + n * n_rep),
        out_specs=[VMEM] * n_feat,
        out_shape=feat_shapes(rows, width, n_feat),
        scratch_shapes=[pltpu.VMEM((rows, width), F32)],
        cost_estimate=cost(4 * rows * weight.size, 8 * rows * width),
        compiler_params=PARAMS,
        name="late_scores",
    )(weight, *[p for parts in pieces for p in parts])


def merge(table, early, late, n_shard):
    rows, width = early[0].shape
    last_rows = late[0].shape[0]
    last_hops = n_shard - 1

    def kernel(table_ref, *refs):
        early_refs, late_refs = refs[:len(early)], refs[len(early):-2]
        out_ref, acc = refs[-2:]
        source = lax.rem(lax.axis_index("shard") + (n_shard - last_hops), jnp.int32(n_shard))

        def total(parts):
            value = parts[0][...]
            for ref in parts[1:]:
                value = value + ref[...].astype(F32)
            return value.reshape(value.shape[0] // 8, 8, width)

        acc[:rows // 8] = total(early_refs)
        put(acc, total(late_refs), table_ref[source, 0], table_ref[source, 1])
        out_ref[...] = acc[:rows // 8].reshape(rows, width).T

    return pl.pallas_call(
        kernel,
        in_specs=[SMEM] + [VMEM] * (len(early) + len(late)),
        out_specs=VMEM,
        out_shape=jax.ShapeDtypeStruct((width, rows), F32),
        scratch_shapes=[pltpu.VMEM(((rows + last_rows) // 8 + 2, 8, width), F32)],
        cost_estimate=cost(0, 8 * rows * width),
        compiler_params=PARAMS,
        name="merge",
    )(table, *early, *late)


def body(train, cluster_ids, precond, query_store, block_slot, pattern):
    n_group, n_shard = lax.axis_size("groups"), lax.axis_size("shard")
    n_feat, n_rep = lax.axis_size("feat"), lax.axis_size("rep")
    feat, rep = lax.axis_index("feat"), lax.axis_index("rep")
    rows = train.shape[0]
    lines = rows // LANES
    base = rows // n_shard
    columns = train.shape[1] // n_rep
    extra = base // 2 if n_shard == 4 else 0
    bulk = base if extra else base + base // 2
    ids = cluster_ids.reshape(-1, LANES)

    last_hops = n_shard - 1

    def with_rep(x):
        return [x] + [shift(x, "rep", n_rep, d) for d in range(1, n_rep)]

    matrices = with_rep(precond[0])

    picked = pick_queries(query_store, block_slot, pattern, n_group)
    pieces = [picked[0]] + [shift(picked[d], "shard", n_shard, d) for d in range(1, n_shard)]

    middle = [(d, 0, bulk) for d in range(1, last_hops)]
    fillers = 2 if bulk % 128 == 0 else 1
    sizes = [n * bulk // 8 for n in (2, 1, 2, 2, 1)] if bulk % 128 == 0 else [bulk // 2] * 2
    final = [(last_hops, sum(sizes[:j]), n) for j, n in enumerate(sizes)]
    *packed, goal = pack_rows(train, ids, columns, bulk, extra, middle + final)
    firsts, seconds = [], []
    parts = [pieces] + [[shift(x, "groups", n_group, d) for x in pieces] for d in range(1, n_group)]
    here = [shift(after(packed[0], *pieces[1:]), "shard", n_shard, 1)]
    urgent = [here[0]]
    if extra:
        far = swap(after(packed[-2], *pieces[1:]), "shard", n_shard, 2)
        urgent.append(far)
    sent_last = packed[len(middle):len(middle) + len(final)]
    last = [shift(after(x, *pieces[1:]), "shard", n_shard, last_hops) for x in sent_last[:fillers]]
    urgent += last
    depth = n_rep * columns
    targets = [(feat + d) % n_feat for d in range(1, n_feat)]
    near_chip = fetch(matrices, targets[0], depth, *pieces[1:])

    table, flag = row_table(ids, lines, bulk, extra, *pieces[1:])
    chosen = join_queries(
        parts, block_slot, pattern, query_store.shape[0], n_feat, n_rep, *near_chip, flag
    )
    queries = [*chosen[:CUTS]] + [shift(chosen[j], "rep", n_rep, j // CUTS) for j in range(CUTS, CUTS * n_rep)]

    sends = [fetched_weights(near_chip, queries, BF16)]
    sends += [partial_weights(matrices, queries, f, depth, BF16) for f in targets[1:]]
    others = [shift(x, "feat", n_feat, d + 1) for d, x in enumerate(sends)]
    own = partial_weights(matrices, queries, feat, depth, F32, *sends)

    for (hops, _, _), x in zip(middle[1:], packed[1:]):
        here.append(shift(after(x, *urgent, *sends), "shard", n_shard, hops))
        urgent = [here[-1]]
    sent_last = [after(x, own) for x in sent_last[fillers:]]
    last_all = [with_rep(after(x, own)) for x in last]

    mine = own_rows(goal, train, bulk, own)
    marks = [own, mine, *sent_last, *[p for x in last_all for p in x[1:]]]
    if extra:
        for d in range(1, n_group):
            flag = jnp.maximum(flag, shift(flag, "groups", n_group, d))

        def second_round(x):
            pair = jnp.concatenate([x, swap(x, "shard", n_shard, 2)])
            return [with_rep(pair), with_rep(swap(pair, "shard", n_shard, 1))]

        def no_round(x):
            empty = unwritten((2 * extra, columns), 2 * n_rep)
            return [[*empty[:n_rep]], [*empty[n_rep:]]]

        seconds = lax.cond(flag[0, 0] > 0, second_round, no_round, after(packed[-1], own))
        near = swap(stack([packed[-3], far], *sends), "shard", n_shard, 1)
        pairs = [stack([x, y], own) for x, y in zip(with_rep(packed[-3]), with_rep(after(far, own)))]
        firsts = [pairs, with_rep(after(near, own))]
        marks += [seconds[0][0], near, *pairs]

    mark = shift(after(jnp.zeros((8, LANES), I32), *marks), "rep", n_rep, 1)
    last += [shift(x, "shard", n_shard, last_hops) for x in sent_last]
    ready = [with_rep(after(x, mark)) for x in here]
    weight, *early = early_scores(
        own, others, mine, ready, middle, firsts, seconds, table, rows, n_feat, n_rep, n_shard, bulk, extra
    )

    def over_feat(shares):
        return [shares[0]] + [shift(shares[d], "feat", n_feat, d) for d in range(1, n_feat)]

    last_all += [with_rep(after(x, *early[1:])) for x in last[fillers:]]
    late = late_scores(last_all, weight, n_feat)
    return merge(table, over_feat(early), over_feat(late), n_shard)[None]


def solution(mesh):
    return jax.shard_map(
        body,
        mesh=mesh,
        in_specs=(
            P(("groups", "shard"), "feat"),
            P("groups"),
            P(("groups", "shard"), None, ("feat", "rep")),
            P("shard", None, ("feat", "rep")),
            P(),
            P(),
        ),
        out_specs=P(("groups", "shard"), ("feat", "rep"), None),
        check_vma=False,
    )
```

```python
import functools

import jax
import jax.numpy as jnp
from jax import lax
from jax.experimental import pallas as pl
from jax.experimental.pallas import tpu as pltpu
from jax.sharding import PartitionSpec as P

F32, BF16, I32 = jnp.float32, jnp.bfloat16, jnp.int32
VMEM = pl.BlockSpec(memory_space=pltpu.VMEM)
ANY = pl.BlockSpec(memory_space=pl.ANY)
HBM = pl.BlockSpec(memory_space=pltpu.HBM)
SMEM = pl.BlockSpec(memory_space=pltpu.SMEM)
PARAMS = pltpu.CompilerParams(vmem_limit_bytes=24 * 2**20)
WIDE = pltpu.CompilerParams(vmem_limit_bytes=32 * 2**20)
FIRST = pltpu.CompilerParams(vmem_limit_bytes=60 * 2**20)
LANES = 128
CUTS = 8


def shift(x, axis, size, by):
    return lax.ppermute(x, axis, [(i, (i + by) % size) for i in range(size)])


def swap(x, axis, size, bit):
    return lax.ppermute(x, axis, [(i, i ^ bit) for i in range(size)])


def dot(a, b):
    return jnp.dot(a, b, preferred_element_type=F32)


def cost(flops, nbytes):
    return pl.CostEstimate(flops=1, bytes_accessed=1, transcendentals=0)


def after(x, *others):
    def kernel(*refs):
        pass

    return pl.pallas_call(
        kernel,
        in_specs=[ANY] * (1 + len(others)),
        out_specs=ANY,
        out_shape=jax.ShapeDtypeStruct(x.shape, x.dtype),
        input_output_aliases={0: 0},
        cost_estimate=cost(0, 0),
        compiler_params=PARAMS,
        name="after",
    )(x, *others)


def unwritten(shape, n):
    def kernel(*refs):
        pass

    return pl.pallas_call(
        kernel,
        out_specs=[ANY] * n,
        out_shape=[jax.ShapeDtypeStruct(shape, BF16)] * n,
        cost_estimate=cost(0, 0),
        compiler_params=PARAMS,
        name="unwritten",
    )()


def stack(parts, *others):
    size, width = parts[0].shape
    n = len(parts)

    def kernel(*refs):
        for j in range(n):
            refs[-1][j * size:(j + 1) * size, :] = refs[j][...]

    return pl.pallas_call(
        kernel,
        in_specs=[VMEM] * n + [ANY] * len(others),
        out_specs=VMEM,
        out_shape=jax.ShapeDtypeStruct((n * size, width), parts[0].dtype),
        cost_estimate=cost(0, 0),
        compiler_params=PARAMS,
        name="stack",
    )(*parts, *others)


def pick_queries(query_store, block_slot, pattern, n_group):
    local_blocks, block_rows, width = query_store.shape
    n_cluster, n_list = pattern.shape
    part = block_rows // n_group

    def kernel(pattern_ref, slot_ref, in_ref, *rest):
        outs, sem = rest[:-1], rest[-1]
        me, group = lax.axis_index("shard"), lax.axis_index("groups")
        copies = []
        for t, out in enumerate(outs):
            target = lax.rem(me + t, jnp.int32(n_cluster))
            found = jnp.int32(0)
            for k in range(n_list):
                slot = slot_ref[pattern_ref[target, k]]
                hit = (lax.div(slot, jnp.int32(local_blocks)) == me).astype(I32)
                found = found + hit * lax.rem(slot, jnp.int32(local_blocks))
            rows = pl.ds(pl.multiple_of(group * part, part), part)
            copies.append(pltpu.make_async_copy(in_ref.at[found, rows], out.at[0], sem.at[t]))
            copies[-1].start()
        for copy in copies:
            copy.wait()

    return pl.pallas_call(
        kernel,
        in_specs=[SMEM, SMEM, ANY],
        out_specs=[VMEM] * n_cluster,
        out_shape=[jax.ShapeDtypeStruct((1, part, width), BF16)] * n_cluster,
        scratch_shapes=[pltpu.SemaphoreType.DMA((n_cluster,))],
        cost_estimate=cost(0, 4 * n_cluster * part * width),
        compiler_params=FIRST,
        name="pick_queries",
    )(pattern, block_slot, query_store)


def join_queries(parts, block_slot, pattern, local_blocks, n_feat, n_rep, *others):
    n_group, n_cluster = len(parts), len(parts[0])
    _, part, width = parts[0][0].shape
    n_list = pattern.shape[1]
    total = n_list * n_group * part
    share = total // (n_feat * n_rep)
    unit = min(share, part)
    half = total // n_rep

    def kernel(pattern_ref, slot_ref, *refs):
        outs, rows_ref = refs[-1 - CUTS * n_rep:-1], refs[-1]
        me, group = lax.axis_index("shard"), lax.axis_index("groups")
        for k in range(n_list):
            owner = lax.div(slot_ref[pattern_ref[me, k]], jnp.int32(local_blocks))
            hops = lax.rem(me + (n_cluster - owner), jnp.int32(n_cluster))
            for d in range(n_group):
                origin = lax.rem(group + (n_group - d), jnp.int32(n_group))
                for h in range(n_cluster):
                    @pl.when(hops == h)
                    def _():
                        for u in range(part // unit):
                            first = (k * n_group + origin) * part + u * unit
                            chunk = lax.div(first, jnp.int32(share))
                            goal = lax.rem(chunk, jnp.int32(n_rep)) * n_feat + lax.div(chunk, jnp.int32(n_rep))
                            goal = pl.multiple_of(goal * share + lax.rem(first, jnp.int32(share)), unit)
                            rows_ref[pl.ds(goal, unit), :] = refs[d * n_cluster + h][0, u * unit:(u + 1) * unit, :]
        for r in range(n_rep):
            @pl.when(lax.axis_index("rep") == r)
            def _():
                for j, out in enumerate(outs):
                    at, first = ((r + j // CUTS) % n_rep) * half, (j % CUTS) * (width // CUTS)
                    out[...] = rows_ref[at:at + half, first:first + width // CUTS].T

    return pl.pallas_call(
        kernel,
        in_specs=[SMEM, SMEM] + [VMEM] * (n_group * n_cluster) + [ANY] * len(others),
        out_specs=[VMEM] * (CUTS * n_rep),
        out_shape=[jax.ShapeDtypeStruct((width // CUTS, half), BF16)] * (CUTS * n_rep),
        scratch_shapes=[pltpu.VMEM((total, width), BF16)],
        cost_estimate=cost(0, 4 * total * width),
        compiler_params=PARAMS,
        name="join_queries",
    )(pattern, block_slot, *[x for line in parts for x in line], *others)


def one_hot(goal_ref, base, size):
    index = lax.broadcasted_iota(I32, (size, LANES), 0) + base
    lines = range(goal_ref.shape[0])
    return jnp.concatenate([(index == goal_ref[a:a + 1, :]).astype(F32).astype(BF16) for a in lines], axis=1)


def select(goal_ref, train_ref, base, size):
    tile = 128 if size % 128 == 0 else size
    found = [dot(one_hot(goal_ref, base + at, tile), train_ref[...]).astype(BF16) for at in range(0, size, tile)]
    return jnp.concatenate(found)


def own_rows(goal, train, bulk, *others):
    rows, width = train.shape
    cuts = 4
    part = width // cuts

    def kernel(goal_ref, train_ref, *rest):
        out_ref, held, sem = rest[-3:]
        copies = [
            pltpu.make_async_copy(train_ref.at[:, c * part:(c + 1) * part], held.at[c], sem.at[c]) for c in range(cuts)
        ]
        for copy in copies:
            copy.start()
        pick = one_hot(goal_ref, lax.axis_index("shard") * bulk, bulk)
        for c, copy in enumerate(copies):
            copy.wait()
            out_ref[:, c * part:(c + 1) * part] = dot(pick, held[c]).astype(BF16)

    return pl.pallas_call(
        kernel,
        in_specs=[VMEM, HBM] + [ANY] * len(others),
        out_specs=VMEM,
        out_shape=jax.ShapeDtypeStruct((bulk, width), BF16),
        scratch_shapes=[pltpu.VMEM((cuts, rows, part), BF16), pltpu.SemaphoreType.DMA((cuts,))],
        cost_estimate=cost(2 * bulk * train.size, 2 * train.size),
        compiler_params=PARAMS,
        name="own_rows",
    )(goal, train, *others)


def pack_rows(train, ids, columns, bulk, extra, cuts):
    rows = train.shape[0]
    lines = rows // LANES
    n_shard = ids.shape[0] // lines

    def kernel(ids_ref, train_ref, *rest):
        outs, goal_ref = rest[:-1], rest[-1]
        me = lax.axis_index("shard")
        own = ids_ref[...]
        masks = [(own == c).astype(F32) for c in range(n_shard)]
        stacked = jnp.concatenate(masks, axis=0).astype(BF16)
        lane_from = lax.broadcasted_iota(I32, (LANES, LANES), 0)
        lane_to = lax.broadcasted_iota(I32, (LANES, LANES), 1)
        in_line = dot(stacked, (lane_from < lane_to).astype(F32).astype(BF16))
        line_sum = dot(stacked, jnp.ones((LANES, LANES), BF16)).astype(BF16)
        size = n_shard * lines
        to = lax.broadcasted_iota(I32, (size, size), 0)
        since = lax.broadcasted_iota(I32, (size, size), 1)
        same = (to // lines) == (since // lines)
        ahead = dot((same & (since < to)).astype(F32).astype(BF16), line_sum)
        whole = dot(same.astype(F32).astype(BF16), line_sum)
        rank = in_line + ahead
        goal = jnp.zeros((lines, LANES), F32)
        past = jnp.zeros((lines, LANES), F32)
        for c in range(n_shard):
            part = slice(c * lines, (c + 1) * lines)
            place = rank[part] + c * bulk
            if extra:
                surplus = n_shard * bulk + past + rank[part] - bulk
                place = jnp.where(rank[part] < bulk, place, surplus)
                past = past + jnp.floor((jnp.maximum(whole[part] - bulk, 0.0) + 15.0) * 0.0625) * 16.0
            goal = goal + masks[c] * place
        goal_ref[...] = goal.astype(I32)

        def fill(out, base):
            out[...] = select(goal_ref, train_ref, base, out.shape[0])

        for out, (hops, first, _) in zip(outs, cuts):
            fill(out, lax.rem(me + hops, jnp.int32(n_shard)) * bulk + first)
        for j, out in enumerate(outs[len(cuts):]):
            fill(out, n_shard * bulk + max(j - 1, 0) * extra)

    shapes = [jax.ShapeDtypeStruct((n, columns), BF16) for _, _, n in cuts]
    shapes += [jax.ShapeDtypeStruct((extra, columns), BF16)] * (3 if extra else 0)
    shapes += [jax.ShapeDtypeStruct((lines, LANES), I32)]
    packed = n_shard * bulk + 2 * extra
    return pl.pallas_call(
        kernel,
        grid=(1,),
        in_specs=[
            pl.BlockSpec((lines, LANES), lambda i: (lax.axis_index("shard"), 0)),
            pl.BlockSpec((rows, columns), lambda i: (0, lax.axis_index("rep"))),
        ],
        out_specs=[VMEM] * len(shapes),
        out_shape=shapes,
        cost_estimate=cost(2 * packed * rows * columns, 2 * (rows + packed) * columns),
        compiler_params=FIRST,
        name="pack_rows",
    )(ids, train)


def partial_weights(matrices, queries, block, depth, dtype, *others):
    width, total = matrices[0].shape[1], queries[0].shape[1]
    tile = 512 if depth % 512 == 0 else depth
    steps = depth // tile
    n = len(matrices)

    def kernel(block_ref, *refs):
        out_ref, held, sem = refs[-3:]
        first = pl.multiple_of(block_ref[0] * depth, depth)
        copies = []
        for i in range(steps):
            for j in range(n):
                source = refs[j].at[pl.ds(first + i * tile, tile)]
                copies.append(pltpu.make_async_copy(source, held.at[j, i], sem.at[i * n + j]))
        for copy in copies:
            copy.start()
        parts = [jnp.concatenate([r[...] for r in refs[n + CUTS * j:n + CUTS * (j + 1)]]) for j in range(n)]
        for i in range(steps):
            value = None
            for j in range(n):
                copies[i * n + j].wait()
                part = dot(held[j, i], parts[j])
                value = part if value is None else value + part
            out_ref[i * tile:(i + 1) * tile, :] = value.astype(dtype)

    return pl.pallas_call(
        kernel,
        in_specs=[SMEM] + [HBM] * n + [VMEM] * (CUTS * n) + [ANY] * len(others),
        out_specs=VMEM,
        out_shape=jax.ShapeDtypeStruct((depth, total), dtype),
        scratch_shapes=[pltpu.VMEM((n, steps, tile, width), BF16), pltpu.SemaphoreType.DMA((steps * n,))],
        cost_estimate=cost(2 * n * depth * width * total, 2 * n * depth * width + 4 * depth * total),
        compiler_params=PARAMS,
        name="partial_weights",
    )(jnp.reshape(block, (1,)).astype(I32), *matrices, *queries, *others)


def fetch(matrices, block, depth, *others):
    width = matrices[0].shape[1]
    n = len(matrices)
    cuts = 4

    def kernel(block_ref, *refs):
        outs, sem = refs[-1 - n:-1], refs[-1]
        first = pl.multiple_of(block_ref[0] * depth, depth)
        copies = []
        for j in range(n):
            for c in range(cuts):
                size = depth // cuts
                source = refs[j].at[pl.ds(first + c * size, size)]
                copies.append(
                    pltpu.make_async_copy(source, outs[j].at[c * size:(c + 1) * size], sem.at[j * cuts + c])
                )
        for copy in copies:
            copy.start()
        for copy in copies:
            copy.wait()

    return pl.pallas_call(
        kernel,
        in_specs=[SMEM] + [HBM] * n + [ANY] * len(others),
        out_specs=[VMEM] * n,
        out_shape=[jax.ShapeDtypeStruct((depth, width), BF16)] * n,
        scratch_shapes=[pltpu.SemaphoreType.DMA((n * cuts,))],
        cost_estimate=cost(0, 2 * n * depth * width),
        compiler_params=PARAMS,
        name="fetch",
    )(jnp.reshape(block, (1,)).astype(I32), *matrices, *others)


def fetched_weights(matrices, queries, dtype):
    depth = matrices[0].shape[0]
    total = queries[0].shape[1]
    tile = 512 if depth % 512 == 0 else depth
    n = len(matrices)

    def kernel(*refs):
        parts = [jnp.concatenate([r[...] for r in refs[n + CUTS * j:n + CUTS * (j + 1)]]) for j in range(n)]
        for at in range(0, depth, tile):
            value = None
            for j in range(n):
                part = dot(refs[j][at:at + tile, :], parts[j])
                value = part if value is None else value + part
            refs[-1][at:at + tile, :] = value.astype(dtype)

    return pl.pallas_call(
        kernel,
        in_specs=[VMEM] * ((1 + CUTS) * n),
        out_specs=VMEM,
        out_shape=jax.ShapeDtypeStruct((depth, total), dtype),
        cost_estimate=cost(2 * n * matrices[0].size * total, 2 * n * matrices[0].size),
        compiler_params=PARAMS,
        name="fetched_weights",
    )(*matrices, *queries)


def row_table(ids, lines, bulk, extra, *others):
    n_shard = ids.shape[0] // lines

    def kernel(ids_ref, *rest):
        table_ref, flag_ref = rest[-2:]
        me = lax.axis_index("shard")
        start = jnp.int32(0)
        most = jnp.int32(0)
        for s in range(n_shard):
            line = ids_ref[s * lines:(s + 1) * lines, :]

            def count(c):
                return jnp.sum((line == c).astype(I32))

            mine = count(me)
            before = jnp.int32(0)
            if extra:
                surplus = jnp.int32(0)
                for c in range(n_shard):
                    over = lax.div(jnp.maximum(count(c) - bulk, 0) + 15, jnp.int32(16)) * 16
                    before = before + jnp.where(c < me, over, 0)
                    surplus = surplus + over
                most = jnp.maximum(most, surplus)
            table_ref[s, 0] = start
            table_ref[s, 1] = jnp.minimum(mine, bulk)
            table_ref[s, 2] = lax.div(before, jnp.int32(16))
            table_ref[s, 3] = jnp.maximum(mine - bulk, 0)
            start = start + mine
        flag_ref[...] = jnp.full((8, LANES), (most > extra).astype(I32))

    return pl.pallas_call(
        kernel,
        in_specs=[VMEM] + [ANY] * len(others),
        out_specs=[SMEM, VMEM],
        out_shape=[jax.ShapeDtypeStruct((n_shard, 4), I32), jax.ShapeDtypeStruct((8, LANES), I32)],
        cost_estimate=cost(0, 4 * ids.size),
        compiler_params=PARAMS,
        name="row_table",
    )(ids, *others)


def put(acc, x, start, count=None):
    tiles, _, width = x.shape
    first, within = lax.div(start, jnp.int32(8)), lax.rem(start, jnp.int32(8))
    turned = pltpu.roll(x, within, 1)
    row = lax.broadcasted_iota(I32, (1, 8, width), 1)
    keep = row < within
    pieces = jnp.where(keep, jnp.concatenate([turned[:1], turned]), jnp.concatenate([turned, turned[-1:]]))
    if count is None:
        pieces = jnp.concatenate([jnp.where(keep, acc[pl.ds(first, 1)], turned[:1]), pieces[1:]])
    else:
        at = lax.broadcasted_iota(I32, (tiles + 1, 8, width), 0) * 8 + lax.broadcasted_iota(
            I32, (tiles + 1, 8, width), 1
        )
        pieces = jnp.where(
            (at >= within) & (at < within + count), pieces, acc[pl.ds(first, tiles + 1)]
        )
    acc[pl.ds(first, tiles + 1)] = pieces


def score(weight_ref, parts, rep):
    total = None
    for d, x in enumerate(parts):
        depth = x.shape[1]
        block = pl.ds(pl.multiple_of(lax.rem(rep + (len(parts) - d), jnp.int32(len(parts))) * depth, depth), depth)
        value = dot(x, weight_ref[block, :])
        total = value if total is None else total + value
    width = total.shape[1] // 2
    total = total[:, :width] + total[:, width:]
    return total.reshape(total.shape[0] // 8, 8, width)


def for_feats(value, outs):
    n = len(outs)
    share = outs[0].shape[1]
    for f in range(n):
        @pl.when(lax.axis_index("feat") == f)
        def _():
            for d, out in enumerate(outs):
                at = ((f + d) % n) * share
                out[...] = value(slice(at, at + share)).astype(out.dtype)


def feat_shapes(rows, width, n_feat):
    share = (rows, width // n_feat)
    return [jax.ShapeDtypeStruct(share, F32)] + [jax.ShapeDtypeStruct(share, BF16)] * (n_feat - 1)


def early_scores(own, others, mine, pieces, cuts, firsts, seconds, table, rows, n_feat, n_rep, n_shard, bulk, extra):
    depth, width = own.shape
    columns = depth // n_rep
    n_other, n_piece = len(others), len(pieces)
    n_first = len(firsts) * n_rep
    last_hops = n_shard - 1

    def kernel(table_ref, *refs):
        own_ref, refs = refs[0], refs[1:]
        other_refs, refs = refs[:n_other], refs[n_other:]
        mine_ref, refs = refs[0], refs[1:]
        piece_refs = [refs[j * n_rep:(j + 1) * n_rep] for j in range(n_piece)]
        refs = refs[n_piece * n_rep:]
        first_refs, second_refs, refs = refs[:n_first], refs[n_first:2 * n_first], refs[2 * n_first:]
        weight_ref, outs, (scored, held, acc, sem) = refs[0], refs[1:-4], refs[-4:]
        me, rep = lax.axis_index("shard"), lax.axis_index("rep")

        def surplus_copies(s, odd):
            apart = jnp.bitwise_xor(me, s)
            rows_in = pl.ds(pl.multiple_of(lax.div(apart, jnp.int32(2)) * extra, extra), extra)
            copies = []
            for j, refs in enumerate([first_refs, second_refs]):
                for d in range(n_rep):
                    goal = held.at[s, d, j * extra:(j + 1) * extra]
                    which = refs[odd * n_rep + d].at[rows_in]
                    copies.append(pltpu.make_async_copy(which, goal, sem.at[s, j * n_rep + d]))
            return copies

        for s in range(n_shard if extra else 0):
            for odd in range(2):
                @pl.when((table_ref[s, 3] > 0) & (jnp.bitwise_and(jnp.bitwise_xor(me, s), 1) == odd))
                def _():
                    for copy in surplus_copies(s, odd):
                        copy.start()

        weight = own_ref[...]
        for ref in other_refs:
            weight = weight + ref[...].astype(F32)
        high = weight.astype(BF16)
        weight_ref[:, :width] = high
        weight_ref[:, width:] = (weight - high.astype(F32)).astype(BF16)

        scored[me] = score(weight_ref, [mine_ref[...]], jnp.int32(0))
        for parts, (hops, first, size) in zip(piece_refs, cuts):
            source = lax.rem(me + (n_shard - hops), jnp.int32(n_shard))
            scored[source, first // 8:(first + size) // 8] = score(weight_ref, [p[...] for p in parts], rep)
        last = lax.rem(me + (n_shard - last_hops), jnp.int32(n_shard))
        for s in range(n_shard):
            start = table_ref[s, 0]

            @pl.when(last != s)
            def _():
                put(acc, scored[s], start)

            if extra:
                @pl.when(table_ref[s, 3] > 0)
                def _():
                    for copy in surplus_copies(s, 0):
                        copy.wait()
                    some = pl.ds(pl.multiple_of(table_ref[s, 2] * 16, 16), extra)
                    x = [held[s, d, some, :] for d in range(n_rep)]
                    put(acc, score(weight_ref, x, rep), start + table_ref[s, 1])
        for_feats(lambda at: acc[:rows // 8, :, at].reshape(rows, width // n_feat), outs)

    count = n_shard * bulk
    surplus = [x for parts in [*firsts, *seconds] for x in parts]
    return pl.pallas_call(
        kernel,
        in_specs=[SMEM] + [VMEM] * (2 + n_other + n_rep * n_piece) + [ANY] * len(surplus),
        out_specs=[VMEM] * (1 + n_feat),
        out_shape=[jax.ShapeDtypeStruct((depth, 2 * width), BF16)] + feat_shapes(rows, width, n_feat),
        scratch_shapes=[
            pltpu.VMEM((n_shard, bulk // 8, 8, width), F32),
            pltpu.VMEM((n_shard if extra else 1, n_rep, 3 * extra + 16, columns), BF16),
            pltpu.VMEM(((rows + bulk + extra) // 8 + 2, 8, width), F32),
            pltpu.SemaphoreType.DMA((n_shard, 2 * n_rep)),
        ],
        cost_estimate=cost(4 * count * depth * width, 10 * depth * width + count * (2 * depth + 4 * width)),
        compiler_params=WIDE,
        name="early_scores",
    )(table, own, *others, mine, *[p for parts in pieces for p in parts], *surplus)


def late_scores(pieces, weight, n_feat):
    n, n_rep = len(pieces), len(pieces[0])
    rows = sum(parts[0].shape[0] for parts in pieces)
    width = weight.shape[1] // 2

    def kernel(weight_ref, *refs):
        part_refs, outs, acc = refs[:n * n_rep], refs[n * n_rep:-1], refs[-1]
        parts = [jnp.concatenate([part_refs[j * n_rep + d][...] for j in range(n)]) for d in range(n_rep)]
        acc[...] = score(weight_ref, parts, lax.axis_index("rep")).reshape(rows, width)
        for_feats(lambda at: acc[:, at], outs)

    return pl.pallas_call(
        kernel,
        in_specs=[VMEM] * (1 + n * n_rep),
        out_specs=[VMEM] * n_feat,
        out_shape=feat_shapes(rows, width, n_feat),
        scratch_shapes=[pltpu.VMEM((rows, width), F32)],
        cost_estimate=cost(4 * rows * weight.size, 8 * rows * width),
        compiler_params=PARAMS,
        name="late_scores",
    )(weight, *[p for parts in pieces for p in parts])


def merge(table, early, late, n_shard):
    rows, width = early[0].shape
    last_rows = late[0].shape[0]
    last_hops = n_shard - 1

    def kernel(table_ref, *refs):
        early_refs, late_refs = refs[:len(early)], refs[len(early):-2]
        out_ref, acc = refs[-2:]
        source = lax.rem(lax.axis_index("shard") + (n_shard - last_hops), jnp.int32(n_shard))

        def total(parts):
            value = parts[0][...]
            for ref in parts[1:]:
                value = value + ref[...].astype(F32)
            return value.reshape(value.shape[0] // 8, 8, width)

        acc[:rows // 8] = total(early_refs)
        put(acc, total(late_refs), table_ref[source, 0], table_ref[source, 1])
        out_ref[...] = acc[:rows // 8].reshape(rows, width).T

    return pl.pallas_call(
        kernel,
        in_specs=[SMEM] + [VMEM] * (len(early) + len(late)),
        out_specs=VMEM,
        out_shape=jax.ShapeDtypeStruct((width, rows), F32),
        scratch_shapes=[pltpu.VMEM(((rows + last_rows) // 8 + 2, 8, width), F32)],
        cost_estimate=cost(0, 8 * rows * width),
        compiler_params=PARAMS,
        name="merge",
    )(table, *early, *late)


def body(train, cluster_ids, precond, query_store, block_slot, pattern):
    n_group, n_shard = lax.axis_size("groups"), lax.axis_size("shard")
    n_feat, n_rep = lax.axis_size("feat"), lax.axis_size("rep")
    feat, rep = lax.axis_index("feat"), lax.axis_index("rep")
    rows = train.shape[0]
    lines = rows // LANES
    base = rows // n_shard
    columns = train.shape[1] // n_rep
    extra = base // 2 if n_shard == 4 else 0
    bulk = base if extra else base + base // 2
    ids = cluster_ids.reshape(-1, LANES)

    last_hops = n_shard - 1

    def with_rep(x):
        return [x] + [shift(x, "rep", n_rep, d) for d in range(1, n_rep)]

    matrices = with_rep(precond[0])

    picked = pick_queries(query_store, block_slot, pattern, n_group)
    pieces = [picked[0]] + [shift(picked[d], "shard", n_shard, d) for d in range(1, n_shard)]

    middle = [(d, 0, bulk) for d in range(1, last_hops)]
    fillers = 2 if bulk % 256 == 0 else 1
    sizes = [n * bulk // 16 for n in ((4, 2, 4, 3, 3) if bulk % 256 == 0 else (8, 8))]
    final = [(last_hops, sum(sizes[:j]), n) for j, n in enumerate(sizes)]
    *packed, goal = pack_rows(train, ids, columns, bulk, extra, middle + final)
    firsts, seconds = [], []
    parts = [pieces] + [[shift(x, "groups", n_group, d) for x in pieces] for d in range(1, n_group)]
    here = [shift(after(packed[0], *pieces[1:]), "shard", n_shard, 1)]
    urgent = [here[0]]
    if extra:
        far = swap(after(packed[-2], *pieces[1:]), "shard", n_shard, 2)
        urgent.append(far)
    sent_last = packed[len(middle):len(middle) + len(final)]
    last = [shift(after(x, *pieces[1:]), "shard", n_shard, last_hops) for x in sent_last[:fillers]]
    urgent += last
    depth = n_rep * columns
    targets = [(feat + d) % n_feat for d in range(1, n_feat)]
    near_chip = fetch(matrices, targets[0], depth, *pieces[1:])

    table, flag = row_table(ids, lines, bulk, extra, *pieces[1:])
    chosen = join_queries(
        parts, block_slot, pattern, query_store.shape[0], n_feat, n_rep, *near_chip, flag
    )
    queries = [*chosen[:CUTS]] + [shift(chosen[j], "rep", n_rep, j // CUTS) for j in range(CUTS, CUTS * n_rep)]

    sends = [fetched_weights(near_chip, queries, BF16)]
    sends += [partial_weights(matrices, queries, f, depth, BF16) for f in targets[1:]]
    others = [shift(x, "feat", n_feat, d + 1) for d, x in enumerate(sends)]
    own = partial_weights(matrices, queries, feat, depth, F32, *sends)

    for (hops, _, _), x in zip(middle[1:], packed[1:]):
        here.append(shift(after(x, *urgent, *sends), "shard", n_shard, hops))
        urgent = [here[-1]]
    sent_last = [after(x, own) for x in sent_last[fillers:]]
    last_all = [with_rep(after(x, own)) for x in last]

    mine = own_rows(goal, train, bulk, own)
    marks = [own, mine, *sent_last, *[p for x in last_all for p in x[1:]]]
    if extra:
        for d in range(1, n_group):
            flag = jnp.maximum(flag, shift(flag, "groups", n_group, d))

        def second_round(x):
            pair = jnp.concatenate([x, swap(x, "shard", n_shard, 2)])
            return [with_rep(pair), with_rep(swap(pair, "shard", n_shard, 1))]

        def no_round(x):
            empty = unwritten((2 * extra, columns), 2 * n_rep)
            return [[*empty[:n_rep]], [*empty[n_rep:]]]

        seconds = lax.cond(flag[0, 0] > 0, second_round, no_round, after(packed[-1], own))
        near = swap(stack([packed[-3], far], *sends), "shard", n_shard, 1)
        pairs = [stack([x, y], own) for x, y in zip(with_rep(packed[-3]), with_rep(after(far, own)))]
        firsts = [pairs, with_rep(after(near, own))]
        marks += [seconds[0][0], near, *pairs]

    mark = shift(after(jnp.zeros((8, LANES), I32), *marks), "rep", n_rep, 1)
    last += [shift(x, "shard", n_shard, last_hops) for x in sent_last]
    ready = [with_rep(after(x, mark)) for x in here]
    weight, *early = early_scores(
        own, others, mine, ready, middle, firsts, seconds, table, rows, n_feat, n_rep, n_shard, bulk, extra
    )

    def over_feat(shares):
        return [shares[0]] + [shift(shares[d], "feat", n_feat, d) for d in range(1, n_feat)]

    last_all += [with_rep(after(x, *early[1:])) for x in last[fillers:]]
    late = late_scores(last_all, weight, n_feat)
    return merge(table, over_feat(early), over_feat(late), n_shard)[None]


def solution(mesh):
    return jax.shard_map(
        body,
        mesh=mesh,
        in_specs=(
            P(("groups", "shard"), "feat"),
            P("groups"),
            P(("groups", "shard"), None, ("feat", "rep")),
            P("shard", None, ("feat", "rep")),
            P(),
            P(),
        ),
        out_specs=P(("groups", "shard"), ("feat", "rep"), None),
        check_vma=False,
    )
```

```python
import functools

import jax
import jax.numpy as jnp
from jax import lax
from jax.experimental import pallas as pl
from jax.experimental.pallas import tpu as pltpu
from jax.sharding import PartitionSpec as P

F32, BF16, I32 = jnp.float32, jnp.bfloat16, jnp.int32
VMEM = pl.BlockSpec(memory_space=pltpu.VMEM)
ANY = pl.BlockSpec(memory_space=pl.ANY)
HBM = pl.BlockSpec(memory_space=pltpu.HBM)
SMEM = pl.BlockSpec(memory_space=pltpu.SMEM)
PARAMS = pltpu.CompilerParams(vmem_limit_bytes=24 * 2**20)
WIDE = pltpu.CompilerParams(vmem_limit_bytes=32 * 2**20)
FIRST = pltpu.CompilerParams(vmem_limit_bytes=60 * 2**20)
LANES = 128
CUTS = 8


def shift(x, axis, size, by):
    return lax.ppermute(x, axis, [(i, (i + by) % size) for i in range(size)])


def swap(x, axis, size, bit):
    return lax.ppermute(x, axis, [(i, i ^ bit) for i in range(size)])


def dot(a, b):
    return jnp.dot(a, b, preferred_element_type=F32)


def cost(flops, nbytes):
    return pl.CostEstimate(flops=1, bytes_accessed=1, transcendentals=0)


def after(x, *others):
    def kernel(*refs):
        pass

    return pl.pallas_call(
        kernel,
        in_specs=[ANY] * (1 + len(others)),
        out_specs=ANY,
        out_shape=jax.ShapeDtypeStruct(x.shape, x.dtype),
        input_output_aliases={0: 0},
        cost_estimate=cost(0, 0),
        compiler_params=PARAMS,
        name="after",
    )(x, *others)


def unwritten(shape, n):
    def kernel(*refs):
        pass

    return pl.pallas_call(
        kernel,
        out_specs=[ANY] * n,
        out_shape=[jax.ShapeDtypeStruct(shape, BF16)] * n,
        cost_estimate=cost(0, 0),
        compiler_params=PARAMS,
        name="unwritten",
    )()


def stack(parts, *others):
    size, width = parts[0].shape
    n = len(parts)

    def kernel(*refs):
        for j in range(n):
            refs[-1][j * size:(j + 1) * size, :] = refs[j][...]

    return pl.pallas_call(
        kernel,
        in_specs=[VMEM] * n + [ANY] * len(others),
        out_specs=VMEM,
        out_shape=jax.ShapeDtypeStruct((n * size, width), parts[0].dtype),
        cost_estimate=cost(0, 0),
        compiler_params=PARAMS,
        name="stack",
    )(*parts, *others)


def pick_queries(query_store, block_slot, pattern, n_group):
    local_blocks, block_rows, width = query_store.shape
    n_cluster, n_list = pattern.shape
    part = block_rows // n_group

    def kernel(pattern_ref, slot_ref, in_ref, *rest):
        outs, sem = rest[:-1], rest[-1]
        me, group = lax.axis_index("shard"), lax.axis_index("groups")
        copies = []
        for t, out in enumerate(outs):
            target = lax.rem(me + t, jnp.int32(n_cluster))
            found = jnp.int32(0)
            for k in range(n_list):
                slot = slot_ref[pattern_ref[target, k]]
                hit = (lax.div(slot, jnp.int32(local_blocks)) == me).astype(I32)
                found = found + hit * lax.rem(slot, jnp.int32(local_blocks))
            rows = pl.ds(pl.multiple_of(group * part, part), part)
            copies.append(pltpu.make_async_copy(in_ref.at[found, rows], out.at[0], sem.at[t]))
            copies[-1].start()
        for copy in copies:
            copy.wait()

    return pl.pallas_call(
        kernel,
        in_specs=[SMEM, SMEM, ANY],
        out_specs=[VMEM] * n_cluster,
        out_shape=[jax.ShapeDtypeStruct((1, part, width), BF16)] * n_cluster,
        scratch_shapes=[pltpu.SemaphoreType.DMA((n_cluster,))],
        cost_estimate=cost(0, 4 * n_cluster * part * width),
        compiler_params=FIRST,
        name="pick_queries",
    )(pattern, block_slot, query_store)


def join_queries(parts, block_slot, pattern, local_blocks, n_feat, n_rep, *others):
    n_group, n_cluster = len(parts), len(parts[0])
    _, part, width = parts[0][0].shape
    n_list = pattern.shape[1]
    total = n_list * n_group * part
    share = total // (n_feat * n_rep)
    unit = min(share, part)
    half = total // n_rep

    def kernel(pattern_ref, slot_ref, *refs):
        outs, rows_ref = refs[-1 - CUTS * n_rep:-1], refs[-1]
        me, group = lax.axis_index("shard"), lax.axis_index("groups")
        for k in range(n_list):
            owner = lax.div(slot_ref[pattern_ref[me, k]], jnp.int32(local_blocks))
            hops = lax.rem(me + (n_cluster - owner), jnp.int32(n_cluster))
            for d in range(n_group):
                origin = lax.rem(group + (n_group - d), jnp.int32(n_group))
                for h in range(n_cluster):
                    @pl.when(hops == h)
                    def _():
                        for u in range(part // unit):
                            first = (k * n_group + origin) * part + u * unit
                            chunk = lax.div(first, jnp.int32(share))
                            goal = lax.rem(chunk, jnp.int32(n_rep)) * n_feat + lax.div(chunk, jnp.int32(n_rep))
                            goal = pl.multiple_of(goal * share + lax.rem(first, jnp.int32(share)), unit)
                            rows_ref[pl.ds(goal, unit), :] = refs[d * n_cluster + h][0, u * unit:(u + 1) * unit, :]
        for r in range(n_rep):
            @pl.when(lax.axis_index("rep") == r)
            def _():
                for j, out in enumerate(outs):
                    at, first = ((r + j // CUTS) % n_rep) * half, (j % CUTS) * (width // CUTS)
                    out[...] = rows_ref[at:at + half, first:first + width // CUTS].T

    return pl.pallas_call(
        kernel,
        in_specs=[SMEM, SMEM] + [VMEM] * (n_group * n_cluster) + [ANY] * len(others),
        out_specs=[VMEM] * (CUTS * n_rep),
        out_shape=[jax.ShapeDtypeStruct((width // CUTS, half), BF16)] * (CUTS * n_rep),
        scratch_shapes=[pltpu.VMEM((total, width), BF16)],
        cost_estimate=cost(0, 4 * total * width),
        compiler_params=PARAMS,
        name="join_queries",
    )(pattern, block_slot, *[x for line in parts for x in line], *others)


def one_hot(goal_ref, base, size):
    index = lax.broadcasted_iota(I32, (size, LANES), 0) + base
    lines = range(goal_ref.shape[0])
    return jnp.concatenate([(index == goal_ref[a:a + 1, :]).astype(F32).astype(BF16) for a in lines], axis=1)


def select(goal_ref, train_ref, base, size):
    tile = 128 if size % 128 == 0 else size
    found = [dot(one_hot(goal_ref, base + at, tile), train_ref[...]).astype(BF16) for at in range(0, size, tile)]
    return jnp.concatenate(found)


def own_rows(goal, train, bulk, *others):
    rows, width = train.shape
    cuts = 4
    part = width // cuts

    def kernel(goal_ref, train_ref, *rest):
        out_ref, held, sem = rest[-3:]
        copies = [
            pltpu.make_async_copy(train_ref.at[:, c * part:(c + 1) * part], held.at[c], sem.at[c]) for c in range(cuts)
        ]
        for copy in copies:
            copy.start()
        pick = one_hot(goal_ref, lax.axis_index("shard") * bulk, bulk)
        for c, copy in enumerate(copies):
            copy.wait()
            out_ref[:, c * part:(c + 1) * part] = dot(pick, held[c]).astype(BF16)

    return pl.pallas_call(
        kernel,
        in_specs=[VMEM, HBM] + [ANY] * len(others),
        out_specs=VMEM,
        out_shape=jax.ShapeDtypeStruct((bulk, width), BF16),
        scratch_shapes=[pltpu.VMEM((cuts, rows, part), BF16), pltpu.SemaphoreType.DMA((cuts,))],
        cost_estimate=cost(2 * bulk * train.size, 2 * train.size),
        compiler_params=PARAMS,
        name="own_rows",
    )(goal, train, *others)


def pack_rows(train, ids, columns, bulk, extra, cuts):
    rows = train.shape[0]
    lines = rows // LANES
    n_shard = ids.shape[0] // lines

    def kernel(ids_ref, train_ref, *rest):
        outs, goal_ref = rest[:-1], rest[-1]
        me = lax.axis_index("shard")
        own = ids_ref[...]
        masks = [(own == c).astype(F32) for c in range(n_shard)]
        stacked = jnp.concatenate(masks, axis=0).astype(BF16)
        lane_from = lax.broadcasted_iota(I32, (LANES, LANES), 0)
        lane_to = lax.broadcasted_iota(I32, (LANES, LANES), 1)
        in_line = dot(stacked, (lane_from < lane_to).astype(F32).astype(BF16))
        line_sum = dot(stacked, jnp.ones((LANES, LANES), BF16)).astype(BF16)
        size = n_shard * lines
        to = lax.broadcasted_iota(I32, (size, size), 0)
        since = lax.broadcasted_iota(I32, (size, size), 1)
        same = (to // lines) == (since // lines)
        ahead = dot((same & (since < to)).astype(F32).astype(BF16), line_sum)
        whole = dot(same.astype(F32).astype(BF16), line_sum)
        rank = in_line + ahead
        goal = jnp.zeros((lines, LANES), F32)
        past = jnp.zeros((lines, LANES), F32)
        for c in range(n_shard):
            part = slice(c * lines, (c + 1) * lines)
            place = rank[part] + c * bulk
            if extra:
                surplus = n_shard * bulk + past + rank[part] - bulk
                place = jnp.where(rank[part] < bulk, place, surplus)
                past = past + jnp.floor((jnp.maximum(whole[part] - bulk, 0.0) + 15.0) * 0.0625) * 16.0
            goal = goal + masks[c] * place
        goal_ref[...] = goal.astype(I32)

        def fill(out, base):
            out[...] = select(goal_ref, train_ref, base, out.shape[0])

        for out, (hops, first, _) in zip(outs, cuts):
            fill(out, lax.rem(me + hops, jnp.int32(n_shard)) * bulk + first)
        for j, out in enumerate(outs[len(cuts):]):
            fill(out, n_shard * bulk + max(j - 1, 0) * extra)

    shapes = [jax.ShapeDtypeStruct((n, columns), BF16) for _, _, n in cuts]
    shapes += [jax.ShapeDtypeStruct((extra, columns), BF16)] * (3 if extra else 0)
    shapes += [jax.ShapeDtypeStruct((lines, LANES), I32)]
    packed = n_shard * bulk + 2 * extra
    return pl.pallas_call(
        kernel,
        grid=(1,),
        in_specs=[
            pl.BlockSpec((lines, LANES), lambda i: (lax.axis_index("shard"), 0)),
            pl.BlockSpec((rows, columns), lambda i: (0, lax.axis_index("rep"))),
        ],
        out_specs=[VMEM] * len(shapes),
        out_shape=shapes,
        cost_estimate=cost(2 * packed * rows * columns, 2 * (rows + packed) * columns),
        compiler_params=FIRST,
        name="pack_rows",
    )(ids, train)


def partial_weights(matrices, queries, block, depth, dtype, *others):
    width, total = matrices[0].shape[1], queries[0].shape[1]
    tile = 512 if depth % 512 == 0 else depth
    steps = depth // tile
    n = len(matrices)

    def kernel(block_ref, *refs):
        out_ref, held, sem = refs[-3:]
        first = pl.multiple_of(block_ref[0] * depth, depth)
        copies = []
        for i in range(steps):
            for j in range(n):
                source = refs[j].at[pl.ds(first + i * tile, tile)]
                copies.append(pltpu.make_async_copy(source, held.at[j, i], sem.at[i * n + j]))
        for copy in copies:
            copy.start()
        parts = [jnp.concatenate([r[...] for r in refs[n + CUTS * j:n + CUTS * (j + 1)]]) for j in range(n)]
        for i in range(steps):
            value = None
            for j in range(n):
                copies[i * n + j].wait()
                part = dot(held[j, i], parts[j])
                value = part if value is None else value + part
            out_ref[i * tile:(i + 1) * tile, :] = value.astype(dtype)

    return pl.pallas_call(
        kernel,
        in_specs=[SMEM] + [HBM] * n + [VMEM] * (CUTS * n) + [ANY] * len(others),
        out_specs=VMEM,
        out_shape=jax.ShapeDtypeStruct((depth, total), dtype),
        scratch_shapes=[pltpu.VMEM((n, steps, tile, width), BF16), pltpu.SemaphoreType.DMA((steps * n,))],
        cost_estimate=cost(2 * n * depth * width * total, 2 * n * depth * width + 4 * depth * total),
        compiler_params=PARAMS,
        name="partial_weights",
    )(jnp.reshape(block, (1,)).astype(I32), *matrices, *queries, *others)


def fetch(matrices, block, depth, *others):
    width = matrices[0].shape[1]
    n = len(matrices)
    cuts = 4

    def kernel(block_ref, *refs):
        outs, sem = refs[-1 - n:-1], refs[-1]
        first = pl.multiple_of(block_ref[0] * depth, depth)
        copies = []
        for j in range(n):
            for c in range(cuts):
                size = depth // cuts
                source = refs[j].at[pl.ds(first + c * size, size)]
                copies.append(
                    pltpu.make_async_copy(source, outs[j].at[c * size:(c + 1) * size], sem.at[j * cuts + c])
                )
        for copy in copies:
            copy.start()
        for copy in copies:
            copy.wait()

    return pl.pallas_call(
        kernel,
        in_specs=[SMEM] + [HBM] * n + [ANY] * len(others),
        out_specs=[VMEM] * n,
        out_shape=[jax.ShapeDtypeStruct((depth, width), BF16)] * n,
        scratch_shapes=[pltpu.SemaphoreType.DMA((n * cuts,))],
        cost_estimate=cost(0, 2 * n * depth * width),
        compiler_params=PARAMS,
        name="fetch",
    )(jnp.reshape(block, (1,)).astype(I32), *matrices, *others)


def fetched_weights(matrices, queries, dtype):
    depth = matrices[0].shape[0]
    total = queries[0].shape[1]
    tile = 512 if depth % 512 == 0 else depth
    n = len(matrices)

    def kernel(*refs):
        parts = [jnp.concatenate([r[...] for r in refs[n + CUTS * j:n + CUTS * (j + 1)]]) for j in range(n)]
        for at in range(0, depth, tile):
            value = None
            for j in range(n):
                part = dot(refs[j][at:at + tile, :], parts[j])
                value = part if value is None else value + part
            refs[-1][at:at + tile, :] = value.astype(dtype)

    return pl.pallas_call(
        kernel,
        in_specs=[VMEM] * ((1 + CUTS) * n),
        out_specs=VMEM,
        out_shape=jax.ShapeDtypeStruct((depth, total), dtype),
        cost_estimate=cost(2 * n * matrices[0].size * total, 2 * n * matrices[0].size),
        compiler_params=PARAMS,
        name="fetched_weights",
    )(*matrices, *queries)


def row_table(ids, lines, bulk, extra, *others):
    n_shard = ids.shape[0] // lines

    def kernel(ids_ref, *rest):
        table_ref, flag_ref = rest[-2:]
        me = lax.axis_index("shard")
        start = jnp.int32(0)
        most = jnp.int32(0)
        for s in range(n_shard):
            line = ids_ref[s * lines:(s + 1) * lines, :]

            def count(c):
                return jnp.sum((line == c).astype(I32))

            mine = count(me)
            before = jnp.int32(0)
            if extra:
                surplus = jnp.int32(0)
                for c in range(n_shard):
                    over = lax.div(jnp.maximum(count(c) - bulk, 0) + 15, jnp.int32(16)) * 16
                    before = before + jnp.where(c < me, over, 0)
                    surplus = surplus + over
                most = jnp.maximum(most, surplus)
            table_ref[s, 0] = start
            table_ref[s, 1] = jnp.minimum(mine, bulk)
            table_ref[s, 2] = lax.div(before, jnp.int32(16))
            table_ref[s, 3] = jnp.maximum(mine - bulk, 0)
            start = start + mine
        flag_ref[...] = jnp.full((8, LANES), (most > extra).astype(I32))

    return pl.pallas_call(
        kernel,
        in_specs=[VMEM] + [ANY] * len(others),
        out_specs=[SMEM, VMEM],
        out_shape=[jax.ShapeDtypeStruct((n_shard, 4), I32), jax.ShapeDtypeStruct((8, LANES), I32)],
        cost_estimate=cost(0, 4 * ids.size),
        compiler_params=PARAMS,
        name="row_table",
    )(ids, *others)


def put(acc, x, start, count=None):
    tiles, _, width = x.shape
    first, within = lax.div(start, jnp.int32(8)), lax.rem(start, jnp.int32(8))
    turned = pltpu.roll(x, within, 1)
    row = lax.broadcasted_iota(I32, (1, 8, width), 1)
    keep = row < within
    pieces = jnp.where(keep, jnp.concatenate([turned[:1], turned]), jnp.concatenate([turned, turned[-1:]]))
    if count is None:
        pieces = jnp.concatenate([jnp.where(keep, acc[pl.ds(first, 1)], turned[:1]), pieces[1:]])
    else:
        at = lax.broadcasted_iota(I32, (tiles + 1, 8, width), 0) * 8 + lax.broadcasted_iota(
            I32, (tiles + 1, 8, width), 1
        )
        pieces = jnp.where(
            (at >= within) & (at < within + count), pieces, acc[pl.ds(first, tiles + 1)]
        )
    acc[pl.ds(first, tiles + 1)] = pieces


def score(weight_ref, parts, rep):
    total = None
    for d, x in enumerate(parts):
        depth = x.shape[1]
        block = pl.ds(pl.multiple_of(lax.rem(rep + (len(parts) - d), jnp.int32(len(parts))) * depth, depth), depth)
        value = dot(x, weight_ref[block, :])
        total = value if total is None else total + value
    width = total.shape[1] // 2
    total = total[:, :width] + total[:, width:]
    return total.reshape(total.shape[0] // 8, 8, width)


def for_feats(value, outs):
    n = len(outs)
    share = outs[0].shape[1]
    for f in range(n):
        @pl.when(lax.axis_index("feat") == f)
        def _():
            for d, out in enumerate(outs):
                at = ((f + d) % n) * share
                out[...] = value(slice(at, at + share)).astype(out.dtype)


def feat_shapes(rows, width, n_feat):
    share = (rows, width // n_feat)
    return [jax.ShapeDtypeStruct(share, F32)] + [jax.ShapeDtypeStruct(share, BF16)] * (n_feat - 1)


def early_scores(own, others, mine, pieces, cuts, firsts, seconds, table, rows, n_feat, n_rep, n_shard, bulk, extra):
    depth, width = own.shape
    columns = depth // n_rep
    n_other, n_piece = len(others), len(pieces)
    n_first = len(firsts) * n_rep
    last_hops = n_shard - 1

    def kernel(table_ref, *refs):
        own_ref, refs = refs[0], refs[1:]
        other_refs, refs = refs[:n_other], refs[n_other:]
        mine_ref, refs = refs[0], refs[1:]
        piece_refs = [refs[j * n_rep:(j + 1) * n_rep] for j in range(n_piece)]
        refs = refs[n_piece * n_rep:]
        first_refs, second_refs, refs = refs[:n_first], refs[n_first:2 * n_first], refs[2 * n_first:]
        weight_ref, outs, (scored, held, acc, sem) = refs[0], refs[1:-4], refs[-4:]
        me, rep = lax.axis_index("shard"), lax.axis_index("rep")

        def surplus_copies(s, odd):
            apart = jnp.bitwise_xor(me, s)
            rows_in = pl.ds(pl.multiple_of(lax.div(apart, jnp.int32(2)) * extra, extra), extra)
            copies = []
            for j, refs in enumerate([first_refs, second_refs]):
                for d in range(n_rep):
                    goal = held.at[s, d, j * extra:(j + 1) * extra]
                    which = refs[odd * n_rep + d].at[rows_in]
                    copies.append(pltpu.make_async_copy(which, goal, sem.at[s, j * n_rep + d]))
            return copies

        for s in range(n_shard if extra else 0):
            for odd in range(2):
                @pl.when((table_ref[s, 3] > 0) & (jnp.bitwise_and(jnp.bitwise_xor(me, s), 1) == odd))
                def _():
                    for copy in surplus_copies(s, odd):
                        copy.start()

        weight = own_ref[...]
        for ref in other_refs:
            weight = weight + ref[...].astype(F32)
        high = weight.astype(BF16)
        weight_ref[:, :width] = high
        weight_ref[:, width:] = (weight - high.astype(F32)).astype(BF16)

        scored[me] = score(weight_ref, [mine_ref[...]], jnp.int32(0))
        for parts, (hops, first, size) in zip(piece_refs, cuts):
            source = lax.rem(me + (n_shard - hops), jnp.int32(n_shard))
            scored[source, first // 8:(first + size) // 8] = score(weight_ref, [p[...] for p in parts], rep)
        last = lax.rem(me + (n_shard - last_hops), jnp.int32(n_shard))
        for s in range(n_shard):
            start = table_ref[s, 0]

            @pl.when(last != s)
            def _():
                put(acc, scored[s], start)

            if extra:
                @pl.when(table_ref[s, 3] > 0)
                def _():
                    for copy in surplus_copies(s, 0):
                        copy.wait()
                    some = pl.ds(pl.multiple_of(table_ref[s, 2] * 16, 16), extra)
                    x = [held[s, d, some, :] for d in range(n_rep)]
                    put(acc, score(weight_ref, x, rep), start + table_ref[s, 1])
        for_feats(lambda at: acc[:rows // 8, :, at].reshape(rows, width // n_feat), outs)

    count = n_shard * bulk
    surplus = [x for parts in [*firsts, *seconds] for x in parts]
    return pl.pallas_call(
        kernel,
        in_specs=[SMEM] + [VMEM] * (2 + n_other + n_rep * n_piece) + [ANY] * len(surplus),
        out_specs=[VMEM] * (1 + n_feat),
        out_shape=[jax.ShapeDtypeStruct((depth, 2 * width), BF16)] + feat_shapes(rows, width, n_feat),
        scratch_shapes=[
            pltpu.VMEM((n_shard, bulk // 8, 8, width), F32),
            pltpu.VMEM((n_shard if extra else 1, n_rep, 3 * extra + 16, columns), BF16),
            pltpu.VMEM(((rows + bulk + extra) // 8 + 2, 8, width), F32),
            pltpu.SemaphoreType.DMA((n_shard, 2 * n_rep)),
        ],
        cost_estimate=cost(4 * count * depth * width, 10 * depth * width + count * (2 * depth + 4 * width)),
        compiler_params=WIDE,
        name="early_scores",
    )(table, own, *others, mine, *[p for parts in pieces for p in parts], *surplus)


def late_scores(pieces, weight, n_feat):
    n, n_rep = len(pieces), len(pieces[0])
    rows = sum(parts[0].shape[0] for parts in pieces)
    width = weight.shape[1] // 2

    def kernel(weight_ref, *refs):
        part_refs, outs, acc = refs[:n * n_rep], refs[n * n_rep:-1], refs[-1]
        parts = [jnp.concatenate([part_refs[j * n_rep + d][...] for j in range(n)]) for d in range(n_rep)]
        acc[...] = score(weight_ref, parts, lax.axis_index("rep")).reshape(rows, width)
        for_feats(lambda at: acc[:, at], outs)

    return pl.pallas_call(
        kernel,
        in_specs=[VMEM] * (1 + n * n_rep),
        out_specs=[VMEM] * n_feat,
        out_shape=feat_shapes(rows, width, n_feat),
        scratch_shapes=[pltpu.VMEM((rows, width), F32)],
        cost_estimate=cost(4 * rows * weight.size, 8 * rows * width),
        compiler_params=PARAMS,
        name="late_scores",
    )(weight, *[p for parts in pieces for p in parts])


def merge(table, early, late, n_shard):
    rows, width = early[0].shape
    last_rows = late[0].shape[0]
    last_hops = n_shard - 1

    def kernel(table_ref, *refs):
        early_refs, late_refs = refs[:len(early)], refs[len(early):-2]
        out_ref, acc = refs[-2:]
        source = lax.rem(lax.axis_index("shard") + (n_shard - last_hops), jnp.int32(n_shard))

        def total(parts):
            value = parts[0][...]
            for ref in parts[1:]:
                value = value + ref[...].astype(F32)
            return value.reshape(value.shape[0] // 8, 8, width)

        acc[:rows // 8] = total(early_refs)
        put(acc, total(late_refs), table_ref[source, 0], table_ref[source, 1])
        out_ref[...] = acc[:rows // 8].reshape(rows, width).T

    return pl.pallas_call(
        kernel,
        in_specs=[SMEM] + [VMEM] * (len(early) + len(late)),
        out_specs=VMEM,
        out_shape=jax.ShapeDtypeStruct((width, rows), F32),
        scratch_shapes=[pltpu.VMEM(((rows + last_rows) // 8 + 2, 8, width), F32)],
        cost_estimate=cost(0, 8 * rows * width),
        compiler_params=PARAMS,
        name="merge",
    )(table, *early, *late)


def body(train, cluster_ids, precond, query_store, block_slot, pattern):
    n_group, n_shard = lax.axis_size("groups"), lax.axis_size("shard")
    n_feat, n_rep = lax.axis_size("feat"), lax.axis_size("rep")
    feat, rep = lax.axis_index("feat"), lax.axis_index("rep")
    rows = train.shape[0]
    lines = rows // LANES
    base = rows // n_shard
    columns = train.shape[1] // n_rep
    extra = base // 2 if n_shard == 4 else 0
    bulk = base if extra else base + base // 2
    ids = cluster_ids.reshape(-1, LANES)

    last_hops = n_shard - 1

    def with_rep(x):
        return [x] + [shift(x, "rep", n_rep, d) for d in range(1, n_rep)]

    matrices = with_rep(precond[0])

    picked = pick_queries(query_store, block_slot, pattern, n_group)
    pieces = [picked[0]] + [shift(picked[d], "shard", n_shard, d) for d in range(1, n_shard)]

    middle = [(d, 0, bulk) for d in range(1, last_hops)]
    fillers = 2 if bulk % 256 == 0 else 1
    sizes = [n * bulk // 16 for n in ((3, 2, 4, 4, 3) if bulk % 256 == 0 else (8, 8))]
    final = [(last_hops, sum(sizes[:j]), n) for j, n in enumerate(sizes)]
    *packed, goal = pack_rows(train, ids, columns, bulk, extra, middle + final)
    firsts, seconds = [], []
    parts = [pieces] + [[shift(x, "groups", n_group, d) for x in pieces] for d in range(1, n_group)]
    here = [shift(after(packed[0], *pieces[1:]), "shard", n_shard, 1)]
    urgent = [here[0]]
    if extra:
        far = swap(after(packed[-2], *pieces[1:]), "shard", n_shard, 2)
        urgent.append(far)
    sent_last = packed[len(middle):len(middle) + len(final)]
    last = [shift(after(x, *pieces[1:]), "shard", n_shard, last_hops) for x in sent_last[:fillers]]
    urgent += last
    depth = n_rep * columns
    targets = [(feat + d) % n_feat for d in range(1, n_feat)]
    near_chip = fetch(matrices, targets[0], depth, *pieces[1:])

    table, flag = row_table(ids, lines, bulk, extra, *pieces[1:])
    chosen = join_queries(
        parts, block_slot, pattern, query_store.shape[0], n_feat, n_rep, *near_chip, flag
    )
    queries = [*chosen[:CUTS]] + [shift(chosen[j], "rep", n_rep, j // CUTS) for j in range(CUTS, CUTS * n_rep)]

    sends = [fetched_weights(near_chip, queries, BF16)]
    sends += [partial_weights(matrices, queries, f, depth, BF16) for f in targets[1:]]
    others = [shift(x, "feat", n_feat, d + 1) for d, x in enumerate(sends)]
    own = partial_weights(matrices, queries, feat, depth, F32, *sends)

    for (hops, _, _), x in zip(middle[1:], packed[1:]):
        here.append(shift(after(x, *urgent, *sends), "shard", n_shard, hops))
        urgent = [here[-1]]
    sent_last = [after(x, own) for x in sent_last[fillers:]]
    last_all = [with_rep(after(x, own)) for x in last]

    mine = own_rows(goal, train, bulk, own)
    marks = [own, mine, *sent_last, *[p for x in last_all for p in x[1:]]]
    if extra:
        for d in range(1, n_group):
            flag = jnp.maximum(flag, shift(flag, "groups", n_group, d))

        def second_round(x):
            pair = jnp.concatenate([x, swap(x, "shard", n_shard, 2)])
            return [with_rep(pair), with_rep(swap(pair, "shard", n_shard, 1))]

        def no_round(x):
            empty = unwritten((2 * extra, columns), 2 * n_rep)
            return [[*empty[:n_rep]], [*empty[n_rep:]]]

        seconds = lax.cond(flag[0, 0] > 0, second_round, no_round, after(packed[-1], own))
        near = swap(stack([packed[-3], far], *sends), "shard", n_shard, 1)
        pairs = [stack([x, y], own) for x, y in zip(with_rep(packed[-3]), with_rep(after(far, own)))]
        firsts = [pairs, with_rep(after(near, own))]
        marks += [seconds[0][0], near, *pairs]

    mark = shift(after(jnp.zeros((8, LANES), I32), *marks), "rep", n_rep, 1)
    last += [shift(x, "shard", n_shard, last_hops) for x in sent_last]
    ready = [with_rep(after(x, mark)) for x in here]
    weight, *early = early_scores(
        own, others, mine, ready, middle, firsts, seconds, table, rows, n_feat, n_rep, n_shard, bulk, extra
    )

    def over_feat(shares):
        return [shares[0]] + [shift(shares[d], "feat", n_feat, d) for d in range(1, n_feat)]

    last_all += [with_rep(after(x, *early[1:])) for x in last[fillers:]]
    late = late_scores(last_all, weight, n_feat)
    return merge(table, over_feat(early), over_feat(late), n_shard)[None]


def solution(mesh):
    return jax.shard_map(
        body,
        mesh=mesh,
        in_specs=(
            P(("groups", "shard"), "feat"),
            P("groups"),
            P(("groups", "shard"), None, ("feat", "rep")),
            P("shard", None, ("feat", "rep")),
            P(),
            P(),
        ),
        out_specs=P(("groups", "shard"), ("feat", "rep"), None),
        check_vma=False,
    )
```

```python
import functools

import jax
import jax.numpy as jnp
from jax import lax
from jax.experimental import pallas as pl
from jax.experimental.pallas import tpu as pltpu
from jax.sharding import PartitionSpec as P

F32, BF16, I32 = jnp.float32, jnp.bfloat16, jnp.int32
VMEM = pl.BlockSpec(memory_space=pltpu.VMEM)
ANY = pl.BlockSpec(memory_space=pl.ANY)
HBM = pl.BlockSpec(memory_space=pltpu.HBM)
SMEM = pl.BlockSpec(memory_space=pltpu.SMEM)
PARAMS = pltpu.CompilerParams(vmem_limit_bytes=24 * 2**20)
WIDE = pltpu.CompilerParams(vmem_limit_bytes=32 * 2**20)
FIRST = pltpu.CompilerParams(vmem_limit_bytes=60 * 2**20)
LANES = 128
CUTS = 8


def shift(x, axis, size, by):
    return lax.ppermute(x, axis, [(i, (i + by) % size) for i in range(size)])


def swap(x, axis, size, bit):
    return lax.ppermute(x, axis, [(i, i ^ bit) for i in range(size)])


def dot(a, b):
    return jnp.dot(a, b, preferred_element_type=F32)


def cost(flops, nbytes):
    return pl.CostEstimate(flops=1, bytes_accessed=1, transcendentals=0)


def after(x, *others):
    def kernel(*refs):
        pass

    return pl.pallas_call(
        kernel,
        in_specs=[ANY] * (1 + len(others)),
        out_specs=ANY,
        out_shape=jax.ShapeDtypeStruct(x.shape, x.dtype),
        input_output_aliases={0: 0},
        cost_estimate=cost(0, 0),
        compiler_params=PARAMS,
        name="after",
    )(x, *others)


def unwritten(shape, n):
    def kernel(*refs):
        pass

    return pl.pallas_call(
        kernel,
        out_specs=[ANY] * n,
        out_shape=[jax.ShapeDtypeStruct(shape, BF16)] * n,
        cost_estimate=cost(0, 0),
        compiler_params=PARAMS,
        name="unwritten",
    )()


def stack(parts, *others):
    size, width = parts[0].shape
    n = len(parts)

    def kernel(*refs):
        for j in range(n):
            refs[-1][j * size:(j + 1) * size, :] = refs[j][...]

    return pl.pallas_call(
        kernel,
        in_specs=[VMEM] * n + [ANY] * len(others),
        out_specs=VMEM,
        out_shape=jax.ShapeDtypeStruct((n * size, width), parts[0].dtype),
        cost_estimate=cost(0, 0),
        compiler_params=PARAMS,
        name="stack",
    )(*parts, *others)


def pick_queries(query_store, block_slot, pattern, n_group):
    local_blocks, block_rows, width = query_store.shape
    n_cluster, n_list = pattern.shape
    part = block_rows // n_group

    def kernel(pattern_ref, slot_ref, in_ref, *rest):
        outs, sem = rest[:-1], rest[-1]
        me, group = lax.axis_index("shard"), lax.axis_index("groups")
        copies = []
        for t, out in enumerate(outs):
            target = lax.rem(me + t, jnp.int32(n_cluster))
            found = jnp.int32(0)
            for k in range(n_list):
                slot = slot_ref[pattern_ref[target, k]]
                hit = (lax.div(slot, jnp.int32(local_blocks)) == me).astype(I32)
                found = found + hit * lax.rem(slot, jnp.int32(local_blocks))
            rows = pl.ds(pl.multiple_of(group * part, part), part)
            copies.append(pltpu.make_async_copy(in_ref.at[found, rows], out.at[0], sem.at[t]))
            copies[-1].start()
        for copy in copies:
            copy.wait()

    return pl.pallas_call(
        kernel,
        in_specs=[SMEM, SMEM, ANY],
        out_specs=[VMEM] * n_cluster,
        out_shape=[jax.ShapeDtypeStruct((1, part, width), BF16)] * n_cluster,
        scratch_shapes=[pltpu.SemaphoreType.DMA((n_cluster,))],
        cost_estimate=cost(0, 4 * n_cluster * part * width),
        compiler_params=FIRST,
        name="pick_queries",
    )(pattern, block_slot, query_store)


def join_queries(parts, block_slot, pattern, local_blocks, n_feat, n_rep, *others):
    n_group, n_cluster = len(parts), len(parts[0])
    _, part, width = parts[0][0].shape
    n_list = pattern.shape[1]
    total = n_list * n_group * part
    share = total // (n_feat * n_rep)
    unit = min(share, part)
    half = total // n_rep

    def kernel(pattern_ref, slot_ref, *refs):
        outs, rows_ref = refs[-1 - CUTS * n_rep:-1], refs[-1]
        me, group = lax.axis_index("shard"), lax.axis_index("groups")
        for k in range(n_list):
            owner = lax.div(slot_ref[pattern_ref[me, k]], jnp.int32(local_blocks))
            hops = lax.rem(me + (n_cluster - owner), jnp.int32(n_cluster))
            for d in range(n_group):
                origin = lax.rem(group + (n_group - d), jnp.int32(n_group))
                for h in range(n_cluster):
                    @pl.when(hops == h)
                    def _():
                        for u in range(part // unit):
                            first = (k * n_group + origin) * part + u * unit
                            chunk = lax.div(first, jnp.int32(share))
                            goal = lax.rem(chunk, jnp.int32(n_rep)) * n_feat + lax.div(chunk, jnp.int32(n_rep))
                            goal = pl.multiple_of(goal * share + lax.rem(first, jnp.int32(share)), unit)
                            rows_ref[pl.ds(goal, unit), :] = refs[d * n_cluster + h][0, u * unit:(u + 1) * unit, :]
        for r in range(n_rep):
            @pl.when(lax.axis_index("rep") == r)
            def _():
                for j, out in enumerate(outs):
                    at, first = ((r + j // CUTS) % n_rep) * half, (j % CUTS) * (width // CUTS)
                    out[...] = rows_ref[at:at + half, first:first + width // CUTS].T

    return pl.pallas_call(
        kernel,
        in_specs=[SMEM, SMEM] + [VMEM] * (n_group * n_cluster) + [ANY] * len(others),
        out_specs=[VMEM] * (CUTS * n_rep),
        out_shape=[jax.ShapeDtypeStruct((width // CUTS, half), BF16)] * (CUTS * n_rep),
        scratch_shapes=[pltpu.VMEM((total, width), BF16)],
        cost_estimate=cost(0, 4 * total * width),
        compiler_params=PARAMS,
        name="join_queries",
    )(pattern, block_slot, *[x for line in parts for x in line], *others)


def one_hot(goal_ref, base, size):
    index = lax.broadcasted_iota(I32, (size, LANES), 0) + base
    lines = range(goal_ref.shape[0])
    return jnp.concatenate([(index == goal_ref[a:a + 1, :]).astype(F32).astype(BF16) for a in lines], axis=1)


def select(goal_ref, train_ref, base, size):
    tile = 128 if size % 128 == 0 else size
    found = [dot(one_hot(goal_ref, base + at, tile), train_ref[...]).astype(BF16) for at in range(0, size, tile)]
    return jnp.concatenate(found)


def own_rows(goal, train, n_shard, n_rep, bulk, extra, *others):
    rows, width = train.shape
    cuts = 2 * n_rep
    part = width // cuts
    per = cuts // n_rep

    def kernel(goal_ref, train_ref, *rest):
        outs, (held, sem) = rest[len(others):-2], rest[-2:]
        copies = [
            pltpu.make_async_copy(train_ref.at[:, c * part:(c + 1) * part], held.at[c], sem.at[c]) for c in range(cuts)
        ]
        for copy in copies:
            copy.start()
        pick = one_hot(goal_ref, lax.axis_index("shard") * bulk, bulk)
        for c, copy in enumerate(copies):
            copy.wait()
            outs[0][:, c * part:(c + 1) * part] = dot(pick, held[c]).astype(BF16)
        if extra:
            second = one_hot(goal_ref, n_shard * bulk + extra, extra)
            for r in range(n_rep):
                @pl.when(lax.axis_index("rep") == r)
                def _():
                    for c in range(per):
                        outs[1][:, c * part:(c + 1) * part] = dot(second, held[r * per + c]).astype(BF16)

    shapes = [jax.ShapeDtypeStruct((bulk, width), BF16)]
    shapes += [jax.ShapeDtypeStruct((extra, width // n_rep), BF16)] * (1 if extra else 0)
    return pl.pallas_call(
        kernel,
        in_specs=[VMEM, HBM] + [ANY] * len(others),
        out_specs=[VMEM] * len(shapes),
        out_shape=shapes,
        scratch_shapes=[pltpu.VMEM((cuts, rows, part), BF16), pltpu.SemaphoreType.DMA((cuts,))],
        cost_estimate=cost(2 * bulk * train.size, 2 * train.size),
        compiler_params=PARAMS,
        name="own_rows",
    )(goal, train, *others)


def pack_rows(train, ids, columns, bulk, extra, cuts):
    rows = train.shape[0]
    lines = rows // LANES
    n_shard = ids.shape[0] // lines

    def kernel(ids_ref, train_ref, *rest):
        outs, goal_ref = rest[:-1], rest[-1]
        me = lax.axis_index("shard")
        own = ids_ref[...]
        masks = [(own == c).astype(F32) for c in range(n_shard)]
        stacked = jnp.concatenate(masks, axis=0).astype(BF16)
        lane_from = lax.broadcasted_iota(I32, (LANES, LANES), 0)
        lane_to = lax.broadcasted_iota(I32, (LANES, LANES), 1)
        in_line = dot(stacked, (lane_from < lane_to).astype(F32).astype(BF16))
        line_sum = dot(stacked, jnp.ones((LANES, LANES), BF16)).astype(BF16)
        size = n_shard * lines
        to = lax.broadcasted_iota(I32, (size, size), 0)
        since = lax.broadcasted_iota(I32, (size, size), 1)
        same = (to // lines) == (since // lines)
        ahead = dot((same & (since < to)).astype(F32).astype(BF16), line_sum)
        whole = dot(same.astype(F32).astype(BF16), line_sum)
        rank = in_line + ahead
        goal = jnp.zeros((lines, LANES), F32)
        past = jnp.zeros((lines, LANES), F32)
        for c in range(n_shard):
            part = slice(c * lines, (c + 1) * lines)
            place = rank[part] + c * bulk
            if extra:
                surplus = n_shard * bulk + past + rank[part] - bulk
                place = jnp.where(rank[part] < bulk, place, surplus)
                past = past + jnp.floor((jnp.maximum(whole[part] - bulk, 0.0) + 15.0) * 0.0625) * 16.0
            goal = goal + masks[c] * place
        goal_ref[...] = goal.astype(I32)

        def fill(out, base):
            out[...] = select(goal_ref, train_ref, base, out.shape[0])

        for out, (hops, first, _) in zip(outs, cuts):
            fill(out, lax.rem(me + hops, jnp.int32(n_shard)) * bulk + first)
        if extra:
            fill(outs[-1], n_shard * bulk)
            outs[-2][...] = outs[-1][...]

    shapes = [jax.ShapeDtypeStruct((n, columns), BF16) for _, _, n in cuts]
    shapes += [jax.ShapeDtypeStruct((extra, columns), BF16)] * (2 if extra else 0)
    shapes += [jax.ShapeDtypeStruct((lines, LANES), I32)]
    packed = n_shard * bulk + 2 * extra
    return pl.pallas_call(
        kernel,
        grid=(1,),
        in_specs=[
            pl.BlockSpec((lines, LANES), lambda i: (lax.axis_index("shard"), 0)),
            pl.BlockSpec((rows, columns), lambda i: (0, lax.axis_index("rep"))),
        ],
        out_specs=[VMEM] * len(shapes),
        out_shape=shapes,
        cost_estimate=cost(2 * packed * rows * columns, 2 * (rows + packed) * columns),
        compiler_params=FIRST,
        name="pack_rows",
    )(ids, train)


def partial_weights(matrices, queries, block, depth, dtype, *others):
    width, total = matrices[0].shape[1], queries[0].shape[1]
    tile = 512 if depth % 512 == 0 else depth
    steps = depth // tile
    n = len(matrices)

    def kernel(block_ref, *refs):
        out_ref, held, sem = refs[-3:]
        first = pl.multiple_of(block_ref[0] * depth, depth)
        copies = []
        for i in range(steps):
            for j in range(n):
                source = refs[j].at[pl.ds(first + i * tile, tile)]
                copies.append(pltpu.make_async_copy(source, held.at[j, i], sem.at[i * n + j]))
        for copy in copies:
            copy.start()
        parts = [jnp.concatenate([r[...] for r in refs[n + CUTS * j:n + CUTS * (j + 1)]]) for j in range(n)]
        for i in range(steps):
            value = None
            for j in range(n):
                copies[i * n + j].wait()
                part = dot(held[j, i], parts[j])
                value = part if value is None else value + part
            out_ref[i * tile:(i + 1) * tile, :] = value.astype(dtype)

    return pl.pallas_call(
        kernel,
        in_specs=[SMEM] + [HBM] * n + [VMEM] * (CUTS * n) + [ANY] * len(others),
        out_specs=VMEM,
        out_shape=jax.ShapeDtypeStruct((depth, total), dtype),
        scratch_shapes=[pltpu.VMEM((n, steps, tile, width), BF16), pltpu.SemaphoreType.DMA((steps * n,))],
        cost_estimate=cost(2 * n * depth * width * total, 2 * n * depth * width + 4 * depth * total),
        compiler_params=PARAMS,
        name="partial_weights",
    )(jnp.reshape(block, (1,)).astype(I32), *matrices, *queries, *others)


def fetch(matrices, block, depth, *others):
    width = matrices[0].shape[1]
    n = len(matrices)
    cuts = 4

    def kernel(block_ref, *refs):
        outs, sem = refs[-1 - n:-1], refs[-1]
        first = pl.multiple_of(block_ref[0] * depth, depth)
        copies = []
        for j in range(n):
            for c in range(cuts):
                size = depth // cuts
                source = refs[j].at[pl.ds(first + c * size, size)]
                copies.append(
                    pltpu.make_async_copy(source, outs[j].at[c * size:(c + 1) * size], sem.at[j * cuts + c])
                )
        for copy in copies:
            copy.start()
        for copy in copies:
            copy.wait()

    return pl.pallas_call(
        kernel,
        in_specs=[SMEM] + [HBM] * n + [ANY] * len(others),
        out_specs=[VMEM] * n,
        out_shape=[jax.ShapeDtypeStruct((depth, width), BF16)] * n,
        scratch_shapes=[pltpu.SemaphoreType.DMA((n * cuts,))],
        cost_estimate=cost(0, 2 * n * depth * width),
        compiler_params=PARAMS,
        name="fetch",
    )(jnp.reshape(block, (1,)).astype(I32), *matrices, *others)


def fetched_weights(matrices, queries, dtype):
    depth = matrices[0].shape[0]
    total = queries[0].shape[1]
    tile = 512 if depth % 512 == 0 else depth
    n = len(matrices)

    def kernel(*refs):
        parts = [jnp.concatenate([r[...] for r in refs[n + CUTS * j:n + CUTS * (j + 1)]]) for j in range(n)]
        for at in range(0, depth, tile):
            value = None
            for j in range(n):
                part = dot(refs[j][at:at + tile, :], parts[j])
                value = part if value is None else value + part
            refs[-1][at:at + tile, :] = value.astype(dtype)

    return pl.pallas_call(
        kernel,
        in_specs=[VMEM] * ((1 + CUTS) * n),
        out_specs=VMEM,
        out_shape=jax.ShapeDtypeStruct((depth, total), dtype),
        cost_estimate=cost(2 * n * matrices[0].size * total, 2 * n * matrices[0].size),
        compiler_params=PARAMS,
        name="fetched_weights",
    )(*matrices, *queries)


def row_table(ids, lines, bulk, extra, *others):
    n_shard = ids.shape[0] // lines

    def kernel(ids_ref, *rest):
        table_ref, flag_ref = rest[-2:]
        me = lax.axis_index("shard")
        start = jnp.int32(0)
        most = jnp.int32(0)
        for s in range(n_shard):
            line = ids_ref[s * lines:(s + 1) * lines, :]

            def count(c):
                return jnp.sum((line == c).astype(I32))

            mine = count(me)
            before = jnp.int32(0)
            if extra:
                surplus = jnp.int32(0)
                for c in range(n_shard):
                    over = lax.div(jnp.maximum(count(c) - bulk, 0) + 15, jnp.int32(16)) * 16
                    before = before + jnp.where(c < me, over, 0)
                    surplus = surplus + over
                most = jnp.maximum(most, surplus)
            table_ref[s, 0] = start
            table_ref[s, 1] = jnp.minimum(mine, bulk)
            table_ref[s, 2] = lax.div(before, jnp.int32(16))
            table_ref[s, 3] = jnp.maximum(mine - bulk, 0)
            start = start + mine
        flag_ref[...] = jnp.full((8, LANES), (most > extra).astype(I32))

    return pl.pallas_call(
        kernel,
        in_specs=[VMEM] + [ANY] * len(others),
        out_specs=[SMEM, VMEM],
        out_shape=[jax.ShapeDtypeStruct((n_shard, 4), I32), jax.ShapeDtypeStruct((8, LANES), I32)],
        cost_estimate=cost(0, 4 * ids.size),
        compiler_params=PARAMS,
        name="row_table",
    )(ids, *others)


def put(acc, x, start, count=None):
    tiles, _, width = x.shape
    first, within = lax.div(start, jnp.int32(8)), lax.rem(start, jnp.int32(8))
    turned = pltpu.roll(x, within, 1)
    row = lax.broadcasted_iota(I32, (1, 8, width), 1)
    keep = row < within
    pieces = jnp.where(keep, jnp.concatenate([turned[:1], turned]), jnp.concatenate([turned, turned[-1:]]))
    if count is None:
        pieces = jnp.concatenate([jnp.where(keep, acc[pl.ds(first, 1)], turned[:1]), pieces[1:]])
    else:
        at = lax.broadcasted_iota(I32, (tiles + 1, 8, width), 0) * 8 + lax.broadcasted_iota(
            I32, (tiles + 1, 8, width), 1
        )
        pieces = jnp.where(
            (at >= within) & (at < within + count), pieces, acc[pl.ds(first, tiles + 1)]
        )
    acc[pl.ds(first, tiles + 1)] = pieces


def score(weight_ref, parts, rep):
    total = None
    for d, x in enumerate(parts):
        depth = x.shape[1]
        block = pl.ds(pl.multiple_of(lax.rem(rep + (len(parts) - d), jnp.int32(len(parts))) * depth, depth), depth)
        value = dot(x, weight_ref[block, :])
        total = value if total is None else total + value
    width = total.shape[1] // 2
    total = total[:, :width] + total[:, width:]
    return total.reshape(total.shape[0] // 8, 8, width)


def for_feats(value, outs):
    n = len(outs)
    share = outs[0].shape[1]
    for f in range(n):
        @pl.when(lax.axis_index("feat") == f)
        def _():
            for d, out in enumerate(outs):
                at = ((f + d) % n) * share
                out[...] = value(slice(at, at + share)).astype(out.dtype)


def feat_shapes(rows, width, n_feat):
    share = (rows, width // n_feat)
    return [jax.ShapeDtypeStruct(share, F32)] + [jax.ShapeDtypeStruct(share, BF16)] * (n_feat - 1)


def early_scores(own, others, mine, pieces, cuts, firsts, seconds, table, rows, n_feat, n_rep, n_shard, bulk, extra):
    depth, width = own.shape
    columns = depth // n_rep
    n_other, n_piece = len(others), len(pieces)
    n_first = len(firsts) * n_rep
    last_hops = n_shard - 1

    def kernel(table_ref, *refs):
        own_ref, refs = refs[0], refs[1:]
        other_refs, refs = refs[:n_other], refs[n_other:]
        mine_ref, refs = refs[0], refs[1:]
        piece_refs = [refs[j * n_rep:(j + 1) * n_rep] for j in range(n_piece)]
        refs = refs[n_piece * n_rep:]
        first_refs, second_refs, refs = refs[:n_first], refs[n_first:2 * n_first], refs[2 * n_first:]
        weight_ref, outs, (scored, held, acc, sem) = refs[0], refs[1:-4], refs[-4:]
        me, rep = lax.axis_index("shard"), lax.axis_index("rep")

        def surplus_copies(s, odd):
            apart = jnp.bitwise_xor(me, s)
            rows_in = pl.ds(pl.multiple_of(lax.div(apart, jnp.int32(2)) * extra, extra), extra)
            copies = []
            for j, refs in enumerate([first_refs, second_refs]):
                for d in range(n_rep):
                    goal = held.at[s, d, j * extra:(j + 1) * extra]
                    which = refs[odd * n_rep + d].at[rows_in]
                    copies.append(pltpu.make_async_copy(which, goal, sem.at[s, j * n_rep + d]))
            return copies

        for s in range(n_shard if extra else 0):
            for odd in range(2):
                @pl.when((table_ref[s, 3] > 0) & (jnp.bitwise_and(jnp.bitwise_xor(me, s), 1) == odd))
                def _():
                    for copy in surplus_copies(s, odd):
                        copy.start()

        weight = own_ref[...]
        for ref in other_refs:
            weight = weight + ref[...].astype(F32)
        high = weight.astype(BF16)
        weight_ref[:, :width] = high
        weight_ref[:, width:] = (weight - high.astype(F32)).astype(BF16)

        scored[me] = score(weight_ref, [mine_ref[...]], jnp.int32(0))
        for parts, (hops, first, size) in zip(piece_refs, cuts):
            source = lax.rem(me + (n_shard - hops), jnp.int32(n_shard))
            scored[source, first // 8:(first + size) // 8] = score(weight_ref, [p[...] for p in parts], rep)
        last = lax.rem(me + (n_shard - last_hops), jnp.int32(n_shard))
        for s in range(n_shard):
            start = table_ref[s, 0]

            @pl.when(last != s)
            def _():
                put(acc, scored[s], start)

            if extra:
                @pl.when(table_ref[s, 3] > 0)
                def _():
                    for copy in surplus_copies(s, 0):
                        copy.wait()
                    some = pl.ds(pl.multiple_of(table_ref[s, 2] * 16, 16), extra)
                    x = [held[s, d, some, :] for d in range(n_rep)]
                    put(acc, score(weight_ref, x, rep), start + table_ref[s, 1])
        for_feats(lambda at: acc[:rows // 8, :, at].reshape(rows, width // n_feat), outs)

    count = n_shard * bulk
    surplus = [x for parts in [*firsts, *seconds] for x in parts]
    return pl.pallas_call(
        kernel,
        in_specs=[SMEM] + [VMEM] * (2 + n_other + n_rep * n_piece) + [ANY] * len(surplus),
        out_specs=[VMEM] * (1 + n_feat),
        out_shape=[jax.ShapeDtypeStruct((depth, 2 * width), BF16)] + feat_shapes(rows, width, n_feat),
        scratch_shapes=[
            pltpu.VMEM((n_shard, bulk // 8, 8, width), F32),
            pltpu.VMEM((n_shard if extra else 1, n_rep, 3 * extra + 16, columns), BF16),
            pltpu.VMEM(((rows + bulk + extra) // 8 + 2, 8, width), F32),
            pltpu.SemaphoreType.DMA((n_shard, 2 * n_rep)),
        ],
        cost_estimate=cost(4 * count * depth * width, 10 * depth * width + count * (2 * depth + 4 * width)),
        compiler_params=WIDE,
        name="early_scores",
    )(table, own, *others, mine, *[p for parts in pieces for p in parts], *surplus)


def late_scores(pieces, weight, n_feat):
    n, n_rep = len(pieces), len(pieces[0])
    rows = sum(parts[0].shape[0] for parts in pieces)
    width = weight.shape[1] // 2

    def kernel(weight_ref, *refs):
        part_refs, outs, acc = refs[:n * n_rep], refs[n * n_rep:-1], refs[-1]
        parts = [jnp.concatenate([part_refs[j * n_rep + d][...] for j in range(n)]) for d in range(n_rep)]
        acc[...] = score(weight_ref, parts, lax.axis_index("rep")).reshape(rows, width)
        for_feats(lambda at: acc[:, at], outs)

    return pl.pallas_call(
        kernel,
        in_specs=[VMEM] * (1 + n * n_rep),
        out_specs=[VMEM] * n_feat,
        out_shape=feat_shapes(rows, width, n_feat),
        scratch_shapes=[pltpu.VMEM((rows, width), F32)],
        cost_estimate=cost(4 * rows * weight.size, 8 * rows * width),
        compiler_params=PARAMS,
        name="late_scores",
    )(weight, *[p for parts in pieces for p in parts])


def merge(table, early, late, n_shard):
    rows, width = early[0].shape
    last_rows = late[0].shape[0]
    last_hops = n_shard - 1

    def kernel(table_ref, *refs):
        early_refs, late_refs = refs[:len(early)], refs[len(early):-2]
        out_ref, acc = refs[-2:]
        source = lax.rem(lax.axis_index("shard") + (n_shard - last_hops), jnp.int32(n_shard))

        def total(parts):
            value = parts[0][...]
            for ref in parts[1:]:
                value = value + ref[...].astype(F32)
            return value.reshape(value.shape[0] // 8, 8, width)

        acc[:rows // 8] = total(early_refs)
        put(acc, total(late_refs), table_ref[source, 0], table_ref[source, 1])
        out_ref[...] = acc[:rows // 8].reshape(rows, width).T

    return pl.pallas_call(
        kernel,
        in_specs=[SMEM] + [VMEM] * (len(early) + len(late)),
        out_specs=VMEM,
        out_shape=jax.ShapeDtypeStruct((width, rows), F32),
        scratch_shapes=[pltpu.VMEM(((rows + last_rows) // 8 + 2, 8, width), F32)],
        cost_estimate=cost(0, 8 * rows * width),
        compiler_params=PARAMS,
        name="merge",
    )(table, *early, *late)


def body(train, cluster_ids, precond, query_store, block_slot, pattern):
    n_group, n_shard = lax.axis_size("groups"), lax.axis_size("shard")
    n_feat, n_rep = lax.axis_size("feat"), lax.axis_size("rep")
    feat, rep = lax.axis_index("feat"), lax.axis_index("rep")
    rows = train.shape[0]
    lines = rows // LANES
    base = rows // n_shard
    columns = train.shape[1] // n_rep
    extra = base // 2 if n_shard == 4 else 0
    bulk = base if extra else base + base // 2
    ids = cluster_ids.reshape(-1, LANES)

    last_hops = n_shard - 1

    def with_rep(x):
        return [x] + [shift(x, "rep", n_rep, d) for d in range(1, n_rep)]

    matrices = with_rep(precond[0])

    picked = pick_queries(query_store, block_slot, pattern, n_group)
    pieces = [picked[0]] + [shift(picked[d], "shard", n_shard, d) for d in range(1, n_shard)]

    middle = [(d, 0, bulk) for d in range(1, last_hops)]
    fillers = 2 if bulk % 256 == 0 else 1
    sizes = [n * bulk // 16 for n in ((3, 2, 4, 4, 3) if bulk % 256 == 0 else (8, 8))]
    final = [(last_hops, sum(sizes[:j]), n) for j, n in enumerate(sizes)]
    *packed, goal = pack_rows(train, ids, columns, bulk, extra, middle + final)
    firsts, seconds = [], []
    parts = [pieces] + [[shift(x, "groups", n_group, d) for x in pieces] for d in range(1, n_group)]
    here = [shift(after(packed[0], pieces[1]), "shard", n_shard, 1)]
    urgent = [here[0]]
    if extra:
        far = swap(after(packed[-1], *pieces[1:]), "shard", n_shard, 2)
        urgent.append(far)
    sent_last = packed[len(middle):len(middle) + len(final)]
    last = [shift(after(x, *pieces[1:]), "shard", n_shard, last_hops) for x in sent_last[:fillers]]
    urgent += last
    depth = n_rep * columns
    targets = [(feat + d) % n_feat for d in range(1, n_feat)]
    near_chip = fetch(matrices, targets[0], depth, *pieces[1:])

    table, flag = row_table(ids, lines, bulk, extra, *pieces[1:])
    chosen = join_queries(
        parts, block_slot, pattern, query_store.shape[0], n_feat, n_rep, *near_chip, flag
    )
    queries = [*chosen[:CUTS]] + [shift(chosen[j], "rep", n_rep, j // CUTS) for j in range(CUTS, CUTS * n_rep)]

    sends = [fetched_weights(near_chip, queries, BF16)]
    sends += [partial_weights(matrices, queries, f, depth, BF16) for f in targets[1:]]
    others = [shift(x, "feat", n_feat, d + 1) for d, x in enumerate(sends)]
    own = partial_weights(matrices, queries, feat, depth, F32, *sends)

    for (hops, _, _), x in zip(middle[1:], packed[1:]):
        here.append(shift(after(x, *urgent, *sends), "shard", n_shard, hops))
        urgent = [here[-1]]
    sent_last = [after(x, own) for x in sent_last[fillers:]]
    last_all = [with_rep(after(x, own)) for x in last]

    mine, *further = own_rows(goal, train, n_shard, n_rep, bulk, extra, own)
    marks = [own, mine, *sent_last, *[p for x in last_all for p in x[1:]]]
    if extra:
        for d in range(1, n_group):
            flag = jnp.maximum(flag, shift(flag, "groups", n_group, d))

        def second_round(x):
            pair = jnp.concatenate([x, swap(x, "shard", n_shard, 2)])
            return [with_rep(pair), with_rep(swap(pair, "shard", n_shard, 1))]

        def no_round(x):
            empty = unwritten((2 * extra, columns), 2 * n_rep)
            return [[*empty[:n_rep]], [*empty[n_rep:]]]

        seconds = lax.cond(flag[0, 0] > 0, second_round, no_round, further[0])
        near = swap(stack([packed[-2], far], *sends), "shard", n_shard, 1)
        pairs = [stack([x, y], own) for x, y in zip(with_rep(packed[-2]), with_rep(after(far, own)))]
        firsts = [pairs, with_rep(after(near, own))]
        marks += [seconds[0][0], near, *pairs]

    mark = shift(after(jnp.zeros((8, LANES), I32), *marks), "rep", n_rep, 1)
    last += [shift(x, "shard", n_shard, last_hops) for x in sent_last]
    ready = [with_rep(after(x, mark)) for x in here]
    weight, *early = early_scores(
        own, others, mine, ready, middle, firsts, seconds, table, rows, n_feat, n_rep, n_shard, bulk, extra
    )

    def over_feat(shares):
        return [shares[0]] + [shift(shares[d], "feat", n_feat, d) for d in range(1, n_feat)]

    last_all += [with_rep(after(x, *early[1:])) for x in last[fillers:]]
    late = late_scores(last_all, weight, n_feat)
    return merge(table, over_feat(early), over_feat(late), n_shard)[None]


def solution(mesh):
    return jax.shard_map(
        body,
        mesh=mesh,
        in_specs=(
            P(("groups", "shard"), "feat"),
            P("groups"),
            P(("groups", "shard"), None, ("feat", "rep")),
            P("shard", None, ("feat", "rep")),
            P(),
            P(),
        ),
        out_specs=P(("groups", "shard"), ("feat", "rep"), None),
        check_vma=False,
    )
```

```python
import functools

import jax
import jax.numpy as jnp
from jax import lax
from jax.experimental import pallas as pl
from jax.experimental.pallas import tpu as pltpu
from jax.sharding import PartitionSpec as P

F32, BF16, I32 = jnp.float32, jnp.bfloat16, jnp.int32
VMEM = pl.BlockSpec(memory_space=pltpu.VMEM)
ANY = pl.BlockSpec(memory_space=pl.ANY)
HBM = pl.BlockSpec(memory_space=pltpu.HBM)
SMEM = pl.BlockSpec(memory_space=pltpu.SMEM)
PARAMS = pltpu.CompilerParams(vmem_limit_bytes=24 * 2**20)
WIDE = pltpu.CompilerParams(vmem_limit_bytes=32 * 2**20)
FIRST = pltpu.CompilerParams(vmem_limit_bytes=60 * 2**20)
LANES = 128
CUTS = 8


def shift(x, axis, size, by):
    return lax.ppermute(x, axis, [(i, (i + by) % size) for i in range(size)])


def swap(x, axis, size, bit):
    return lax.ppermute(x, axis, [(i, i ^ bit) for i in range(size)])


def dot(a, b):
    return jnp.dot(a, b, preferred_element_type=F32)


def cost(flops, nbytes):
    return pl.CostEstimate(flops=1, bytes_accessed=1, transcendentals=0)


def after(x, *others):
    def kernel(*refs):
        pass

    return pl.pallas_call(
        kernel,
        in_specs=[ANY] * (1 + len(others)),
        out_specs=ANY,
        out_shape=jax.ShapeDtypeStruct(x.shape, x.dtype),
        input_output_aliases={0: 0},
        cost_estimate=cost(0, 0),
        compiler_params=PARAMS,
        name="after",
    )(x, *others)


def unwritten(shape, n):
    def kernel(*refs):
        pass

    return pl.pallas_call(
        kernel,
        out_specs=[ANY] * n,
        out_shape=[jax.ShapeDtypeStruct(shape, BF16)] * n,
        cost_estimate=cost(0, 0),
        compiler_params=PARAMS,
        name="unwritten",
    )()


def stack(parts, *others):
    size, width = parts[0].shape
    n = len(parts)

    def kernel(*refs):
        for j in range(n):
            refs[-1][j * size:(j + 1) * size, :] = refs[j][...]

    return pl.pallas_call(
        kernel,
        in_specs=[VMEM] * n + [ANY] * len(others),
        out_specs=VMEM,
        out_shape=jax.ShapeDtypeStruct((n * size, width), parts[0].dtype),
        cost_estimate=cost(0, 0),
        compiler_params=PARAMS,
        name="stack",
    )(*parts, *others)


def pick_queries(query_store, block_slot, pattern, n_group):
    local_blocks, block_rows, width = query_store.shape
    n_cluster, n_list = pattern.shape
    part = block_rows // n_group

    def kernel(pattern_ref, slot_ref, in_ref, *rest):
        outs, sem = rest[:-1], rest[-1]
        me, group = lax.axis_index("shard"), lax.axis_index("groups")
        copies = []
        for t, out in enumerate(outs):
            target = lax.rem(me + t, jnp.int32(n_cluster))
            found = jnp.int32(0)
            for k in range(n_list):
                slot = slot_ref[pattern_ref[target, k]]
                hit = (lax.div(slot, jnp.int32(local_blocks)) == me).astype(I32)
                found = found + hit * lax.rem(slot, jnp.int32(local_blocks))
            rows = pl.ds(pl.multiple_of(group * part, part), part)
            copies.append(pltpu.make_async_copy(in_ref.at[found, rows], out.at[0], sem.at[t]))
            copies[-1].start()
        for copy in copies:
            copy.wait()

    return pl.pallas_call(
        kernel,
        in_specs=[SMEM, SMEM, ANY],
        out_specs=[VMEM] * n_cluster,
        out_shape=[jax.ShapeDtypeStruct((1, part, width), BF16)] * n_cluster,
        scratch_shapes=[pltpu.SemaphoreType.DMA((n_cluster,))],
        cost_estimate=cost(0, 4 * n_cluster * part * width),
        compiler_params=FIRST,
        name="pick_queries",
    )(pattern, block_slot, query_store)


def join_queries(parts, block_slot, pattern, local_blocks, n_feat, n_rep, *others):
    n_group, n_cluster = len(parts), len(parts[0])
    _, part, width = parts[0][0].shape
    n_list = pattern.shape[1]
    total = n_list * n_group * part
    share = total // (n_feat * n_rep)
    unit = min(share, part)
    half = total // n_rep

    def kernel(pattern_ref, slot_ref, *refs):
        outs, rows_ref = refs[-1 - CUTS * n_rep:-1], refs[-1]
        me, group = lax.axis_index("shard"), lax.axis_index("groups")
        for k in range(n_list):
            owner = lax.div(slot_ref[pattern_ref[me, k]], jnp.int32(local_blocks))
            hops = lax.rem(me + (n_cluster - owner), jnp.int32(n_cluster))
            for d in range(n_group):
                origin = lax.rem(group + (n_group - d), jnp.int32(n_group))
                for h in range(n_cluster):
                    @pl.when(hops == h)
                    def _():
                        for u in range(part // unit):
                            first = (k * n_group + origin) * part + u * unit
                            chunk = lax.div(first, jnp.int32(share))
                            goal = lax.rem(chunk, jnp.int32(n_rep)) * n_feat + lax.div(chunk, jnp.int32(n_rep))
                            goal = pl.multiple_of(goal * share + lax.rem(first, jnp.int32(share)), unit)
                            rows_ref[pl.ds(goal, unit), :] = refs[d * n_cluster + h][0, u * unit:(u + 1) * unit, :]
        for r in range(n_rep):
            @pl.when(lax.axis_index("rep") == r)
            def _():
                for j, out in enumerate(outs):
                    at, first = ((r + j // CUTS) % n_rep) * half, (j % CUTS) * (width // CUTS)
                    out[...] = rows_ref[at:at + half, first:first + width // CUTS].T

    return pl.pallas_call(
        kernel,
        in_specs=[SMEM, SMEM] + [VMEM] * (n_group * n_cluster) + [ANY] * len(others),
        out_specs=[VMEM] * (CUTS * n_rep),
        out_shape=[jax.ShapeDtypeStruct((width // CUTS, half), BF16)] * (CUTS * n_rep),
        scratch_shapes=[pltpu.VMEM((total, width), BF16)],
        cost_estimate=cost(0, 4 * total * width),
        compiler_params=PARAMS,
        name="join_queries",
    )(pattern, block_slot, *[x for line in parts for x in line], *others)


def one_hot(goal_ref, base, size):
    index = lax.broadcasted_iota(I32, (size, LANES), 0) + base
    lines = range(goal_ref.shape[0])
    return jnp.concatenate([(index == goal_ref[a:a + 1, :]).astype(F32).astype(BF16) for a in lines], axis=1)


def select(goal_ref, train_ref, base, size):
    tile = 128 if size % 128 == 0 else size
    found = [dot(one_hot(goal_ref, base + at, tile), train_ref[...]).astype(BF16) for at in range(0, size, tile)]
    return jnp.concatenate(found)


def own_rows(goal, train, bulk, *others):
    rows, width = train.shape
    cuts = 4
    part = width // cuts

    def kernel(goal_ref, train_ref, *rest):
        out_ref, held, sem = rest[-3:]
        copies = [
            pltpu.make_async_copy(train_ref.at[:, c * part:(c + 1) * part], held.at[c], sem.at[c]) for c in range(cuts)
        ]
        for copy in copies:
            copy.start()
        pick = one_hot(goal_ref, lax.axis_index("shard") * bulk, bulk)
        for c, copy in enumerate(copies):
            copy.wait()
            out_ref[:, c * part:(c + 1) * part] = dot(pick, held[c]).astype(BF16)

    return pl.pallas_call(
        kernel,
        in_specs=[VMEM, HBM] + [ANY] * len(others),
        out_specs=VMEM,
        out_shape=jax.ShapeDtypeStruct((bulk, width), BF16),
        scratch_shapes=[pltpu.VMEM((cuts, rows, part), BF16), pltpu.SemaphoreType.DMA((cuts,))],
        cost_estimate=cost(2 * bulk * train.size, 2 * train.size),
        compiler_params=PARAMS,
        name="own_rows",
    )(goal, train, *others)


def pack_rows(train, ids, columns, bulk, extra, cuts):
    rows = train.shape[0]
    lines = rows // LANES
    n_shard = ids.shape[0] // lines

    def kernel(ids_ref, train_ref, *rest):
        outs, goal_ref = rest[:-1], rest[-1]
        me = lax.axis_index("shard")
        own = ids_ref[...]
        masks = [(own == c).astype(F32) for c in range(n_shard)]
        stacked = jnp.concatenate(masks, axis=0).astype(BF16)
        lane_from = lax.broadcasted_iota(I32, (LANES, LANES), 0)
        lane_to = lax.broadcasted_iota(I32, (LANES, LANES), 1)
        in_line = dot(stacked, (lane_from < lane_to).astype(F32).astype(BF16))
        line_sum = dot(stacked, jnp.ones((LANES, LANES), BF16)).astype(BF16)
        size = n_shard * lines
        to = lax.broadcasted_iota(I32, (size, size), 0)
        since = lax.broadcasted_iota(I32, (size, size), 1)
        same = (to // lines) == (since // lines)
        ahead = dot((same & (since < to)).astype(F32).astype(BF16), line_sum)
        whole = dot(same.astype(F32).astype(BF16), line_sum)
        rank = in_line + ahead
        goal = jnp.zeros((lines, LANES), F32)
        past = jnp.zeros((lines, LANES), F32)
        for c in range(n_shard):
            part = slice(c * lines, (c + 1) * lines)
            place = rank[part] + c * bulk
            if extra:
                surplus = n_shard * bulk + past + rank[part] - bulk
                place = jnp.where(rank[part] < bulk, place, surplus)
                past = past + jnp.floor((jnp.maximum(whole[part] - bulk, 0.0) + 15.0) * 0.0625) * 16.0
            goal = goal + masks[c] * place
        goal_ref[...] = goal.astype(I32)

        def fill(out, base):
            out[...] = select(goal_ref, train_ref, base, out.shape[0])

        for out, (hops, first, _) in zip(outs, cuts):
            fill(out, lax.rem(me + hops, jnp.int32(n_shard)) * bulk + first)
        for j, out in enumerate(outs[len(cuts):]):
            fill(out, n_shard * bulk + max(j - 1, 0) * extra)

    shapes = [jax.ShapeDtypeStruct((n, columns), BF16) for _, _, n in cuts]
    shapes += [jax.ShapeDtypeStruct((extra, columns), BF16)] * (3 if extra else 0)
    shapes += [jax.ShapeDtypeStruct((lines, LANES), I32)]
    packed = n_shard * bulk + 2 * extra
    return pl.pallas_call(
        kernel,
        grid=(1,),
        in_specs=[
            pl.BlockSpec((lines, LANES), lambda i: (lax.axis_index("shard"), 0)),
            pl.BlockSpec((rows, columns), lambda i: (0, lax.axis_index("rep"))),
        ],
        out_specs=[VMEM] * len(shapes),
        out_shape=shapes,
        cost_estimate=cost(2 * packed * rows * columns, 2 * (rows + packed) * columns),
        compiler_params=FIRST,
        name="pack_rows",
    )(ids, train)


def partial_weights(matrices, queries, block, depth, dtype, *others):
    width, total = matrices[0].shape[1], queries[0].shape[1]
    tile = 512 if depth % 512 == 0 else depth
    steps = depth // tile
    n = len(matrices)

    def kernel(block_ref, *refs):
        out_ref, held, sem = refs[-3:]
        first = pl.multiple_of(block_ref[0] * depth, depth)
        copies = []
        for i in range(steps):
            for j in range(n):
                source = refs[j].at[pl.ds(first + i * tile, tile)]
                copies.append(pltpu.make_async_copy(source, held.at[j, i], sem.at[i * n + j]))
        for copy in copies:
            copy.start()
        parts = [jnp.concatenate([r[...] for r in refs[n + CUTS * j:n + CUTS * (j + 1)]]) for j in range(n)]
        for i in range(steps):
            value = None
            for j in range(n):
                copies[i * n + j].wait()
                part = dot(held[j, i], parts[j])
                value = part if value is None else value + part
            out_ref[i * tile:(i + 1) * tile, :] = value.astype(dtype)

    return pl.pallas_call(
        kernel,
        in_specs=[SMEM] + [HBM] * n + [VMEM] * (CUTS * n) + [ANY] * len(others),
        out_specs=VMEM,
        out_shape=jax.ShapeDtypeStruct((depth, total), dtype),
        scratch_shapes=[pltpu.VMEM((n, steps, tile, width), BF16), pltpu.SemaphoreType.DMA((steps * n,))],
        cost_estimate=cost(2 * n * depth * width * total, 2 * n * depth * width + 4 * depth * total),
        compiler_params=PARAMS,
        name="partial_weights",
    )(jnp.reshape(block, (1,)).astype(I32), *matrices, *queries, *others)


def fetch(matrices, block, depth, *others):
    width = matrices[0].shape[1]
    n = len(matrices)
    cuts = 4

    def kernel(block_ref, *refs):
        outs, sem = refs[-1 - n:-1], refs[-1]
        first = pl.multiple_of(block_ref[0] * depth, depth)
        copies = []
        for j in range(n):
            for c in range(cuts):
                size = depth // cuts
                source = refs[j].at[pl.ds(first + c * size, size)]
                copies.append(
                    pltpu.make_async_copy(source, outs[j].at[c * size:(c + 1) * size], sem.at[j * cuts + c])
                )
        for copy in copies:
            copy.start()
        for copy in copies:
            copy.wait()

    return pl.pallas_call(
        kernel,
        in_specs=[SMEM] + [HBM] * n + [ANY] * len(others),
        out_specs=[VMEM] * n,
        out_shape=[jax.ShapeDtypeStruct((depth, width), BF16)] * n,
        scratch_shapes=[pltpu.SemaphoreType.DMA((n * cuts,))],
        cost_estimate=cost(0, 2 * n * depth * width),
        compiler_params=PARAMS,
        name="fetch",
    )(jnp.reshape(block, (1,)).astype(I32), *matrices, *others)


def fetched_weights(matrices, queries, dtype):
    depth = matrices[0].shape[0]
    total = queries[0].shape[1]
    tile = 512 if depth % 512 == 0 else depth
    n = len(matrices)

    def kernel(*refs):
        parts = [jnp.concatenate([r[...] for r in refs[n + CUTS * j:n + CUTS * (j + 1)]]) for j in range(n)]
        for at in range(0, depth, tile):
            value = None
            for j in range(n):
                part = dot(refs[j][at:at + tile, :], parts[j])
                value = part if value is None else value + part
            refs[-1][at:at + tile, :] = value.astype(dtype)

    return pl.pallas_call(
        kernel,
        in_specs=[VMEM] * ((1 + CUTS) * n),
        out_specs=VMEM,
        out_shape=jax.ShapeDtypeStruct((depth, total), dtype),
        cost_estimate=cost(2 * n * matrices[0].size * total, 2 * n * matrices[0].size),
        compiler_params=PARAMS,
        name="fetched_weights",
    )(*matrices, *queries)


def row_table(ids, lines, bulk, extra, *others):
    n_shard = ids.shape[0] // lines

    def kernel(ids_ref, *rest):
        table_ref, flag_ref = rest[-2:]
        me = lax.axis_index("shard")
        start = jnp.int32(0)
        most = jnp.int32(0)
        for s in range(n_shard):
            line = ids_ref[s * lines:(s + 1) * lines, :]

            def count(c):
                return jnp.sum((line == c).astype(I32))

            mine = count(me)
            before = jnp.int32(0)
            if extra:
                surplus = jnp.int32(0)
                for c in range(n_shard):
                    over = lax.div(jnp.maximum(count(c) - bulk, 0) + 15, jnp.int32(16)) * 16
                    before = before + jnp.where(c < me, over, 0)
                    surplus = surplus + over
                most = jnp.maximum(most, surplus)
            table_ref[s, 0] = start
            table_ref[s, 1] = jnp.minimum(mine, bulk)
            table_ref[s, 2] = lax.div(before, jnp.int32(16))
            table_ref[s, 3] = jnp.maximum(mine - bulk, 0)
            start = start + mine
        flag_ref[...] = jnp.full((8, LANES), (most > extra).astype(I32))

    return pl.pallas_call(
        kernel,
        in_specs=[VMEM] + [ANY] * len(others),
        out_specs=[SMEM, VMEM],
        out_shape=[jax.ShapeDtypeStruct((n_shard, 4), I32), jax.ShapeDtypeStruct((8, LANES), I32)],
        cost_estimate=cost(0, 4 * ids.size),
        compiler_params=PARAMS,
        name="row_table",
    )(ids, *others)


def put(acc, x, start, count=None):
    tiles, _, width = x.shape
    first, within = lax.div(start, jnp.int32(8)), lax.rem(start, jnp.int32(8))
    turned = pltpu.roll(x, within, 1)
    row = lax.broadcasted_iota(I32, (1, 8, width), 1)
    keep = row < within
    pieces = jnp.where(keep, jnp.concatenate([turned[:1], turned]), jnp.concatenate([turned, turned[-1:]]))
    if count is None:
        pieces = jnp.concatenate([jnp.where(keep, acc[pl.ds(first, 1)], turned[:1]), pieces[1:]])
    else:
        at = lax.broadcasted_iota(I32, (tiles + 1, 8, width), 0) * 8 + lax.broadcasted_iota(
            I32, (tiles + 1, 8, width), 1
        )
        pieces = jnp.where(
            (at >= within) & (at < within + count), pieces, acc[pl.ds(first, tiles + 1)]
        )
    acc[pl.ds(first, tiles + 1)] = pieces


def score(weight_ref, parts, rep):
    total = None
    for d, x in enumerate(parts):
        depth = x.shape[1]
        block = pl.ds(pl.multiple_of(lax.rem(rep + (len(parts) - d), jnp.int32(len(parts))) * depth, depth), depth)
        value = dot(x, weight_ref[block, :])
        total = value if total is None else total + value
    width = total.shape[1] // 2
    total = total[:, :width] + total[:, width:]
    return total.reshape(total.shape[0] // 8, 8, width)


def for_feats(value, outs):
    n = len(outs)
    share = outs[0].shape[1]
    for f in range(n):
        @pl.when(lax.axis_index("feat") == f)
        def _():
            for d, out in enumerate(outs):
                at = ((f + d) % n) * share
                out[...] = value(slice(at, at + share)).astype(out.dtype)


def feat_shapes(rows, width, n_feat):
    share = (rows, width // n_feat)
    return [jax.ShapeDtypeStruct(share, F32)] + [jax.ShapeDtypeStruct(share, BF16)] * (n_feat - 1)


def early_scores(own, others, mine, pieces, cuts, firsts, seconds, table, rows, n_feat, n_rep, n_shard, bulk, extra):
    depth, width = own.shape
    columns = depth // n_rep
    n_other, n_piece = len(others), len(pieces)
    n_first = len(firsts) * n_rep
    last_hops = n_shard - 1

    def kernel(table_ref, *refs):
        own_ref, refs = refs[0], refs[1:]
        other_refs, refs = refs[:n_other], refs[n_other:]
        mine_ref, refs = refs[0], refs[1:]
        piece_refs = [refs[j * n_rep:(j + 1) * n_rep] for j in range(n_piece)]
        refs = refs[n_piece * n_rep:]
        first_refs, second_refs, refs = refs[:n_first], refs[n_first:2 * n_first], refs[2 * n_first:]
        weight_ref, outs, (scored, held, acc, sem) = refs[0], refs[1:-4], refs[-4:]
        me, rep = lax.axis_index("shard"), lax.axis_index("rep")

        def surplus_copies(s, odd):
            apart = jnp.bitwise_xor(me, s)
            rows_in = pl.ds(pl.multiple_of(lax.div(apart, jnp.int32(2)) * extra, extra), extra)
            copies = []
            for j, refs in enumerate([first_refs, second_refs]):
                for d in range(n_rep):
                    goal = held.at[s, d, j * extra:(j + 1) * extra]
                    which = refs[odd * n_rep + d].at[rows_in]
                    copies.append(pltpu.make_async_copy(which, goal, sem.at[s, j * n_rep + d]))
            return copies

        for s in range(n_shard if extra else 0):
            for odd in range(2):
                @pl.when((table_ref[s, 3] > 0) & (jnp.bitwise_and(jnp.bitwise_xor(me, s), 1) == odd))
                def _():
                    for copy in surplus_copies(s, odd):
                        copy.start()

        weight = own_ref[...]
        for ref in other_refs:
            weight = weight + ref[...].astype(F32)
        high = weight.astype(BF16)
        weight_ref[:, :width] = high
        weight_ref[:, width:] = (weight - high.astype(F32)).astype(BF16)

        scored[me] = score(weight_ref, [mine_ref[...]], jnp.int32(0))
        for parts, (hops, first, size) in zip(piece_refs, cuts):
            source = lax.rem(me + (n_shard - hops), jnp.int32(n_shard))
            scored[source, first // 8:(first + size) // 8] = score(weight_ref, [p[...] for p in parts], rep)
        last = lax.rem(me + (n_shard - last_hops), jnp.int32(n_shard))
        for s in range(n_shard):
            start = table_ref[s, 0]

            @pl.when(last != s)
            def _():
                put(acc, scored[s], start)

            if extra:
                @pl.when(table_ref[s, 3] > 0)
                def _():
                    for copy in surplus_copies(s, 0):
                        copy.wait()
                    some = pl.ds(pl.multiple_of(table_ref[s, 2] * 16, 16), extra)
                    x = [held[s, d, some, :] for d in range(n_rep)]
                    put(acc, score(weight_ref, x, rep), start + table_ref[s, 1])
        for_feats(lambda at: acc[:rows // 8, :, at].reshape(rows, width // n_feat), outs)

    count = n_shard * bulk
    surplus = [x for parts in [*firsts, *seconds] for x in parts]
    return pl.pallas_call(
        kernel,
        in_specs=[SMEM] + [VMEM] * (2 + n_other + n_rep * n_piece) + [ANY] * len(surplus),
        out_specs=[VMEM] * (1 + n_feat),
        out_shape=[jax.ShapeDtypeStruct((depth, 2 * width), BF16)] + feat_shapes(rows, width, n_feat),
        scratch_shapes=[
            pltpu.VMEM((n_shard, bulk // 8, 8, width), F32),
            pltpu.VMEM((n_shard if extra else 1, n_rep, 3 * extra + 16, columns), BF16),
            pltpu.VMEM(((rows + bulk + extra) // 8 + 2, 8, width), F32),
            pltpu.SemaphoreType.DMA((n_shard, 2 * n_rep)),
        ],
        cost_estimate=cost(4 * count * depth * width, 10 * depth * width + count * (2 * depth + 4 * width)),
        compiler_params=WIDE,
        name="early_scores",
    )(table, own, *others, mine, *[p for parts in pieces for p in parts], *surplus)


def late_scores(pieces, weight, n_feat):
    n, n_rep = len(pieces), len(pieces[0])
    rows = sum(parts[0].shape[0] for parts in pieces)
    width = weight.shape[1] // 2

    def kernel(weight_ref, *refs):
        part_refs, outs, acc = refs[:n * n_rep], refs[n * n_rep:-1], refs[-1]
        parts = [jnp.concatenate([part_refs[j * n_rep + d][...] for j in range(n)]) for d in range(n_rep)]
        acc[...] = score(weight_ref, parts, lax.axis_index("rep")).reshape(rows, width)
        for_feats(lambda at: acc[:, at], outs)

    return pl.pallas_call(
        kernel,
        in_specs=[VMEM] * (1 + n * n_rep),
        out_specs=[VMEM] * n_feat,
        out_shape=feat_shapes(rows, width, n_feat),
        scratch_shapes=[pltpu.VMEM((rows, width), F32)],
        cost_estimate=cost(4 * rows * weight.size, 8 * rows * width),
        compiler_params=PARAMS,
        name="late_scores",
    )(weight, *[p for parts in pieces for p in parts])


def merge(table, early, late, n_shard):
    rows, width = early[0].shape
    last_rows = late[0].shape[0]
    last_hops = n_shard - 1

    def kernel(table_ref, *refs):
        early_refs, late_refs = refs[:len(early)], refs[len(early):-2]
        out_ref, acc = refs[-2:]
        source = lax.rem(lax.axis_index("shard") + (n_shard - last_hops), jnp.int32(n_shard))

        def total(parts):
            value = parts[0][...]
            for ref in parts[1:]:
                value = value + ref[...].astype(F32)
            return value.reshape(value.shape[0] // 8, 8, width)

        acc[:rows // 8] = total(early_refs)
        put(acc, total(late_refs), table_ref[source, 0], table_ref[source, 1])
        out_ref[...] = acc[:rows // 8].reshape(rows, width).T

    return pl.pallas_call(
        kernel,
        in_specs=[SMEM] + [VMEM] * (len(early) + len(late)),
        out_specs=VMEM,
        out_shape=jax.ShapeDtypeStruct((width, rows), F32),
        scratch_shapes=[pltpu.VMEM(((rows + last_rows) // 8 + 2, 8, width), F32)],
        cost_estimate=cost(0, 8 * rows * width),
        compiler_params=PARAMS,
        name="merge",
    )(table, *early, *late)


def body(train, cluster_ids, precond, query_store, block_slot, pattern):
    n_group, n_shard = lax.axis_size("groups"), lax.axis_size("shard")
    n_feat, n_rep = lax.axis_size("feat"), lax.axis_size("rep")
    feat, rep = lax.axis_index("feat"), lax.axis_index("rep")
    rows = train.shape[0]
    lines = rows // LANES
    base = rows // n_shard
    columns = train.shape[1] // n_rep
    extra = base // 2 if n_shard == 4 else 0
    bulk = base if extra else base + base // 2
    ids = cluster_ids.reshape(-1, LANES)

    last_hops = n_shard - 1

    def with_rep(x):
        return [x] + [shift(x, "rep", n_rep, d) for d in range(1, n_rep)]

    matrices = with_rep(precond[0])

    picked = pick_queries(query_store, block_slot, pattern, n_group)
    pieces = [picked[0]] + [shift(picked[d], "shard", n_shard, d) for d in range(1, n_shard)]

    middle = [(d, 0, bulk) for d in range(1, last_hops)]
    fillers = 2 if bulk % 256 == 0 else 1
    sizes = [n * bulk // 16 for n in ((3, 2, 4, 4, 3) if bulk % 256 == 0 else (8, 8))]
    final = [(last_hops, sum(sizes[:j]), n) for j, n in enumerate(sizes)]
    *packed, goal = pack_rows(train, ids, columns, bulk, extra, middle + final)
    firsts, seconds = [], []
    parts = [pieces] + [[shift(x, "groups", n_group, d) for x in pieces] for d in range(1, n_group)]
    here = [shift(after(packed[0], pieces[1], pieces[-1]), "shard", n_shard, 1)]
    urgent = [here[0]]
    if extra:
        far = swap(after(packed[-2], *pieces[1:]), "shard", n_shard, 2)
        urgent.append(far)
    sent_last = packed[len(middle):len(middle) + len(final)]
    last = [shift(after(x, *pieces[1:]), "shard", n_shard, last_hops) for x in sent_last[:fillers]]
    urgent += last
    depth = n_rep * columns
    targets = [(feat + d) % n_feat for d in range(1, n_feat)]
    near_chip = fetch(matrices, targets[0], depth, *pieces[1:])

    table, flag = row_table(ids, lines, bulk, extra, *pieces[1:])
    chosen = join_queries(
        parts, block_slot, pattern, query_store.shape[0], n_feat, n_rep, *near_chip, flag
    )
    queries = [*chosen[:CUTS]] + [shift(chosen[j], "rep", n_rep, j // CUTS) for j in range(CUTS, CUTS * n_rep)]

    sends = [fetched_weights(near_chip, queries, BF16)]
    sends += [partial_weights(matrices, queries, f, depth, BF16) for f in targets[1:]]
    others = [shift(x, "feat", n_feat, d + 1) for d, x in enumerate(sends)]
    own = partial_weights(matrices, queries, feat, depth, F32, *sends)

    for (hops, _, _), x in zip(middle[1:], packed[1:]):
        here.append(shift(after(x, *urgent, *sends), "shard", n_shard, hops))
        urgent = [here[-1]]
    sent_last = [after(x, own) for x in sent_last[fillers:]]
    last_all = [with_rep(after(x, own)) for x in last]

    mine = own_rows(goal, train, bulk, own)
    marks = [own, mine, *sent_last, *[p for x in last_all for p in x[1:]]]
    if extra:
        for d in range(1, n_group):
            flag = jnp.maximum(flag, shift(flag, "groups", n_group, d))

        def second_round(x):
            pair = jnp.concatenate([x, swap(x, "shard", n_shard, 2)])
            return [with_rep(pair), with_rep(swap(pair, "shard", n_shard, 1))]

        def no_round(x):
            empty = unwritten((2 * extra, columns), 2 * n_rep)
            return [[*empty[:n_rep]], [*empty[n_rep:]]]

        seconds = lax.cond(flag[0, 0] > 0, second_round, no_round, after(packed[-1], own))
        near = swap(stack([packed[-3], far], *sends), "shard", n_shard, 1)
        pairs = [stack([x, y], own) for x, y in zip(with_rep(packed[-3]), with_rep(after(far, own)))]
        firsts = [pairs, with_rep(after(near, own))]
        marks += [seconds[0][0], near, *pairs]

    mark = shift(after(jnp.zeros((8, LANES), I32), *marks), "rep", n_rep, 1)
    last += [shift(x, "shard", n_shard, last_hops) for x in sent_last]
    ready = [with_rep(after(x, mark)) for x in here]
    weight, *early = early_scores(
        own, others, mine, ready, middle, firsts, seconds, table, rows, n_feat, n_rep, n_shard, bulk, extra
    )

    def over_feat(shares):
        return [shares[0]] + [shift(shares[d], "feat", n_feat, d) for d in range(1, n_feat)]

    last_all += [with_rep(after(x, *early[1:])) for x in last[fillers:]]
    late = late_scores(last_all, weight, n_feat)
    return merge(table, over_feat(early), over_feat(late), n_shard)[None]


def solution(mesh):
    return jax.shard_map(
        body,
        mesh=mesh,
        in_specs=(
            P(("groups", "shard"), "feat"),
            P("groups"),
            P(("groups", "shard"), None, ("feat", "rep")),
            P("shard", None, ("feat", "rep")),
            P(),
            P(),
        ),
        out_specs=P(("groups", "shard"), ("feat", "rep"), None),
        check_vma=False,
    )
```

```python
import functools

import jax
import jax.numpy as jnp
from jax import lax
from jax.experimental import pallas as pl
from jax.experimental.pallas import tpu as pltpu
from jax.sharding import PartitionSpec as P

F32, BF16, I32 = jnp.float32, jnp.bfloat16, jnp.int32
VMEM = pl.BlockSpec(memory_space=pltpu.VMEM)
ANY = pl.BlockSpec(memory_space=pl.ANY)
HBM = pl.BlockSpec(memory_space=pltpu.HBM)
SMEM = pl.BlockSpec(memory_space=pltpu.SMEM)
PARAMS = pltpu.CompilerParams(vmem_limit_bytes=24 * 2**20)
WIDE = pltpu.CompilerParams(vmem_limit_bytes=32 * 2**20)
FIRST = pltpu.CompilerParams(vmem_limit_bytes=60 * 2**20)
LANES = 128
CUTS = 8


def shift(x, axis, size, by):
    return lax.ppermute(x, axis, [(i, (i + by) % size) for i in range(size)])


def swap(x, axis, size, bit):
    return lax.ppermute(x, axis, [(i, i ^ bit) for i in range(size)])


def dot(a, b):
    return jnp.dot(a, b, preferred_element_type=F32)


def cost(flops, nbytes):
    return pl.CostEstimate(flops=1, bytes_accessed=1, transcendentals=0)


def after(x, *others):
    def kernel(*refs):
        pass

    return pl.pallas_call(
        kernel,
        in_specs=[ANY] * (1 + len(others)),
        out_specs=ANY,
        out_shape=jax.ShapeDtypeStruct(x.shape, x.dtype),
        input_output_aliases={0: 0},
        cost_estimate=cost(0, 0),
        compiler_params=PARAMS,
        name="after",
    )(x, *others)


def unwritten(shape, n):
    def kernel(*refs):
        pass

    return pl.pallas_call(
        kernel,
        out_specs=[ANY] * n,
        out_shape=[jax.ShapeDtypeStruct(shape, BF16)] * n,
        cost_estimate=cost(0, 0),
        compiler_params=PARAMS,
        name="unwritten",
    )()


def stack(parts, *others):
    size, width = parts[0].shape
    n = len(parts)

    def kernel(*refs):
        for j in range(n):
            refs[-1][j * size:(j + 1) * size, :] = refs[j][...]

    return pl.pallas_call(
        kernel,
        in_specs=[VMEM] * n + [ANY] * len(others),
        out_specs=VMEM,
        out_shape=jax.ShapeDtypeStruct((n * size, width), parts[0].dtype),
        cost_estimate=cost(0, 0),
        compiler_params=PARAMS,
        name="stack",
    )(*parts, *others)


def pick_queries(query_store, block_slot, pattern, n_group):
    local_blocks, block_rows, width = query_store.shape
    n_cluster, n_list = pattern.shape
    part = block_rows // n_group

    def kernel(pattern_ref, slot_ref, in_ref, *outs):
        me = lax.axis_index("shard")
        for t, out in enumerate(outs):
            target = lax.rem(me + t, jnp.int32(n_cluster))
            found = jnp.int32(0)
            for k in range(n_list):
                slot = slot_ref[pattern_ref[target, k]]
                hit = (lax.div(slot, jnp.int32(local_blocks)) == me).astype(I32)
                found = found + hit * lax.rem(slot, jnp.int32(local_blocks))
            out[0] = in_ref[found]

    return pl.pallas_call(
        kernel,
        grid=(1,),
        in_specs=[SMEM, SMEM, pl.BlockSpec((local_blocks, part, width), lambda i: (0, lax.axis_index("groups"), 0))],
        out_specs=[VMEM] * n_cluster,
        out_shape=[jax.ShapeDtypeStruct((1, part, width), BF16)] * n_cluster,
        cost_estimate=cost(0, 4 * n_cluster * part * width),
        compiler_params=FIRST,
        name="pick_queries",
    )(pattern, block_slot, query_store)


def join_queries(parts, block_slot, pattern, local_blocks, n_feat, n_rep, *others):
    n_group, n_cluster = len(parts), len(parts[0])
    _, part, width = parts[0][0].shape
    n_list = pattern.shape[1]
    total = n_list * n_group * part
    share = total // (n_feat * n_rep)
    unit = min(share, part)
    half = total // n_rep

    def kernel(pattern_ref, slot_ref, *refs):
        outs, rows_ref = refs[-1 - CUTS * n_rep:-1], refs[-1]
        me, group = lax.axis_index("shard"), lax.axis_index("groups")
        for k in range(n_list):
            owner = lax.div(slot_ref[pattern_ref[me, k]], jnp.int32(local_blocks))
            hops = lax.rem(me + (n_cluster - owner), jnp.int32(n_cluster))
            for d in range(n_group):
                origin = lax.rem(group + (n_group - d), jnp.int32(n_group))
                for h in range(n_cluster):
                    @pl.when(hops == h)
                    def _():
                        for u in range(part // unit):
                            first = (k * n_group + origin) * part + u * unit
                            chunk = lax.div(first, jnp.int32(share))
                            goal = lax.rem(chunk, jnp.int32(n_rep)) * n_feat + lax.div(chunk, jnp.int32(n_rep))
                            goal = pl.multiple_of(goal * share + lax.rem(first, jnp.int32(share)), unit)
                            rows_ref[pl.ds(goal, unit), :] = refs[d * n_cluster + h][0, u * unit:(u + 1) * unit, :]
        for r in range(n_rep):
            @pl.when(lax.axis_index("rep") == r)
            def _():
                for j, out in enumerate(outs):
                    at, first = ((r + j // CUTS) % n_rep) * half, (j % CUTS) * (width // CUTS)
                    out[...] = rows_ref[at:at + half, first:first + width // CUTS].T

    return pl.pallas_call(
        kernel,
        in_specs=[SMEM, SMEM] + [VMEM] * (n_group * n_cluster) + [ANY] * len(others),
        out_specs=[VMEM] * (CUTS * n_rep),
        out_shape=[jax.ShapeDtypeStruct((width // CUTS, half), BF16)] * (CUTS * n_rep),
        scratch_shapes=[pltpu.VMEM((total, width), BF16)],
        cost_estimate=cost(0, 4 * total * width),
        compiler_params=PARAMS,
        name="join_queries",
    )(pattern, block_slot, *[x for line in parts for x in line], *others)


def one_hot(goal_ref, base, size):
    index = lax.broadcasted_iota(I32, (size, LANES), 0) + base
    lines = range(goal_ref.shape[0])
    return jnp.concatenate([(index == goal_ref[a:a + 1, :]).astype(F32).astype(BF16) for a in lines], axis=1)


def select(goal_ref, train_ref, base, size):
    tile = 128 if size % 128 == 0 else size
    found = [dot(one_hot(goal_ref, base + at, tile), train_ref[...]).astype(BF16) for at in range(0, size, tile)]
    return jnp.concatenate(found)


def own_rows(goal, train, bulk, *others):
    rows, width = train.shape
    cuts = 4
    part = width // cuts

    def kernel(goal_ref, train_ref, *rest):
        out_ref, held, sem = rest[-3:]
        copies = [
            pltpu.make_async_copy(train_ref.at[:, c * part:(c + 1) * part], held.at[c], sem.at[c]) for c in range(cuts)
        ]
        for copy in copies:
            copy.start()
        pick = one_hot(goal_ref, lax.axis_index("shard") * bulk, bulk)
        for c, copy in enumerate(copies):
            copy.wait()
            out_ref[:, c * part:(c + 1) * part] = dot(pick, held[c]).astype(BF16)

    return pl.pallas_call(
        kernel,
        in_specs=[VMEM, HBM] + [ANY] * len(others),
        out_specs=VMEM,
        out_shape=jax.ShapeDtypeStruct((bulk, width), BF16),
        scratch_shapes=[pltpu.VMEM((cuts, rows, part), BF16), pltpu.SemaphoreType.DMA((cuts,))],
        cost_estimate=cost(2 * bulk * train.size, 2 * train.size),
        compiler_params=PARAMS,
        name="own_rows",
    )(goal, train, *others)


def pack_rows(train, ids, columns, bulk, extra, cuts):
    rows = train.shape[0]
    lines = rows // LANES
    n_shard = ids.shape[0] // lines

    def kernel(ids_ref, train_ref, *rest):
        outs, goal_ref = rest[:-1], rest[-1]
        me = lax.axis_index("shard")
        own = ids_ref[...]
        masks = [(own == c).astype(F32) for c in range(n_shard)]
        stacked = jnp.concatenate(masks, axis=0).astype(BF16)
        lane_from = lax.broadcasted_iota(I32, (LANES, LANES), 0)
        lane_to = lax.broadcasted_iota(I32, (LANES, LANES), 1)
        in_line = dot(stacked, (lane_from < lane_to).astype(F32).astype(BF16))
        line_sum = dot(stacked, jnp.ones((LANES, LANES), BF16)).astype(BF16)
        size = n_shard * lines
        to = lax.broadcasted_iota(I32, (size, size), 0)
        since = lax.broadcasted_iota(I32, (size, size), 1)
        same = (to // lines) == (since // lines)
        ahead = dot((same & (since < to)).astype(F32).astype(BF16), line_sum)
        whole = dot(same.astype(F32).astype(BF16), line_sum)
        rank = in_line + ahead
        goal = jnp.zeros((lines, LANES), F32)
        past = jnp.zeros((lines, LANES), F32)
        for c in range(n_shard):
            part = slice(c * lines, (c + 1) * lines)
            place = rank[part] + c * bulk
            if extra:
                surplus = n_shard * bulk + past + rank[part] - bulk
                place = jnp.where(rank[part] < bulk, place, surplus)
                past = past + jnp.floor((jnp.maximum(whole[part] - bulk, 0.0) + 15.0) * 0.0625) * 16.0
            goal = goal + masks[c] * place
        goal_ref[...] = goal.astype(I32)

        def fill(out, base):
            out[...] = select(goal_ref, train_ref, base, out.shape[0])

        for out, (hops, first, _) in zip(outs, cuts):
            fill(out, lax.rem(me + hops, jnp.int32(n_shard)) * bulk + first)
        for j, out in enumerate(outs[len(cuts):]):
            fill(out, n_shard * bulk + max(j - 1, 0) * extra)

    shapes = [jax.ShapeDtypeStruct((n, columns), BF16) for _, _, n in cuts]
    shapes += [jax.ShapeDtypeStruct((extra, columns), BF16)] * (3 if extra else 0)
    shapes += [jax.ShapeDtypeStruct((lines, LANES), I32)]
    packed = n_shard * bulk + 2 * extra
    return pl.pallas_call(
        kernel,
        grid=(1,),
        in_specs=[
            pl.BlockSpec((lines, LANES), lambda i: (lax.axis_index("shard"), 0)),
            pl.BlockSpec((rows, columns), lambda i: (0, lax.axis_index("rep"))),
        ],
        out_specs=[VMEM] * len(shapes),
        out_shape=shapes,
        cost_estimate=cost(2 * packed * rows * columns, 2 * (rows + packed) * columns),
        compiler_params=FIRST,
        name="pack_rows",
    )(ids, train)


def partial_weights(matrices, queries, block, depth, dtype, *others):
    width, total = matrices[0].shape[1], queries[0].shape[1]
    tile = 512 if depth % 512 == 0 else depth
    steps = depth // tile
    n = len(matrices)

    def kernel(block_ref, *refs):
        out_ref, held, sem = refs[-3:]
        first = pl.multiple_of(block_ref[0] * depth, depth)
        copies = []
        for i in range(steps):
            for j in range(n):
                source = refs[j].at[pl.ds(first + i * tile, tile)]
                copies.append(pltpu.make_async_copy(source, held.at[j, i], sem.at[i * n + j]))
        for copy in copies:
            copy.start()
        parts = [jnp.concatenate([r[...] for r in refs[n + CUTS * j:n + CUTS * (j + 1)]]) for j in range(n)]
        for i in range(steps):
            value = None
            for j in range(n):
                copies[i * n + j].wait()
                part = dot(held[j, i], parts[j])
                value = part if value is None else value + part
            out_ref[i * tile:(i + 1) * tile, :] = value.astype(dtype)

    return pl.pallas_call(
        kernel,
        in_specs=[SMEM] + [HBM] * n + [VMEM] * (CUTS * n) + [ANY] * len(others),
        out_specs=VMEM,
        out_shape=jax.ShapeDtypeStruct((depth, total), dtype),
        scratch_shapes=[pltpu.VMEM((n, steps, tile, width), BF16), pltpu.SemaphoreType.DMA((steps * n,))],
        cost_estimate=cost(2 * n * depth * width * total, 2 * n * depth * width + 4 * depth * total),
        compiler_params=PARAMS,
        name="partial_weights",
    )(jnp.reshape(block, (1,)).astype(I32), *matrices, *queries, *others)


def fetch(matrices, block, depth, *others):
    width = matrices[0].shape[1]
    n = len(matrices)
    cuts = 4

    def kernel(block_ref, *refs):
        outs, sem = refs[-1 - n:-1], refs[-1]
        first = pl.multiple_of(block_ref[0] * depth, depth)
        copies = []
        for j in range(n):
            for c in range(cuts):
                size = depth // cuts
                source = refs[j].at[pl.ds(first + c * size, size)]
                copies.append(
                    pltpu.make_async_copy(source, outs[j].at[c * size:(c + 1) * size], sem.at[j * cuts + c])
                )
        for copy in copies:
            copy.start()
        for copy in copies:
            copy.wait()

    return pl.pallas_call(
        kernel,
        in_specs=[SMEM] + [HBM] * n + [ANY] * len(others),
        out_specs=[VMEM] * n,
        out_shape=[jax.ShapeDtypeStruct((depth, width), BF16)] * n,
        scratch_shapes=[pltpu.SemaphoreType.DMA((n * cuts,))],
        cost_estimate=cost(0, 2 * n * depth * width),
        compiler_params=PARAMS,
        name="fetch",
    )(jnp.reshape(block, (1,)).astype(I32), *matrices, *others)


def fetched_weights(matrices, queries, dtype):
    depth = matrices[0].shape[0]
    total = queries[0].shape[1]
    tile = 512 if depth % 512 == 0 else depth
    n = len(matrices)

    def kernel(*refs):
        parts = [jnp.concatenate([r[...] for r in refs[n + CUTS * j:n + CUTS * (j + 1)]]) for j in range(n)]
        for at in range(0, depth, tile):
            value = None
            for j in range(n):
                part = dot(refs[j][at:at + tile, :], parts[j])
                value = part if value is None else value + part
            refs[-1][at:at + tile, :] = value.astype(dtype)

    return pl.pallas_call(
        kernel,
        in_specs=[VMEM] * ((1 + CUTS) * n),
        out_specs=VMEM,
        out_shape=jax.ShapeDtypeStruct((depth, total), dtype),
        cost_estimate=cost(2 * n * matrices[0].size * total, 2 * n * matrices[0].size),
        compiler_params=PARAMS,
        name="fetched_weights",
    )(*matrices, *queries)


def row_table(ids, lines, bulk, extra, *others):
    n_shard = ids.shape[0] // lines

    def kernel(ids_ref, *rest):
        table_ref, flag_ref = rest[-2:]
        me = lax.axis_index("shard")
        start = jnp.int32(0)
        most = jnp.int32(0)
        for s in range(n_shard):
            line = ids_ref[s * lines:(s + 1) * lines, :]

            def count(c):
                return jnp.sum((line == c).astype(I32))

            mine = count(me)
            before = jnp.int32(0)
            if extra:
                surplus = jnp.int32(0)
                for c in range(n_shard):
                    over = lax.div(jnp.maximum(count(c) - bulk, 0) + 15, jnp.int32(16)) * 16
                    before = before + jnp.where(c < me, over, 0)
                    surplus = surplus + over
                most = jnp.maximum(most, surplus)
            table_ref[s, 0] = start
            table_ref[s, 1] = jnp.minimum(mine, bulk)
            table_ref[s, 2] = lax.div(before, jnp.int32(16))
            table_ref[s, 3] = jnp.maximum(mine - bulk, 0)
            start = start + mine
        flag_ref[...] = jnp.full((8, LANES), (most > extra).astype(I32))

    return pl.pallas_call(
        kernel,
        in_specs=[VMEM] + [ANY] * len(others),
        out_specs=[SMEM, VMEM],
        out_shape=[jax.ShapeDtypeStruct((n_shard, 4), I32), jax.ShapeDtypeStruct((8, LANES), I32)],
        cost_estimate=cost(0, 4 * ids.size),
        compiler_params=PARAMS,
        name="row_table",
    )(ids, *others)


def put(acc, x, start, count=None):
    tiles, _, width = x.shape
    first, within = lax.div(start, jnp.int32(8)), lax.rem(start, jnp.int32(8))
    turned = pltpu.roll(x, within, 1)
    row = lax.broadcasted_iota(I32, (1, 8, width), 1)
    keep = row < within
    pieces = jnp.where(keep, jnp.concatenate([turned[:1], turned]), jnp.concatenate([turned, turned[-1:]]))
    if count is None:
        pieces = jnp.concatenate([jnp.where(keep, acc[pl.ds(first, 1)], turned[:1]), pieces[1:]])
    else:
        at = lax.broadcasted_iota(I32, (tiles + 1, 8, width), 0) * 8 + lax.broadcasted_iota(
            I32, (tiles + 1, 8, width), 1
        )
        pieces = jnp.where(
            (at >= within) & (at < within + count), pieces, acc[pl.ds(first, tiles + 1)]
        )
    acc[pl.ds(first, tiles + 1)] = pieces


def score(weight_ref, parts, rep):
    total = None
    for d, x in enumerate(parts):
        depth = x.shape[1]
        block = pl.ds(pl.multiple_of(lax.rem(rep + (len(parts) - d), jnp.int32(len(parts))) * depth, depth), depth)
        value = dot(x, weight_ref[block, :])
        total = value if total is None else total + value
    width = total.shape[1] // 2
    total = total[:, :width] + total[:, width:]
    return total.reshape(total.shape[0] // 8, 8, width)


def for_feats(value, outs):
    n = len(outs)
    share = outs[0].shape[1]
    for f in range(n):
        @pl.when(lax.axis_index("feat") == f)
        def _():
            for d, out in enumerate(outs):
                at = ((f + d) % n) * share
                out[...] = value(slice(at, at + share)).astype(out.dtype)


def feat_shapes(rows, width, n_feat):
    share = (rows, width // n_feat)
    return [jax.ShapeDtypeStruct(share, F32)] + [jax.ShapeDtypeStruct(share, BF16)] * (n_feat - 1)


def early_scores(own, others, mine, pieces, cuts, firsts, seconds, table, rows, n_feat, n_rep, n_shard, bulk, extra):
    depth, width = own.shape
    columns = depth // n_rep
    n_other, n_piece = len(others), len(pieces)
    n_first = len(firsts) * n_rep
    last_hops = n_shard - 1

    def kernel(table_ref, *refs):
        own_ref, refs = refs[0], refs[1:]
        other_refs, refs = refs[:n_other], refs[n_other:]
        mine_ref, refs = refs[0], refs[1:]
        piece_refs = [refs[j * n_rep:(j + 1) * n_rep] for j in range(n_piece)]
        refs = refs[n_piece * n_rep:]
        first_refs, second_refs, refs = refs[:n_first], refs[n_first:2 * n_first], refs[2 * n_first:]
        weight_ref, outs, (scored, held, acc, sem) = refs[0], refs[1:-4], refs[-4:]
        me, rep = lax.axis_index("shard"), lax.axis_index("rep")

        def surplus_copies(s, odd):
            apart = jnp.bitwise_xor(me, s)
            rows_in = pl.ds(pl.multiple_of(lax.div(apart, jnp.int32(2)) * extra, extra), extra)
            copies = []
            for j, refs in enumerate([first_refs, second_refs]):
                for d in range(n_rep):
                    goal = held.at[s, d, j * extra:(j + 1) * extra]
                    which = refs[odd * n_rep + d].at[rows_in]
                    copies.append(pltpu.make_async_copy(which, goal, sem.at[s, j * n_rep + d]))
            return copies

        for s in range(n_shard if extra else 0):
            for odd in range(2):
                @pl.when((table_ref[s, 3] > 0) & (jnp.bitwise_and(jnp.bitwise_xor(me, s), 1) == odd))
                def _():
                    for copy in surplus_copies(s, odd):
                        copy.start()

        weight = own_ref[...]
        for ref in other_refs:
            weight = weight + ref[...].astype(F32)
        high = weight.astype(BF16)
        weight_ref[:, :width] = high
        weight_ref[:, width:] = (weight - high.astype(F32)).astype(BF16)

        scored[me] = score(weight_ref, [mine_ref[...]], jnp.int32(0))
        for parts, (hops, first, size) in zip(piece_refs, cuts):
            source = lax.rem(me + (n_shard - hops), jnp.int32(n_shard))
            scored[source, first // 8:(first + size) // 8] = score(weight_ref, [p[...] for p in parts], rep)
        last = lax.rem(me + (n_shard - last_hops), jnp.int32(n_shard))
        for s in range(n_shard):
            start = table_ref[s, 0]

            @pl.when(last != s)
            def _():
                put(acc, scored[s], start)

            if extra:
                @pl.when(table_ref[s, 3] > 0)
                def _():
                    for copy in surplus_copies(s, 0):
                        copy.wait()
                    some = pl.ds(pl.multiple_of(table_ref[s, 2] * 16, 16), extra)
                    x = [held[s, d, some, :] for d in range(n_rep)]
                    put(acc, score(weight_ref, x, rep), start + table_ref[s, 1])
        for_feats(lambda at: acc[:rows // 8, :, at].reshape(rows, width // n_feat), outs)

    count = n_shard * bulk
    surplus = [x for parts in [*firsts, *seconds] for x in parts]
    return pl.pallas_call(
        kernel,
        in_specs=[SMEM] + [VMEM] * (2 + n_other + n_rep * n_piece) + [ANY] * len(surplus),
        out_specs=[VMEM] * (1 + n_feat),
        out_shape=[jax.ShapeDtypeStruct((depth, 2 * width), BF16)] + feat_shapes(rows, width, n_feat),
        scratch_shapes=[
            pltpu.VMEM((n_shard, bulk // 8, 8, width), F32),
            pltpu.VMEM((n_shard if extra else 1, n_rep, 3 * extra + 16, columns), BF16),
            pltpu.VMEM(((rows + bulk + extra) // 8 + 2, 8, width), F32),
            pltpu.SemaphoreType.DMA((n_shard, 2 * n_rep)),
        ],
        cost_estimate=cost(4 * count * depth * width, 10 * depth * width + count * (2 * depth + 4 * width)),
        compiler_params=WIDE,
        name="early_scores",
    )(table, own, *others, mine, *[p for parts in pieces for p in parts], *surplus)


def late_scores(pieces, weight, n_feat):
    n, n_rep = len(pieces), len(pieces[0])
    rows = sum(parts[0].shape[0] for parts in pieces)
    width = weight.shape[1] // 2

    def kernel(weight_ref, *refs):
        part_refs, outs, acc = refs[:n * n_rep], refs[n * n_rep:-1], refs[-1]
        parts = [jnp.concatenate([part_refs[j * n_rep + d][...] for j in range(n)]) for d in range(n_rep)]
        acc[...] = score(weight_ref, parts, lax.axis_index("rep")).reshape(rows, width)
        for_feats(lambda at: acc[:, at], outs)

    return pl.pallas_call(
        kernel,
        in_specs=[VMEM] * (1 + n * n_rep),
        out_specs=[VMEM] * n_feat,
        out_shape=feat_shapes(rows, width, n_feat),
        scratch_shapes=[pltpu.VMEM((rows, width), F32)],
        cost_estimate=cost(4 * rows * weight.size, 8 * rows * width),
        compiler_params=PARAMS,
        name="late_scores",
    )(weight, *[p for parts in pieces for p in parts])


def merge(table, early, late, n_shard):
    rows, width = early[0].shape
    last_rows = late[0].shape[0]
    last_hops = n_shard - 1

    def kernel(table_ref, *refs):
        early_refs, late_refs = refs[:len(early)], refs[len(early):-2]
        out_ref, acc = refs[-2:]
        source = lax.rem(lax.axis_index("shard") + (n_shard - last_hops), jnp.int32(n_shard))

        def total(parts):
            value = parts[0][...]
            for ref in parts[1:]:
                value = value + ref[...].astype(F32)
            return value.reshape(value.shape[0] // 8, 8, width)

        acc[:rows // 8] = total(early_refs)
        put(acc, total(late_refs), table_ref[source, 0], table_ref[source, 1])
        out_ref[...] = acc[:rows // 8].reshape(rows, width).T

    return pl.pallas_call(
        kernel,
        in_specs=[SMEM] + [VMEM] * (len(early) + len(late)),
        out_specs=VMEM,
        out_shape=jax.ShapeDtypeStruct((width, rows), F32),
        scratch_shapes=[pltpu.VMEM(((rows + last_rows) // 8 + 2, 8, width), F32)],
        cost_estimate=cost(0, 8 * rows * width),
        compiler_params=PARAMS,
        name="merge",
    )(table, *early, *late)


def body(train, cluster_ids, precond, query_store, block_slot, pattern):
    n_group, n_shard = lax.axis_size("groups"), lax.axis_size("shard")
    n_feat, n_rep = lax.axis_size("feat"), lax.axis_size("rep")
    feat, rep = lax.axis_index("feat"), lax.axis_index("rep")
    rows = train.shape[0]
    lines = rows // LANES
    base = rows // n_shard
    columns = train.shape[1] // n_rep
    extra = base // 2 if n_shard == 4 else 0
    bulk = base if extra else base + base // 2
    ids = cluster_ids.reshape(-1, LANES)

    last_hops = n_shard - 1

    def with_rep(x):
        return [x] + [shift(x, "rep", n_rep, d) for d in range(1, n_rep)]

    matrices = with_rep(precond[0])

    picked = pick_queries(query_store, block_slot, pattern, n_group)
    pieces = [picked[0]] + [shift(picked[d], "shard", n_shard, d) for d in range(1, n_shard)]

    middle = [(d, 0, bulk) for d in range(1, last_hops)]
    fillers = 2 if bulk % 256 == 0 else 1
    sizes = [n * bulk // 16 for n in ((3, 2, 4, 4, 3) if bulk % 256 == 0 else (8, 8))]
    final = [(last_hops, sum(sizes[:j]), n) for j, n in enumerate(sizes)]
    *packed, goal = pack_rows(train, ids, columns, bulk, extra, middle + final)
    firsts, seconds = [], []
    parts = [pieces] + [[shift(x, "groups", n_group, d) for x in pieces] for d in range(1, n_group)]
    here = [shift(after(packed[0], *pieces[1:]), "shard", n_shard, 1)]
    urgent = [here[0]]
    if extra:
        far = swap(after(packed[-2], *pieces[1:]), "shard", n_shard, 2)
        urgent.append(far)
    sent_last = packed[len(middle):len(middle) + len(final)]
    last = [shift(after(x, *pieces[1:]), "shard", n_shard, last_hops) for x in sent_last[:fillers]]
    urgent += last
    depth = n_rep * columns
    targets = [(feat + d) % n_feat for d in range(1, n_feat)]
    near_chip = fetch(matrices, targets[0], depth, *pieces[1:])

    table, flag = row_table(ids, lines, bulk, extra, *pieces[1:])
    chosen = join_queries(
        parts, block_slot, pattern, query_store.shape[0], n_feat, n_rep, *near_chip, flag
    )
    queries = [*chosen[:CUTS]] + [shift(chosen[j], "rep", n_rep, j // CUTS) for j in range(CUTS, CUTS * n_rep)]

    sends = [fetched_weights(near_chip, queries, BF16)]
    sends += [partial_weights(matrices, queries, f, depth, BF16) for f in targets[1:]]
    others = [shift(x, "feat", n_feat, d + 1) for d, x in enumerate(sends)]
    own = partial_weights(matrices, queries, feat, depth, F32, *sends)

    for (hops, _, _), x in zip(middle[1:], packed[1:]):
        here.append(shift(after(x, *urgent, *sends), "shard", n_shard, hops))
        urgent = [here[-1]]
    sent_last = [after(x, own) for x in sent_last[fillers:]]
    last_all = [with_rep(after(x, own)) for x in last]

    mine = own_rows(goal, train, bulk, own)
    marks = [own, mine, *sent_last, *[p for x in last_all for p in x[1:]]]
    if extra:
        for d in range(1, n_group):
            flag = jnp.maximum(flag, shift(flag, "groups", n_group, d))

        def second_round(x):
            pair = jnp.concatenate([x, swap(x, "shard", n_shard, 2)])
            return [with_rep(pair), with_rep(swap(pair, "shard", n_shard, 1))]

        def no_round(x):
            empty = unwritten((2 * extra, columns), 2 * n_rep)
            return [[*empty[:n_rep]], [*empty[n_rep:]]]

        seconds = lax.cond(flag[0, 0] > 0, second_round, no_round, after(packed[-1], own))
        near = swap(stack([packed[-3], far], *sends), "shard", n_shard, 1)
        pairs = [stack([x, y], own) for x, y in zip(with_rep(packed[-3]), with_rep(after(far, own)))]
        firsts = [pairs, with_rep(after(near, own))]
        marks += [seconds[0][0], near, *pairs]

    mark = shift(after(jnp.zeros((8, LANES), I32), *marks), "rep", n_rep, 1)
    last += [shift(x, "shard", n_shard, last_hops) for x in sent_last]
    ready = [with_rep(after(x, mark)) for x in here]
    weight, *early = early_scores(
        own, others, mine, ready, middle, firsts, seconds, table, rows, n_feat, n_rep, n_shard, bulk, extra
    )

    def over_feat(shares):
        return [shares[0]] + [shift(shares[d], "feat", n_feat, d) for d in range(1, n_feat)]

    last_all += [with_rep(after(x, *early[1:])) for x in last[fillers:]]
    late = late_scores(last_all, weight, n_feat)
    return merge(table, over_feat(early), over_feat(late), n_shard)[None]


def solution(mesh):
    return jax.shard_map(
        body,
        mesh=mesh,
        in_specs=(
            P(("groups", "shard"), "feat"),
            P("groups"),
            P(("groups", "shard"), None, ("feat", "rep")),
            P("shard", None, ("feat", "rep")),
            P(),
            P(),
        ),
        out_specs=P(("groups", "shard"), ("feat", "rep"), None),
        check_vma=False,
    )
```

```python
import functools

import jax
import jax.numpy as jnp
from jax import lax
from jax.experimental import pallas as pl
from jax.experimental.pallas import tpu as pltpu
from jax.sharding import PartitionSpec as P

F32, BF16, I32 = jnp.float32, jnp.bfloat16, jnp.int32
VMEM = pl.BlockSpec(memory_space=pltpu.VMEM)
ANY = pl.BlockSpec(memory_space=pl.ANY)
HBM = pl.BlockSpec(memory_space=pltpu.HBM)
SMEM = pl.BlockSpec(memory_space=pltpu.SMEM)
PARAMS = pltpu.CompilerParams(vmem_limit_bytes=24 * 2**20)
WIDE = pltpu.CompilerParams(vmem_limit_bytes=32 * 2**20)
FIRST = pltpu.CompilerParams(vmem_limit_bytes=60 * 2**20)
LANES = 128
CUTS = 8


def shift(x, axis, size, by):
    return lax.ppermute(x, axis, [(i, (i + by) % size) for i in range(size)])


def swap(x, axis, size, bit):
    return lax.ppermute(x, axis, [(i, i ^ bit) for i in range(size)])


def dot(a, b):
    return jnp.dot(a, b, preferred_element_type=F32)


def cost(flops, nbytes):
    return pl.CostEstimate(flops=1, bytes_accessed=1, transcendentals=0)


def after(x, *others):
    def kernel(*refs):
        pass

    return pl.pallas_call(
        kernel,
        in_specs=[ANY] * (1 + len(others)),
        out_specs=ANY,
        out_shape=jax.ShapeDtypeStruct(x.shape, x.dtype),
        input_output_aliases={0: 0},
        cost_estimate=cost(0, 0),
        compiler_params=PARAMS,
        name="after",
    )(x, *others)


def unwritten(shape, n):
    def kernel(*refs):
        pass

    return pl.pallas_call(
        kernel,
        out_specs=[ANY] * n,
        out_shape=[jax.ShapeDtypeStruct(shape, BF16)] * n,
        cost_estimate=cost(0, 0),
        compiler_params=PARAMS,
        name="unwritten",
    )()


def stack(parts, *others):
    size, width = parts[0].shape
    n = len(parts)

    def kernel(*refs):
        for j in range(n):
            refs[-1][j * size:(j + 1) * size, :] = refs[j][...]

    return pl.pallas_call(
        kernel,
        in_specs=[VMEM] * n + [ANY] * len(others),
        out_specs=VMEM,
        out_shape=jax.ShapeDtypeStruct((n * size, width), parts[0].dtype),
        cost_estimate=cost(0, 0),
        compiler_params=PARAMS,
        name="stack",
    )(*parts, *others)


def pick_queries(query_store, block_slot, pattern, n_group):
    local_blocks, block_rows, width = query_store.shape
    n_cluster, n_list = pattern.shape
    part = block_rows // n_group

    def kernel(pattern_ref, slot_ref, in_ref, *outs):
        me = lax.axis_index("shard")
        for t, out in enumerate(outs):
            target = lax.rem(me + t, jnp.int32(n_cluster))
            found = jnp.int32(0)
            for k in range(n_list):
                slot = slot_ref[pattern_ref[target, k]]
                hit = (lax.div(slot, jnp.int32(local_blocks)) == me).astype(I32)
                found = found + hit * lax.rem(slot, jnp.int32(local_blocks))
            out[0] = in_ref[found]

    return pl.pallas_call(
        kernel,
        grid=(1,),
        in_specs=[SMEM, SMEM, pl.BlockSpec((local_blocks, part, width), lambda i: (0, lax.axis_index("groups"), 0))],
        out_specs=[VMEM] * n_cluster,
        out_shape=[jax.ShapeDtypeStruct((1, part, width), BF16)] * n_cluster,
        cost_estimate=cost(0, 4 * n_cluster * part * width),
        compiler_params=FIRST,
        name="pick_queries",
    )(pattern, block_slot, query_store)


def join_queries(parts, block_slot, pattern, local_blocks, n_feat, n_rep, *others):
    n_group, n_cluster = len(parts), len(parts[0])
    _, part, width = parts[0][0].shape
    n_list = pattern.shape[1]
    total = n_list * n_group * part
    share = total // (n_feat * n_rep)
    unit = min(share, part)
    half = total // n_rep

    def kernel(pattern_ref, slot_ref, *refs):
        outs, rows_ref = refs[-1 - CUTS * n_rep:-1], refs[-1]
        me, group = lax.axis_index("shard"), lax.axis_index("groups")
        for k in range(n_list):
            owner = lax.div(slot_ref[pattern_ref[me, k]], jnp.int32(local_blocks))
            hops = lax.rem(me + (n_cluster - owner), jnp.int32(n_cluster))
            for d in range(n_group):
                origin = lax.rem(group + (n_group - d), jnp.int32(n_group))
                for h in range(n_cluster):
                    @pl.when(hops == h)
                    def _():
                        for u in range(part // unit):
                            first = (k * n_group + origin) * part + u * unit
                            chunk = lax.div(first, jnp.int32(share))
                            goal = lax.rem(chunk, jnp.int32(n_rep)) * n_feat + lax.div(chunk, jnp.int32(n_rep))
                            goal = pl.multiple_of(goal * share + lax.rem(first, jnp.int32(share)), unit)
                            rows_ref[pl.ds(goal, unit), :] = refs[d * n_cluster + h][0, u * unit:(u + 1) * unit, :]
        for r in range(n_rep):
            @pl.when(lax.axis_index("rep") == r)
            def _():
                for j, out in enumerate(outs):
                    at, first = ((r + j // CUTS) % n_rep) * half, (j % CUTS) * (width // CUTS)
                    out[...] = rows_ref[at:at + half, first:first + width // CUTS].T

    return pl.pallas_call(
        kernel,
        in_specs=[SMEM, SMEM] + [VMEM] * (n_group * n_cluster) + [ANY] * len(others),
        out_specs=[VMEM] * (CUTS * n_rep),
        out_shape=[jax.ShapeDtypeStruct((width // CUTS, half), BF16)] * (CUTS * n_rep),
        scratch_shapes=[pltpu.VMEM((total, width), BF16)],
        cost_estimate=cost(0, 4 * total * width),
        compiler_params=PARAMS,
        name="join_queries",
    )(pattern, block_slot, *[x for line in parts for x in line], *others)


def one_hot(goal_ref, base, size):
    index = lax.broadcasted_iota(I32, (size, LANES), 0) + base
    lines = range(goal_ref.shape[0])
    return jnp.concatenate([(index == goal_ref[a:a + 1, :]).astype(F32).astype(BF16) for a in lines], axis=1)


def select(goal_ref, train_ref, base, size):
    tile = 128 if size % 128 == 0 else size
    found = [dot(one_hot(goal_ref, base + at, tile), train_ref[...]).astype(BF16) for at in range(0, size, tile)]
    return jnp.concatenate(found)


def own_rows(goal, train, bulk, *others):
    rows, width = train.shape
    cuts = 4
    part = width // cuts

    def kernel(goal_ref, train_ref, *rest):
        out_ref, held, sem = rest[-3:]
        copies = [
            pltpu.make_async_copy(train_ref.at[:, c * part:(c + 1) * part], held.at[c], sem.at[c]) for c in range(cuts)
        ]
        for copy in copies:
            copy.start()
        pick = one_hot(goal_ref, lax.axis_index("shard") * bulk, bulk)
        for c, copy in enumerate(copies):
            copy.wait()
            out_ref[:, c * part:(c + 1) * part] = dot(pick, held[c]).astype(BF16)

    return pl.pallas_call(
        kernel,
        in_specs=[VMEM, HBM] + [ANY] * len(others),
        out_specs=VMEM,
        out_shape=jax.ShapeDtypeStruct((bulk, width), BF16),
        scratch_shapes=[pltpu.VMEM((cuts, rows, part), BF16), pltpu.SemaphoreType.DMA((cuts,))],
        cost_estimate=cost(2 * bulk * train.size, 2 * train.size),
        compiler_params=PARAMS,
        name="own_rows",
    )(goal, train, *others)


def pack_rows(train, ids, columns, bulk, extra, cuts):
    rows = train.shape[0]
    lines = rows // LANES
    n_shard = ids.shape[0] // lines

    def kernel(ids_ref, train_ref, *rest):
        outs, goal_ref, held, sem = rest[:-3], rest[-3], rest[-2], rest[-1]
        me = lax.axis_index("shard")
        mine = pl.ds(pl.multiple_of(lax.axis_index("rep") * columns, columns), columns)
        copy = pltpu.make_async_copy(train_ref.at[:, mine], held, sem)
        copy.start()
        own = ids_ref[...]
        masks = [(own == c).astype(F32) for c in range(n_shard)]
        stacked = jnp.concatenate(masks, axis=0).astype(BF16)
        lane_from = lax.broadcasted_iota(I32, (LANES, LANES), 0)
        lane_to = lax.broadcasted_iota(I32, (LANES, LANES), 1)
        in_line = dot(stacked, (lane_from < lane_to).astype(F32).astype(BF16))
        line_sum = dot(stacked, jnp.ones((LANES, LANES), BF16)).astype(BF16)
        size = n_shard * lines
        to = lax.broadcasted_iota(I32, (size, size), 0)
        since = lax.broadcasted_iota(I32, (size, size), 1)
        same = (to // lines) == (since // lines)
        ahead = dot((same & (since < to)).astype(F32).astype(BF16), line_sum)
        whole = dot(same.astype(F32).astype(BF16), line_sum)
        rank = in_line + ahead
        goal = jnp.zeros((lines, LANES), F32)
        past = jnp.zeros((lines, LANES), F32)
        for c in range(n_shard):
            part = slice(c * lines, (c + 1) * lines)
            place = rank[part] + c * bulk
            if extra:
                surplus = n_shard * bulk + past + rank[part] - bulk
                place = jnp.where(rank[part] < bulk, place, surplus)
                past = past + jnp.floor((jnp.maximum(whole[part] - bulk, 0.0) + 15.0) * 0.0625) * 16.0
            goal = goal + masks[c] * place
        goal_ref[...] = goal.astype(I32)

        copy.wait()

        def fill(out, base):
            out[...] = select(goal_ref, held, base, out.shape[0])

        for out, (hops, first, _) in zip(outs, cuts):
            fill(out, lax.rem(me + hops, jnp.int32(n_shard)) * bulk + first)
        for j, out in enumerate(outs[len(cuts):]):
            fill(out, n_shard * bulk + max(j - 1, 0) * extra)

    shapes = [jax.ShapeDtypeStruct((n, columns), BF16) for _, _, n in cuts]
    shapes += [jax.ShapeDtypeStruct((extra, columns), BF16)] * (3 if extra else 0)
    shapes += [jax.ShapeDtypeStruct((lines, LANES), I32)]
    packed = n_shard * bulk + 2 * extra
    return pl.pallas_call(
        kernel,
        grid=(1,),
        in_specs=[
            pl.BlockSpec((lines, LANES), lambda i: (lax.axis_index("shard"), 0)),
            ANY,
        ],
        out_specs=[VMEM] * len(shapes),
        out_shape=shapes,
        scratch_shapes=[pltpu.VMEM((rows, columns), BF16), pltpu.SemaphoreType.DMA],
        cost_estimate=cost(2 * packed * rows * columns, 2 * (rows + packed) * columns),
        compiler_params=FIRST,
        name="pack_rows",
    )(ids, train)


def partial_weights(matrices, queries, block, depth, dtype, *others):
    width, total = matrices[0].shape[1], queries[0].shape[1]
    tile = 512 if depth % 512 == 0 else depth
    steps = depth // tile
    n = len(matrices)

    def kernel(block_ref, *refs):
        out_ref, held, sem = refs[-3:]
        first = pl.multiple_of(block_ref[0] * depth, depth)
        copies = []
        for i in range(steps):
            for j in range(n):
                source = refs[j].at[pl.ds(first + i * tile, tile)]
                copies.append(pltpu.make_async_copy(source, held.at[j, i], sem.at[i * n + j]))
        for copy in copies:
            copy.start()
        parts = [jnp.concatenate([r[...] for r in refs[n + CUTS * j:n + CUTS * (j + 1)]]) for j in range(n)]
        for i in range(steps):
            value = None
            for j in range(n):
                copies[i * n + j].wait()
                part = dot(held[j, i], parts[j])
                value = part if value is None else value + part
            out_ref[i * tile:(i + 1) * tile, :] = value.astype(dtype)

    return pl.pallas_call(
        kernel,
        in_specs=[SMEM] + [HBM] * n + [VMEM] * (CUTS * n) + [ANY] * len(others),
        out_specs=VMEM,
        out_shape=jax.ShapeDtypeStruct((depth, total), dtype),
        scratch_shapes=[pltpu.VMEM((n, steps, tile, width), BF16), pltpu.SemaphoreType.DMA((steps * n,))],
        cost_estimate=cost(2 * n * depth * width * total, 2 * n * depth * width + 4 * depth * total),
        compiler_params=PARAMS,
        name="partial_weights",
    )(jnp.reshape(block, (1,)).astype(I32), *matrices, *queries, *others)


def fetch(matrices, block, depth, *others):
    width = matrices[0].shape[1]
    n = len(matrices)
    cuts = 4

    def kernel(block_ref, *refs):
        outs, sem = refs[-1 - n:-1], refs[-1]
        first = pl.multiple_of(block_ref[0] * depth, depth)
        copies = []
        for j in range(n):
            for c in range(cuts):
                size = depth // cuts
                source = refs[j].at[pl.ds(first + c * size, size)]
                copies.append(
                    pltpu.make_async_copy(source, outs[j].at[c * size:(c + 1) * size], sem.at[j * cuts + c])
                )
        for copy in copies:
            copy.start()
        for copy in copies:
            copy.wait()

    return pl.pallas_call(
        kernel,
        in_specs=[SMEM] + [HBM] * n + [ANY] * len(others),
        out_specs=[VMEM] * n,
        out_shape=[jax.ShapeDtypeStruct((depth, width), BF16)] * n,
        scratch_shapes=[pltpu.SemaphoreType.DMA((n * cuts,))],
        cost_estimate=cost(0, 2 * n * depth * width),
        compiler_params=PARAMS,
        name="fetch",
    )(jnp.reshape(block, (1,)).astype(I32), *matrices, *others)


def fetched_weights(matrices, queries, dtype):
    depth = matrices[0].shape[0]
    total = queries[0].shape[1]
    tile = 512 if depth % 512 == 0 else depth
    n = len(matrices)

    def kernel(*refs):
        parts = [jnp.concatenate([r[...] for r in refs[n + CUTS * j:n + CUTS * (j + 1)]]) for j in range(n)]
        for at in range(0, depth, tile):
            value = None
            for j in range(n):
                part = dot(refs[j][at:at + tile, :], parts[j])
                value = part if value is None else value + part
            refs[-1][at:at + tile, :] = value.astype(dtype)

    return pl.pallas_call(
        kernel,
        in_specs=[VMEM] * ((1 + CUTS) * n),
        out_specs=VMEM,
        out_shape=jax.ShapeDtypeStruct((depth, total), dtype),
        cost_estimate=cost(2 * n * matrices[0].size * total, 2 * n * matrices[0].size),
        compiler_params=PARAMS,
        name="fetched_weights",
    )(*matrices, *queries)


def row_table(ids, lines, bulk, extra, *others):
    n_shard = ids.shape[0] // lines

    def kernel(ids_ref, *rest):
        table_ref, flag_ref = rest[-2:]
        me = lax.axis_index("shard")
        start = jnp.int32(0)
        most = jnp.int32(0)
        for s in range(n_shard):
            line = ids_ref[s * lines:(s + 1) * lines, :]

            def count(c):
                return jnp.sum((line == c).astype(I32))

            mine = count(me)
            before = jnp.int32(0)
            if extra:
                surplus = jnp.int32(0)
                for c in range(n_shard):
                    over = lax.div(jnp.maximum(count(c) - bulk, 0) + 15, jnp.int32(16)) * 16
                    before = before + jnp.where(c < me, over, 0)
                    surplus = surplus + over
                most = jnp.maximum(most, surplus)
            table_ref[s, 0] = start
            table_ref[s, 1] = jnp.minimum(mine, bulk)
            table_ref[s, 2] = lax.div(before, jnp.int32(16))
            table_ref[s, 3] = jnp.maximum(mine - bulk, 0)
            start = start + mine
        flag_ref[...] = jnp.full((8, LANES), (most > extra).astype(I32))

    return pl.pallas_call(
        kernel,
        in_specs=[VMEM] + [ANY] * len(others),
        out_specs=[SMEM, VMEM],
        out_shape=[jax.ShapeDtypeStruct((n_shard, 4), I32), jax.ShapeDtypeStruct((8, LANES), I32)],
        cost_estimate=cost(0, 4 * ids.size),
        compiler_params=PARAMS,
        name="row_table",
    )(ids, *others)


def put(acc, x, start, count=None):
    tiles, _, width = x.shape
    first, within = lax.div(start, jnp.int32(8)), lax.rem(start, jnp.int32(8))
    turned = pltpu.roll(x, within, 1)
    row = lax.broadcasted_iota(I32, (1, 8, width), 1)
    keep = row < within
    pieces = jnp.where(keep, jnp.concatenate([turned[:1], turned]), jnp.concatenate([turned, turned[-1:]]))
    if count is None:
        pieces = jnp.concatenate([jnp.where(keep, acc[pl.ds(first, 1)], turned[:1]), pieces[1:]])
    else:
        at = lax.broadcasted_iota(I32, (tiles + 1, 8, width), 0) * 8 + lax.broadcasted_iota(
            I32, (tiles + 1, 8, width), 1
        )
        pieces = jnp.where(
            (at >= within) & (at < within + count), pieces, acc[pl.ds(first, tiles + 1)]
        )
    acc[pl.ds(first, tiles + 1)] = pieces


def score(weight_ref, parts, rep):
    total = None
    for d, x in enumerate(parts):
        depth = x.shape[1]
        block = pl.ds(pl.multiple_of(lax.rem(rep + (len(parts) - d), jnp.int32(len(parts))) * depth, depth), depth)
        value = dot(x, weight_ref[block, :])
        total = value if total is None else total + value
    width = total.shape[1] // 2
    total = total[:, :width] + total[:, width:]
    return total.reshape(total.shape[0] // 8, 8, width)


def for_feats(value, outs):
    n = len(outs)
    share = outs[0].shape[1]
    for f in range(n):
        @pl.when(lax.axis_index("feat") == f)
        def _():
            for d, out in enumerate(outs):
                at = ((f + d) % n) * share
                out[...] = value(slice(at, at + share)).astype(out.dtype)


def feat_shapes(rows, width, n_feat):
    share = (rows, width // n_feat)
    return [jax.ShapeDtypeStruct(share, F32)] + [jax.ShapeDtypeStruct(share, BF16)] * (n_feat - 1)


def early_scores(own, others, mine, pieces, cuts, firsts, seconds, table, rows, n_feat, n_rep, n_shard, bulk, extra):
    depth, width = own.shape
    columns = depth // n_rep
    n_other, n_piece = len(others), len(pieces)
    n_first = len(firsts) * n_rep
    last_hops = n_shard - 1

    def kernel(table_ref, *refs):
        own_ref, refs = refs[0], refs[1:]
        other_refs, refs = refs[:n_other], refs[n_other:]
        mine_ref, refs = refs[0], refs[1:]
        piece_refs = [refs[j * n_rep:(j + 1) * n_rep] for j in range(n_piece)]
        refs = refs[n_piece * n_rep:]
        first_refs, second_refs, refs = refs[:n_first], refs[n_first:2 * n_first], refs[2 * n_first:]
        weight_ref, outs, (scored, held, acc, sem) = refs[0], refs[1:-4], refs[-4:]
        me, rep = lax.axis_index("shard"), lax.axis_index("rep")

        def surplus_copies(s, odd):
            apart = jnp.bitwise_xor(me, s)
            rows_in = pl.ds(pl.multiple_of(lax.div(apart, jnp.int32(2)) * extra, extra), extra)
            copies = []
            for j, refs in enumerate([first_refs, second_refs]):
                for d in range(n_rep):
                    goal = held.at[s, d, j * extra:(j + 1) * extra]
                    which = refs[odd * n_rep + d].at[rows_in]
                    copies.append(pltpu.make_async_copy(which, goal, sem.at[s, j * n_rep + d]))
            return copies

        for s in range(n_shard if extra else 0):
            for odd in range(2):
                @pl.when((table_ref[s, 3] > 0) & (jnp.bitwise_and(jnp.bitwise_xor(me, s), 1) == odd))
                def _():
                    for copy in surplus_copies(s, odd):
                        copy.start()

        weight = own_ref[...]
        for ref in other_refs:
            weight = weight + ref[...].astype(F32)
        high = weight.astype(BF16)
        weight_ref[:, :width] = high
        weight_ref[:, width:] = (weight - high.astype(F32)).astype(BF16)

        scored[me] = score(weight_ref, [mine_ref[...]], jnp.int32(0))
        for parts, (hops, first, size) in zip(piece_refs, cuts):
            source = lax.rem(me + (n_shard - hops), jnp.int32(n_shard))
            scored[source, first // 8:(first + size) // 8] = score(weight_ref, [p[...] for p in parts], rep)
        last = lax.rem(me + (n_shard - last_hops), jnp.int32(n_shard))
        for s in range(n_shard):
            start = table_ref[s, 0]

            @pl.when(last != s)
            def _():
                put(acc, scored[s], start)

            if extra:
                @pl.when(table_ref[s, 3] > 0)
                def _():
                    for copy in surplus_copies(s, 0):
                        copy.wait()
                    some = pl.ds(pl.multiple_of(table_ref[s, 2] * 16, 16), extra)
                    x = [held[s, d, some, :] for d in range(n_rep)]
                    put(acc, score(weight_ref, x, rep), start + table_ref[s, 1])
        for_feats(lambda at: acc[:rows // 8, :, at].reshape(rows, width // n_feat), outs)

    count = n_shard * bulk
    surplus = [x for parts in [*firsts, *seconds] for x in parts]
    return pl.pallas_call(
        kernel,
        in_specs=[SMEM] + [VMEM] * (2 + n_other + n_rep * n_piece) + [ANY] * len(surplus),
        out_specs=[VMEM] * (1 + n_feat),
        out_shape=[jax.ShapeDtypeStruct((depth, 2 * width), BF16)] + feat_shapes(rows, width, n_feat),
        scratch_shapes=[
            pltpu.VMEM((n_shard, bulk // 8, 8, width), F32),
            pltpu.VMEM((n_shard if extra else 1, n_rep, 3 * extra + 16, columns), BF16),
            pltpu.VMEM(((rows + bulk + extra) // 8 + 2, 8, width), F32),
            pltpu.SemaphoreType.DMA((n_shard, 2 * n_rep)),
        ],
        cost_estimate=cost(4 * count * depth * width, 10 * depth * width + count * (2 * depth + 4 * width)),
        compiler_params=WIDE,
        name="early_scores",
    )(table, own, *others, mine, *[p for parts in pieces for p in parts], *surplus)


def late_scores(pieces, weight, n_feat):
    n, n_rep = len(pieces), len(pieces[0])
    rows = sum(parts[0].shape[0] for parts in pieces)
    width = weight.shape[1] // 2

    def kernel(weight_ref, *refs):
        part_refs, outs, acc = refs[:n * n_rep], refs[n * n_rep:-1], refs[-1]
        parts = [jnp.concatenate([part_refs[j * n_rep + d][...] for j in range(n)]) for d in range(n_rep)]
        acc[...] = score(weight_ref, parts, lax.axis_index("rep")).reshape(rows, width)
        for_feats(lambda at: acc[:, at], outs)

    return pl.pallas_call(
        kernel,
        in_specs=[VMEM] * (1 + n * n_rep),
        out_specs=[VMEM] * n_feat,
        out_shape=feat_shapes(rows, width, n_feat),
        scratch_shapes=[pltpu.VMEM((rows, width), F32)],
        cost_estimate=cost(4 * rows * weight.size, 8 * rows * width),
        compiler_params=PARAMS,
        name="late_scores",
    )(weight, *[p for parts in pieces for p in parts])


def merge(table, early, late, n_shard):
    rows, width = early[0].shape
    last_rows = late[0].shape[0]
    last_hops = n_shard - 1

    def kernel(table_ref, *refs):
        early_refs, late_refs = refs[:len(early)], refs[len(early):-2]
        out_ref, acc = refs[-2:]
        source = lax.rem(lax.axis_index("shard") + (n_shard - last_hops), jnp.int32(n_shard))

        def total(parts):
            value = parts[0][...]
            for ref in parts[1:]:
                value = value + ref[...].astype(F32)
            return value.reshape(value.shape[0] // 8, 8, width)

        acc[:rows // 8] = total(early_refs)
        put(acc, total(late_refs), table_ref[source, 0], table_ref[source, 1])
        out_ref[...] = acc[:rows // 8].reshape(rows, width).T

    return pl.pallas_call(
        kernel,
        in_specs=[SMEM] + [VMEM] * (len(early) + len(late)),
        out_specs=VMEM,
        out_shape=jax.ShapeDtypeStruct((width, rows), F32),
        scratch_shapes=[pltpu.VMEM(((rows + last_rows) // 8 + 2, 8, width), F32)],
        cost_estimate=cost(0, 8 * rows * width),
        compiler_params=PARAMS,
        name="merge",
    )(table, *early, *late)


def body(train, cluster_ids, precond, query_store, block_slot, pattern):
    n_group, n_shard = lax.axis_size("groups"), lax.axis_size("shard")
    n_feat, n_rep = lax.axis_size("feat"), lax.axis_size("rep")
    feat, rep = lax.axis_index("feat"), lax.axis_index("rep")
    rows = train.shape[0]
    lines = rows // LANES
    base = rows // n_shard
    columns = train.shape[1] // n_rep
    extra = base // 2 if n_shard == 4 else 0
    bulk = base if extra else base + base // 2
    ids = cluster_ids.reshape(-1, LANES)

    last_hops = n_shard - 1

    def with_rep(x):
        return [x] + [shift(x, "rep", n_rep, d) for d in range(1, n_rep)]

    matrices = with_rep(precond[0])

    picked = pick_queries(query_store, block_slot, pattern, n_group)
    pieces = [picked[0]] + [shift(picked[d], "shard", n_shard, d) for d in range(1, n_shard)]

    middle = [(d, 0, bulk) for d in range(1, last_hops)]
    fillers = 2 if bulk % 256 == 0 else 1
    sizes = [n * bulk // 16 for n in ((3, 2, 4, 4, 3) if bulk % 256 == 0 else (8, 8))]
    final = [(last_hops, sum(sizes[:j]), n) for j, n in enumerate(sizes)]
    *packed, goal = pack_rows(train, ids, columns, bulk, extra, middle + final)
    firsts, seconds = [], []
    parts = [pieces] + [[shift(x, "groups", n_group, d) for x in pieces] for d in range(1, n_group)]
    here = [shift(after(packed[0], *pieces[1:]), "shard", n_shard, 1)]
    urgent = [here[0]]
    if extra:
        far = swap(after(packed[-2], *pieces[1:]), "shard", n_shard, 2)
        urgent.append(far)
    sent_last = packed[len(middle):len(middle) + len(final)]
    last = [shift(after(x, *pieces[1:]), "shard", n_shard, last_hops) for x in sent_last[:fillers]]
    urgent += last
    depth = n_rep * columns
    targets = [(feat + d) % n_feat for d in range(1, n_feat)]
    near_chip = fetch(matrices, targets[0], depth, *pieces[1:])

    table, flag = row_table(ids, lines, bulk, extra, *pieces[1:])
    chosen = join_queries(
        parts, block_slot, pattern, query_store.shape[0], n_feat, n_rep, *near_chip, flag
    )
    queries = [*chosen[:CUTS]] + [shift(chosen[j], "rep", n_rep, j // CUTS) for j in range(CUTS, CUTS * n_rep)]

    sends = [fetched_weights(near_chip, queries, BF16)]
    sends += [partial_weights(matrices, queries, f, depth, BF16) for f in targets[1:]]
    others = [shift(x, "feat", n_feat, d + 1) for d, x in enumerate(sends)]
    own = partial_weights(matrices, queries, feat, depth, F32, *sends)

    for (hops, _, _), x in zip(middle[1:], packed[1:]):
        here.append(shift(after(x, *urgent, *sends), "shard", n_shard, hops))
        urgent = [here[-1]]
    sent_last = [after(x, own) for x in sent_last[fillers:]]
    last_all = [with_rep(after(x, own)) for x in last]

    mine = own_rows(goal, train, bulk, own)
    marks = [own, mine, *sent_last, *[p for x in last_all for p in x[1:]]]
    if extra:
        for d in range(1, n_group):
            flag = jnp.maximum(flag, shift(flag, "groups", n_group, d))

        def second_round(x):
            pair = jnp.concatenate([x, swap(x, "shard", n_shard, 2)])
            return [with_rep(pair), with_rep(swap(pair, "shard", n_shard, 1))]

        def no_round(x):
            empty = unwritten((2 * extra, columns), 2 * n_rep)
            return [[*empty[:n_rep]], [*empty[n_rep:]]]

        seconds = lax.cond(flag[0, 0] > 0, second_round, no_round, after(packed[-1], own))
        near = swap(stack([packed[-3], far], *sends), "shard", n_shard, 1)
        pairs = [stack([x, y], own) for x, y in zip(with_rep(packed[-3]), with_rep(after(far, own)))]
        firsts = [pairs, with_rep(after(near, own))]
        marks += [seconds[0][0], near, *pairs]

    mark = shift(after(jnp.zeros((8, LANES), I32), *marks), "rep", n_rep, 1)
    last += [shift(x, "shard", n_shard, last_hops) for x in sent_last]
    ready = [with_rep(after(x, mark)) for x in here]
    weight, *early = early_scores(
        own, others, mine, ready, middle, firsts, seconds, table, rows, n_feat, n_rep, n_shard, bulk, extra
    )

    def over_feat(shares):
        return [shares[0]] + [shift(shares[d], "feat", n_feat, d) for d in range(1, n_feat)]

    last_all += [with_rep(after(x, *early[1:])) for x in last[fillers:]]
    late = late_scores(last_all, weight, n_feat)
    return merge(table, over_feat(early), over_feat(late), n_shard)[None]


def solution(mesh):
    return jax.shard_map(
        body,
        mesh=mesh,
        in_specs=(
            P(("groups", "shard"), "feat"),
            P("groups"),
            P(("groups", "shard"), None, ("feat", "rep")),
            P("shard", None, ("feat", "rep")),
            P(),
            P(),
        ),
        out_specs=P(("groups", "shard"), ("feat", "rep"), None),
        check_vma=False,
    )
```
